128 devices in a mesh: gx: 2 (over core), gy: 2 (over z_lo), gzs: 32 (over y, z_hi, x).
Axes of the slice: x: 4, y: 4, z: 4 (z_hi: 2, z_lo: 2; z = z_hi * 2 + z_lo), core: 2. Of those that a mesh axis runs over, the one named last changes fastest.
Arguments:
- states: float32 [32, 32, 512, 128], P('gx', 'gy', 'gzs'), may hold values from -6 to 6
- potential: float32 [32, 32, 512], P('gx', 'gy', 'gzs'), may hold values from -6 to 2
- atom_sites: int32 [512, 3], P(('gx', 'gy', 'gzs')), may hold values from 0 to 511, as said below
- projectors: float32 [512, 9, 9, 9], P(('gx', 'gy', 'gzs')), may hold values from -0.21875 to 0.21875
- energies: float32 [512], P(('gx', 'gy', 'gzs')), may hold values from 2 to 16
Outputs:
- orbitals: float32 [32, 32, 512, 128], P('gx', 'gy', 'gzs')
The draws below stay inside these ranges and needn't reach their ends.
Inputs may be any that keep to these rules, and one draw needn't show every extreme that they name: `atom_sites`: each atom's cell lies in the block of cells held by the device that holds the atom's row: along the first dimension within [16 i, 16 (i + 1)) for that device's index i along gx, and likewise with 16 and gy, 16 and gzs.
All inputs are finite; a program needn't handle non-finite values.
Results may differ from the reference program's by a relative error of at most 0.00005.
Values sent between devices are 32-bit elements; how exact they have to be, the bound alone decides.
No kernel may reach another device: no remote copies, remote signals or barrier semaphores. Data moves between devices by JAX's collectives and lax.ppermute only.
A program may use at most 128 MiB of HBM per device.

```python
import math
import jax
import jax.numpy as jnp
from jax import lax

CX = 16
CY = 16
CZ = 16
ATOM_DEV = 4
S = 128
R = 4
W = 9
NX = 32
NY = 32
NZ = 512
NCELLS = 524288
NATOMS = 512


def draw_atom_sites(key, part):
    key = jax.random.fold_in(key, 11)
    blocks_y = NY // CY
    blocks_z = NZ // CZ
    rows = jnp.arange(NATOMS, dtype=jnp.int32)
    owner = rows // ATOM_DEV
    block_x = owner // (blocks_y * blocks_z)
    block_y = owner // blocks_z % blocks_y
    block_z = owner % blocks_z
    corner = jnp.stack([block_x * CX, block_y * CY, block_z * CZ], axis=1)
    limits = jnp.array([CX, CY, CZ], dtype=jnp.int32)
    inside = jax.random.randint(key, (NATOMS, 3), 0, limits[None, :], dtype=jnp.int32)
    inside = jnp.where((rows == 0)[:, None], jnp.zeros_like(inside), inside)
    inside = jnp.where((rows == NATOMS - 1)[:, None], jnp.broadcast_to(limits[None, :] - 1, inside.shape), inside)
    return (corner + inside).astype(jnp.int32)


def steps_of(rng, extent, pieces, least, high):
    factor_of, own = 1.0, jax.random.fold_in(rng, 6)
    for position, blocks in pieces:
        steps = jnp.exp(jax.random.uniform(jax.random.fold_in(own, position), (blocks,), jnp.float32, least / len(pieces), high / len(pieces)))
        factor_of = factor_of * jnp.repeat(steps, extent[position] // blocks).reshape([-1 if axis == position else 1 for axis in range(len(extent))])
    return factor_of


def normal_values(rng, extent, spread, reach, shards=(), kind=jnp.bfloat16):
    values = jax.random.normal(rng, extent, jnp.float32) * spread
    if len(shards) > 0:
        values = steps_of(rng, extent, shards, -0.22, 0.18) * values
    return jnp.clip(values, min=-reach, max=reach).astype(kind)


def setup_inputs(seed: int = 0) -> dict:
    splits = jax.random.split(jax.random.key(seed), 6)
    states = normal_values(splits[0], (NX, NY, NZ, S), 1.0, 6.0, ((0, 2), (1, 2), (2, 32)), jnp.float32)
    potential = jnp.clip(-6.0 + 8.0 * jax.random.uniform(splits[1], (NX, NY, NZ), jnp.float32) ** steps_of(splits[1], (NX, NY, NZ), ((0, 2), (1, 2), (2, 32)), -0.2, 0.2), -6.0, 2.0)
    atom_sites = draw_atom_sites(jax.random.fold_in(splits[5], 71), 0)
    projectors = normal_values(splits[3], (NATOMS, W, W, W), (W * W * W) ** -0.5, 0.21875, ((0, 128),), jnp.float32)
    energies = jnp.clip(jnp.exp(math.log(16.0) - 2.0794415 * jax.random.uniform(splits[4], (NATOMS,), jnp.float32) ** steps_of(splits[4], (NATOMS,), ((0, 128),), -0.2, 0.2)), 2.0, 16.0)
    return dict(states=states, potential=potential, atom_sites=atom_sites, projectors=projectors, energies=energies)


grid_step = 0.6
filter_centre = 36.0
filter_half = 26.0
HIGH = lax.Precision.HIGHEST

def second_weights():
    weights = []
    for k in range(1, 7):
        top = 2.0 * (-1) ** (k + 1) * math.factorial(6) ** 2
        under = k * k * math.factorial(6 - k) * math.factorial(6 + k)
        weights.append(top / under)
    return (-2.0 * sum(weights), weights)

def kinetic(field):
    centre, weights = second_weights()
    total = 3.0 * centre * field
    for axis in range(3):
        for k in range(1, 7):
            total = total + weights[k - 1] * (jnp.roll(field, -k, axis) + jnp.roll(field, k, axis))
    return -0.5 / (grid_step * grid_step) * total

def nonlocal_term(field, atom_sites, projectors, energies):
    taps = jnp.arange(W, dtype=jnp.int32) - R
    index_x = (atom_sites[:, 0][:, None] + taps[None, :]) % NX
    index_y = (atom_sites[:, 1][:, None] + taps[None, :]) % NY
    index_z = (atom_sites[:, 2][:, None] + taps[None, :]) % NZ
    grid_x = index_x[:, :, None, None]
    grid_y = index_y[:, None, :, None]
    grid_z = index_z[:, None, None, :]
    patch = field[grid_x, grid_y, grid_z]
    coef = jnp.einsum('aijk,aijkb->ab', projectors, patch, precision=HIGH)
    weighted = energies[:, None] * coef
    values = projectors[..., None] * weighted[:, None, None, None, :]
    return jnp.zeros_like(field).at[grid_x, grid_y, grid_z].add(values)

def hamiltonian(field, potential, atom_sites, projectors, energies):
    return kinetic(field) + potential[..., None] * field + nonlocal_term(field, atom_sites, projectors, energies)

def reference(states, potential, atom_sites, projectors, energies):
    blocks = jnp.moveaxis(states.reshape(NX, NY, NZ, S // 16, 16), 3, 0)

    def filter_block(block):
        first = (hamiltonian(block, potential, atom_sites, projectors, energies) - filter_centre * block) / filter_half
        applied = hamiltonian(first, potential, atom_sites, projectors, energies)
        return 2.0 * (applied - filter_centre * first) / filter_half - block
    second = jnp.moveaxis(lax.map(filter_block, blocks), 0, 3).reshape(NCELLS, S)
    gram = jnp.dot(second.T, second, precision=HIGH) / NCELLS
    lower = jnp.linalg.cholesky(gram)
    inverse = lax.linalg.triangular_solve(lower, jnp.eye(S, dtype=jnp.float32), left_side=True, lower=True)
    orbitals = jnp.dot(second, inverse.T, precision=HIGH)
    return orbitals.reshape(NX, NY, NZ, S)
```

```python
import math

import jax
import jax.numpy as jnp
from jax import lax
from jax.experimental import pallas as pl
from jax.experimental.pallas import tpu as pltpu
from jax.sharding import PartitionSpec as P

AXES = ("gx", "gy", "gzs")
H = 6
C = 16
ROWS = C * C
CELLS = C * C * C
S = 128
W = 9
R = 4
NEAR = 48
F32 = jnp.float32
BF16 = jnp.bfloat16

grid_step = 0.6
filter_centre = 36.0
filter_half = 26.0


def weights():
    taps = []
    for k in range(1, 7):
        top = 2.0 * (-1) ** (k + 1) * math.factorial(6) ** 2
        under = k * k * math.factorial(6 - k) * math.factorial(6 + k)
        taps.append(top / under)
    scale = -0.5 / (grid_step * grid_step)
    off = [scale * t / filter_half for t in taps]
    diagonal = 3.0 * scale * (-2.0 * sum(taps))
    return off, diagonal


OFF, DIAGONAL = weights()


def params(mib):
    return pltpu.CompilerParams(vmem_limit_bytes=mib * 1024 * 1024)


def cost(flops, nbytes):
    return pl.CostEstimate(flops=flops, bytes_accessed=nbytes, transcendentals=0)


def sds(shape, dtype=F32):
    return jax.ShapeDtypeStruct(shape, dtype)


def split(value):
    high = value.astype(BF16)
    low = (value - high.astype(F32)).astype(BF16)
    return high, low


def mm(a, b):
    return jnp.dot(a, b, preferred_element_type=F32)


def tap_sum(at, index):
    total = None
    for k in range(1, 7):
        term = OFF[k - 1] * (at(index + k) + at(index - k))
        total = term if total is None else total + term
    return total


def pack_kernel(s_ref, edge_ref, mid_ref, head_ref, tail_ref):
    def body(x, _):
        edge_ref[x, 0:96, :] = s_ref[x, 0:96, :]
        edge_ref[x, 96:192, :] = s_ref[x, 160:256, :]
        mid_ref[x] = s_ref[x, 96:160, :]
        for z in range(H):
            head_ref[z, x] = s_ref[x, pl.ds(z, C, stride=C), :]
            tail_ref[z, x] = s_ref[x, pl.ds(C - H + z, C, stride=C), :]
        return 0

    lax.fori_loop(0, C, body, 0)


def pack(s):
    return pl.pallas_call(
        pack_kernel,
        out_shape=[sds((C, 192, S)), sds((C, 64, S)), sds((H, C, C, S)), sds((H, C, C, S))],
        compiler_params=params(32),
        cost_estimate=cost(1000, 6 << 20),
        name="pack",
    )(s)


def fill_z(ext_ref, s_ref, low_ref, high_ref):
    def body(x, _):
        for y in range(C):
            ext_ref[x, y * 32 + 8 : y * 32 + 24, :] = s_ref[x, y * C : (y + 1) * C, :]
        for z in range(H):
            ext_ref[x, pl.ds(2 + z, C, stride=32), :] = low_ref[z, x]
            ext_ref[x, pl.ds(24 + z, C, stride=32), :] = high_ref[z, x]
        return 0

    lax.fori_loop(0, C, body, 0)


def z_taps(ext_ref, x, y):
    return tap_sum(lambda k: ext_ref[x, y * 32 + 8 + k : y * 32 + 24 + k, :], 0)


def x_ring(own_ref, mate_ref, rows):
    def at(x):
        if x < 0:
            return mate_ref[C + x, rows, :]
        if x >= C:
            return mate_ref[x - C, rows, :]
        return own_ref[x, rows, :]

    return [at(x) for x in range(-H, C + H)]


def side_kernel(s_ref, mate_ref, low_ref, high_ref, out_ref, ext_ref):
    fill_z(ext_ref, s_ref, low_ref, high_ref)

    def along_z(x, _):
        for y in range(C):
            out_ref[x, y * C : (y + 1) * C, :] = z_taps(ext_ref, x, y)
        return 0

    lax.fori_loop(0, C, along_z, 0)

    def along_x(block, _):
        rows = pl.ds(pl.multiple_of(block * 8, 8), 8)
        ring = x_ring(s_ref, mate_ref, rows)
        for x in range(C):
            out_ref[x, rows, :] += tap_sum(lambda i: ring[H + i], x)
        return 0

    lax.fori_loop(0, ROWS // 8, along_x, 0)


def side(s, mate, low, high):
    return pl.pallas_call(
        side_kernel,
        out_shape=sds((C, ROWS, S)),
        scratch_shapes=[pltpu.VMEM((C, C * 32, S), F32)],
        compiler_params=params(48),
        cost_estimate=cost(1 << 25, 8 << 20),
        name="side",
    )(s, mate, low, high)


def prep_kernel(table_ref, place_ref, pot_ref, near_ref, near_t_ref, vb_ref, a1_ref, a2_ref, g_ref):
    sub = lax.broadcasted_iota(jnp.int32, (8, 128), 0)
    px = jnp.broadcast_to(place_ref[0:1, :], (8, 128))
    py = jnp.broadcast_to(place_ref[1:2, :], (8, 128))
    pz = jnp.broadcast_to(place_ref[2:3, :], (8, 128))
    zero = jnp.zeros((8, 128), F32)

    for half in range(2):
        dz = sub + half * 8 - pz + R
        masks = [dz == t for t in range(W)]

        def place_z(ij, _, half=half, masks=masks):
            acc = zero
            for t in range(W):
                row = table_ref[t, pl.ds(ij, 1), :]
                acc = jnp.where(masks[t], jnp.broadcast_to(row, (8, 128)), acc)
            a1_ref[ij, half * 8 : half * 8 + 8, :] = acc
            return 0

        lax.fori_loop(0, W * W, place_z, 0)

    def place_y(y, _):
        dy = (y - py + R) & 31
        masks = [dy == t for t in range(W)]
        for i in range(W):
            for half in range(2):
                acc = zero
                for t in range(W):
                    acc = jnp.where(masks[t], a1_ref[i * W + t, half * 8 : half * 8 + 8, :], acc)
                a2_ref[i, y, half * 8 : half * 8 + 8, :] = acc
        return 0

    lax.fori_loop(0, 2 * C, place_y, 0)

    def place_x(x, _):
        dx = (x - px + R) & 31
        masks = [dx == t for t in range(W)]

        def per_y(y, _):
            side_index = y // C
            inner = y - side_index * C
            for half in range(2):
                acc = zero
                for t in range(W):
                    acc = jnp.where(masks[t], a2_ref[t, y, half * 8 : half * 8 + 8, :], acc)
                g_ref[half * 8 : half * 8 + 8, :] = acc
            value = g_ref[...]
            high, low = split(value)
            row = pl.multiple_of(x * ROWS + inner * C, C)
            near_ref[side_index, 0, pl.ds(row, C), :] = high
            near_ref[side_index, 1, pl.ds(row, C), :] = low
            return 0

        lax.fori_loop(0, 2 * C, per_y, 0)
        return 0

    lax.fori_loop(0, C, place_x, 0)

    for block in range(CELLS // 128):
        rows = slice(block * 128, block * 128 + 128)
        for part in range(2):
            turned = near_ref[0, part, rows, :].astype(F32).T
            near_t_ref[part * NEAR : (part + 1) * NEAR, rows] = turned[:NEAR].astype(BF16)

    def spread(row, _):
        for part in range(2):
            line = (pot_ref[part, pl.ds(row, 1), :] + (DIAGONAL - filter_centre)) * (1.0 / filter_half)
            start = pl.multiple_of(row * 128, 128)
            vb_ref[part, pl.ds(start, 128), :] = jnp.broadcast_to(line, (128, 128)).T
        return 0

    lax.fori_loop(0, CELLS // 128, spread, 0)


def prep(table, place, pot):
    return pl.pallas_call(
        prep_kernel,
        out_shape=[sds((2, 2, CELLS, 128), BF16), sds((2 * NEAR, CELLS), BF16), sds((2, CELLS, S))],
        scratch_shapes=[
            pltpu.VMEM((W * W, C, 128), F32),
            pltpu.VMEM((W, 2 * C, C, 128), F32),
            pltpu.VMEM((C, 128), F32),
        ],
        compiler_params=params(48),
        cost_estimate=cost(1 << 25, 10 << 20),
        name="prep",
    )(table, place, pot)


def project(near_t_ref, field_ref):
    total = jnp.zeros((NEAR, S), F32)
    for x in range(C):
        high, low = split(field_ref[x])
        columns = slice(x * ROWS, (x + 1) * ROWS)
        both = mm(near_t_ref[:, columns], high)
        total = total + (both[:NEAR] + both[NEAR:]) + mm(near_t_ref[:NEAR, columns], low)
    return total


def coef_kernel(near_t_ref, s_ref, out_ref):
    out_ref[...] = project(near_t_ref, s_ref)


def coef(near_t, s):
    return pl.pallas_call(
        coef_kernel,
        out_shape=sds((NEAR, S)),
        compiler_params=params(32),
        cost_estimate=cost(1 << 27, 3 << 20),
        name="coef",
    )(near_t, s)


def apply_near(near_ref, side_index, w_ref, x):
    rows = pl.ds(pl.multiple_of(x * ROWS, ROWS), ROWS)
    high, low = split(w_ref[...])
    g_high = near_ref[side_index, 0, rows, :]
    g_low = near_ref[side_index, 1, rows, :]
    return mm(g_high, high) + (mm(g_high, low) + mm(g_low, high))


def first_kernel(
    s_ref, side_ref, edge_ref, vb_ref, near_ref, near_t_ref, w_ref, first_ref, mix_ref, q_ref, head_ref, tail_ref, coef_ref
):
    def body(x, _):
        q_ref[x] = apply_near(near_ref, 0, w_ref, x)
        for half in range(2):

            def rows(y, half=half):
                return slice(y * C + half * 8, y * C + half * 8 + 8)

            ring = {y: s_ref[x, rows(y), :] for y in range(C)}
            for y in range(H):
                ring[C + y] = edge_ref[x, rows(y), :]
                ring[y - H] = edge_ref[x, rows(H + y), :]
            for y in range(C):
                dy = tap_sum(lambda i: ring[i], y)
                vrow = pl.ds(pl.multiple_of(x * ROWS + y * C + half * 8, 8), 8)
                q = dy + vb_ref[0, vrow, :] * ring[y] + q_ref[x, rows(y), :]
                q_ref[x, rows(y), :] = q
                first = side_ref[x, rows(y), :] + q
                first_ref[x, rows(y), :] = first
                mix_ref[x, rows(y), :] = first + dy
        for z in range(H):
            head_ref[z, x] = mix_ref[x, pl.ds(z, C, stride=C), :]
            tail_ref[z, x] = mix_ref[x, pl.ds(C - H + z, C, stride=C), :]
        return 0

    lax.fori_loop(0, C, body, 0)
    coef_ref[...] = project(near_t_ref, first_ref)


def make_first(s, side_part, edge, vb, near, near_t, weighted):
    full = sds((C, ROWS, S))
    halo = sds((H, C, C, S))
    return pl.pallas_call(
        first_kernel,
        out_shape=[full, full, full, halo, halo, sds((NEAR, S))],
        compiler_params=params(56),
        cost_estimate=cost(1 << 27, 20 << 20),
        name="first",
    )(s, side_part, edge, vb, near, near_t, weighted)


def base_kernel(s_ref, edge_ref, mid_ref, vb_ref, near_ref, w_ref, q_ref, first_ref, mix_ref, mate_ref, out_ref, n_ref):
    def body(x, _):
        n_ref[...] = apply_near(near_ref, 1, w_ref, x)
        for half in range(2):

            def rows(y, half=half):
                return slice(y * C + half * 8, y * C + half * 8 + 8)

            def other(y):
                if y < H:
                    return edge_ref[x, rows(y), :]
                if y < C - H:
                    return mid_ref[x, rows(y - H), :]
                return edge_ref[x, rows(y - 4), :]

            ring = [s_ref[x, rows(y), :] for y in range(C)] + [other(y) for y in range(C)]
            q = {y: q_ref[x, rows(y), :] for y in range(C)}
            for y in list(range(H)) + list(range(C - H, C)):
                dy = tap_sum(lambda i: ring[i % 32], C + y)
                vrow = pl.ds(pl.multiple_of(x * ROWS + y * C + half * 8, 8), 8)
                q[C + y] = dy + vb_ref[1, vrow, :] * ring[C + y] + n_ref[rows(y), :]
            for y in range(C):
                dq = tap_sum(lambda i: q[i % 32], y)
                vrow = pl.ds(pl.multiple_of(x * ROWS + y * C + half * 8, 8), 8)
                dq = dq + vb_ref[0, vrow, :] * first_ref[x, rows(y), :]
                out_ref[x, rows(y), :] = 2.0 * dq - ring[y]
        return 0

    lax.fori_loop(0, C, body, 0)

    def along_x(block, _):
        rows = pl.ds(pl.multiple_of(block * 8, 8), 8)
        ring = x_ring(mix_ref, mate_ref, rows)
        for x in range(C):
            out_ref[x, rows, :] += 2.0 * tap_sum(lambda i: ring[H + i], x)
        return 0

    lax.fori_loop(0, ROWS // 8, along_x, 0)


def make_base(s, edge, mid, vb, near, weighted, q, first, mix, mate):
    return pl.pallas_call(
        base_kernel,
        out_shape=sds((C, ROWS, S)),
        scratch_shapes=[pltpu.VMEM((ROWS, S), F32)],
        compiler_params=params(56),
        cost_estimate=cost(1 << 27, 24 << 20),
        name="base",
    )(s, edge, mid, vb, near, weighted, q, first, mix, mate)


def second_kernel(base_ref, mix_ref, low_ref, high_ref, near_ref, w_ref, second_ref, gram_ref, ext_ref, cross_ref):
    fill_z(ext_ref, mix_ref, low_ref, high_ref)
    gram_ref[...] = jnp.zeros((S, S), F32)
    cross_ref[...] = jnp.zeros((S, S), F32)

    def body(x, _):
        second_ref[x] = base_ref[x] + 2.0 * apply_near(near_ref, 0, w_ref, x)
        for y in range(C):
            rows = slice(y * C, (y + 1) * C)
            second_ref[x, rows, :] += 2.0 * z_taps(ext_ref, x, y)
        high, low = split(second_ref[x])
        turned = high.T
        gram_ref[...] += mm(turned, high)
        cross_ref[...] += mm(turned, low)
        return 0

    lax.fori_loop(0, C, body, 0)
    cross = cross_ref[...]
    gram_ref[...] += cross + cross.T


def make_second(base, mix, low, high, near, weighted):
    return pl.pallas_call(
        second_kernel,
        out_shape=[sds((C, ROWS, S)), sds((S, S))],
        scratch_shapes=[pltpu.VMEM((C, C * 32, S), F32), pltpu.VMEM((S, S), F32)],
        compiler_params=params(56),
        cost_estimate=cost(1 << 27, 12 << 20),
        name="second",
    )(base, mix, low, high, near, weighted)


def turn_kernel(second_ref, inverse_ref, out_ref):
    high, low = split(second_ref[...])
    i_high, i_low = split(inverse_ref[...].T)
    out_ref[...] = mm(high, i_high) + (mm(high, i_low) + mm(low, i_high))


def turn(second, inverse):
    block = 512
    return pl.pallas_call(
        turn_kernel,
        grid=(CELLS // block,),
        in_specs=[pl.BlockSpec((block, S), lambda i: (i, 0)), pl.BlockSpec((S, S), lambda i: (0, 0))],
        out_specs=pl.BlockSpec((block, S), lambda i: (i, 0)),
        out_shape=sds((CELLS, S)),
        compiler_params=params(32),
        cost_estimate=cost(1 << 28, 4 << 20),
        name="turn",
    )(second, inverse)


def per_device(states, potential, atom_sites, projectors, energies):
    gx, gy, gzs = (lax.axis_index(a) for a in AXES)
    depth = lax.axis_size("gzs")

    def swap(value, axis):
        return lax.ppermute(value, axis, [(0, 1), (1, 0)])

    def up(value):
        return lax.ppermute(value, "gzs", [(i, (i + 1) % depth) for i in range(depth)])

    def down(value):
        return lax.ppermute(value, "gzs", [((i + 1) % depth, i) for i in range(depth)])

    def both(value, axis, index):
        other = swap(value, axis)
        return jnp.where(index == 0, jnp.concatenate([value, other]), jnp.concatenate([other, value]))

    s = states.reshape(C, ROWS, S)

    atoms = jnp.concatenate(
        [
            projectors.reshape(4, W * W * W),
            atom_sites.astype(F32),
            energies[:, None],
            jnp.zeros((4, 768 - W * W * W - 4), F32),
        ],
        axis=1,
    )
    atoms = both(both(atoms, "gy", gy), "gx", gx)
    near = jnp.concatenate([up(atoms), atoms, down(atoms)])
    pot = potential.reshape(32, 128)
    pot = jnp.stack([pot, swap(pot, "gy")])

    edge, mid, head, tail = pack(s)
    edge = swap(edge, "gy")
    low, high = up(tail), down(head)
    mate = swap(s, "gx")
    mid = swap(mid, "gy")

    sites = near[:, 729:732].astype(jnp.int32)
    slab = jnp.repeat(jnp.arange(-1, 2, dtype=jnp.int32), 16) * C
    place = jnp.stack([sites[:, 0] - gx * C, sites[:, 1] - gy * C, sites[:, 2] % C + slab])
    place = jnp.pad(place, ((0, 5), (0, 80)), constant_values=1000)
    energy = near[:, 732:733] * (1.0 / filter_half)
    table = near[:, :729].reshape(NEAR, W * W, W).transpose(2, 1, 0)
    table = jnp.pad(table, ((0, 0), (0, 7), (0, 80)))
    near_g, near_t, vb = prep(table, place, pot)

    def weigh(part):
        part = part + swap(part, "gx")
        part = part + swap(part, "gy")
        own = part[16:32] + up(part[32:48]) + down(part[0:16])
        weighted = jnp.concatenate([up(own), own, down(own)]) * energy
        return jnp.pad(weighted, ((0, 80), (0, 0)))

    weighted = weigh(coef(near_t, s))
    side_part = side(s, mate, low, high)
    first, mix, q, head, tail, part = make_first(s, side_part, edge, vb, near_g, near_t, weighted)
    low, high = up(tail), down(head)
    mate = swap(mix, "gx")
    weighted_two = weigh(part)
    base = make_base(s, edge, mid, vb, near_g, weighted, q, first, mix, mate)
    second, gram = make_second(base, mix, low, high, near_g, weighted_two)

    def exchange(value, flip):
        count = 2 * 2 * depth
        return value + lax.ppermute(value, AXES, [(d, d ^ flip) for d in range(count)])

    for flip in (64, 32, 36, 1, 3, 8, 24):
        gram = exchange(gram, flip)
    gram = gram * (1.0 / (CELLS * 4 * depth))
    lower = jnp.linalg.cholesky(gram)
    inverse = lax.linalg.triangular_solve(lower, jnp.eye(S, dtype=F32), left_side=True, lower=True)
    orbitals = turn(second.reshape(CELLS, S), inverse)
    return orbitals.reshape(C, C, C, S)


def solution(mesh):
    return jax.shard_map(
        per_device,
        mesh=mesh,
        in_specs=(
            P("gx", "gy", "gzs", None),
            P("gx", "gy", "gzs"),
            P(("gx", "gy", "gzs"), None),
            P(("gx", "gy", "gzs"), None, None, None),
            P(("gx", "gy", "gzs")),
        ),
        out_specs=P("gx", "gy", "gzs", None),
        check_vma=False,
    )
```

```python
import math

import jax
import jax.numpy as jnp
from jax import lax
from jax.experimental import pallas as pl
from jax.experimental.pallas import tpu as pltpu
from jax.sharding import PartitionSpec as P

AXES = ("gx", "gy", "gzs")
H = 6
C = 16
ROWS = C * C
CELLS = C * C * C
S = 128
W = 9
R = 4
NEAR = 48
TAPS = W * W * W
F32 = jnp.float32
BF16 = jnp.bfloat16

grid_step = 0.6
filter_centre = 36.0
filter_half = 26.0


def weights():
    taps = []
    for k in range(1, 7):
        top = 2.0 * (-1) ** (k + 1) * math.factorial(6) ** 2
        under = k * k * math.factorial(6 - k) * math.factorial(6 + k)
        taps.append(top / under)
    scale = -0.5 / (grid_step * grid_step)
    off = [scale * t / filter_half for t in taps]
    diagonal = 3.0 * scale * (-2.0 * sum(taps))
    return off, diagonal


OFF, DIAGONAL = weights()


def params(mib):
    return pltpu.CompilerParams(vmem_limit_bytes=mib * 1024 * 1024)


def cost(flops, nbytes):
    return pl.CostEstimate(flops=flops, bytes_accessed=nbytes, transcendentals=0)


def sds(shape, dtype=F32):
    return jax.ShapeDtypeStruct(shape, dtype)


def split(value):
    high = value.astype(BF16)
    low = (value - high.astype(F32)).astype(BF16)
    return high, low


def mm(a, b):
    return jnp.dot(a, b, preferred_element_type=F32)


def tap_sum(at, index):
    total = None
    for k in range(1, 7):
        term = OFF[k - 1] * (at(index + k) + at(index - k))
        total = term if total is None else total + term
    return total


def stride_rows(z):
    return pl.ds(z, C, stride=C)


def plane_spec(rows=ROWS):
    return pl.BlockSpec((1, rows, S), lambda i: (i, 0, 0))


def halo_spec():
    return pl.BlockSpec((H, 1, C, S), lambda i: (0, i, 0, 0))


def part_spec(part):
    return pl.BlockSpec((1, 1, ROWS, S), lambda i: (part, i, 0, 0))


def whole(rows=S):
    return pl.BlockSpec((rows, S), lambda i: (0, 0))


FULL = sds((C, ROWS, S))
HALO = sds((H, C, C, S))


def pack_kernel(s_ref, edge_ref, mid_ref, head_ref, tail_ref):
    edge_ref[0, 0:96, :] = s_ref[0, 0:96, :]
    edge_ref[0, 96:192, :] = s_ref[0, 160:256, :]
    mid_ref[0] = s_ref[0, 96:160, :]
    for z in range(H):
        head_ref[z, 0] = s_ref[0, stride_rows(z), :]
        tail_ref[z, 0] = s_ref[0, stride_rows(C - H + z), :]


def pack(s):
    return pl.pallas_call(
        pack_kernel,
        grid=(C,),
        in_specs=[plane_spec()],
        out_specs=[plane_spec(192), plane_spec(64), halo_spec(), halo_spec()],
        out_shape=[sds((C, 192, S)), sds((C, 64, S)), HALO, HALO],
        compiler_params=params(16),
        cost_estimate=cost(1000, 6 << 20),
        name="pack",
    )(s)


def z_taps(ext_ref, x, y):
    return tap_sum(lambda k: ext_ref[x, y * 32 + 8 + k : y * 32 + 24 + k, :], 0)


def side_kernel(*refs):
    if len(refs) == 6:
        s_ref, mate_ref, low_ref, high_ref, out_ref, ext_ref = refs
    else:
        s_ref, mate_ref, out_ref, ext_ref = refs
        low_ref = high_ref = None

    def along_z(x, _):
        for y in range(C):
            ext_ref[x, y * 32 + 8 : y * 32 + 24, :] = s_ref[x, y * C : (y + 1) * C, :]
            if low_ref is None:
                ext_ref[x, y * 32 : y * 32 + 8, :] = jnp.zeros((8, S), F32)
                ext_ref[x, y * 32 + 24 : y * 32 + 32, :] = jnp.zeros((8, S), F32)
        if low_ref is not None:
            for z in range(H):
                ext_ref[x, pl.ds(2 + z, C, stride=32), :] = low_ref[z, x]
                ext_ref[x, pl.ds(24 + z, C, stride=32), :] = high_ref[z, x]
        for y in range(C):
            out_ref[x, y * C : (y + 1) * C, :] = z_taps(ext_ref, x, y)
        return 0

    lax.fori_loop(0, C, along_z, 0)

    def along_x(block, _):
        rows = pl.ds(pl.multiple_of(block * 8, 8), 8)
        ring = [mate_ref[C - H + i, rows, :] for i in range(H)]
        ring += [s_ref[x, rows, :] for x in range(C)]
        ring += [mate_ref[i, rows, :] for i in range(H)]
        for x in range(C):
            out_ref[x, rows, :] += tap_sum(lambda i: ring[H + i], x)
        return 0

    lax.fori_loop(0, ROWS // 8, along_x, 0)


def side(name, *arrays):
    return pl.pallas_call(
        side_kernel,
        out_shape=FULL,
        scratch_shapes=[pltpu.VMEM((C, C * 32, S), F32)],
        compiler_params=params(48),
        cost_estimate=cost(1 << 25, 8 << 20),
        name=name,
    )(*arrays)


def tap_weight(distance):
    value = jnp.zeros(distance.shape, F32)
    for k in range(1, 7):
        value = jnp.where(distance == k, OFF[k - 1], value)
    return value


def ring_tables(coordinate):
    masks, factors = [], []
    for t in range(W):
        away = (coordinate - t) & 31
        masks.append(away == 0)
        factors.append(tap_weight(jnp.minimum(away, 32 - away)))
    return masks, factors


def prep_kernel(
    near_ref, corner_ref, pot_ref, s_ref, gg_ref, vb_ref, coef_ref, table_ref, a1_ref, a1z_ref, a2_ref, a2s_ref, turn_ref
):
    for block in range(6):
        columns = slice(block * 128, block * 128 + 128)
        table_ref[columns, :] = near_ref[:, columns].T

    def spread(row, _):
        for part in range(2):
            line = (pot_ref[part, pl.ds(row, 1), :] + (DIAGONAL - filter_centre)) * (1.0 / filter_half)
            start = pl.multiple_of(row * 128, 128)
            vb_ref[part, pl.ds(start, 128), :] = jnp.broadcast_to(line, (128, 128)).T
        return 0

    lax.fori_loop(0, CELLS // 128, spread, 0)

    shape = (8, 128)
    sub = lax.broadcasted_iota(jnp.int32, shape, 0)
    lane = lax.broadcasted_iota(jnp.int32, shape, 1)
    sites = [jnp.broadcast_to(table_ref[TAPS + d : TAPS + d + 1, :], shape).astype(jnp.int32) for d in range(3)]
    px = sites[0] - corner_ref[0]
    py = sites[1] - corner_ref[1]
    pz = (sites[2] & 15) + (((lane & 63) >> 4) - 1) * C
    zero = jnp.zeros(shape, F32)

    for half in range(2):
        dz = sub + half * 8 - pz + R
        masks = [dz == t for t in range(W)]
        factors = [tap_weight(jnp.abs(dz - t)) for t in range(W)]

        def place_z(ij, _, half=half, masks=masks, factors=factors):
            acc = zero
            along = zero
            for t in range(W):
                row = jnp.broadcast_to(table_ref[pl.ds(ij * W + t, 1), :], shape)
                acc = jnp.where(masks[t], row, acc)
                along = along + factors[t] * row
            a1_ref[ij, half * 8 : half * 8 + 8, :] = acc
            a1z_ref[ij, half * 8 : half * 8 + 8, :] = along
            return 0

        lax.fori_loop(0, W * W, place_z, 0)

    def place_y(y, _):
        masks, factors = ring_tables(y - py + R)
        for i in range(W):
            for half in range(2):
                rows = slice(half * 8, half * 8 + 8)
                acc = zero
                along = zero
                moved = zero
                for t in range(W):
                    value = a1_ref[i * W + t, rows, :]
                    acc = jnp.where(masks[t], value, acc)
                    along = along + factors[t] * value
                    moved = jnp.where(masks[t], a1z_ref[i * W + t, rows, :], moved)
                a2_ref[i, y, rows, :] = acc
                a2s_ref[i, y, rows, :] = along + moved
        return 0

    lax.fori_loop(0, C, place_y, 0)

    def place_x(x, _):
        masks, factors = ring_tables(x - px + R)

        def per_y(y, _):
            row = pl.multiple_of(x * ROWS + y * C, C)
            halves = []
            for half in range(2):
                rows = slice(half * 8, half * 8 + 8)
                acc = zero
                along = zero
                moved = zero
                for t in range(W):
                    value = a2_ref[t, y, rows, :]
                    acc = jnp.where(masks[t], value, acc)
                    along = along + factors[t] * value
                    moved = jnp.where(masks[t], a2s_ref[t, y, rows, :], moved)
                vrow = pl.ds(pl.multiple_of(row + half * 8, 8), 8)
                halves.append(jnp.where(lane < 64, acc, along + moved + vb_ref[0, vrow, :] * acc))
            high, low = split(jnp.concatenate(halves, axis=0))
            gg_ref[0, pl.ds(row, C), :] = high
            gg_ref[1, pl.ds(row, C), :] = low
            return 0

        lax.fori_loop(0, C, per_y, 0)
        return 0

    lax.fori_loop(0, C, place_x, 0)

    coef_ref[...] = jnp.zeros((3, NEAR, S), F32)

    def contract(x, _):
        rows = pl.ds(pl.multiple_of(x * ROWS, ROWS), ROWS)
        g_high, g_low = gg_ref[0, rows, :], gg_ref[1, rows, :]
        turn_ref[0] = g_high.T
        turn_ref[1] = g_low.T
        t_high, t_low = turn_ref[0], turn_ref[1]
        high, low = split(s_ref[x])
        got = mm(t_high, high) + (mm(t_high, low) + mm(t_low, high))
        coef_ref[0] += got[:NEAR]
        coef_ref[1] += got[64 : 64 + NEAR]
        t_high, t_low = t_high[:NEAR], t_low[:NEAR]
        coef_ref[2] += mm(t_high, g_high) + (mm(t_high, g_low) + mm(t_low, g_high))
        return 0

    lax.fori_loop(0, C, contract, 0)


def prep(near, corner, pot, s):
    vmem = pl.BlockSpec(memory_space=pltpu.VMEM)
    return pl.pallas_call(
        prep_kernel,
        in_specs=[vmem, pl.BlockSpec(memory_space=pltpu.SMEM), vmem, vmem],
        out_shape=[sds((2, CELLS, S), BF16), sds((2, CELLS, S)), sds((3, NEAR, S))],
        scratch_shapes=[
            pltpu.VMEM((768, 128), F32),
            pltpu.VMEM((W * W, C, 128), F32),
            pltpu.VMEM((W * W, C, 128), F32),
            pltpu.VMEM((W, C, C, 128), F32),
            pltpu.VMEM((W, C, C, 128), F32),
            pltpu.VMEM((2, S, ROWS), BF16),
        ],
        compiler_params=params(48),
        cost_estimate=cost(1 << 27, 10 << 20),
        name="prep",
    )(near, corner, pot, s)


def first_kernel(s_ref, side_ref, edge_ref, vb_ref, q_ref, mix_ref, head_ref, tail_ref):
    for half in range(2):

        def rows(y, half=half):
            return slice(y * C + half * 8, y * C + half * 8 + 8)

        ring = {y: s_ref[0, rows(y), :] for y in range(C)}
        for y in range(H):
            ring[C + y] = edge_ref[0, rows(y), :]
            ring[y - H] = edge_ref[0, rows(H + y), :]
        for y in range(C):
            dy = tap_sum(lambda i: ring[i], y)
            q = dy + vb_ref[0, 0, rows(y), :] * ring[y]
            q_ref[0, rows(y), :] = q
            mix_ref[0, rows(y), :] = side_ref[0, rows(y), :] + q + dy
    for z in range(H):
        head_ref[z, 0] = mix_ref[0, stride_rows(z), :]
        tail_ref[z, 0] = mix_ref[0, stride_rows(C - H + z), :]


def make_first(s, side_part, edge, vb):
    return pl.pallas_call(
        first_kernel,
        grid=(C,),
        in_specs=[plane_spec(), plane_spec(), plane_spec(192), part_spec(0)],
        out_specs=[plane_spec(), plane_spec(), halo_spec(), halo_spec()],
        out_shape=[FULL, FULL, HALO, HALO],
        compiler_params=params(16),
        cost_estimate=cost(1 << 24, 14 << 20),
        name="first",
    )(s, side_part, edge, vb)


def base_kernel(s_ref, edge_ref, mid_ref, vb_ref, vb_mate_ref, q_ref, side_ref, part_ref, out_ref):
    for half in range(2):

        def rows(y, half=half):
            return slice(y * C + half * 8, y * C + half * 8 + 8)

        def other(y):
            if y < H:
                return edge_ref[0, rows(y), :]
            if y < C - H:
                return mid_ref[0, rows(y - H), :]
            return edge_ref[0, rows(y - 4), :]

        ring = [s_ref[0, rows(y), :] for y in range(C)] + [other(y) for y in range(C)]
        q = {y: q_ref[0, rows(y), :] for y in range(C)}
        for y in list(range(H)) + list(range(C - H, C)):
            q[C + y] = tap_sum(lambda i: ring[i % 32], C + y) + vb_mate_ref[0, 0, rows(y), :] * ring[C + y]
        for y in range(C):
            total = tap_sum(lambda i: q[i % 32], y)
            total = total + vb_ref[0, 0, rows(y), :] * (side_ref[0, rows(y), :] + q[y])
            out_ref[0, rows(y), :] = 2.0 * (total + part_ref[0, rows(y), :]) - ring[y]


def make_base(s, edge, mid, vb, q, side_part, part):
    return pl.pallas_call(
        base_kernel,
        grid=(C,),
        in_specs=[plane_spec(), plane_spec(192), plane_spec(64), part_spec(0), part_spec(1)] + [plane_spec()] * 3,
        out_specs=plane_spec(),
        out_shape=FULL,
        compiler_params=params(16),
        cost_estimate=cost(1 << 25, 16 << 20),
        name="base",
    )(s, edge, mid, vb, vb, q, side_part, part)


def second_kernel(base_ref, low_ref, high_ref, gg_high_ref, gg_low_ref, w_ref, second_ref, gram_ref, cross_ref):
    step = pl.program_id(0)

    @pl.when(step == 0)
    def _():
        gram_ref[...] = jnp.zeros((S, S), F32)
        cross_ref[...] = jnp.zeros((S, S), F32)

    w_high, w_low = split(2.0 * w_ref[...])
    g_high, g_low = gg_high_ref[0, 0], gg_low_ref[0, 0]
    second_ref[0] = base_ref[0] + (mm(g_high, w_high) + (mm(g_high, w_low) + mm(g_low, w_high)))
    low = [low_ref[j, 0] for j in range(H)]
    high = [high_ref[j, 0] for j in range(H)]
    for z in range(H):
        add = sum((2.0 * OFF[k - 1]) * low[z - k + H] for k in range(z + 1, H + 1))
        second_ref[0, stride_rows(z), :] += add
        add = sum((2.0 * OFF[H + j - z - 1]) * high[j] for j in range(z + 1))
        second_ref[0, stride_rows(C - H + z), :] += add
    s_high, s_low = split(second_ref[0])
    turned = s_high.T
    gram_ref[...] += mm(turned, s_high)
    cross_ref[...] += mm(turned, s_low)

    @pl.when(step == C - 1)
    def _():
        cross = cross_ref[...]
        gram_ref[...] += cross + cross.T


def make_second(base, low, high, gg, weighted):
    return pl.pallas_call(
        second_kernel,
        grid=(C,),
        in_specs=[plane_spec(), halo_spec(), halo_spec(), part_spec(0), part_spec(1), whole()],
        out_specs=[plane_spec(), whole()],
        out_shape=[FULL, sds((S, S))],
        scratch_shapes=[pltpu.VMEM((S, S), F32)],
        compiler_params=params(16),
        cost_estimate=cost(1 << 27, 8 << 20),
        name="second",
    )(base, low, high, gg, gg, weighted)


def exact(a, b):
    return jnp.dot(a, b, precision=lax.Precision.HIGHEST, preferred_element_type=F32)


def inverse_factor(gram_ref, a_ref, x_ref, state_ref):
    row = lax.broadcasted_iota(jnp.int32, (S, S), 0)
    column = lax.broadcasted_iota(jnp.int32, (S, S), 1)
    unit = jnp.where(row == column, 1.0, 0.0)
    gram = gram_ref[...]
    diagonal = jnp.where(row == column, gram, 0.0)
    down = lax.rsqrt(jnp.sum(diagonal, axis=1, keepdims=True))
    across = lax.rsqrt(jnp.sum(diagonal, axis=0, keepdims=True))
    a_ref[...] = gram * down * across
    x_ref[...] = unit

    def residual():
        x = x_ref[...]
        return unit - exact(exact(x, a_ref[...]), x.T)

    def size(e):
        return jnp.sum(e * e)

    def improve(e):
        lower = jnp.where(row > column, e, jnp.where(row == column, 0.5 * e, 0.0))
        x_ref[...] += exact(lower, x_ref[...])

    state_ref[0] = 0
    start = unit - a_ref[...]
    start_size = size(start)

    @pl.when(start_size < 0.16)
    def _():
        improve(start)
        state_ref[0] = jnp.where(start_size < 1e-6, 2, 1)

    for _ in range(5):

        @pl.when(state_ref[0] == 1)
        def _():
            e = residual()
            e_size = size(e)
            improve(e)
            state_ref[0] = jnp.where(e_size < 1e-6, 2, 1)

    @pl.when(state_ref[0] != 2)
    def _():
        x_ref[...] = unit
        lanes = lax.broadcasted_iota(jnp.int32, (1, S), 1)

        def step(j, _):
            line = a_ref[pl.ds(j, 1), :]
            scale = lax.rsqrt(jnp.sum(jnp.where(lanes == j, line, 0.0), axis=1, keepdims=True))
            a = a_ref[...]
            factor = jnp.sum(jnp.where(column == j, a, 0.0), axis=1, keepdims=True) * scale
            factor = jnp.where(row[:, :1] > j, factor, 0.0)
            x_line = x_ref[pl.ds(j, 1), :] * scale
            a_ref[...] = a - factor * (line * scale)
            x_ref[...] = jnp.where(row == j, x_line, x_ref[...] - factor * x_line)
            return 0

        lax.fori_loop(0, S, step, 0)

    x_ref[...] = x_ref[...] * across


def turn_kernel(second_ref, gram_ref, out_ref, a_ref, x_ref, i_high_ref, i_low_ref, state_ref):
    @pl.when(pl.program_id(0) == 0)
    def _():
        inverse_factor(gram_ref, a_ref, x_ref, state_ref)
        i_high, i_low = split(x_ref[...].T)
        i_high_ref[...] = i_high
        i_low_ref[...] = i_low

    high, low = split(second_ref[...])
    i_high = i_high_ref[...]
    out_ref[...] = mm(high, i_high) + (mm(high, i_low_ref[...]) + mm(low, i_high))


def turn(second, gram):
    block = 512
    return pl.pallas_call(
        turn_kernel,
        grid=(CELLS // block,),
        in_specs=[pl.BlockSpec((block, S), lambda i: (i, 0)), whole()],
        out_specs=pl.BlockSpec((block, S), lambda i: (i, 0)),
        out_shape=sds((CELLS, S)),
        scratch_shapes=[pltpu.VMEM((S, S), F32)] * 2 + [pltpu.VMEM((S, S), BF16)] * 2 + [pltpu.SMEM((1,), jnp.int32)],
        compiler_params=params(16),
        cost_estimate=cost(1 << 28, 4 << 20),
        name="turn",
    )(second, gram)


def per_device(states, potential, atom_sites, projectors, energies):
    gx, gy = lax.axis_index("gx"), lax.axis_index("gy")
    depth = lax.axis_size("gzs")

    def swap(value, axis):
        return lax.ppermute(value, axis, [(0, 1), (1, 0)])

    def up(value):
        return lax.ppermute(value, "gzs", [(i, (i + 1) % depth) for i in range(depth)])

    def down(value):
        return lax.ppermute(value, "gzs", [((i + 1) % depth, i) for i in range(depth)])

    def both(value, axis, index, dim):
        other = swap(value, axis)
        return jnp.where(index == 0, jnp.concatenate([value, other], dim), jnp.concatenate([other, value], dim))

    s = states.reshape(C, ROWS, S)

    atoms = jnp.concatenate(
        [
            projectors.reshape(4, TAPS),
            atom_sites.astype(F32),
            energies[:, None] * (1.0 / filter_half),
            jnp.zeros((4, 768 - TAPS - 4), F32),
        ],
        axis=1,
    )
    atoms = jnp.stack([up(atoms), atoms, down(atoms)])
    atoms = both(atoms, "gx", gx, 1)
    edge, mid, head, tail = pack(s)
    edge, atoms = lax.optimization_barrier((edge, atoms))
    pot = potential.reshape(32, 128)
    parcel = jnp.concatenate([atoms.reshape(144, 128), pot])
    parcel_mate = swap(parcel, "gy")
    edge = swap(edge, "gy")
    mate = swap(s, "gx")
    atoms_mate = parcel_mate[:144].reshape(3, 8, 768)
    near = jnp.where(
        gy == 0,
        jnp.stack([atoms.reshape(3, 2, 4, 768), atoms_mate.reshape(3, 2, 4, 768)], 2),
        jnp.stack([atoms_mate.reshape(3, 2, 4, 768), atoms.reshape(3, 2, 4, 768)], 2),
    ).reshape(NEAR, 768)
    low, high = up(tail), down(head)
    gap = jnp.zeros((16, 768), F32)
    energy = near[16:32, TAPS + 3 : TAPS + 4]
    corner = jnp.stack([gx * C, gy * C]).astype(jnp.int32)
    gg, vb, part = prep(jnp.concatenate([near, gap, near, gap]), corner, jnp.stack([pot, parcel_mate[144:]]), s)

    part = part + swap(part, "gx")
    below, above = up(part[:, 32:48]), down(part[:, 0:16])
    zeros = jnp.zeros((16, 16), F32)
    pair = part[2, 16:32, :NEAR]
    pair = pair + jnp.concatenate([below[2, :, 16:48], zeros], 1) + jnp.concatenate([zeros, above[2, :, 0:32]], 1)
    own = jnp.concatenate([part[:2, 16:32] + below[:2] + above[:2], jnp.pad(pair, ((0, 0), (0, S - NEAR)))[None]])
    own = own + swap(own, "gy")
    mid, own = lax.optimization_barrier((mid, own))
    mid = swap(mid, "gy")
    one = own[0] * energy
    one = jnp.concatenate([up(one), one, down(one)])
    two = (own[1] + jnp.dot(own[2, :, :NEAR], one, precision=lax.Precision.HIGHEST)) * energy
    two = jnp.concatenate([up(two), two, down(two)])
    gap = jnp.zeros((16, S), F32)
    weighted = jnp.concatenate([two, gap, one, gap])

    vb = vb.reshape(2, C, ROWS, S)
    side_part = side("side", s, mate, low, high)
    q, mix, head, tail = make_first(s, side_part, edge, vb)
    low, high = up(tail), down(head)
    mate = swap(mix, "gx")
    part = side("side_again", mix, mate)
    base = make_base(s, edge, mid, vb, q, side_part, part)
    second, gram = make_second(base, low, high, gg.reshape(2, C, ROWS, S), weighted)

    def exchange(value, flip):
        return value + lax.ppermute(value, AXES, [(d, d ^ flip) for d in range(4 * depth)])

    for flip in (64, 32, 36, 1, 3, 8, 24):
        gram = exchange(gram, flip)
    gram = gram * (1.0 / (CELLS * 4 * depth))
    orbitals = turn(second.reshape(CELLS, S), gram)
    return orbitals.reshape(C, C, C, S)


def solution(mesh):
    return jax.shard_map(
        per_device,
        mesh=mesh,
        in_specs=(
            P("gx", "gy", "gzs", None),
            P("gx", "gy", "gzs"),
            P(("gx", "gy", "gzs"), None),
            P(("gx", "gy", "gzs"), None, None, None),
            P(("gx", "gy", "gzs")),
        ),
        out_specs=P("gx", "gy", "gzs", None),
        check_vma=False,
    )
```

```python
import math

import jax
import jax.numpy as jnp
from jax import lax
from jax.experimental import pallas as pl
from jax.experimental.pallas import tpu as pltpu
from jax.sharding import PartitionSpec as P

AXES = ("gx", "gy", "gzs")
H = 6
C = 16
ROWS = C * C
CELLS = C * C * C
S = 128
W = 9
R = 4
NEAR = 48
TAPS = W * W * W
F32 = jnp.float32
BF16 = jnp.bfloat16

grid_step = 0.6
filter_centre = 36.0
filter_half = 26.0


def weights():
    taps = []
    for k in range(1, 7):
        top = 2.0 * (-1) ** (k + 1) * math.factorial(6) ** 2
        under = k * k * math.factorial(6 - k) * math.factorial(6 + k)
        taps.append(top / under)
    scale = -0.5 / (grid_step * grid_step)
    off = [scale * t / filter_half for t in taps]
    diagonal = 3.0 * scale * (-2.0 * sum(taps))
    return off, diagonal


OFF, DIAGONAL = weights()


def params(mib):
    return pltpu.CompilerParams(vmem_limit_bytes=mib * 1024 * 1024)


def cost(flops, nbytes):
    return pl.CostEstimate(flops=flops, bytes_accessed=nbytes, transcendentals=0)


def sds(shape, dtype=F32):
    return jax.ShapeDtypeStruct(shape, dtype)


def split(value):
    high = value.astype(BF16)
    low = (value - high.astype(F32)).astype(BF16)
    return high, low


def mm(a, b):
    return jnp.dot(a, b, preferred_element_type=F32)


def tap_sum(at, index):
    total = None
    for k in range(1, 7):
        term = OFF[k - 1] * (at(index + k) + at(index - k))
        total = term if total is None else total + term
    return total


B = 4
STEPS = C // B
CUT = 12


def stride_rows(z):
    return pl.ds(z, C, stride=C)


def plane_spec(rows=ROWS):
    return pl.BlockSpec((B, rows, S), lambda i: (i, 0, 0))


def halo_spec():
    return pl.BlockSpec((H, B, C, S), lambda i: (0, i, 0, 0))


def part_spec(part):
    return pl.BlockSpec((1, B, ROWS, S), lambda i: (part, i, 0, 0))


def whole(rows=S):
    return pl.BlockSpec((rows, S), lambda i: (0, 0))


def edge_specs():
    return [
        pl.BlockSpec((B, 192, S), lambda i: (jnp.minimum(i, CUT // B - 1), 0, 0)),
        pl.BlockSpec((B, 192, S), lambda i: (jnp.maximum(i - CUT // B, 0), 0, 0)),
    ]


def per_plane(body):
    def step(p, _):
        body(p)
        return 0

    lax.fori_loop(0, B, step, 0)


FULL = sds((C, ROWS, S))
HALO = sds((H, C, C, S))
EDGES = [sds((CUT, 192, S)), sds((C - CUT, 192, S))]


def halves(y, half):
    return slice(y * C + half * 8, y * C + half * 8 + 8)


def pack_kernel(s_ref, one_ref, two_ref, mid_ref, head_ref, tail_ref):
    step = pl.program_id(0)

    def edges(out_ref):
        out_ref[:, 0:96, :] = s_ref[:, 0:96, :]
        out_ref[:, 96:192, :] = s_ref[:, 160:256, :]

    @pl.when(step < CUT // B)
    def _():
        edges(one_ref)

    @pl.when(step >= CUT // B)
    def _():
        edges(two_ref)

    mid_ref[...] = s_ref[:, 96:160, :]
    for p in range(B):
        for z in range(H):
            head_ref[z, p] = s_ref[p, stride_rows(z), :]
            tail_ref[z, p] = s_ref[p, stride_rows(C - H + z), :]


def pack(s):
    return pl.pallas_call(
        pack_kernel,
        grid=(STEPS,),
        in_specs=[plane_spec()],
        out_specs=edge_specs() + [plane_spec(64), halo_spec(), halo_spec()],
        out_shape=EDGES + [sds((C, 64, S)), HALO, HALO],
        compiler_params=params(12),
        cost_estimate=cost(1 << 33, 6 << 20),
        name="pack",
    )(s)


def along_x(s_ref, mate_ref, out_ref, add):
    def column(block, _):
        rows = pl.ds(pl.multiple_of(block * 8, 8), 8)
        ring = [mate_ref[C - H + i, rows, :] for i in range(H)]
        ring += [s_ref[x, rows, :] for x in range(C)]
        ring += [mate_ref[i, rows, :] for i in range(H)]
        for x in range(C):
            value = tap_sum(lambda i: ring[H + i], x)
            if add:
                value = value + out_ref[x, rows, :]
            out_ref[x, rows, :] = value
        return 0

    lax.fori_loop(0, ROWS // 8, column, 0)


def z_taps(ext_ref, y):
    return tap_sum(lambda k: ext_ref[y * 32 + 8 + k : y * 32 + 24 + k, :], 0)


def side_x_kernel(s_ref, mate_ref, out_ref):
    along_x(s_ref, mate_ref, out_ref, False)


def side_x(s, mate):
    return pl.pallas_call(
        side_x_kernel,
        out_shape=FULL,
        compiler_params=params(12),
        cost_estimate=cost(1 << 24, 6 << 20),
        name="side_x",
    )(s, mate)


def side_z_kernel(s_ref, part_ref, low_ref, high_ref, out_ref, ext_ref):
    def plane(x, _):
        for y in range(C):
            ext_ref[y * 32 + 8 : y * 32 + 24, :] = s_ref[x, y * C : (y + 1) * C, :]
        for z in range(H):
            ext_ref[pl.ds(2 + z, C, stride=32), :] = low_ref[z, x]
            ext_ref[pl.ds(24 + z, C, stride=32), :] = high_ref[z, x]
        for y in range(C):
            rows = slice(y * C, (y + 1) * C)
            out_ref[x, rows, :] = part_ref[x, rows, :] + z_taps(ext_ref, y)
        return 0

    lax.fori_loop(0, C, plane, 0)


def side_z(s, part, low, high):
    return pl.pallas_call(
        side_z_kernel,
        out_shape=FULL,
        scratch_shapes=[pltpu.VMEM((C * 32, S), F32)],
        compiler_params=params(14),
        cost_estimate=cost(1 << 24, 8 << 20),
        name="side_z",
    )(s, part, low, high)


def side_again_kernel(s_ref, mate_ref, out_ref, ext_ref):
    for y in range(C):
        ext_ref[y * 32 : y * 32 + 8, :] = jnp.zeros((8, S), F32)
        ext_ref[y * 32 + 24 : y * 32 + 32, :] = jnp.zeros((8, S), F32)

    def plane(x, _):
        for y in range(C):
            ext_ref[y * 32 + 8 : y * 32 + 24, :] = s_ref[x, y * C : (y + 1) * C, :]
        for y in range(C):
            out_ref[x, y * C : (y + 1) * C, :] = z_taps(ext_ref, y)
        return 0

    lax.fori_loop(0, C, plane, 0)
    along_x(s_ref, mate_ref, out_ref, True)


def side_again(s, mate):
    return pl.pallas_call(
        side_again_kernel,
        out_shape=FULL,
        scratch_shapes=[pltpu.VMEM((C * 32, S), F32)],
        compiler_params=params(12),
        cost_estimate=cost(1 << 25, 6 << 20),
        name="side_again",
    )(s, mate)


def tap_weight(distance):
    value = jnp.zeros(distance.shape, F32)
    for k in range(1, 7):
        value = jnp.where(distance == k, OFF[k - 1], value)
    return value


def ring_tables(coordinate):
    masks, factors = [], []
    for t in range(W):
        away = (coordinate - t) & 31
        masks.append(away == 0)
        factors.append(tap_weight(jnp.minimum(away, 32 - away)))
    return masks, factors


def spread_rows(pot_ref, vb_ref):
    def spread(row, _):
        line = (pot_ref[pl.ds(row, 1), :] + (DIAGONAL - filter_centre)) * (1.0 / filter_half)
        start = pl.multiple_of(row * 128, 128)
        vb_ref[pl.ds(start, 128), :] = jnp.broadcast_to(line, (128, 128)).T
        return 0

    lax.fori_loop(0, CELLS // 128, spread, 0)


def spread(pot):
    return pl.pallas_call(
        spread_rows,
        out_shape=sds((CELLS, S)),
        compiler_params=params(8),
        cost_estimate=cost(1 << 20, 2 << 20),
        name="spread",
    )(pot)


def prep_kernel(near_ref, corner_ref, vb_ref, s_ref, gg_ref, coef_ref, table_ref, a1_ref, a1z_ref, a2_ref, a2s_ref):
    for block in range(6):
        columns = slice(block * 128, block * 128 + 128)
        table_ref[columns, :] = near_ref[:, columns].T

    shape = (8, 128)
    sub = lax.broadcasted_iota(jnp.int32, shape, 0)
    lane = lax.broadcasted_iota(jnp.int32, shape, 1)
    first_lanes = lane < 64
    sites = [jnp.broadcast_to(table_ref[TAPS + d : TAPS + d + 1, :], shape).astype(jnp.int32) for d in range(3)]
    px = sites[0] - corner_ref[0]
    py = sites[1] - corner_ref[1]
    pz = (sites[2] & 15) + (((lane & 63) >> 4) - 1) * C
    zero = jnp.zeros(shape, F32)

    dz = sub + (lane >> 6) * 8 - pz + R
    z_masks = [dz == t for t in range(W)]
    z_factors = [tap_weight(jnp.abs(dz - t)) for t in range(W)]

    def place_z(ij, _):
        acc = zero
        along = zero
        for t in range(W):
            row = jnp.broadcast_to(table_ref[pl.ds(ij * W + t, 1), :], shape)
            acc = jnp.where(z_masks[t], row, acc)
            along = along + z_factors[t] * row
        a1_ref[ij] = acc
        a1z_ref[ij] = along
        return 0

    lax.fori_loop(0, W * W, place_z, 0)

    def place_y(y, _):
        masks, factors = ring_tables(y - py + R)
        for i in range(W):
            acc = zero
            along = zero
            moved = zero
            for t in range(W):
                value = a1_ref[i * W + t]
                acc = jnp.where(masks[t], value, acc)
                along = along + factors[t] * value
                moved = jnp.where(masks[t], a1z_ref[i * W + t], moved)
            a2_ref[i, y] = acc
            a2s_ref[i, y] = along + moved
        return 0

    lax.fori_loop(0, C, place_y, 0)

    def place_x(x, _):
        masks, factors = ring_tables(x - px + R)

        def per_y(y, _):
            row = pl.multiple_of(x * ROWS + y * C, C)
            acc = zero
            along = zero
            moved = zero
            for t in range(W):
                value = a2_ref[t, y]
                acc = jnp.where(masks[t], value, acc)
                along = along + factors[t] * value
                moved = jnp.where(masks[t], a2s_ref[t, y], moved)
            v = vb_ref[pl.ds(row, C), :]
            moved = along + moved + jnp.where(first_lanes, v[:8], v[8:]) * acc
            lower = jnp.where(first_lanes, acc, pltpu.roll(moved, 64, 1))
            upper = jnp.where(first_lanes, pltpu.roll(acc, 64, 1), moved)
            high, low = split(jnp.concatenate([lower, upper], axis=0))
            gg_ref[0, pl.ds(row, C), :] = high
            gg_ref[1, pl.ds(row, C), :] = low
            return 0

        lax.fori_loop(0, C, per_y, 0)
        return 0

    lax.fori_loop(0, C, place_x, 0)

    coef_ref[...] = jnp.zeros((3, NEAR, S), F32)

    def contract(x, _):
        rows = pl.ds(pl.multiple_of(x * 2 * ROWS, ROWS), 2 * ROWS)
        g_high, g_low = gg_ref[0, rows, :], gg_ref[1, rows, :]
        t_high, t_low = g_high.T, g_low.T
        high, low = split(s_ref[rows, :])
        got = mm(t_high, high) + (mm(t_high, low) + mm(t_low, high))
        t_high, t_low = t_high[:NEAR], t_low[:NEAR]
        pair = mm(t_high, g_high) + (mm(t_high, g_low) + mm(t_low, g_high))
        for slab in range(3):
            rows = slice(slab * C, slab * C + C)
            coef_ref[slab, 0:16] += got[rows]
            coef_ref[slab, 16:32] += got[64 + slab * C : 80 + slab * C]
            coef_ref[slab, 32:48] += pair[rows]
        return 0

    lax.fori_loop(0, C // 2, contract, 0)


def prep(near, corner, vb, s):
    vmem = pl.BlockSpec(memory_space=pltpu.VMEM)
    return pl.pallas_call(
        prep_kernel,
        in_specs=[vmem, pl.BlockSpec(memory_space=pltpu.SMEM), vmem, vmem],
        out_shape=[sds((2, CELLS, S), BF16), sds((3, NEAR, S))],
        scratch_shapes=[
            pltpu.VMEM((768, 128), F32),
            pltpu.VMEM((W * W, 8, 128), F32),
            pltpu.VMEM((W * W, 8, 128), F32),
            pltpu.VMEM((W, C, 8, 128), F32),
            pltpu.VMEM((W, C, 8, 128), F32),
        ],
        compiler_params=params(16),
        cost_estimate=cost(1 << 27, 10 << 20),
        name="prep",
    )(near, corner, vb, s.reshape(CELLS, S))


def merge_kernel(part_ref, below_ref, above_ref, out_ref):
    out_ref[0:32, :] = part_ref[1, 0:32, :] + below_ref[0:32, :] + above_ref[0:32, :]
    lane = lax.broadcasted_iota(jnp.int32, (16, 128), 1)
    below = jnp.where(lane < 32, pltpu.roll(below_ref[32:48, :], 112, 1), 0.0)
    above = jnp.where((lane >= 16) & (lane < 48), pltpu.roll(above_ref[32:48, :], 16, 1), 0.0)
    out_ref[32:48, :] = jnp.where(lane < 48, part_ref[1, 32:48, :], 0.0) + below + above


def merge(part, below, above):
    return pl.pallas_call(merge_kernel, out_shape=sds((NEAR, S)), compiler_params=params(4), name="merge")(part, below, above)


def weigh_kernel(own_ref, other_ref, energy_ref, one_ref, rest_ref):
    total = own_ref[...] + other_ref[...]
    one_ref[...] = total[0:16] * energy_ref[...]
    rest_ref[...] = total[16:48]


def weigh(own, other, energy):
    return pl.pallas_call(
        weigh_kernel, out_shape=[sds((16, S)), sds((32, S))], compiler_params=params(4), name="weigh"
    )(own, other, energy)


def again_kernel(rest_ref, below_ref, one_ref, above_ref, energy_ref, two_ref):
    near = jnp.concatenate([below_ref[...], one_ref[...], above_ref[...], jnp.zeros((S - NEAR, S), F32)])
    two_ref[...] = (rest_ref[0:16, :] + exact(rest_ref[16:32, :], near)) * energy_ref[...]


def again(rest, below, one, above, energy):
    return pl.pallas_call(again_kernel, out_shape=sds((16, S)), compiler_params=params(4), name="again")(
        rest, below, one, above, energy
    )


def first_kernel(s_ref, side_ref, edge_one_ref, edge_two_ref, vb_ref, q_ref, mix_ref, head_ref, tail_ref):
    def planes(edge_ref):
        def plane(p):
            for half in range(2):
                ring = {y: s_ref[p, halves(y, half), :] for y in range(C)}
                for y in range(H):
                    ring[C + y] = edge_ref[p, halves(y, half), :]
                    ring[y - H] = edge_ref[p, halves(H + y, half), :]
                for y in range(C):
                    rows = halves(y, half)
                    dy = tap_sum(lambda i: ring[i], y)
                    q = dy + vb_ref[p, rows, :] * ring[y]
                    q_ref[p, rows, :] = q
                    mix_ref[p, rows, :] = side_ref[p, rows, :] + q + dy
            for z in range(H):
                head_ref[z, p] = mix_ref[p, stride_rows(z), :]
                tail_ref[z, p] = mix_ref[p, stride_rows(C - H + z), :]

        per_plane(plane)

    step = pl.program_id(0)

    @pl.when(step < CUT // B)
    def _():
        planes(edge_one_ref)

    @pl.when(step >= CUT // B)
    def _():
        planes(edge_two_ref)


def make_first(s, side_part, edges, vb):
    return pl.pallas_call(
        first_kernel,
        grid=(STEPS,),
        in_specs=[plane_spec(), plane_spec()] + edge_specs() + [plane_spec()],
        out_specs=[plane_spec(), plane_spec(), halo_spec(), halo_spec()],
        out_shape=[FULL, FULL, HALO, HALO],
        compiler_params=params(16),
        cost_estimate=cost(1 << 24, 14 << 20),
        name="first",
    )(s, side_part, *edges, vb)


def base_kernel(s_ref, edge_one_ref, edge_two_ref, mid_ref, vb_ref, vb_mate_ref, q_ref, side_ref, part_ref, out_ref):
    def planes(edge_ref):
        def plane(p):
            for half in range(2):

                def other(y, half=half):
                    if y < H:
                        return edge_ref[p, halves(y, half), :]
                    if y < C - H:
                        return mid_ref[p, halves(y - H, half), :]
                    return edge_ref[p, halves(y - 4, half), :]

                ring = [s_ref[p, halves(y, half), :] for y in range(C)] + [other(y) for y in range(C)]
                q = {y: q_ref[p, halves(y, half), :] for y in range(C)}
                for y in list(range(H)) + list(range(C - H, C)):
                    v = vb_mate_ref[p, halves(y, half), :]
                    q[C + y] = tap_sum(lambda i: ring[i % 32], C + y) + v * ring[C + y]
                for y in range(C):
                    rows = halves(y, half)
                    total = tap_sum(lambda i: q[i % 32], y)
                    total = total + vb_ref[p, rows, :] * (side_ref[p, rows, :] + q[y])
                    out_ref[p, rows, :] = 2.0 * (total + part_ref[p, rows, :]) - ring[y]

        per_plane(plane)

    step = pl.program_id(0)

    @pl.when(step < CUT // B)
    def _():
        planes(edge_one_ref)

    @pl.when(step >= CUT // B)
    def _():
        planes(edge_two_ref)


def make_base(s, edges, mid, vb, vb_mate, q, side_part, part):
    return pl.pallas_call(
        base_kernel,
        grid=(STEPS,),
        in_specs=[plane_spec()] + edge_specs() + [plane_spec(64)] + [plane_spec()] * 5,
        out_specs=plane_spec(),
        out_shape=FULL,
        compiler_params=params(16),
        cost_estimate=cost(1 << 25, 16 << 20),
        name="base",
    )(s, *edges, mid, vb, vb_mate, q, side_part, part)


def second_kernel(base_ref, low_ref, high_ref, gg_high_ref, gg_low_ref, *rest):
    weighted = rest[:6]
    second_ref, gram_ref, cross_ref, w_ref = rest[6:]
    step = pl.program_id(0)

    @pl.when(step == 0)
    def _():
        gram_ref[...] = jnp.zeros((S, S), F32)
        cross_ref[...] = jnp.zeros((S, S), F32)
        w_ref[...] = jnp.zeros((S, S), F32)
        for j in range(3):
            w_ref[j * C : j * C + C, :] = 2.0 * weighted[j][...]
            w_ref[64 + j * C : 80 + j * C, :] = 2.0 * weighted[3 + j][...]

    w_high, w_low = split(w_ref[...])

    def plane(p):
        g_high, g_low = gg_high_ref[0, p], gg_low_ref[0, p]
        second_ref[p] = base_ref[p] + (mm(g_high, w_high) + (mm(g_high, w_low) + mm(g_low, w_high)))
        low = [low_ref[j, p] for j in range(H)]
        high = [high_ref[j, p] for j in range(H)]
        for z in range(H):
            add = sum((2.0 * OFF[k - 1]) * low[z - k + H] for k in range(z + 1, H + 1))
            second_ref[p, stride_rows(z), :] += add
            add = sum((2.0 * OFF[H + j - z - 1]) * high[j] for j in range(z + 1))
            second_ref[p, stride_rows(C - H + z), :] += add
        s_high, s_low = split(second_ref[p])
        turned = s_high.T
        gram_ref[...] += mm(turned, s_high)
        cross_ref[...] += mm(turned, s_low)

    per_plane(plane)

    @pl.when(step == STEPS - 1)
    def _():
        cross = cross_ref[...]
        gram_ref[...] += cross + cross.T


def make_second(base, low, high, gg, weighted):
    return pl.pallas_call(
        second_kernel,
        grid=(STEPS,),
        in_specs=[plane_spec(), halo_spec(), halo_spec(), part_spec(0), part_spec(1)] + [whole(C)] * 6,
        out_specs=[plane_spec(), whole()],
        out_shape=[FULL, sds((S, S))],
        scratch_shapes=[pltpu.VMEM((S, S), F32), pltpu.VMEM((S, S), F32)],
        compiler_params=params(16),
        cost_estimate=cost(1 << 27, 8 << 20),
        name="second",
    )(base, low, high, gg, gg, *weighted)


def exact(a, b):
    return jnp.dot(a, b, precision=lax.Precision.HIGHEST, preferred_element_type=F32)


def inverse_factor(gram_ref, a_ref, x_ref, state_ref):
    row = lax.broadcasted_iota(jnp.int32, (S, S), 0)
    column = lax.broadcasted_iota(jnp.int32, (S, S), 1)
    unit = jnp.where(row == column, 1.0, 0.0)
    gram = gram_ref[...]
    diagonal = jnp.where(row == column, gram, 0.0)
    down = lax.rsqrt(jnp.sum(diagonal, axis=1, keepdims=True))
    across = lax.rsqrt(jnp.sum(diagonal, axis=0, keepdims=True))
    a_ref[...] = gram * down * across
    x_ref[...] = unit

    def residual():
        x = x_ref[...]
        return unit - exact(exact(x, a_ref[...]), x.T)

    def size(e):
        return jnp.sum(e * e)

    def improve(e):
        lower = jnp.where(row > column, e, jnp.where(row == column, 0.5 * e, 0.0))
        x_ref[...] += exact(lower, x_ref[...])

    state_ref[0] = 0
    start = unit - a_ref[...]
    start_size = size(start)

    @pl.when(start_size < 0.16)
    def _():
        improve(start)
        state_ref[0] = jnp.where(start_size < 1e-6, 2, 1)

    for _ in range(5):

        @pl.when(state_ref[0] == 1)
        def _():
            e = residual()
            e_size = size(e)
            improve(e)
            state_ref[0] = jnp.where(e_size < 1e-6, 2, 1)

    @pl.when(state_ref[0] != 2)
    def _():
        x_ref[...] = unit
        lanes = lax.broadcasted_iota(jnp.int32, (1, S), 1)

        def step(j, _):
            line = a_ref[pl.ds(j, 1), :]
            scale = lax.rsqrt(jnp.sum(jnp.where(lanes == j, line, 0.0), axis=1, keepdims=True))
            a = a_ref[...]
            factor = jnp.sum(jnp.where(column == j, a, 0.0), axis=1, keepdims=True) * scale
            factor = jnp.where(row[:, :1] > j, factor, 0.0)
            x_line = x_ref[pl.ds(j, 1), :] * scale
            a_ref[...] = a - factor * (line * scale)
            x_ref[...] = jnp.where(row == j, x_line, x_ref[...] - factor * x_line)
            return 0

        lax.fori_loop(0, S, step, 0)

    x_ref[...] = x_ref[...] * across


def turn_kernel(second_ref, gram_ref, out_ref, a_ref, x_ref, i_high_ref, i_low_ref, state_ref):
    @pl.when(pl.program_id(0) == 0)
    def _():
        inverse_factor(gram_ref, a_ref, x_ref, state_ref)
        i_high, i_low = split(x_ref[...].T)
        i_high_ref[...] = i_high
        i_low_ref[...] = i_low

    i_high, i_low = i_high_ref[...], i_low_ref[...]

    def plane(p):
        high, low = split(second_ref[p])
        out_ref[p] = mm(high, i_high) + (mm(high, i_low) + mm(low, i_high))

    per_plane(plane)


def turn(second, gram):
    return pl.pallas_call(
        turn_kernel,
        grid=(STEPS,),
        in_specs=[plane_spec(), whole()],
        out_specs=plane_spec(),
        out_shape=FULL,
        scratch_shapes=[pltpu.VMEM((S, S), F32)] * 2 + [pltpu.VMEM((S, S), BF16)] * 2 + [pltpu.SMEM((1,), jnp.int32)],
        compiler_params=params(16),
        cost_estimate=cost(1 << 28, 4 << 20),
        name="turn",
    )(second, gram)


def per_device(states, potential, atom_sites, projectors, energies):
    gx, gy = lax.axis_index("gx"), lax.axis_index("gy")
    depth = lax.axis_size("gzs")
    count = 4 * depth
    barrier = lax.optimization_barrier

    def send(value, flip=0, move=0):
        def target(d):
            return (d // depth * depth ^ flip) + (d + move) % depth

        return lax.ppermute(value, AXES, [(d, target(d)) for d in range(count)])

    over_x, over_y = 2 * depth, depth
    s = states.reshape(C, ROWS, S)
    pot = potential.reshape(32, 128)

    atoms = jnp.concatenate(
        [projectors.reshape(4, TAPS), atom_sites.astype(F32), energies[:, None], jnp.zeros((4, 768 - TAPS - 4), F32)],
        axis=1,
    )
    parcel = jnp.concatenate([atoms.reshape(24, 128), pot])
    parcel_mate = send(parcel, over_y)
    below, above = send(atoms, 0, 1), send(atoms, 0, -1)
    below_mate, above_mate = send(atoms, over_y, 1), send(atoms, over_y, -1)
    packed = pack(barrier((s, atoms))[0])
    edges, mid, head, tail = packed[:2], packed[2], packed[3], packed[4]
    edge_one = send(edges[0], over_y)
    low, high = send(tail, 0, 1), send(head, 0, -1)
    mine = jnp.stack([below, atoms, above])
    other = jnp.stack([below_mate, parcel_mate[:24].reshape(4, 768), above_mate])
    column = jnp.where(gy == 0, jnp.concatenate([mine, other], 1), jnp.concatenate([other, mine], 1))
    column_mate = send(column, over_x)
    s_mate, _ = barrier((s, column))
    mate = send(s_mate, over_x)
    near = jnp.where(
        gx == 0, jnp.concatenate([column, column_mate], 1), jnp.concatenate([column_mate, column], 1)
    ).reshape(NEAR, 768)
    gap = jnp.zeros((16, 768), F32)
    energy = near[16:32, TAPS + 3 : TAPS + 4] * (1.0 / filter_half)
    corner = jnp.stack([gx * C, gy * C]).astype(jnp.int32)
    vb = spread(pot)
    beside = side_x(s, mate)
    near, beside = barrier((jnp.concatenate([near, gap, near, gap]), beside))
    gg, part = prep(near, corner, vb, s)

    part = part + send(part, over_x)
    own = merge(part, send(part[2], 0, 1), send(part[0], 0, -1))
    edge_two, own = barrier((edges[1], own))
    own_mate = send(own, over_y)
    edge_two = send(edge_two, over_y)
    one, rest = weigh(own, own_mate, energy)
    mid, one = barrier((mid, one))
    mid = send(mid, over_y)
    ones = [send(one, 0, 1), one, send(one, 0, -1)]

    vb = vb.reshape(C, ROWS, S)
    vb_mate = spread(parcel_mate[24:]).reshape(C, ROWS, S)
    side_part = side_z(s, beside, low, high)
    edge_two, ones = barrier((edge_two, ones))
    edges = [edge_one, edge_two]
    two = again(rest, *ones, energy)
    twos = [send(two, 0, 1), two, send(two, 0, -1)]
    q, mix, head, tail = make_first(s, side_part, edges, vb)
    low, high = send(tail, 0, 1), send(head, 0, -1)
    mate = send(mix, over_x)
    part = side_again(mix, mate)
    base = make_base(s, edges, mid, vb, vb_mate, q, side_part, part)
    second, gram = make_second(base, low, high, gg.reshape(2, C, ROWS, S), twos + ones)

    for flip in (64, 32, 36, 1, 3, 8, 24):
        gram = gram + lax.ppermute(gram, AXES, [(d, d ^ flip) for d in range(count)])
    gram = gram * (1.0 / (CELLS * count))
    return turn(second, gram).reshape(C, C, C, S)


def solution(mesh):
    return jax.shard_map(
        per_device,
        mesh=mesh,
        in_specs=(
            P("gx", "gy", "gzs", None),
            P("gx", "gy", "gzs"),
            P(("gx", "gy", "gzs"), None),
            P(("gx", "gy", "gzs"), None, None, None),
            P(("gx", "gy", "gzs")),
        ),
        out_specs=P("gx", "gy", "gzs", None),
        check_vma=False,
    )
```

```python
import math

import jax
import jax.numpy as jnp
from jax import lax
from jax.experimental import pallas as pl
from jax.experimental.pallas import tpu as pltpu
from jax.sharding import PartitionSpec as P

AXES = ("gx", "gy", "gzs")
H = 6
C = 16
ROWS = C * C
CELLS = C * C * C
S = 128
W = 9
R = 4
NEAR = 48
TAPS = W * W * W
F32 = jnp.float32
BF16 = jnp.bfloat16

grid_step = 0.6
filter_centre = 36.0
filter_half = 26.0


def weights():
    taps = []
    for k in range(1, 7):
        top = 2.0 * (-1) ** (k + 1) * math.factorial(6) ** 2
        under = k * k * math.factorial(6 - k) * math.factorial(6 + k)
        taps.append(top / under)
    scale = -0.5 / (grid_step * grid_step)
    off = [scale * t / filter_half for t in taps]
    diagonal = 3.0 * scale * (-2.0 * sum(taps))
    return off, diagonal


OFF, DIAGONAL = weights()


def params(mib):
    return pltpu.CompilerParams(vmem_limit_bytes=mib * 1024 * 1024)


def cost(flops, nbytes):
    return pl.CostEstimate(flops=flops, bytes_accessed=nbytes, transcendentals=0)


def sds(shape, dtype=F32):
    return jax.ShapeDtypeStruct(shape, dtype)


def split(value):
    high = value.astype(BF16)
    low = (value - high.astype(F32)).astype(BF16)
    return high, low


def mm(a, b):
    return jnp.dot(a, b, preferred_element_type=F32)


def tap_sum(at, index):
    total = None
    for k in range(1, 7):
        term = OFF[k - 1] * (at(index + k) + at(index - k))
        total = term if total is None else total + term
    return total


B = 4
STEPS = C // B
N = 2
CUTS = (0, 6, 14, 16)


def stride_rows(z):
    return pl.ds(z, C, stride=C)


def plane_spec(rows=ROWS, planes=B):
    return pl.BlockSpec((planes, rows, S), lambda i: (i, 0, 0))


def halo_spec(planes=B):
    return pl.BlockSpec((H, planes, C, S), lambda i: (0, i, 0, 0))


def part_spec(part):
    return pl.BlockSpec((1, B, ROWS, S), lambda i: (part, i, 0, 0))


def whole(rows=S):
    return pl.BlockSpec((rows, S), lambda i: (0, 0))


def edge_specs():
    def spec(start, stop):
        return pl.BlockSpec((N, 192, S), lambda i: (jnp.clip(i - start // N, 0, (stop - start) // N - 1), 0, 0))

    return [spec(start, stop) for start, stop in zip(CUTS, CUTS[1:])]


def for_piece(pieces, body):
    step = pl.program_id(0)
    for piece, start, stop in zip(pieces, CUTS, CUTS[1:]):

        @pl.when((step >= start // N) & (step < stop // N))
        def _(piece=piece):
            body(piece)


FULL = sds((C, ROWS, S))
HALO = sds((H, C, C, S))
EDGES = [sds((stop - start, 192, S)) for start, stop in zip(CUTS, CUTS[1:])]


def halves(y, half):
    return slice(y * C + half * 8, y * C + half * 8 + 8)


def pack_kernel(s_ref, *refs):
    mid_ref, head_ref, tail_ref = refs[3:]

    def edges(out_ref):
        out_ref[:, 0:96, :] = s_ref[:, 0:96, :]
        out_ref[:, 96:192, :] = s_ref[:, 160:256, :]

    for_piece(refs[:3], edges)
    mid_ref[...] = s_ref[:, 96:160, :]
    for p in range(N):
        for z in range(H):
            head_ref[z, p] = s_ref[p, stride_rows(z), :]
            tail_ref[z, p] = s_ref[p, stride_rows(C - H + z), :]


def pack(s):
    return pl.pallas_call(
        pack_kernel,
        grid=(C // N,),
        in_specs=[plane_spec(ROWS, N)],
        out_specs=edge_specs() + [plane_spec(64, N), halo_spec(N), halo_spec(N)],
        out_shape=EDGES + [sds((C, 64, S)), HALO, HALO],
        compiler_params=params(12),
        cost_estimate=cost(1 << 32, 6 << 20),
        name="pack",
    )(s)


def along_x(s_ref, mate_ref, out_ref, add):
    def column(block, _):
        rows = pl.ds(pl.multiple_of(block * 8, 8), 8)
        ring = [mate_ref[C - H + i, rows, :] for i in range(H)]
        ring += [s_ref[x, rows, :] for x in range(C)]
        ring += [mate_ref[i, rows, :] for i in range(H)]
        for x in range(C):
            value = tap_sum(lambda i: ring[H + i], x)
            if add:
                value = value + out_ref[x, rows, :]
            out_ref[x, rows, :] = value
        return 0

    lax.fori_loop(0, ROWS // 8, column, 0)


def z_taps(ext_ref, y):
    return tap_sum(lambda k: ext_ref[y * 32 + 8 + k : y * 32 + 24 + k, :], 0)


def side_x_kernel(s_ref, mate_ref, out_ref):
    along_x(s_ref, mate_ref, out_ref, False)


def side_x(s, mate):
    return pl.pallas_call(
        side_x_kernel,
        out_shape=FULL,
        compiler_params=params(12),
        cost_estimate=cost(1 << 24, 6 << 20),
        name="side_x",
    )(s, mate)


def side_z_kernel(s_ref, part_ref, low_ref, high_ref, out_ref, ext_ref):
    def plane(x, _):
        for y in range(C):
            ext_ref[y * 32 + 8 : y * 32 + 24, :] = s_ref[x, y * C : (y + 1) * C, :]
        for z in range(H):
            ext_ref[pl.ds(2 + z, C, stride=32), :] = low_ref[z, x]
            ext_ref[pl.ds(24 + z, C, stride=32), :] = high_ref[z, x]
        for y in range(C):
            rows = slice(y * C, (y + 1) * C)
            out_ref[x, rows, :] = part_ref[x, rows, :] + z_taps(ext_ref, y)
        return 0

    lax.fori_loop(0, C, plane, 0)


def side_z(s, part, low, high):
    return pl.pallas_call(
        side_z_kernel,
        out_shape=FULL,
        scratch_shapes=[pltpu.VMEM((C * 32, S), F32)],
        compiler_params=params(14),
        cost_estimate=cost(1 << 24, 8 << 20),
        name="side_z",
    )(s, part, low, high)


def side_again_kernel(s_ref, mate_ref, out_ref, ext_ref):
    for y in range(C):
        ext_ref[y * 32 : y * 32 + 8, :] = jnp.zeros((8, S), F32)
        ext_ref[y * 32 + 24 : y * 32 + 32, :] = jnp.zeros((8, S), F32)

    def plane(x, _):
        for y in range(C):
            ext_ref[y * 32 + 8 : y * 32 + 24, :] = s_ref[x, y * C : (y + 1) * C, :]
        for y in range(C):
            out_ref[x, y * C : (y + 1) * C, :] = z_taps(ext_ref, y)
        return 0

    lax.fori_loop(0, C, plane, 0)
    along_x(s_ref, mate_ref, out_ref, True)


def side_again(s, mate):
    return pl.pallas_call(
        side_again_kernel,
        out_shape=FULL,
        scratch_shapes=[pltpu.VMEM((C * 32, S), F32)],
        compiler_params=params(12),
        cost_estimate=cost(1 << 25, 6 << 20),
        name="side_again",
    )(s, mate)


def tap_weight(distance):
    value = jnp.zeros(distance.shape, F32)
    for k in range(1, 7):
        value = jnp.where(distance == k, OFF[k - 1], value)
    return value


def ring_tables(coordinate):
    masks, factors = [], []
    for t in range(W):
        away = (coordinate - t) & 31
        masks.append(away == 0)
        factors.append(tap_weight(jnp.minimum(away, 32 - away)))
    return masks, factors


def spread_rows(pot_ref, vb_ref):
    def spread(row, _):
        line = (pot_ref[pl.ds(row, 1), :] + (DIAGONAL - filter_centre)) * (1.0 / filter_half)
        start = pl.multiple_of(row * 128, 128)
        vb_ref[pl.ds(start, 128), :] = jnp.broadcast_to(line, (128, 128)).T
        return 0

    lax.fori_loop(0, CELLS // 128, spread, 0, unroll=8)


def spread(pot):
    return pl.pallas_call(
        spread_rows,
        out_shape=sds((CELLS, S)),
        compiler_params=params(8),
        cost_estimate=cost(1 << 20, 2 << 20),
        name="spread",
    )(pot)


def prep_kernel(near_ref, corner_ref, vb_ref, s_ref, gg_ref, coef_ref, table_ref, a1_ref, a1z_ref, a2_ref, a2s_ref):
    for block in range(6):
        columns = slice(block * 128, block * 128 + 128)
        table_ref[columns, :] = near_ref[:, columns].T

    shape = (8, 128)
    sub = lax.broadcasted_iota(jnp.int32, shape, 0)
    lane = lax.broadcasted_iota(jnp.int32, shape, 1)
    first_lanes = lane < 64
    sites = [jnp.broadcast_to(table_ref[TAPS + d : TAPS + d + 1, :], shape).astype(jnp.int32) for d in range(3)]
    px = sites[0] - corner_ref[0]
    py = sites[1] - corner_ref[1]
    pz = (sites[2] & 15) + (((lane & 63) >> 4) - 1) * C
    zero = jnp.zeros(shape, F32)

    dz = sub + (lane >> 6) * 8 - pz + R
    z_masks = [dz == t for t in range(W)]
    z_factors = [tap_weight(jnp.abs(dz - t)) for t in range(W)]

    def place_z(ij, _):
        acc = zero
        along = zero
        for t in range(W):
            row = jnp.broadcast_to(table_ref[pl.ds(ij * W + t, 1), :], shape)
            acc = jnp.where(z_masks[t], row, acc)
            along = along + z_factors[t] * row
        a1_ref[ij] = acc
        a1z_ref[ij] = along
        return 0

    lax.fori_loop(0, W * W, place_z, 0, unroll=3)

    def place_y(y, _):
        masks, factors = ring_tables(y - py + R)
        for i in range(W):
            acc = zero
            along = zero
            moved = zero
            for t in range(W):
                value = a1_ref[i * W + t]
                acc = jnp.where(masks[t], value, acc)
                along = along + factors[t] * value
                moved = jnp.where(masks[t], a1z_ref[i * W + t], moved)
            a2_ref[i, y] = acc
            a2s_ref[i, y] = along + moved
        return 0

    lax.fori_loop(0, C, place_y, 0)

    def place_x(x, _):
        masks, factors = ring_tables(x - px + R)

        def per_y(y, _):
            row = pl.multiple_of(x * ROWS + y * C, C)
            acc = zero
            along = zero
            moved = zero
            for t in range(W):
                value = a2_ref[t, y]
                acc = jnp.where(masks[t], value, acc)
                along = along + factors[t] * value
                moved = jnp.where(masks[t], a2s_ref[t, y], moved)
            v = vb_ref[pl.ds(row, C), :]
            moved = along + moved + jnp.where(first_lanes, v[:8], v[8:]) * acc
            lower = jnp.where(first_lanes, acc, pltpu.roll(moved, 64, 1))
            upper = jnp.where(first_lanes, pltpu.roll(acc, 64, 1), moved)
            high, low = split(jnp.concatenate([lower, upper], axis=0))
            gg_ref[0, pl.ds(row, C), :] = high
            gg_ref[1, pl.ds(row, C), :] = low
            return 0

        lax.fori_loop(0, C, per_y, 0, unroll=16)
        return 0

    lax.fori_loop(0, C, place_x, 0)

    coef_ref[...] = jnp.zeros((3, NEAR, S), F32)

    def contract(x, _):
        rows = pl.ds(pl.multiple_of(x * 2 * ROWS, ROWS), 2 * ROWS)
        g_high, g_low = gg_ref[0, rows, :], gg_ref[1, rows, :]
        t_high, t_low = g_high.T, g_low.T
        high, low = split(s_ref[rows, :])
        got = mm(t_high, high) + (mm(t_high, low) + mm(t_low, high))
        t_high, t_low = t_high[:NEAR], t_low[:NEAR]
        pair = mm(t_high, g_high) + (mm(t_high, g_low) + mm(t_low, g_high))
        for slab in range(3):
            rows = slice(slab * C, slab * C + C)
            coef_ref[slab, 0:16] += got[rows]
            coef_ref[slab, 16:32] += got[64 + slab * C : 80 + slab * C]
            coef_ref[slab, 32:48] += pair[rows]
        return 0

    lax.fori_loop(0, C // 2, contract, 0, unroll=2)


def prep(near, corner, vb, s):
    vmem = pl.BlockSpec(memory_space=pltpu.VMEM)
    return pl.pallas_call(
        prep_kernel,
        in_specs=[vmem, pl.BlockSpec(memory_space=pltpu.SMEM), vmem, vmem],
        out_shape=[sds((2, CELLS, S), BF16), sds((3, NEAR, S))],
        scratch_shapes=[
            pltpu.VMEM((768, 128), F32),
            pltpu.VMEM((W * W, 8, 128), F32),
            pltpu.VMEM((W * W, 8, 128), F32),
            pltpu.VMEM((W, C, 8, 128), F32),
            pltpu.VMEM((W, C, 8, 128), F32),
        ],
        compiler_params=params(16),
        cost_estimate=cost(1 << 27, 10 << 20),
        name="prep",
    )(near, corner, vb, s.reshape(CELLS, S))


def merge_kernel(part_ref, below_ref, above_ref, out_ref):
    out_ref[0:32, :] = part_ref[1, 0:32, :] + below_ref[0:32, :] + above_ref[0:32, :]
    lane = lax.broadcasted_iota(jnp.int32, (16, 128), 1)
    below = jnp.where(lane < 32, pltpu.roll(below_ref[32:48, :], 112, 1), 0.0)
    above = jnp.where((lane >= 16) & (lane < 48), pltpu.roll(above_ref[32:48, :], 16, 1), 0.0)
    out_ref[32:48, :] = jnp.where(lane < 48, part_ref[1, 32:48, :], 0.0) + below + above


def merge(part, below, above):
    return pl.pallas_call(merge_kernel, out_shape=sds((NEAR, S)), compiler_params=params(4), name="merge")(part, below, above)


def weigh_kernel(own_ref, other_ref, energy_ref, one_ref, rest_ref):
    total = own_ref[...] + other_ref[...]
    one_ref[...] = total[0:16] * energy_ref[...]
    rest_ref[...] = total[16:48]


def weigh(own, other, energy):
    return pl.pallas_call(
        weigh_kernel, out_shape=[sds((16, S)), sds((32, S))], compiler_params=params(4), name="weigh"
    )(own, other, energy)


def again_kernel(rest_ref, below_ref, one_ref, above_ref, energy_ref, two_ref):
    near = jnp.concatenate([below_ref[...], one_ref[...], above_ref[...], jnp.zeros((S - NEAR, S), F32)])
    two_ref[...] = (rest_ref[0:16, :] + exact(rest_ref[16:32, :], near)) * energy_ref[...]


def again(rest, below, one, above, energy):
    return pl.pallas_call(again_kernel, out_shape=sds((16, S)), compiler_params=params(4), name="again")(
        rest, below, one, above, energy
    )


def first_kernel(s_ref, side_ref, vb_ref, *refs):
    q_ref, mix_ref, head_ref, tail_ref = refs[3:]

    def planes(edge_ref):
        for p in range(N):
            for half in range(2):
                ring = {y: s_ref[p, halves(y, half), :] for y in range(C)}
                for y in range(H):
                    ring[C + y] = edge_ref[p, halves(y, half), :]
                    ring[y - H] = edge_ref[p, halves(H + y, half), :]
                for y in range(C):
                    rows = halves(y, half)
                    dy = tap_sum(lambda i: ring[i], y)
                    q = dy + vb_ref[p, rows, :] * ring[y]
                    q_ref[p, rows, :] = q
                    mix_ref[p, rows, :] = side_ref[p, rows, :] + q + dy
            for z in range(H):
                head_ref[z, p] = mix_ref[p, stride_rows(z), :]
                tail_ref[z, p] = mix_ref[p, stride_rows(C - H + z), :]

    for_piece(refs[:3], planes)


def make_first(s, side_part, vb, edges):
    return pl.pallas_call(
        first_kernel,
        grid=(C // N,),
        in_specs=[plane_spec(ROWS, N)] * 3 + edge_specs(),
        out_specs=[plane_spec(ROWS, N), plane_spec(ROWS, N), halo_spec(N), halo_spec(N)],
        out_shape=[FULL, FULL, HALO, HALO],
        compiler_params=params(16),
        cost_estimate=cost(1 << 24, 14 << 20),
        name="first",
    )(s, side_part, vb, *edges)


def base_kernel(s_ref, mid_ref, vb_ref, vb_mate_ref, q_ref, side_ref, part_ref, *refs):
    out_ref = refs[3]

    def planes(edge_ref):
        for p in range(N):
            for half in range(2):

                def other(y, p=p, half=half):
                    if y < H:
                        return edge_ref[p, halves(y, half), :]
                    if y < C - H:
                        return mid_ref[p, halves(y - H, half), :]
                    return edge_ref[p, halves(y - 4, half), :]

                ring = [s_ref[p, halves(y, half), :] for y in range(C)] + [other(y) for y in range(C)]
                q = {y: q_ref[p, halves(y, half), :] for y in range(C)}
                for y in list(range(H)) + list(range(C - H, C)):
                    v = vb_mate_ref[p, halves(y, half), :]
                    q[C + y] = tap_sum(lambda i: ring[i % 32], C + y) + v * ring[C + y]
                for y in range(C):
                    rows = halves(y, half)
                    total = tap_sum(lambda i: q[i % 32], y)
                    total = total + vb_ref[p, rows, :] * (side_ref[p, rows, :] + q[y])
                    out_ref[p, rows, :] = 2.0 * (total + part_ref[p, rows, :]) - ring[y]

    for_piece(refs[:3], planes)


def make_base(s, mid, vb, vb_mate, q, side_part, part, edges):
    return pl.pallas_call(
        base_kernel,
        grid=(C // N,),
        in_specs=[plane_spec(ROWS, N), plane_spec(64, N)] + [plane_spec(ROWS, N)] * 5 + edge_specs(),
        out_specs=plane_spec(ROWS, N),
        out_shape=FULL,
        compiler_params=params(16),
        cost_estimate=cost(1 << 25, 16 << 20),
        name="base",
    )(s, mid, vb, vb_mate, q, side_part, part, *edges)


def second_kernel(base_ref, low_ref, high_ref, gg_high_ref, gg_low_ref, *rest):
    weighted = rest[:6]
    second_ref, gram_ref, cross_ref, w_ref, halo_ref = rest[6:]
    step = pl.program_id(0)

    @pl.when(step == 0)
    def _():
        gram_ref[...] = jnp.zeros((S, S), F32)
        cross_ref[...] = jnp.zeros((S, S), F32)
        w_ref[...] = jnp.zeros((S, S), F32)
        halo_ref[...] = jnp.zeros((B, ROWS, S), F32)
        for j in range(3):
            w_ref[j * C : j * C + C, :] = 2.0 * weighted[j][...]
            w_ref[64 + j * C : 80 + j * C, :] = 2.0 * weighted[3 + j][...]

    for p in range(B):
        low = [low_ref[j, p] for j in range(H)]
        high = [high_ref[j, p] for j in range(H)]
        for z in range(H):
            add = sum((2.0 * OFF[k - 1]) * low[z - k + H] for k in range(z + 1, H + 1))
            halo_ref[p, stride_rows(z), :] = add
            add = sum((2.0 * OFF[H + j - z - 1]) * high[j] for j in range(z + 1))
            halo_ref[p, stride_rows(C - H + z), :] = add

    w_high, w_low = split(w_ref[...])
    gram = jnp.zeros((S, S), F32)
    cross = jnp.zeros((S, S), F32)
    for p in range(B):
        g_high, g_low = gg_high_ref[0, p], gg_low_ref[0, p]
        value = base_ref[p] + halo_ref[p] + (mm(g_high, w_high) + (mm(g_high, w_low) + mm(g_low, w_high)))
        second_ref[p] = value
        s_high, s_low = split(value)
        turned = s_high.T
        gram += mm(turned, s_high)
        cross += mm(turned, s_low)
    gram_ref[...] += gram
    cross_ref[...] += cross

    @pl.when(step == STEPS - 1)
    def _():
        cross = cross_ref[...]
        gram_ref[...] += cross + cross.T


def make_second(base, low, high, gg, weighted):
    return pl.pallas_call(
        second_kernel,
        grid=(STEPS,),
        in_specs=[plane_spec(), halo_spec(), halo_spec(), part_spec(0), part_spec(1)] + [whole(C)] * 6,
        out_specs=[plane_spec(), whole()],
        out_shape=[FULL, sds((S, S))],
        scratch_shapes=[pltpu.VMEM((S, S), F32), pltpu.VMEM((S, S), F32), pltpu.VMEM((B, ROWS, S), F32)],
        compiler_params=params(16),
        cost_estimate=cost(1 << 27, 8 << 20),
        name="second",
    )(base, low, high, gg, gg, *weighted)


def exact(a, b):
    return jnp.dot(a, b, precision=lax.Precision.HIGHEST, preferred_element_type=F32)


def inverse_factor(gram_ref, a_ref, x_ref, state_ref):
    row = lax.broadcasted_iota(jnp.int32, (S, S), 0)
    column = lax.broadcasted_iota(jnp.int32, (S, S), 1)
    unit = jnp.where(row == column, 1.0, 0.0)
    gram = gram_ref[...]
    diagonal = jnp.where(row == column, gram, 0.0)
    down = lax.rsqrt(jnp.sum(diagonal, axis=1, keepdims=True))
    across = lax.rsqrt(jnp.sum(diagonal, axis=0, keepdims=True))
    a_ref[...] = gram * down * across
    x_ref[...] = unit

    def residual():
        x = x_ref[...]
        return unit - exact(exact(x, a_ref[...]), x.T)

    def size(e):
        return jnp.sum(e * e)

    def improve(e):
        lower = jnp.where(row > column, e, jnp.where(row == column, 0.5 * e, 0.0))
        x_ref[...] += exact(lower, x_ref[...])

    state_ref[0] = 0
    start = unit - a_ref[...]
    start_size = size(start)

    @pl.when(start_size < 0.16)
    def _():
        improve(start)
        state_ref[0] = jnp.where(start_size < 1e-6, 2, 1)

    for _ in range(5):

        @pl.when(state_ref[0] == 1)
        def _():
            e = residual()
            e_size = size(e)
            improve(e)
            state_ref[0] = jnp.where(e_size < 1e-6, 2, 1)

    @pl.when(state_ref[0] != 2)
    def _():
        x_ref[...] = unit
        lanes = lax.broadcasted_iota(jnp.int32, (1, S), 1)

        def step(j, _):
            line = a_ref[pl.ds(j, 1), :]
            scale = lax.rsqrt(jnp.sum(jnp.where(lanes == j, line, 0.0), axis=1, keepdims=True))
            a = a_ref[...]
            factor = jnp.sum(jnp.where(column == j, a, 0.0), axis=1, keepdims=True) * scale
            factor = jnp.where(row[:, :1] > j, factor, 0.0)
            x_line = x_ref[pl.ds(j, 1), :] * scale
            a_ref[...] = a - factor * (line * scale)
            x_ref[...] = jnp.where(row == j, x_line, x_ref[...] - factor * x_line)
            return 0

        lax.fori_loop(0, S, step, 0)

    x_ref[...] = x_ref[...] * across


def turn_kernel(second_ref, gram_ref, out_ref, a_ref, x_ref, i_high_ref, i_low_ref, state_ref):
    @pl.when(pl.program_id(0) == 0)
    def _():
        inverse_factor(gram_ref, a_ref, x_ref, state_ref)
        i_high, i_low = split(x_ref[...].T)
        i_high_ref[...] = i_high
        i_low_ref[...] = i_low

    i_high, i_low = i_high_ref[...], i_low_ref[...]

    for p in range(B):
        high, low = split(second_ref[p])
        out_ref[p] = mm(high, i_high) + (mm(high, i_low) + mm(low, i_high))


def turn(second, gram):
    return pl.pallas_call(
        turn_kernel,
        grid=(STEPS,),
        in_specs=[plane_spec(), whole()],
        out_specs=plane_spec(),
        out_shape=FULL,
        scratch_shapes=[pltpu.VMEM((S, S), F32)] * 2 + [pltpu.VMEM((S, S), BF16)] * 2 + [pltpu.SMEM((1,), jnp.int32)],
        compiler_params=params(16),
        cost_estimate=cost(1 << 28, 4 << 20),
        name="turn",
    )(second, gram)


def per_device(states, potential, atom_sites, projectors, energies):
    gx, gy = lax.axis_index("gx"), lax.axis_index("gy")
    depth = lax.axis_size("gzs")
    count = 4 * depth
    barrier = lax.optimization_barrier

    def send(value, flip=0, move=0):
        def target(d):
            return (d // depth * depth ^ flip) + (d + move) % depth

        return lax.ppermute(value, AXES, [(d, target(d)) for d in range(count)])

    over_x, over_y = 2 * depth, depth
    s = states.reshape(C, ROWS, S)
    pot = potential.reshape(32, 128)

    atoms = jnp.concatenate(
        [projectors.reshape(4, TAPS), atom_sites.astype(F32), energies[:, None], jnp.zeros((4, 768 - TAPS - 4), F32)],
        axis=1,
    )
    mate = send(s, over_x)
    below, above = send(atoms, 0, 1), send(atoms, 0, -1)
    one_edge, two_edge, three_edge, mid, head, tail = pack(s)
    one_edge = send(one_edge, over_y)
    mine = jnp.stack([below, atoms, above])
    head, tail, mine = barrier((head, tail, mine))
    parcel = send(jnp.concatenate([mine.reshape(72, 128), pot]), over_y)
    low, high = send(tail, 0, 1), send(head, 0, -1)
    other, two_edge = barrier((parcel[:72].reshape(3, 4, 768), two_edge))
    two_edge = send(two_edge, over_y)
    column = jnp.where(gy == 0, jnp.concatenate([mine, other], 1), jnp.concatenate([other, mine], 1))
    column_mate = send(column, over_x)
    near = jnp.where(
        gx == 0, jnp.concatenate([column, column_mate], 1), jnp.concatenate([column_mate, column], 1)
    ).reshape(NEAR, 768)
    gap = jnp.zeros((16, 768), F32)
    energy = near[16:32, TAPS + 3 : TAPS + 4] * (1.0 / filter_half)
    corner = jnp.stack([gx * C, gy * C]).astype(jnp.int32)
    vb = spread(pot)
    beside = side_x(s, mate)
    near, beside, one_edge = barrier((jnp.concatenate([near, gap, near, gap]), beside, one_edge))
    gg, part = prep(near, corner, vb, s)

    part = part + send(part, over_x)
    own = merge(part, send(part[2], 0, 1), send(part[0], 0, -1))
    three_edge, own = barrier((three_edge, own))
    own_mate = send(own, over_y)
    three_edge = send(three_edge, over_y)
    one, rest = weigh(own, own_mate, energy)
    mid, one, two_edge = barrier((mid, one, two_edge))
    mid = send(mid, over_y)
    ones = [send(one, 0, 1), one, send(one, 0, -1)]

    vb = vb.reshape(C, ROWS, S)
    vb_mate = spread(parcel[72:]).reshape(C, ROWS, S)
    side_part = side_z(s, beside, low, high)
    three_edge, ones = barrier((three_edge, ones))
    edges = [one_edge, two_edge, three_edge]
    two = again(rest, *ones, energy)
    twos = [send(two, 0, 1), two, send(two, 0, -1)]
    q, mix, head, tail = make_first(s, side_part, vb, edges)
    low, high = send(tail, 0, 1), send(head, 0, -1)
    mate = send(mix, over_x)
    part = side_again(mix, mate)
    base = make_base(s, mid, vb, vb_mate, q, side_part, part, edges)
    second, gram = make_second(base, low, high, gg.reshape(2, C, ROWS, S), twos + ones)

    for flip in (64, 32, 36, 1, 3, 8, 24):
        gram = gram + lax.ppermute(gram, AXES, [(d, d ^ flip) for d in range(count)])
    gram = gram * (1.0 / (CELLS * count))
    return turn(second, gram).reshape(C, C, C, S)


def solution(mesh):
    return jax.shard_map(
        per_device,
        mesh=mesh,
        in_specs=(
            P("gx", "gy", "gzs", None),
            P("gx", "gy", "gzs"),
            P(("gx", "gy", "gzs"), None),
            P(("gx", "gy", "gzs"), None, None, None),
            P(("gx", "gy", "gzs")),
        ),
        out_specs=P("gx", "gy", "gzs", None),
        check_vma=False,
    )
```

```python
import math

import jax
import jax.numpy as jnp
from jax import lax
from jax.experimental import pallas as pl
from jax.experimental.pallas import tpu as pltpu
from jax.sharding import PartitionSpec as P

AXES = ("gx", "gy", "gzs")
H = 6
C = 16
ROWS = C * C
CELLS = C * C * C
S = 128
W = 9
R = 4
NEAR = 48
TAPS = W * W * W
F32 = jnp.float32
BF16 = jnp.bfloat16

grid_step = 0.6
filter_centre = 36.0
filter_half = 26.0


def weights():
    taps = []
    for k in range(1, 7):
        top = 2.0 * (-1) ** (k + 1) * math.factorial(6) ** 2
        under = k * k * math.factorial(6 - k) * math.factorial(6 + k)
        taps.append(top / under)
    scale = -0.5 / (grid_step * grid_step)
    off = [scale * t / filter_half for t in taps]
    diagonal = 3.0 * scale * (-2.0 * sum(taps))
    return off, diagonal


OFF, DIAGONAL = weights()


def params(mib):
    return pltpu.CompilerParams(vmem_limit_bytes=mib * 1024 * 1024)


def cost(flops, nbytes):
    return pl.CostEstimate(flops=flops, bytes_accessed=nbytes, transcendentals=0)


def sds(shape, dtype=F32):
    return jax.ShapeDtypeStruct(shape, dtype)


def split(value):
    high = value.astype(BF16)
    low = (value - high.astype(F32)).astype(BF16)
    return high, low


def mm(a, b):
    return jnp.dot(a, b, preferred_element_type=F32)


def tap_sum(at, index):
    total = None
    for k in range(1, 7):
        term = OFF[k - 1] * (at(index + k) + at(index - k))
        total = term if total is None else total + term
    return total


B = 4
STEPS = C // B
N = 2
CUTS = (0, 6, 16)


def stride_rows(z):
    return pl.ds(z, C, stride=C)


def plane_spec(rows=ROWS, planes=B):
    return pl.BlockSpec((planes, rows, S), lambda i: (i, 0, 0))


def halo_spec(planes=B):
    return pl.BlockSpec((H, planes, C, S), lambda i: (0, i, 0, 0))


def part_spec(part):
    return pl.BlockSpec((1, B, ROWS, S), lambda i: (part, i, 0, 0))


def whole(rows=S):
    return pl.BlockSpec((rows, S), lambda i: (0, 0))


def edge_specs():
    def spec(start, stop):
        return pl.BlockSpec((N, 192, S), lambda i: (jnp.clip(i - start // N, 0, (stop - start) // N - 1), 0, 0))

    return [spec(start, stop) for start, stop in zip(CUTS, CUTS[1:])]


def for_piece(pieces, body):
    step = pl.program_id(0)
    for piece, start, stop in zip(pieces, CUTS, CUTS[1:]):

        @pl.when((step >= start // N) & (step < stop // N))
        def _(piece=piece):
            body(piece)


FULL = sds((C, ROWS, S))
FULL_ROWS = sds((CELLS, S))
HALO = sds((H, C, C, S))
EDGES = [sds((stop - start, 192, S)) for start, stop in zip(CUTS, CUTS[1:])]


def halves(y, half):
    return slice(y * C + half * 8, y * C + half * 8 + 8)


def pack_edges(s_ref, out_ref):
    out_ref[:, 0:96, :] = s_ref[:, 0:96, :]
    out_ref[:, 96:192, :] = s_ref[:, 160:256, :]


def pack_kernel(s_ref, edge_ref, head_ref, tail_ref):
    @pl.when(pl.program_id(0) < CUTS[1] // N)
    def _():
        pack_edges(s_ref, edge_ref)

    for p in range(N):
        for z in range(H):
            head_ref[z, p] = s_ref[p, stride_rows(z), :]
            tail_ref[z, p] = s_ref[p, stride_rows(C - H + z), :]


def pack(s):
    return pl.pallas_call(
        pack_kernel,
        grid=(C // N,),
        in_specs=[plane_spec(ROWS, N)],
        out_specs=edge_specs()[:1] + [halo_spec(N), halo_spec(N)],
        out_shape=EDGES[:1] + [HALO, HALO],
        compiler_params=params(12),
        cost_estimate=cost(1 << 32, 6 << 20),
        name="pack",
    )(s)


def pack_rest_kernel(s_ref, edge_ref, mid_ref):
    @pl.when(pl.program_id(0) >= CUTS[1] // N)
    def _():
        pack_edges(s_ref, edge_ref)

    mid_ref[...] = s_ref[:, 96:160, :]


def pack_rest(s):
    return pl.pallas_call(
        pack_rest_kernel,
        grid=(C // N,),
        in_specs=[plane_spec(ROWS, N)],
        out_specs=edge_specs()[1:] + [plane_spec(64, N)],
        out_shape=EDGES[1:] + [sds((C, 64, S))],
        compiler_params=params(12),
        cost_estimate=cost(1 << 31, 4 << 20),
        name="pack_rest",
    )(s)


def stack_kernel(*refs):
    start = 0
    for ref in refs[:-1]:
        refs[-1][start : start + ref.shape[0], :] = ref[...]
        start += ref.shape[0]


def stack(*arrays):
    rows = sum(a.shape[0] for a in arrays)
    return pl.pallas_call(stack_kernel, out_shape=sds((rows, S)), compiler_params=params(4), name="stack")(*arrays)


def along_x(s_ref, mate_ref, out_ref, add):
    def column(block, _):
        rows = pl.ds(pl.multiple_of(block * 8, 8), 8)
        ring = [mate_ref[C - H + i, rows, :] for i in range(H)]
        ring += [s_ref[x, rows, :] for x in range(C)]
        ring += [mate_ref[i, rows, :] for i in range(H)]
        for x in range(C):
            value = tap_sum(lambda i: ring[H + i], x)
            if add:
                value = value + out_ref[x, rows, :]
            out_ref[x, rows, :] = value
        return 0

    lax.fori_loop(0, ROWS // 8, column, 0)


def z_taps(ext_ref, y):
    return tap_sum(lambda k: ext_ref[y * 32 + 8 + k : y * 32 + 24 + k, :], 0)


def side_x_kernel(s_ref, mate_ref, out_ref):
    along_x(s_ref, mate_ref, out_ref, False)


def side_x(s, mate):
    return pl.pallas_call(
        side_x_kernel,
        out_shape=FULL,
        compiler_params=params(12),
        cost_estimate=cost(1 << 24, 6 << 20),
        name="side_x",
    )(s, mate)


def side_z_kernel(s_ref, part_ref, low_ref, high_ref, out_ref, ext_ref):
    def plane(x, _):
        for y in range(C):
            ext_ref[y * 32 + 8 : y * 32 + 24, :] = s_ref[x, y * C : (y + 1) * C, :]
        for z in range(H):
            ext_ref[pl.ds(2 + z, C, stride=32), :] = low_ref[z, x]
            ext_ref[pl.ds(24 + z, C, stride=32), :] = high_ref[z, x]
        for y in range(C):
            rows = slice(y * C, (y + 1) * C)
            out_ref[x, rows, :] = part_ref[x, rows, :] + z_taps(ext_ref, y)
        return 0

    lax.fori_loop(0, C, plane, 0)


def side_z(s, part, low, high):
    return pl.pallas_call(
        side_z_kernel,
        out_shape=FULL,
        scratch_shapes=[pltpu.VMEM((C * 32, S), F32)],
        compiler_params=params(14),
        cost_estimate=cost(1 << 24, 8 << 20),
        name="side_z",
    )(s, part, low, high)


def side_again_kernel(s_ref, mate_ref, out_ref, ext_ref):
    for y in range(C):
        ext_ref[y * 32 : y * 32 + 8, :] = jnp.zeros((8, S), F32)
        ext_ref[y * 32 + 24 : y * 32 + 32, :] = jnp.zeros((8, S), F32)

    def plane(x, _):
        for y in range(C):
            ext_ref[y * 32 + 8 : y * 32 + 24, :] = s_ref[x, y * C : (y + 1) * C, :]
        for y in range(C):
            out_ref[x, y * C : (y + 1) * C, :] = z_taps(ext_ref, y)
        return 0

    lax.fori_loop(0, C, plane, 0)
    along_x(s_ref, mate_ref, out_ref, True)


def side_again(s, mate):
    return pl.pallas_call(
        side_again_kernel,
        out_shape=FULL,
        scratch_shapes=[pltpu.VMEM((C * 32, S), F32)],
        compiler_params=params(12),
        cost_estimate=cost(1 << 25, 6 << 20),
        name="side_again",
    )(s, mate)


def tap_weight(distance):
    value = jnp.zeros(distance.shape, F32)
    for k in range(1, 7):
        value = jnp.where(distance == k, OFF[k - 1], value)
    return value


def ring_tables(coordinate):
    masks, factors = [], []
    for t in range(W):
        away = (coordinate - t) & 31
        masks.append(away == 0)
        factors.append(tap_weight(jnp.minimum(away, 32 - away)))
    return masks, factors


def spread_kernel(parcel_ref, vb_ref):
    def spread_row(row, _):
        line = (parcel_ref[pl.ds(72 + row, 1), :] + (DIAGONAL - filter_centre)) * (1.0 / filter_half)
        start = pl.multiple_of(row * 128, 128)
        vb_ref[pl.ds(start, 128), :] = jnp.broadcast_to(line, (128, 128)).T
        return 0

    lax.fori_loop(0, CELLS // 128, spread_row, 0, unroll=8)


def spread(parcel):
    return pl.pallas_call(
        spread_kernel,
        out_shape=FULL_ROWS,
        compiler_params=params(8),
        cost_estimate=cost(1 << 20, 2 << 20),
        name="spread",
    )(parcel)


def prep_kernel(*refs):
    parcels = refs[:4]
    corner_ref, vb_ref, s_ref, gg_ref, coef_ref, energy_ref, near_ref, table_ref, a1_ref, a1z_ref, a2_ref, a2s_ref = refs[4:]
    upper_x, upper_y = corner_ref[0] > 0, corner_ref[1] > 0
    for slab in range(3):
        own, over_x, over_y, over_xy = [parcel[slab * 24 : slab * 24 + 24, :] for parcel in parcels]
        same_x = [jnp.where(upper_y, over_y, own), jnp.where(upper_y, own, over_y)]
        other_x = [jnp.where(upper_y, over_xy, over_x), jnp.where(upper_y, over_x, over_xy)]
        ordered = [jnp.where(upper_x, o, m) for m, o in zip(same_x, other_x)]
        ordered += [jnp.where(upper_x, m, o) for m, o in zip(same_x, other_x)]
        for j in range(4):
            near_ref[slab * 96 + j * 24 : slab * 96 + j * 24 + 24, :] = ordered[j]
    blank = jnp.zeros((16, 128), F32)
    for block in range(6):
        rows = near_ref[pl.ds(block, NEAR, stride=6), :]
        table_ref[block * 128 : block * 128 + 128, :] = jnp.concatenate([rows, blank, rows, blank]).T
    at = TAPS + 3 - 640
    energy_ref[...] = jnp.broadcast_to(rows[:, at : at + 1] * (1.0 / filter_half), (NEAR, S))

    shape = (8, 128)
    sub = lax.broadcasted_iota(jnp.int32, shape, 0)
    lane = lax.broadcasted_iota(jnp.int32, shape, 1)
    first_lanes = lane < 64
    sites = [jnp.broadcast_to(table_ref[TAPS + d : TAPS + d + 1, :], shape).astype(jnp.int32) for d in range(3)]
    px = sites[0] - corner_ref[0]
    py = sites[1] - corner_ref[1]
    pz = (sites[2] & 15) + (((lane & 63) >> 4) - 1) * C
    zero = jnp.zeros(shape, F32)

    dz = sub + (lane >> 6) * 8 - pz + R
    z_masks = [dz == t for t in range(W)]
    z_factors = [tap_weight(jnp.abs(dz - t)) for t in range(W)]

    def place_z(ij, _):
        acc = zero
        along = zero
        for t in range(W):
            row = jnp.broadcast_to(table_ref[pl.ds(ij * W + t, 1), :], shape)
            acc = jnp.where(z_masks[t], row, acc)
            along = along + z_factors[t] * row
        a1_ref[ij] = acc
        a1z_ref[ij] = along
        return 0

    lax.fori_loop(0, W * W, place_z, 0, unroll=3)

    def place_y(y, _):
        masks, factors = ring_tables(y - py + R)
        for i in range(W):
            acc = zero
            along = zero
            moved = zero
            for t in range(W):
                value = a1_ref[i * W + t]
                acc = jnp.where(masks[t], value, acc)
                along = along + factors[t] * value
                moved = jnp.where(masks[t], a1z_ref[i * W + t], moved)
            a2_ref[i, y] = acc
            a2s_ref[i, y] = along + moved
        return 0

    lax.fori_loop(0, C, place_y, 0)

    def place_x(x, _):
        masks, factors = ring_tables(x - px + R)

        def per_y(y, _):
            row = pl.multiple_of(x * ROWS + y * C, C)
            acc = zero
            along = zero
            moved = zero
            for t in range(W):
                value = a2_ref[t, y]
                acc = jnp.where(masks[t], value, acc)
                along = along + factors[t] * value
                moved = jnp.where(masks[t], a2s_ref[t, y], moved)
            v = vb_ref[pl.ds(row, C), :]
            moved = along + moved + jnp.where(first_lanes, v[:8], v[8:]) * acc
            lower = jnp.where(first_lanes, acc, pltpu.roll(moved, 64, 1))
            upper = jnp.where(first_lanes, pltpu.roll(acc, 64, 1), moved)
            high, low = split(jnp.concatenate([lower, upper], axis=0))
            gg_ref[0, pl.ds(row, C), :] = high
            gg_ref[1, pl.ds(row, C), :] = low
            return 0

        lax.fori_loop(0, C, per_y, 0, unroll=16)
        return 0

    lax.fori_loop(0, C, place_x, 0)

    coef_ref[...] = jnp.zeros((3, NEAR, S), F32)

    def contract(x, _):
        rows = pl.ds(pl.multiple_of(x * 2 * ROWS, ROWS), 2 * ROWS)
        g_high, g_low = gg_ref[0, rows, :], gg_ref[1, rows, :]
        t_high, t_low = g_high.T, g_low.T
        high, low = split(s_ref[rows, :])
        got = mm(t_high, high) + (mm(t_high, low) + mm(t_low, high))
        t_high, t_low = t_high[:NEAR], t_low[:NEAR]
        pair = mm(t_high, g_high) + (mm(t_high, g_low) + mm(t_low, g_high))
        for slab in range(3):
            rows = slice(slab * C, slab * C + C)
            coef_ref[slab, 0:16] += got[rows]
            coef_ref[slab, 16:32] += got[64 + slab * C : 80 + slab * C]
            coef_ref[slab, 32:48] += pair[rows]
        return 0

    lax.fori_loop(0, C // 2, contract, 0, unroll=2)


def prep(parcels, corner, vb, s):
    vmem = pl.BlockSpec(memory_space=pltpu.VMEM)
    return pl.pallas_call(
        prep_kernel,
        in_specs=[vmem] * 4 + [pl.BlockSpec(memory_space=pltpu.SMEM), vmem, vmem],
        out_shape=[sds((2, CELLS, S), BF16), sds((3, NEAR, S)), sds((NEAR, S))],
        scratch_shapes=[
            pltpu.VMEM((288, 128), F32),
            pltpu.VMEM((768, 128), F32),
            pltpu.VMEM((W * W, 8, 128), F32),
            pltpu.VMEM((W * W, 8, 128), F32),
            pltpu.VMEM((W, C, 8, 128), F32),
            pltpu.VMEM((W, C, 8, 128), F32),
        ],
        compiler_params=params(16),
        cost_estimate=cost(1 << 27, 10 << 20),
        name="prep",
    )(*parcels, corner, vb, s.reshape(CELLS, S))


def merge_kernel(part_ref, below_ref, above_ref, energy_ref, out_ref):
    one = part_ref[1, 0:16, :] + below_ref[0:16, :] + above_ref[0:16, :]
    out_ref[0:16, :] = one * energy_ref[16:32, :]
    out_ref[16:32, :] = part_ref[1, 16:32, :] + below_ref[16:32, :] + above_ref[16:32, :]
    lane = lax.broadcasted_iota(jnp.int32, (16, 128), 1)
    below = jnp.where(lane < 32, pltpu.roll(below_ref[32:48, :], 112, 1), 0.0)
    above = jnp.where((lane >= 16) & (lane < 48), pltpu.roll(above_ref[32:48, :], 16, 1), 0.0)
    out_ref[32:48, :] = jnp.where(lane < 48, part_ref[1, 32:48, :], 0.0) + below + above


def merge(part, below, above, energy):
    return pl.pallas_call(merge_kernel, out_shape=sds((NEAR, S)), compiler_params=params(4), name="merge")(
        part, below, above, energy
    )


def first_kernel(s_ref, side_ref, vb_ref, *refs):
    q_ref, mix_ref, head_ref, tail_ref = refs[2:]

    def planes(edge_ref):
        for p in range(N):
            for half in range(2):
                ring = {y: s_ref[p, halves(y, half), :] for y in range(C)}
                for y in range(H):
                    ring[C + y] = edge_ref[p, halves(y, half), :]
                    ring[y - H] = edge_ref[p, halves(H + y, half), :]
                for y in range(C):
                    rows = halves(y, half)
                    dy = tap_sum(lambda i: ring[i], y)
                    q = dy + vb_ref[p, rows, :] * ring[y]
                    q_ref[p, rows, :] = q
                    mix_ref[p, rows, :] = side_ref[p, rows, :] + q + dy
            for z in range(H):
                head_ref[z, p] = mix_ref[p, stride_rows(z), :]
                tail_ref[z, p] = mix_ref[p, stride_rows(C - H + z), :]

    for_piece(refs[:2], planes)


def make_first(s, side_part, vb, edges):
    return pl.pallas_call(
        first_kernel,
        grid=(C // N,),
        in_specs=[plane_spec(ROWS, N)] * 3 + edge_specs(),
        out_specs=[plane_spec(ROWS, N), plane_spec(ROWS, N), halo_spec(N), halo_spec(N)],
        out_shape=[FULL, FULL, HALO, HALO],
        compiler_params=params(16),
        cost_estimate=cost(1 << 24, 14 << 20),
        name="first",
    )(s, side_part, vb, *edges)


def base_kernel(s_ref, mid_ref, vb_ref, vb_mate_ref, q_ref, side_ref, part_ref, *refs):
    out_ref = refs[2]

    def planes(edge_ref):
        for p in range(N):
            for half in range(2):

                def other(y, p=p, half=half):
                    if y < H:
                        return edge_ref[p, halves(y, half), :]
                    if y < C - H:
                        return mid_ref[p, halves(y - H, half), :]
                    return edge_ref[p, halves(y - 4, half), :]

                ring = [s_ref[p, halves(y, half), :] for y in range(C)] + [other(y) for y in range(C)]
                q = {y: q_ref[p, halves(y, half), :] for y in range(C)}
                for y in list(range(H)) + list(range(C - H, C)):
                    v = vb_mate_ref[p, halves(y, half), :]
                    q[C + y] = tap_sum(lambda i: ring[i % 32], C + y) + v * ring[C + y]
                for y in range(C):
                    rows = halves(y, half)
                    total = tap_sum(lambda i: q[i % 32], y)
                    total = total + vb_ref[p, rows, :] * (side_ref[p, rows, :] + q[y])
                    out_ref[p, rows, :] = 2.0 * (total + part_ref[p, rows, :]) - ring[y]

    for_piece(refs[:2], planes)


def make_base(s, mid, vb, vb_mate, q, side_part, part, edges):
    return pl.pallas_call(
        base_kernel,
        grid=(C // N,),
        in_specs=[plane_spec(ROWS, N), plane_spec(64, N)] + [plane_spec(ROWS, N)] * 5 + edge_specs(),
        out_specs=plane_spec(ROWS, N),
        out_shape=FULL,
        compiler_params=params(16),
        cost_estimate=cost(1 << 25, 16 << 20),
        name="base",
    )(s, mid, vb, vb_mate, q, side_part, part, *edges)


def second_kernel(base_ref, low_ref, high_ref, gg_high_ref, gg_low_ref, *rest):
    own_ref, mate_ref, energy_ref, second_ref, gram_ref, cross_ref, w_ref, halo_ref = rest
    step = pl.program_id(0)

    @pl.when(step == 0)
    def _():
        gram_ref[...] = jnp.zeros((S, S), F32)
        cross_ref[...] = jnp.zeros((S, S), F32)
        w_ref[...] = jnp.zeros((S, S), F32)
        halo_ref[...] = jnp.zeros((B, ROWS, S), F32)
        total = own_ref[...] + mate_ref[...]
        ones = [total[i : i + 16] for i in (0, 16, 64, 112, 160)]
        for j in range(3):
            row = 16 + j * NEAR
            beside = jnp.concatenate(ones[j : j + 3] + [jnp.zeros((S - NEAR, S), F32)])
            two = total[row + 16 : row + 32] + exact(total[row + 32 : row + 48], beside)
            two = two * energy_ref[j * C : j * C + C, :]
            w_ref[j * C : j * C + C, :] = 2.0 * two
            w_ref[64 + j * C : 80 + j * C, :] = 2.0 * ones[j + 1]

    for p in range(B):
        low = [low_ref[j, p] for j in range(H)]
        high = [high_ref[j, p] for j in range(H)]
        for z in range(H):
            add = sum((2.0 * OFF[k - 1]) * low[z - k + H] for k in range(z + 1, H + 1))
            halo_ref[p, stride_rows(z), :] = add
            add = sum((2.0 * OFF[H + j - z - 1]) * high[j] for j in range(z + 1))
            halo_ref[p, stride_rows(C - H + z), :] = add

    w_high, w_low = split(w_ref[...])
    gram = jnp.zeros((S, S), F32)
    cross = jnp.zeros((S, S), F32)
    for p in range(B):
        g_high, g_low = gg_high_ref[0, p], gg_low_ref[0, p]
        value = base_ref[p] + halo_ref[p] + (mm(g_high, w_high) + (mm(g_high, w_low) + mm(g_low, w_high)))
        second_ref[p] = value
        s_high, s_low = split(value)
        turned = s_high.T
        gram += mm(turned, s_high)
        cross += mm(turned, s_low)
    gram_ref[...] += gram
    cross_ref[...] += cross

    @pl.when(step == STEPS - 1)
    def _():
        cross = cross_ref[...]
        gram_ref[...] += cross + cross.T


def make_second(base, low, high, gg, weighted):
    return pl.pallas_call(
        second_kernel,
        grid=(STEPS,),
        in_specs=[plane_spec(), halo_spec(), halo_spec(), part_spec(0), part_spec(1)]
        + [whole(3 * NEAR + 32), whole(3 * NEAR + 32), whole(NEAR)],
        out_specs=[plane_spec(), whole()],
        out_shape=[FULL, sds((S, S))],
        scratch_shapes=[pltpu.VMEM((S, S), F32), pltpu.VMEM((S, S), F32), pltpu.VMEM((B, ROWS, S), F32)],
        compiler_params=params(16),
        cost_estimate=cost(1 << 27, 8 << 20),
        name="second",
    )(base, low, high, gg, gg, *weighted)


def exact(a, b):
    return jnp.dot(a, b, precision=lax.Precision.HIGHEST, preferred_element_type=F32)


def inverse_factor(gram_ref, a_ref, x_ref, state_ref):
    row = lax.broadcasted_iota(jnp.int32, (S, S), 0)
    column = lax.broadcasted_iota(jnp.int32, (S, S), 1)
    unit = jnp.where(row == column, 1.0, 0.0)
    gram = gram_ref[...]
    diagonal = jnp.where(row == column, gram, 0.0)
    down = lax.rsqrt(jnp.sum(diagonal, axis=1, keepdims=True))
    across = lax.rsqrt(jnp.sum(diagonal, axis=0, keepdims=True))
    a_ref[...] = gram * down * across
    x_ref[...] = unit

    def residual():
        x = x_ref[...]
        return unit - exact(exact(x, a_ref[...]), x.T)

    def size(e):
        return jnp.sum(e * e)

    def improve(e):
        lower = jnp.where(row > column, e, jnp.where(row == column, 0.5 * e, 0.0))
        x_ref[...] += exact(lower, x_ref[...])

    state_ref[0] = 0
    start = unit - a_ref[...]
    start_size = size(start)

    @pl.when(start_size < 0.16)
    def _():
        improve(start)
        state_ref[0] = jnp.where(start_size < 1e-6, 2, 1)

    for _ in range(5):

        @pl.when(state_ref[0] == 1)
        def _():
            e = residual()
            e_size = size(e)
            improve(e)
            state_ref[0] = jnp.where(e_size < 1e-6, 2, 1)

    @pl.when(state_ref[0] != 2)
    def _():
        x_ref[...] = unit
        lanes = lax.broadcasted_iota(jnp.int32, (1, S), 1)

        def step(j, _):
            line = a_ref[pl.ds(j, 1), :]
            scale = lax.rsqrt(jnp.sum(jnp.where(lanes == j, line, 0.0), axis=1, keepdims=True))
            a = a_ref[...]
            factor = jnp.sum(jnp.where(column == j, a, 0.0), axis=1, keepdims=True) * scale
            factor = jnp.where(row[:, :1] > j, factor, 0.0)
            x_line = x_ref[pl.ds(j, 1), :] * scale
            a_ref[...] = a - factor * (line * scale)
            x_ref[...] = jnp.where(row == j, x_line, x_ref[...] - factor * x_line)
            return 0

        lax.fori_loop(0, S, step, 0)

    x_ref[...] = x_ref[...] * across


def turn_kernel(second_ref, gram_ref, out_ref, a_ref, x_ref, i_high_ref, i_low_ref, state_ref):
    @pl.when(pl.program_id(0) == 0)
    def _():
        inverse_factor(gram_ref, a_ref, x_ref, state_ref)
        i_high, i_low = split(x_ref[...].T)
        i_high_ref[...] = i_high
        i_low_ref[...] = i_low

    i_high, i_low = i_high_ref[...], i_low_ref[...]

    for p in range(B):
        high, low = split(second_ref[p])
        out_ref[p] = mm(high, i_high) + (mm(high, i_low) + mm(low, i_high))


def turn(second, gram):
    return pl.pallas_call(
        turn_kernel,
        grid=(STEPS,),
        in_specs=[plane_spec(), whole()],
        out_specs=plane_spec(),
        out_shape=FULL,
        scratch_shapes=[pltpu.VMEM((S, S), F32)] * 2 + [pltpu.VMEM((S, S), BF16)] * 2 + [pltpu.SMEM((1,), jnp.int32)],
        compiler_params=params(16),
        cost_estimate=cost(1 << 28, 4 << 20),
        name="turn",
    )(second, gram)


def per_device(states, potential, atom_sites, projectors, energies):
    gx, gy = lax.axis_index("gx"), lax.axis_index("gy")
    depth = lax.axis_size("gzs")
    count = 4 * depth
    barrier = lax.optimization_barrier

    def send(value, flip=0, move=0):
        def target(d):
            return (d // depth * depth ^ flip) + (d + move) % depth

        return lax.ppermute(value, AXES, [(d, target(d)) for d in range(count)])

    over_x, over_y = 2 * depth, depth
    s = states.reshape(C, ROWS, S)
    pot = potential.reshape(32, 128)

    atoms = jnp.concatenate(
        [projectors.reshape(4, TAPS), atom_sites.astype(F32), energies[:, None], jnp.zeros((4, 768 - TAPS - 4), F32)],
        axis=1,
    ).reshape(24, 128)
    mate = send(s, over_x)
    below, above = send(atoms, 0, 1), send(atoms, 0, -1)
    one_edge, head, tail = pack(s)
    one_edge = send(one_edge, over_y)
    head, tail, below, above = barrier((head, tail, below, above))
    parcel = stack(below, atoms, above, pot)
    parcel_y = send(parcel, over_y)
    parcel_x = send(parcel, over_x)
    low, high = send(tail, 0, 1), send(head, 0, -1)
    two_edge, mid = pack_rest(s)
    vb = spread(parcel)
    beside = side_x(s, mate)
    parcel_y, two_edge, beside = barrier((parcel_y, two_edge, beside))
    two_edge = send(two_edge, over_y)
    parcel_xy = send(parcel_y, over_x)
    corner = jnp.stack([gx * C, gy * C]).astype(jnp.int32)
    parcel_xy, one_edge = barrier((parcel_xy, one_edge))
    gg, part, energy = prep([parcel, parcel_x, parcel_y, parcel_xy], corner, vb, s)

    part = part + send(part, over_x)
    own = merge(part, send(part[2], 0, 1), send(part[0], 0, -1), energy)
    side_part = side_z(s, beside, low, high)
    own, side_part = barrier((own, side_part))
    coefs = stack(send(own[:16], 0, 2), send(own, 0, 1), own, send(own, 0, -1), send(own[:16], 0, -2))
    coefs, two_edge = barrier((coefs, two_edge))
    coefs_mate = send(coefs, over_y)

    edges = [one_edge, two_edge]
    vb = vb.reshape(C, ROWS, S)
    q, mix, head, tail = make_first(s, side_part, vb, edges)
    low, high = send(tail, 0, 1), send(head, 0, -1)
    mate = send(mix, over_x)
    mid, coefs_mate = barrier((mid, coefs_mate))
    mid = send(mid, over_y)
    vb_mate = spread(parcel_y).reshape(C, ROWS, S)
    part = side_again(mix, mate)
    base = make_base(s, mid, vb, vb_mate, q, side_part, part, edges)
    second, gram = make_second(base, low, high, gg.reshape(2, C, ROWS, S), [coefs, coefs_mate, energy])

    for flip in (64, 32, 36, 1, 3, 8, 24):
        gram = gram + lax.ppermute(gram, AXES, [(d, d ^ flip) for d in range(count)])
    gram = gram * (1.0 / (CELLS * count))
    return turn(second, gram).reshape(C, C, C, S)


def solution(mesh):
    return jax.shard_map(
        per_device,
        mesh=mesh,
        in_specs=(
            P("gx", "gy", "gzs", None),
            P("gx", "gy", "gzs"),
            P(("gx", "gy", "gzs"), None),
            P(("gx", "gy", "gzs"), None, None, None),
            P(("gx", "gy", "gzs")),
        ),
        out_specs=P("gx", "gy", "gzs", None),
        check_vma=False,
    )
```

```python
import math

import jax
import jax.numpy as jnp
from jax import lax
from jax.experimental import pallas as pl
from jax.experimental.pallas import tpu as pltpu
from jax.sharding import PartitionSpec as P

AXES = ("gx", "gy", "gzs")
H = 6
C = 16
ROWS = C * C
CELLS = C * C * C
S = 128
W = 9
R = 4
NEAR = 48
TAPS = W * W * W
F32 = jnp.float32
BF16 = jnp.bfloat16

grid_step = 0.6
filter_centre = 36.0
filter_half = 26.0


def weights():
    taps = []
    for k in range(1, 7):
        top = 2.0 * (-1) ** (k + 1) * math.factorial(6) ** 2
        under = k * k * math.factorial(6 - k) * math.factorial(6 + k)
        taps.append(top / under)
    scale = -0.5 / (grid_step * grid_step)
    off = [scale * t / filter_half for t in taps]
    diagonal = 3.0 * scale * (-2.0 * sum(taps))
    return off, diagonal


OFF, DIAGONAL = weights()


def params(mib):
    return pltpu.CompilerParams(vmem_limit_bytes=mib * 1024 * 1024)


def cost(flops, nbytes):
    return pl.CostEstimate(flops=flops, bytes_accessed=nbytes, transcendentals=0)


def sds(shape, dtype=F32):
    return jax.ShapeDtypeStruct(shape, dtype)


def split(value):
    high = value.astype(BF16)
    low = (value - high.astype(F32)).astype(BF16)
    return high, low


def mm(a, b):
    return jnp.dot(a, b, preferred_element_type=F32)


def tap_sum(at, index):
    total = None
    for k in range(1, 7):
        term = OFF[k - 1] * (at(index + k) + at(index - k))
        total = term if total is None else total + term
    return total


B = 4
STEPS = C // B
N = 2
CUTS = (0, 4, 16)


def stride_rows(z):
    return pl.ds(z, C, stride=C)


def plane_spec(rows=ROWS, planes=B):
    return pl.BlockSpec((planes, rows, S), lambda i: (i, 0, 0))


def halo_spec(planes=B):
    return pl.BlockSpec((H, planes, C, S), lambda i: (0, i, 0, 0))


def part_spec(part):
    return pl.BlockSpec((1, B, ROWS, S), lambda i: (part, i, 0, 0))


def whole(rows=S):
    return pl.BlockSpec((rows, S), lambda i: (0, 0))


def edge_specs():
    def spec(start, stop):
        return pl.BlockSpec((N, 192, S), lambda i: (jnp.clip(i - start // N, 0, (stop - start) // N - 1), 0, 0))

    return [spec(start, stop) for start, stop in zip(CUTS, CUTS[1:])]


def for_piece(pieces, body):
    step = pl.program_id(0)
    for piece, start, stop in zip(pieces, CUTS, CUTS[1:]):

        @pl.when((step >= start // N) & (step < stop // N))
        def _(piece=piece):
            body(piece)


FULL = sds((C, ROWS, S))
FULL_ROWS = sds((CELLS, S))
HALO_ROWS = H * ROWS
MESSAGE = sds((HALO_ROWS + 2 * NEAR, S))
HALO = sds((H, C, C, S))
EDGES = [sds((stop - start, 192, S)) for start, stop in zip(CUTS, CUTS[1:])]


def halo_rows(x, z):
    return pl.ds(pl.multiple_of(z * ROWS + x * C, C), C)


def halves(y, half):
    return slice(y * C + half * 8, y * C + half * 8 + 8)


def pack_edges(s_ref, out_ref):
    out_ref[:, 0:96, :] = s_ref[:, 0:96, :]
    out_ref[:, 96:192, :] = s_ref[:, 160:256, :]


def pack_kernel(s_ref, edge_ref, head_ref, tail_ref):
    @pl.when(pl.program_id(0) < CUTS[1] // N)
    def _():
        pack_edges(s_ref, edge_ref)

    for p in range(N):
        for z in range(H):
            head_ref[z, p] = s_ref[p, stride_rows(z), :]
            tail_ref[z, p] = s_ref[p, stride_rows(C - H + z), :]


def pack(s):
    return pl.pallas_call(
        pack_kernel,
        grid=(C // N,),
        in_specs=[plane_spec(ROWS, N)],
        out_specs=edge_specs()[:1] + [halo_spec(N), halo_spec(N)],
        out_shape=EDGES[:1] + [HALO, HALO],
        compiler_params=params(12),
        cost_estimate=cost(1 << 32, 6 << 20),
        name="pack",
    )(s)


def pack_rest_kernel(s_ref, edge_ref, mid_ref):
    @pl.when(pl.program_id(0) >= CUTS[1] // N)
    def _():
        pack_edges(s_ref, edge_ref)

    mid_ref[...] = s_ref[:, 96:160, :]


def pack_rest(s):
    return pl.pallas_call(
        pack_rest_kernel,
        grid=(C // N,),
        in_specs=[plane_spec(ROWS, N)],
        out_specs=edge_specs()[1:] + [plane_spec(64, N)],
        out_shape=EDGES[1:] + [sds((C, 64, S))],
        compiler_params=params(12),
        cost_estimate=cost(1 << 31, 4 << 20),
        name="pack_rest",
    )(s)


def stack_kernel(*refs):
    start = 0
    for ref in refs[:-1]:
        refs[-1][start : start + ref.shape[0], :] = ref[...]
        start += ref.shape[0]


def stack(*arrays):
    rows = sum(a.shape[0] for a in arrays)
    return pl.pallas_call(stack_kernel, out_shape=sds((rows, S)), compiler_params=params(4), name="stack")(*arrays)


def along_x(s_ref, mate_ref, out_ref, add):
    def column(block, _):
        rows = pl.ds(pl.multiple_of(block * 8, 8), 8)
        ring = [mate_ref[C - H + i, rows, :] for i in range(H)]
        ring += [s_ref[x, rows, :] for x in range(C)]
        ring += [mate_ref[i, rows, :] for i in range(H)]
        for x in range(C):
            value = tap_sum(lambda i: ring[H + i], x)
            if add:
                value = value + out_ref[x, rows, :]
            out_ref[x, rows, :] = value
        return 0

    lax.fori_loop(0, ROWS // 8, column, 0)


def z_taps(ext_ref, y):
    return tap_sum(lambda k: ext_ref[y * 32 + 8 + k : y * 32 + 24 + k, :], 0)


def side_x_kernel(s_ref, mate_ref, out_ref):
    along_x(s_ref, mate_ref, out_ref, False)


def side_x(s, mate):
    return pl.pallas_call(
        side_x_kernel,
        out_shape=FULL,
        compiler_params=params(12),
        cost_estimate=cost(1 << 24, 6 << 20),
        name="side_x",
    )(s, mate)


def side_z_kernel(s_ref, part_ref, low_ref, high_ref, out_ref, ext_ref):
    def plane(x, _):
        for y in range(C):
            ext_ref[y * 32 + 8 : y * 32 + 24, :] = s_ref[x, y * C : (y + 1) * C, :]
        for z in range(H):
            ext_ref[pl.ds(2 + z, C, stride=32), :] = low_ref[z, x]
            ext_ref[pl.ds(24 + z, C, stride=32), :] = high_ref[z, x]
        for y in range(C):
            rows = slice(y * C, (y + 1) * C)
            out_ref[x, rows, :] = part_ref[x, rows, :] + z_taps(ext_ref, y)
        return 0

    lax.fori_loop(0, C, plane, 0)


def side_z(s, part, low, high):
    return pl.pallas_call(
        side_z_kernel,
        out_shape=FULL,
        scratch_shapes=[pltpu.VMEM((C * 32, S), F32)],
        compiler_params=params(14),
        cost_estimate=cost(1 << 24, 8 << 20),
        name="side_z",
    )(s, part, low, high)


def side_again_kernel(s_ref, mate_ref, out_ref, ext_ref):
    for y in range(C):
        ext_ref[y * 32 : y * 32 + 8, :] = jnp.zeros((8, S), F32)
        ext_ref[y * 32 + 24 : y * 32 + 32, :] = jnp.zeros((8, S), F32)

    def plane(x, _):
        for y in range(C):
            ext_ref[y * 32 + 8 : y * 32 + 24, :] = s_ref[x, y * C : (y + 1) * C, :]
        for y in range(C):
            out_ref[x, y * C : (y + 1) * C, :] = z_taps(ext_ref, y)
        return 0

    lax.fori_loop(0, C, plane, 0)
    along_x(s_ref, mate_ref, out_ref, True)


def side_again(s, mate):
    return pl.pallas_call(
        side_again_kernel,
        out_shape=FULL,
        scratch_shapes=[pltpu.VMEM((C * 32, S), F32)],
        compiler_params=params(12),
        cost_estimate=cost(1 << 25, 6 << 20),
        name="side_again",
    )(s, mate)


def tap_weight(distance):
    value = jnp.zeros(distance.shape, F32)
    for k in range(1, 7):
        value = jnp.where(distance == k, OFF[k - 1], value)
    return value


def ring_tables(coordinate):
    masks, factors = [], []
    for t in range(W):
        away = (coordinate - t) & 31
        masks.append(away == 0)
        factors.append(tap_weight(jnp.minimum(away, 32 - away)))
    return masks, factors


def spread_kernel(parcel_ref, vb_ref):
    def spread_row(row, _):
        line = (parcel_ref[pl.ds(72 + row, 1), :] + (DIAGONAL - filter_centre)) * (1.0 / filter_half)
        start = pl.multiple_of(row * 128, 128)
        vb_ref[pl.ds(start, 128), :] = jnp.broadcast_to(line, (128, 128)).T
        return 0

    lax.fori_loop(0, CELLS // 128, spread_row, 0, unroll=8)


def spread(parcel):
    return pl.pallas_call(
        spread_kernel,
        out_shape=FULL_ROWS,
        compiler_params=params(8),
        cost_estimate=cost(1 << 20, 2 << 20),
        name="spread",
    )(parcel)


def prep_kernel(*refs):
    parcels = refs[:4]
    corner_ref, vb_ref, s_ref, gg_ref, coef_ref, energy_ref, near_ref, table_ref, a1_ref, a1z_ref, a2_ref, a2s_ref = refs[4:]
    upper_x, upper_y = corner_ref[0] > 0, corner_ref[1] > 0
    for slab in range(3):
        own, over_x, over_y, over_xy = [parcel[slab * 24 : slab * 24 + 24, :] for parcel in parcels]
        same_x = [jnp.where(upper_y, over_y, own), jnp.where(upper_y, own, over_y)]
        other_x = [jnp.where(upper_y, over_xy, over_x), jnp.where(upper_y, over_x, over_xy)]
        ordered = [jnp.where(upper_x, o, m) for m, o in zip(same_x, other_x)]
        ordered += [jnp.where(upper_x, m, o) for m, o in zip(same_x, other_x)]
        for j in range(4):
            near_ref[slab * 96 + j * 24 : slab * 96 + j * 24 + 24, :] = ordered[j]
    blank = jnp.zeros((16, 128), F32)
    for block in range(6):
        rows = near_ref[pl.ds(block, NEAR, stride=6), :]
        table_ref[block * 128 : block * 128 + 128, :] = jnp.concatenate([rows, blank, rows, blank]).T
    at = TAPS + 3 - 640
    energy_ref[...] = jnp.broadcast_to(rows[:, at : at + 1] * (1.0 / filter_half), (NEAR, S))

    shape = (8, 128)
    sub = lax.broadcasted_iota(jnp.int32, shape, 0)
    lane = lax.broadcasted_iota(jnp.int32, shape, 1)
    first_lanes = lane < 64
    sites = [jnp.broadcast_to(table_ref[TAPS + d : TAPS + d + 1, :], shape).astype(jnp.int32) for d in range(3)]
    px = sites[0] - corner_ref[0]
    py = sites[1] - corner_ref[1]
    pz = (sites[2] & 15) + (((lane & 63) >> 4) - 1) * C
    zero = jnp.zeros(shape, F32)

    dz = sub + (lane >> 6) * 8 - pz + R
    z_masks = [dz == t for t in range(W)]
    z_factors = [tap_weight(jnp.abs(dz - t)) for t in range(W)]

    def place_z(ij, _):
        acc = zero
        along = zero
        for t in range(W):
            row = jnp.broadcast_to(table_ref[pl.ds(ij * W + t, 1), :], shape)
            acc = jnp.where(z_masks[t], row, acc)
            along = along + z_factors[t] * row
        a1_ref[ij] = acc
        a1z_ref[ij] = along
        return 0

    lax.fori_loop(0, W * W, place_z, 0, unroll=3)

    def place_y(y, _):
        masks, factors = ring_tables(y - py + R)
        for i in range(W):
            acc = zero
            along = zero
            moved = zero
            for t in range(W):
                value = a1_ref[i * W + t]
                acc = jnp.where(masks[t], value, acc)
                along = along + factors[t] * value
                moved = jnp.where(masks[t], a1z_ref[i * W + t], moved)
            a2_ref[i, y] = acc
            a2s_ref[i, y] = along + moved
        return 0

    lax.fori_loop(0, C, place_y, 0)

    def place_x(x, _):
        masks, factors = ring_tables(x - px + R)

        def per_y(y, _):
            row = pl.multiple_of(x * ROWS + y * C, C)
            acc = zero
            along = zero
            moved = zero
            for t in range(W):
                value = a2_ref[t, y]
                acc = jnp.where(masks[t], value, acc)
                along = along + factors[t] * value
                moved = jnp.where(masks[t], a2s_ref[t, y], moved)
            v = vb_ref[pl.ds(row, C), :]
            moved = along + moved + jnp.where(first_lanes, v[:8], v[8:]) * acc
            lower = jnp.where(first_lanes, acc, pltpu.roll(moved, 64, 1))
            upper = jnp.where(first_lanes, pltpu.roll(acc, 64, 1), moved)
            high, low = split(jnp.concatenate([lower, upper], axis=0))
            gg_ref[0, pl.ds(row, C), :] = high
            gg_ref[1, pl.ds(row, C), :] = low
            return 0

        lax.fori_loop(0, C, per_y, 0, unroll=16)
        return 0

    lax.fori_loop(0, C, place_x, 0)

    coef_ref[...] = jnp.zeros((3, NEAR, S), F32)

    def contract(x, _):
        rows = pl.ds(pl.multiple_of(x * 2 * ROWS, ROWS), 2 * ROWS)
        g_high, g_low = gg_ref[0, rows, :], gg_ref[1, rows, :]
        t_high, t_low = g_high.T, g_low.T
        high, low = split(s_ref[rows, :])
        got = mm(t_high, high) + (mm(t_high, low) + mm(t_low, high))
        t_high, t_low = t_high[:NEAR], t_low[:NEAR]
        pair = mm(t_high, g_high) + (mm(t_high, g_low) + mm(t_low, g_high))
        for slab in range(3):
            rows = slice(slab * C, slab * C + C)
            coef_ref[slab, 0:16] += got[rows]
            coef_ref[slab, 16:32] += got[64 + slab * C : 80 + slab * C]
            coef_ref[slab, 32:48] += pair[rows]
        return 0

    lax.fori_loop(0, C // 2, contract, 0, unroll=2)


def prep(parcels, corner, vb, s):
    vmem = pl.BlockSpec(memory_space=pltpu.VMEM)
    return pl.pallas_call(
        prep_kernel,
        in_specs=[vmem] * 4 + [pl.BlockSpec(memory_space=pltpu.SMEM), vmem, vmem],
        out_shape=[sds((2, CELLS, S), BF16), sds((3, NEAR, S)), sds((NEAR, S))],
        scratch_shapes=[
            pltpu.VMEM((288, 128), F32),
            pltpu.VMEM((768, 128), F32),
            pltpu.VMEM((W * W, 8, 128), F32),
            pltpu.VMEM((W * W, 8, 128), F32),
            pltpu.VMEM((W, C, 8, 128), F32),
            pltpu.VMEM((W, C, 8, 128), F32),
        ],
        compiler_params=params(16),
        cost_estimate=cost(1 << 27, 10 << 20),
        name="prep",
    )(*parcels, corner, vb, s.reshape(CELLS, S))


def move_pair(shares, away):
    lane = lax.broadcasted_iota(jnp.int32, (16, 128), 1)
    keep = (lane < 32) if away < 0 else (lane >= 16) & (lane < 48)
    pair = jnp.where(keep, pltpu.roll(shares[32:48], (away * 16) % 128, 1), 0.0)
    return jnp.concatenate([shares[0:32], pair])


def first_kernel(s_ref, side_ref, vb_ref, *refs):
    part_ref, mate_ref, q_ref, mix_ref, head_ref, tail_ref = refs[2:]
    step = pl.program_id(0)

    @pl.when(step == 0)
    def _():
        for j in range(2):
            rows = slice(HALO_ROWS + j * NEAR, HALO_ROWS + (j + 1) * NEAR)
            head_ref[rows, :] = part_ref[j] + mate_ref[j]
            tail_ref[rows, :] = part_ref[j + 1] + mate_ref[j + 1]

    def planes(edge_ref):
        for p in range(N):
            for half in range(2):
                ring = {y: s_ref[p, halves(y, half), :] for y in range(C)}
                for y in range(H):
                    ring[C + y] = edge_ref[p, halves(y, half), :]
                    ring[y - H] = edge_ref[p, halves(H + y, half), :]
                for y in range(C):
                    rows = halves(y, half)
                    dy = tap_sum(lambda i: ring[i], y)
                    q = dy + vb_ref[p, rows, :] * ring[y]
                    q_ref[p, rows, :] = q
                    mix_ref[p, rows, :] = side_ref[p, rows, :] + q + dy
            for z in range(H):
                rows = halo_rows(step * N + p, z)
                head_ref[rows, :] = mix_ref[p, stride_rows(z), :]
                tail_ref[rows, :] = mix_ref[p, stride_rows(C - H + z), :]

    for_piece(refs[:2], planes)


def make_first(s, side_part, vb, edges, part, part_mate):
    shares = pl.BlockSpec((3, NEAR, S), lambda i: (0, 0, 0))
    return pl.pallas_call(
        first_kernel,
        grid=(C // N,),
        in_specs=[plane_spec(ROWS, N)] * 3 + edge_specs() + [shares] * 2,
        out_specs=[plane_spec(ROWS, N), plane_spec(ROWS, N), whole(MESSAGE.shape[0]), whole(MESSAGE.shape[0])],
        out_shape=[FULL, FULL, MESSAGE, MESSAGE],
        compiler_params=params(16),
        cost_estimate=cost(1 << 24, 14 << 20),
        name="first",
    )(s, side_part, vb, *edges, part, part_mate)


def base_kernel(s_ref, mid_ref, vb_ref, vb_mate_ref, q_ref, side_ref, part_ref, *refs):
    out_ref = refs[2]

    def planes(edge_ref):
        for p in range(N):
            for half in range(2):

                def other(y, p=p, half=half):
                    if y < H:
                        return edge_ref[p, halves(y, half), :]
                    if y < C - H:
                        return mid_ref[p, halves(y - H, half), :]
                    return edge_ref[p, halves(y - 4, half), :]

                ring = [s_ref[p, halves(y, half), :] for y in range(C)] + [other(y) for y in range(C)]
                q = {y: q_ref[p, halves(y, half), :] for y in range(C)}
                for y in list(range(H)) + list(range(C - H, C)):
                    v = vb_mate_ref[p, halves(y, half), :]
                    q[C + y] = tap_sum(lambda i: ring[i % 32], C + y) + v * ring[C + y]
                for y in range(C):
                    rows = halves(y, half)
                    total = tap_sum(lambda i: q[i % 32], y)
                    total = total + vb_ref[p, rows, :] * (side_ref[p, rows, :] + q[y])
                    out_ref[p, rows, :] = 2.0 * (total + part_ref[p, rows, :]) - ring[y]

    for_piece(refs[:2], planes)


def make_base(s, mid, vb, vb_mate, q, side_part, part, edges):
    return pl.pallas_call(
        base_kernel,
        grid=(C // N,),
        in_specs=[plane_spec(ROWS, N), plane_spec(64, N)] + [plane_spec(ROWS, N)] * 5 + edge_specs(),
        out_specs=plane_spec(ROWS, N),
        out_shape=FULL,
        compiler_params=params(16),
        cost_estimate=cost(1 << 25, 16 << 20),
        name="base",
    )(s, mid, vb, vb_mate, q, side_part, part, *edges)


def second_kernel(base_ref, low_ref, high_ref, gg_high_ref, gg_low_ref, *rest):
    part_ref, mate_ref, energy_ref, second_ref, gram_ref, cross_ref, w_ref, halo_ref = rest
    step = pl.program_id(0)

    @pl.when(step == 0)
    def _():
        gram_ref[...] = jnp.zeros((S, S), F32)
        cross_ref[...] = jnp.zeros((S, S), F32)
        w_ref[...] = jnp.zeros((S, S), F32)
        halo_ref[...] = jnp.zeros((B, ROWS, S), F32)
        mine = [part_ref[j] + mate_ref[j] for j in range(3)]
        below = [move_pair(low_ref[HALO_ROWS + j * NEAR : HALO_ROWS + (j + 1) * NEAR, :], -1) for j in range(2)]
        above = [move_pair(high_ref[HALO_ROWS + j * NEAR : HALO_ROWS + (j + 1) * NEAR, :], 1) for j in range(2)]
        slabs = [mine[0] + below[0], mine[1] + below[1] + above[0], mine[2] + above[1]]
        near = jnp.concatenate([slab[0:16] for slab in slabs]) * energy_ref[...]
        lane = lax.broadcasted_iota(jnp.int32, (NEAR, S), 1)
        pair = jnp.where(lane < NEAR, jnp.concatenate([slab[32:48] for slab in slabs]), 0.0)
        two = jnp.concatenate([slab[16:32] for slab in slabs])
        two = two + exact(pair, jnp.concatenate([near, jnp.zeros((S - NEAR, S), F32)]))
        w_ref[0:NEAR, :] = 2.0 * energy_ref[...] * two
        w_ref[64 : 64 + NEAR, :] = 2.0 * near

    for p in range(B):
        low = [low_ref[halo_rows(step * B + p, j), :] for j in range(H)]
        high = [high_ref[halo_rows(step * B + p, j), :] for j in range(H)]
        for z in range(H):
            add = sum((2.0 * OFF[k - 1]) * low[z - k + H] for k in range(z + 1, H + 1))
            halo_ref[p, stride_rows(z), :] = add
            add = sum((2.0 * OFF[H + j - z - 1]) * high[j] for j in range(z + 1))
            halo_ref[p, stride_rows(C - H + z), :] = add

    w_high, w_low = split(w_ref[...])
    gram = jnp.zeros((S, S), F32)
    cross = jnp.zeros((S, S), F32)
    for p in range(B):
        g_high, g_low = gg_high_ref[0, p], gg_low_ref[0, p]
        value = base_ref[p] + halo_ref[p] + (mm(g_high, w_high) + (mm(g_high, w_low) + mm(g_low, w_high)))
        second_ref[p] = value
        s_high, s_low = split(value)
        turned = s_high.T
        gram += mm(turned, s_high)
        cross += mm(turned, s_low)
    gram_ref[...] += gram
    cross_ref[...] += cross

    @pl.when(step == STEPS - 1)
    def _():
        cross = cross_ref[...]
        gram_ref[...] += cross + cross.T


def make_second(base, low, high, gg, weighted):
    shares = pl.BlockSpec((3, NEAR, S), lambda i: (0, 0, 0))
    return pl.pallas_call(
        second_kernel,
        grid=(STEPS,),
        in_specs=[plane_spec(), whole(MESSAGE.shape[0]), whole(MESSAGE.shape[0]), part_spec(0), part_spec(1)]
        + [shares, shares, whole(NEAR)],
        out_specs=[plane_spec(), whole()],
        out_shape=[FULL, sds((S, S))],
        scratch_shapes=[pltpu.VMEM((S, S), F32), pltpu.VMEM((S, S), F32), pltpu.VMEM((B, ROWS, S), F32)],
        compiler_params=params(16),
        cost_estimate=cost(1 << 27, 8 << 20),
        name="second",
    )(base, low, high, gg, gg, *weighted)


def exact(a, b):
    return jnp.dot(a, b, precision=lax.Precision.HIGHEST, preferred_element_type=F32)


def inverse_factor(gram_ref, a_ref, x_ref, state_ref):
    row = lax.broadcasted_iota(jnp.int32, (S, S), 0)
    column = lax.broadcasted_iota(jnp.int32, (S, S), 1)
    unit = jnp.where(row == column, 1.0, 0.0)
    gram = gram_ref[...]
    diagonal = jnp.where(row == column, gram, 0.0)
    down = lax.rsqrt(jnp.sum(diagonal, axis=1, keepdims=True))
    across = lax.rsqrt(jnp.sum(diagonal, axis=0, keepdims=True))
    a_ref[...] = gram * down * across
    x_ref[...] = unit

    def residual():
        x = x_ref[...]
        return unit - exact(exact(x, a_ref[...]), x.T)

    def size(e):
        return jnp.sum(e * e)

    def improve(e):
        lower = jnp.where(row > column, e, jnp.where(row == column, 0.5 * e, 0.0))
        x_ref[...] += exact(lower, x_ref[...])

    state_ref[0] = 0
    start = unit - a_ref[...]
    start_size = size(start)

    @pl.when(start_size < 0.16)
    def _():
        improve(start)
        state_ref[0] = jnp.where(start_size < 1e-6, 2, 1)

    for _ in range(5):

        @pl.when(state_ref[0] == 1)
        def _():
            e = residual()
            e_size = size(e)
            improve(e)
            state_ref[0] = jnp.where(e_size < 1e-6, 2, 1)

    @pl.when(state_ref[0] != 2)
    def _():
        x_ref[...] = unit
        lanes = lax.broadcasted_iota(jnp.int32, (1, S), 1)

        def step(j, _):
            line = a_ref[pl.ds(j, 1), :]
            scale = lax.rsqrt(jnp.sum(jnp.where(lanes == j, line, 0.0), axis=1, keepdims=True))
            a = a_ref[...]
            factor = jnp.sum(jnp.where(column == j, a, 0.0), axis=1, keepdims=True) * scale
            factor = jnp.where(row[:, :1] > j, factor, 0.0)
            x_line = x_ref[pl.ds(j, 1), :] * scale
            a_ref[...] = a - factor * (line * scale)
            x_ref[...] = jnp.where(row == j, x_line, x_ref[...] - factor * x_line)
            return 0

        lax.fori_loop(0, S, step, 0)

    x_ref[...] = x_ref[...] * across


def turn_kernel(second_ref, gram_ref, out_ref, a_ref, x_ref, i_high_ref, i_low_ref, state_ref):
    @pl.when(pl.program_id(0) == 0)
    def _():
        inverse_factor(gram_ref, a_ref, x_ref, state_ref)
        i_high, i_low = split(x_ref[...].T)
        i_high_ref[...] = i_high
        i_low_ref[...] = i_low

    i_high, i_low = i_high_ref[...], i_low_ref[...]

    for p in range(B):
        high, low = split(second_ref[p])
        out_ref[p] = mm(high, i_high) + (mm(high, i_low) + mm(low, i_high))


def turn(second, gram):
    return pl.pallas_call(
        turn_kernel,
        grid=(STEPS,),
        in_specs=[plane_spec(), whole()],
        out_specs=plane_spec(),
        out_shape=FULL,
        scratch_shapes=[pltpu.VMEM((S, S), F32)] * 2 + [pltpu.VMEM((S, S), BF16)] * 2 + [pltpu.SMEM((1,), jnp.int32)],
        compiler_params=params(16),
        cost_estimate=cost(1 << 28, 4 << 20),
        name="turn",
    )(second, gram)


def per_device(states, potential, atom_sites, projectors, energies):
    gx, gy = lax.axis_index("gx"), lax.axis_index("gy")
    depth = lax.axis_size("gzs")
    count = 4 * depth
    barrier = lax.optimization_barrier

    def send(value, flip=0, move=0):
        def target(d):
            return (d // depth * depth ^ flip) + (d + move) % depth

        return lax.ppermute(value, AXES, [(d, target(d)) for d in range(count)])

    over_x, over_y = 2 * depth, depth
    s = states.reshape(C, ROWS, S)
    pot = potential.reshape(32, 128)

    atoms = jnp.concatenate(
        [projectors.reshape(4, TAPS), atom_sites.astype(F32), energies[:, None], jnp.zeros((4, 768 - TAPS - 4), F32)],
        axis=1,
    ).reshape(24, 128)
    mate = send(s, over_x)
    below, above = send(atoms, 0, 1), send(atoms, 0, -1)
    one_edge, head, tail = pack(s)
    one_edge = send(one_edge, over_y)
    head, tail, below, above = barrier((head, tail, below, above))
    parcel = stack(below, atoms, above, pot)
    parcel_y = send(parcel, over_y)
    parcel_x = send(parcel, over_x)
    low, high = send(tail, 0, 1), send(head, 0, -1)
    two_edge, mid = pack_rest(s)
    vb = spread(parcel)
    beside = side_x(s, mate)
    parcel_y, one_edge, two_edge, beside = barrier((parcel_y, one_edge, two_edge, beside))
    two_edge = send(two_edge, over_y)
    parcel_xy = send(parcel_y, over_x)
    corner = jnp.stack([gx * C, gy * C]).astype(jnp.int32)
    gg, part, energy = prep([parcel, parcel_x, parcel_y, parcel_xy], corner, vb, s)

    part = part + send(part, over_x)
    part_mate = send(part, over_y)
    side_part = side_z(s, beside, low, high)
    edges = [one_edge, two_edge]
    vb = vb.reshape(C, ROWS, S)
    q, mix, head, tail = make_first(s, side_part, vb, edges, part, part_mate)
    low, high = send(tail, 0, 1), send(head, 0, -1)
    mate = send(mix, over_x)
    mid, part_mate = barrier((mid, part_mate))
    mid = send(mid, over_y)
    vb_mate = spread(parcel_y).reshape(C, ROWS, S)
    part_two = side_again(mix, mate)
    base = make_base(s, mid, vb, vb_mate, q, side_part, part_two, edges)
    second, gram = make_second(base, low, high, gg.reshape(2, C, ROWS, S), [part, part_mate, energy])

    for flip in (64, 32, 36, 1, 3, 8, 24):
        gram = gram + lax.ppermute(gram, AXES, [(d, d ^ flip) for d in range(count)])
    gram = gram * (1.0 / (CELLS * count))
    return turn(second, gram).reshape(C, C, C, S)


def solution(mesh):
    return jax.shard_map(
        per_device,
        mesh=mesh,
        in_specs=(
            P("gx", "gy", "gzs", None),
            P("gx", "gy", "gzs"),
            P(("gx", "gy", "gzs"), None),
            P(("gx", "gy", "gzs"), None, None, None),
            P(("gx", "gy", "gzs")),
        ),
        out_specs=P("gx", "gy", "gzs", None),
        check_vma=False,
    )
```

```python
import math

import jax
import jax.numpy as jnp
from jax import lax
from jax.experimental import pallas as pl
from jax.experimental.pallas import tpu as pltpu
from jax.sharding import PartitionSpec as P

AXES = ("gx", "gy", "gzs")
H = 6
C = 16
ROWS = C * C
CELLS = C * C * C
S = 128
W = 9
R = 4
NEAR = 48
TAPS = W * W * W
F32 = jnp.float32
BF16 = jnp.bfloat16

grid_step = 0.6
filter_centre = 36.0
filter_half = 26.0


def weights():
    taps = []
    for k in range(1, 7):
        top = 2.0 * (-1) ** (k + 1) * math.factorial(6) ** 2
        under = k * k * math.factorial(6 - k) * math.factorial(6 + k)
        taps.append(top / under)
    scale = -0.5 / (grid_step * grid_step)
    off = [scale * t / filter_half for t in taps]
    diagonal = 3.0 * scale * (-2.0 * sum(taps))
    return off, diagonal


OFF, DIAGONAL = weights()


def params(mib):
    return pltpu.CompilerParams(vmem_limit_bytes=mib * 1024 * 1024)


def cost(flops, nbytes):
    return pl.CostEstimate(flops=flops, bytes_accessed=nbytes, transcendentals=0)


def sds(shape, dtype=F32):
    return jax.ShapeDtypeStruct(shape, dtype)


def split(value):
    high = value.astype(BF16)
    low = (value - high.astype(F32)).astype(BF16)
    return high, low


def mm(a, b):
    return jnp.dot(a, b, preferred_element_type=F32)


def tap_sum(at, index):
    total = None
    for k in range(1, 7):
        term = OFF[k - 1] * (at(index + k) + at(index - k))
        total = term if total is None else total + term
    return total


B = 4
STEPS = C // B
N = 2
CUTS = (0, 6, 12, 16)


def stride_rows(z):
    return pl.ds(z, C, stride=C)


def plane_spec(rows=ROWS, planes=B):
    return pl.BlockSpec((planes, rows, S), lambda i: (i, 0, 0))


def halo_spec(planes=B):
    return pl.BlockSpec((H, planes, C, S), lambda i: (0, i, 0, 0))


def part_spec(part):
    return pl.BlockSpec((1, B, ROWS, S), lambda i: (part, i, 0, 0))


def whole(rows=S):
    return pl.BlockSpec((rows, S), lambda i: (0, 0))


def edge_specs():
    def spec(start, stop):
        return pl.BlockSpec((N, 192, S), lambda i: (jnp.clip(i - start // N, 0, (stop - start) // N - 1), 0, 0))

    return [spec(start, stop) for start, stop in zip(CUTS, CUTS[1:])]


def for_piece(pieces, body, inner_ref=None):
    step = pl.program_id(0)
    for j, (start, stop) in enumerate(zip(CUTS, CUTS[1:])):
        here = (step >= start // N) & (step < stop // N)
        if inner_ref is None or j < len(CUTS) - 2:

            @pl.when(here)
            def _(j=j):
                body(pieces[j])

        else:
            inner = inner_ref[0] == 1

            @pl.when(here & inner)
            def _(j=j):
                body(pieces[j])

            @pl.when(here & jnp.logical_not(inner))
            def _(j=j):
                body(pieces[j + 1])


SCALARS = pl.BlockSpec(memory_space=pltpu.SMEM)
FULL = sds((C, ROWS, S))
FULL_ROWS = sds((CELLS, S))
HALO_ROWS = H * ROWS
MESSAGE = sds((HALO_ROWS + 2 * NEAR, S))
HALO = sds((H, C, C, S))
EDGES = [sds((stop - start, 192, S)) for start, stop in zip(CUTS, CUTS[1:])]


def halo_rows(x, z):
    return pl.ds(pl.multiple_of(z * ROWS + x * C, C), C)


def halves(y, half):
    return slice(y * C + half * 8, y * C + half * 8 + 8)


def pack_edges(s_ref, out_ref):
    out_ref[:, 0:96, :] = s_ref[:, 0:96, :]
    out_ref[:, 96:192, :] = s_ref[:, 160:256, :]


def pack_kernel(s_ref, edge_ref, head_ref, tail_ref):
    @pl.when(pl.program_id(0) < CUTS[1] // N)
    def _():
        pack_edges(s_ref, edge_ref)

    for p in range(N):
        for z in range(H):
            head_ref[z, p] = s_ref[p, stride_rows(z), :]
            tail_ref[z, p] = s_ref[p, stride_rows(C - H + z), :]


def pack(s):
    return pl.pallas_call(
        pack_kernel,
        grid=(C // N,),
        in_specs=[plane_spec(ROWS, N)],
        out_specs=edge_specs()[:1] + [halo_spec(N), halo_spec(N)],
        out_shape=EDGES[:1] + [HALO, HALO],
        compiler_params=params(12),
        cost_estimate=cost(1 << 32, 6 << 20),
        name="pack",
    )(s)


def pack_rest_kernel(s_ref, two_ref, three_ref, mid_ref):
    for_piece([None, two_ref, three_ref], lambda out_ref: out_ref is None or pack_edges(s_ref, out_ref))
    mid_ref[...] = s_ref[:, 96:160, :]


def pack_rest(s):
    return pl.pallas_call(
        pack_rest_kernel,
        grid=(C // N,),
        in_specs=[plane_spec(ROWS, N)],
        out_specs=edge_specs()[1:] + [plane_spec(64, N)],
        out_shape=EDGES[1:] + [sds((C, 64, S))],
        compiler_params=params(12),
        cost_estimate=cost(1 << 31, 4 << 20),
        name="pack_rest",
    )(s)


def stack_kernel(*refs):
    start = 0
    for ref in refs[:-1]:
        refs[-1][start : start + ref.shape[0], :] = ref[...]
        start += ref.shape[0]


def stack(*arrays):
    rows = sum(a.shape[0] for a in arrays)
    return pl.pallas_call(stack_kernel, out_shape=sds((rows, S)), compiler_params=params(4), name="stack")(*arrays)


def along_x(s_ref, mate_ref, out_ref, add):
    def column(block, _):
        rows = pl.ds(pl.multiple_of(block * 8, 8), 8)
        ring = [mate_ref[C - H + i, rows, :] for i in range(H)]
        ring += [s_ref[x, rows, :] for x in range(C)]
        ring += [mate_ref[i, rows, :] for i in range(H)]
        for x in range(C):
            value = tap_sum(lambda i: ring[H + i], x)
            if add:
                value = value + out_ref[x, rows, :]
            out_ref[x, rows, :] = value
        return 0

    lax.fori_loop(0, ROWS // 8, column, 0)


def z_taps(ext_ref, y):
    return tap_sum(lambda k: ext_ref[y * 32 + 8 + k : y * 32 + 24 + k, :], 0)


def side_x_kernel(s_ref, mate_ref, out_ref):
    along_x(s_ref, mate_ref, out_ref, False)


def side_x(s, mate):
    return pl.pallas_call(
        side_x_kernel,
        out_shape=FULL,
        compiler_params=params(12),
        cost_estimate=cost(1 << 24, 6 << 20),
        name="side_x",
    )(s, mate)


def side_z_kernel(s_ref, part_ref, low_ref, high_ref, out_ref, ext_ref):
    def plane(x, _):
        for y in range(C):
            ext_ref[y * 32 + 8 : y * 32 + 24, :] = s_ref[x, y * C : (y + 1) * C, :]
        for z in range(H):
            ext_ref[pl.ds(2 + z, C, stride=32), :] = low_ref[z, x]
            ext_ref[pl.ds(24 + z, C, stride=32), :] = high_ref[z, x]
        for y in range(C):
            rows = slice(y * C, (y + 1) * C)
            out_ref[x, rows, :] = part_ref[x, rows, :] + z_taps(ext_ref, y)
        return 0

    lax.fori_loop(0, C, plane, 0)


def side_z(s, part, low, high):
    return pl.pallas_call(
        side_z_kernel,
        out_shape=FULL,
        scratch_shapes=[pltpu.VMEM((C * 32, S), F32)],
        compiler_params=params(14),
        cost_estimate=cost(1 << 24, 8 << 20),
        name="side_z",
    )(s, part, low, high)


def side_again_kernel(s_ref, mate_ref, out_ref, ext_ref):
    for y in range(C):
        ext_ref[y * 32 : y * 32 + 8, :] = jnp.zeros((8, S), F32)
        ext_ref[y * 32 + 24 : y * 32 + 32, :] = jnp.zeros((8, S), F32)

    def plane(x, _):
        for y in range(C):
            ext_ref[y * 32 + 8 : y * 32 + 24, :] = s_ref[x, y * C : (y + 1) * C, :]
        for y in range(C):
            out_ref[x, y * C : (y + 1) * C, :] = z_taps(ext_ref, y)
        return 0

    lax.fori_loop(0, C, plane, 0)
    along_x(s_ref, mate_ref, out_ref, True)


def side_again(s, mate):
    return pl.pallas_call(
        side_again_kernel,
        out_shape=FULL,
        scratch_shapes=[pltpu.VMEM((C * 32, S), F32)],
        compiler_params=params(12),
        cost_estimate=cost(1 << 25, 6 << 20),
        name="side_again",
    )(s, mate)


def tap_weight(distance):
    value = jnp.zeros(distance.shape, F32)
    for k in range(1, 7):
        value = jnp.where(distance == k, OFF[k - 1], value)
    return value


def ring_tables(coordinate):
    masks, factors = [], []
    for t in range(W):
        away = (coordinate - t) & 31
        masks.append(away == 0)
        factors.append(tap_weight(jnp.minimum(away, 32 - away)))
    return masks, factors


def spread_kernel(parcel_ref, vb_ref):
    def spread_row(row, _):
        line = (parcel_ref[pl.ds(72 + row, 1), :] + (DIAGONAL - filter_centre)) * (1.0 / filter_half)
        start = pl.multiple_of(row * 128, 128)
        vb_ref[pl.ds(start, 128), :] = jnp.broadcast_to(line, (128, 128)).T
        return 0

    lax.fori_loop(0, CELLS // 128, spread_row, 0, unroll=8)


def spread(parcel):
    return pl.pallas_call(
        spread_kernel,
        out_shape=FULL_ROWS,
        compiler_params=params(8),
        cost_estimate=cost(1 << 20, 2 << 20),
        name="spread",
    )(parcel)


def prep_kernel(*refs):
    parcels = refs[:4]
    corner_ref, vb_ref, s_ref, gg_ref, coef_ref, energy_ref, near_ref, table_ref, a1_ref, a1z_ref, a2_ref, a2s_ref = refs[4:]
    upper_x, upper_y = corner_ref[0] > 0, corner_ref[1] > 0
    for slab in range(3):
        own, over_x, over_y, over_xy = [parcel[slab * 24 : slab * 24 + 24, :] for parcel in parcels]
        same_x = [jnp.where(upper_y, over_y, own), jnp.where(upper_y, own, over_y)]
        other_x = [jnp.where(upper_y, over_xy, over_x), jnp.where(upper_y, over_x, over_xy)]
        ordered = [jnp.where(upper_x, o, m) for m, o in zip(same_x, other_x)]
        ordered += [jnp.where(upper_x, m, o) for m, o in zip(same_x, other_x)]
        for j in range(4):
            near_ref[slab * 96 + j * 24 : slab * 96 + j * 24 + 24, :] = ordered[j]
    blank = jnp.zeros((16, 128), F32)
    for block in range(6):
        rows = near_ref[pl.ds(block, NEAR, stride=6), :]
        table_ref[block * 128 : block * 128 + 128, :] = jnp.concatenate([rows, blank, rows, blank]).T
    at = TAPS + 3 - 640
    energy_ref[...] = jnp.broadcast_to(rows[:, at : at + 1] * (1.0 / filter_half), (NEAR, S))

    shape = (8, 128)
    sub = lax.broadcasted_iota(jnp.int32, shape, 0)
    lane = lax.broadcasted_iota(jnp.int32, shape, 1)
    first_lanes = lane < 64
    sites = [jnp.broadcast_to(table_ref[TAPS + d : TAPS + d + 1, :], shape).astype(jnp.int32) for d in range(3)]
    px = sites[0] - corner_ref[0]
    py = sites[1] - corner_ref[1]
    pz = (sites[2] & 15) + (((lane & 63) >> 4) - 1) * C
    zero = jnp.zeros(shape, F32)

    dz = sub + (lane >> 6) * 8 - pz + R
    z_masks = [dz == t for t in range(W)]
    z_factors = [tap_weight(jnp.abs(dz - t)) for t in range(W)]

    def place_z(ij, _):
        acc = zero
        along = zero
        for t in range(W):
            row = jnp.broadcast_to(table_ref[pl.ds(ij * W + t, 1), :], shape)
            acc = jnp.where(z_masks[t], row, acc)
            along = along + z_factors[t] * row
        a1_ref[ij] = acc
        a1z_ref[ij] = along
        return 0

    lax.fori_loop(0, W * W, place_z, 0, unroll=3)

    def place_y(y, _):
        masks, factors = ring_tables(y - py + R)
        for i in range(W):
            acc = zero
            along = zero
            moved = zero
            for t in range(W):
                value = a1_ref[i * W + t]
                acc = jnp.where(masks[t], value, acc)
                along = along + factors[t] * value
                moved = jnp.where(masks[t], a1z_ref[i * W + t], moved)
            a2_ref[i, y] = acc
            a2s_ref[i, y] = along + moved
        return 0

    lax.fori_loop(0, C, place_y, 0)

    def place_x(x, _):
        masks, factors = ring_tables(x - px + R)

        def per_y(y, _):
            row = pl.multiple_of(x * ROWS + y * C, C)
            acc = zero
            along = zero
            moved = zero
            for t in range(W):
                value = a2_ref[t, y]
                acc = jnp.where(masks[t], value, acc)
                along = along + factors[t] * value
                moved = jnp.where(masks[t], a2s_ref[t, y], moved)
            v = vb_ref[pl.ds(row, C), :]
            moved = along + moved + jnp.where(first_lanes, v[:8], v[8:]) * acc
            lower = jnp.where(first_lanes, acc, pltpu.roll(moved, 64, 1))
            upper = jnp.where(first_lanes, pltpu.roll(acc, 64, 1), moved)
            high, low = split(jnp.concatenate([lower, upper], axis=0))
            gg_ref[0, pl.ds(row, C), :] = high
            gg_ref[1, pl.ds(row, C), :] = low
            return 0

        lax.fori_loop(0, C, per_y, 0, unroll=16)
        return 0

    lax.fori_loop(0, C, place_x, 0)

    coef_ref[...] = jnp.zeros((3, NEAR, S), F32)

    def contract(x, _):
        rows = pl.ds(pl.multiple_of(x * 2 * ROWS, ROWS), 2 * ROWS)
        g_high, g_low = gg_ref[0, rows, :], gg_ref[1, rows, :]
        t_high, t_low = g_high.T, g_low.T
        high, low = split(s_ref[rows, :])
        got = mm(t_high, high) + (mm(t_high, low) + mm(t_low, high))
        t_high, t_low = t_high[:NEAR], t_low[:NEAR]
        pair = mm(t_high, g_high) + (mm(t_high, g_low) + mm(t_low, g_high))
        for slab in range(3):
            rows = slice(slab * C, slab * C + C)
            coef_ref[slab, 0:16] += got[rows]
            coef_ref[slab, 16:32] += got[64 + slab * C : 80 + slab * C]
            coef_ref[slab, 32:48] += pair[rows]
        return 0

    lax.fori_loop(0, C // 2, contract, 0, unroll=2)


def prep(parcels, corner, vb, s):
    vmem = pl.BlockSpec(memory_space=pltpu.VMEM)
    return pl.pallas_call(
        prep_kernel,
        in_specs=[vmem] * 4 + [pl.BlockSpec(memory_space=pltpu.SMEM), vmem, vmem],
        out_shape=[sds((2, CELLS, S), BF16), sds((3, NEAR, S)), sds((NEAR, S))],
        scratch_shapes=[
            pltpu.VMEM((288, 128), F32),
            pltpu.VMEM((768, 128), F32),
            pltpu.VMEM((W * W, 8, 128), F32),
            pltpu.VMEM((W * W, 8, 128), F32),
            pltpu.VMEM((W, C, 8, 128), F32),
            pltpu.VMEM((W, C, 8, 128), F32),
        ],
        compiler_params=params(16),
        cost_estimate=cost(1 << 27, 10 << 20),
        name="prep",
    )(*parcels, corner, vb, s.reshape(CELLS, S))


def move_pair(shares, away):
    lane = lax.broadcasted_iota(jnp.int32, (16, 128), 1)
    keep = (lane < 32) if away < 0 else (lane >= 16) & (lane < 48)
    pair = jnp.where(keep, pltpu.roll(shares[32:48], (away * 16) % 128, 1), 0.0)
    return jnp.concatenate([shares[0:32], pair])


def first_kernel(s_ref, side_ref, vb_ref, *refs):
    inner_ref, part_ref, mate_ref, q_ref, mix_ref, head_ref, tail_ref = refs[4:]
    step = pl.program_id(0)

    @pl.when(step == 0)
    def _():
        for j in range(2):
            rows = slice(HALO_ROWS + j * NEAR, HALO_ROWS + (j + 1) * NEAR)
            head_ref[rows, :] = part_ref[j] + mate_ref[j]
            tail_ref[rows, :] = part_ref[j + 1] + mate_ref[j + 1]

    def planes(edge_ref):
        for p in range(N):
            for half in range(2):
                ring = {y: s_ref[p, halves(y, half), :] for y in range(C)}
                for y in range(H):
                    ring[C + y] = edge_ref[p, halves(y, half), :]
                    ring[y - H] = edge_ref[p, halves(H + y, half), :]
                for y in range(C):
                    rows = halves(y, half)
                    dy = tap_sum(lambda i: ring[i], y)
                    q = dy + vb_ref[p, rows, :] * ring[y]
                    q_ref[p, rows, :] = q
                    mix_ref[p, rows, :] = side_ref[p, rows, :] + q + dy
            for z in range(H):
                rows = halo_rows(step * N + p, z)
                head_ref[rows, :] = mix_ref[p, stride_rows(z), :]
                tail_ref[rows, :] = mix_ref[p, stride_rows(C - H + z), :]

    for_piece(refs[:4], planes, inner_ref)


def make_first(s, side_part, vb, edges, inner, part, part_mate):
    shares = pl.BlockSpec((3, NEAR, S), lambda i: (0, 0, 0))
    return pl.pallas_call(
        first_kernel,
        grid=(C // N,),
        in_specs=[plane_spec(ROWS, N)] * 3 + edge_specs() + edge_specs()[-1:] + [SCALARS] + [shares] * 2,
        out_specs=[plane_spec(ROWS, N), plane_spec(ROWS, N), whole(MESSAGE.shape[0]), whole(MESSAGE.shape[0])],
        out_shape=[FULL, FULL, MESSAGE, MESSAGE],
        compiler_params=params(16),
        cost_estimate=cost(1 << 24, 14 << 20),
        name="first",
    )(s, side_part, vb, *edges, inner, part, part_mate)


def base_kernel(s_ref, mid_ref, vb_ref, vb_mate_ref, q_ref, side_ref, part_ref, *refs):
    inner_ref, out_ref = refs[4:]

    def planes(edge_ref):
        for p in range(N):
            for half in range(2):

                def other(y, p=p, half=half):
                    if y < H:
                        return edge_ref[p, halves(y, half), :]
                    if y < C - H:
                        return mid_ref[p, halves(y - H, half), :]
                    return edge_ref[p, halves(y - 4, half), :]

                ring = [s_ref[p, halves(y, half), :] for y in range(C)] + [other(y) for y in range(C)]
                q = {y: q_ref[p, halves(y, half), :] for y in range(C)}
                for y in list(range(H)) + list(range(C - H, C)):
                    v = vb_mate_ref[p, halves(y, half), :]
                    q[C + y] = tap_sum(lambda i: ring[i % 32], C + y) + v * ring[C + y]
                for y in range(C):
                    rows = halves(y, half)
                    total = tap_sum(lambda i: q[i % 32], y)
                    total = total + vb_ref[p, rows, :] * (side_ref[p, rows, :] + q[y])
                    out_ref[p, rows, :] = 2.0 * (total + part_ref[p, rows, :]) - ring[y]

    for_piece(refs[:4], planes, inner_ref)


def make_base(s, mid, vb, vb_mate, q, side_part, part, edges, inner):
    return pl.pallas_call(
        base_kernel,
        grid=(C // N,),
        in_specs=[plane_spec(ROWS, N), plane_spec(64, N)]
        + [plane_spec(ROWS, N)] * 5
        + edge_specs()
        + edge_specs()[-1:]
        + [SCALARS],
        out_specs=plane_spec(ROWS, N),
        out_shape=FULL,
        compiler_params=params(16),
        cost_estimate=cost(1 << 25, 16 << 20),
        name="base",
    )(s, mid, vb, vb_mate, q, side_part, part, *edges, inner)


def second_kernel(base_ref, low_ref, high_ref, gg_high_ref, gg_low_ref, *rest):
    part_ref, mate_ref, energy_ref, second_ref, gram_ref, cross_ref, w_ref, halo_ref = rest
    step = pl.program_id(0)

    @pl.when(step == 0)
    def _():
        gram_ref[...] = jnp.zeros((S, S), F32)
        cross_ref[...] = jnp.zeros((S, S), F32)
        w_ref[...] = jnp.zeros((S, S), F32)
        halo_ref[...] = jnp.zeros((B, ROWS, S), F32)
        mine = [part_ref[j] + mate_ref[j] for j in range(3)]
        below = [move_pair(low_ref[HALO_ROWS + j * NEAR : HALO_ROWS + (j + 1) * NEAR, :], -1) for j in range(2)]
        above = [move_pair(high_ref[HALO_ROWS + j * NEAR : HALO_ROWS + (j + 1) * NEAR, :], 1) for j in range(2)]
        slabs = [mine[0] + below[0], mine[1] + below[1] + above[0], mine[2] + above[1]]
        near = jnp.concatenate([slab[0:16] for slab in slabs]) * energy_ref[...]
        lane = lax.broadcasted_iota(jnp.int32, (NEAR, S), 1)
        pair = jnp.where(lane < NEAR, jnp.concatenate([slab[32:48] for slab in slabs]), 0.0)
        two = jnp.concatenate([slab[16:32] for slab in slabs])
        two = two + exact(pair, jnp.concatenate([near, jnp.zeros((S - NEAR, S), F32)]))
        w_ref[0:NEAR, :] = 2.0 * energy_ref[...] * two
        w_ref[64 : 64 + NEAR, :] = 2.0 * near

    for p in range(B):
        low = [low_ref[halo_rows(step * B + p, j), :] for j in range(H)]
        high = [high_ref[halo_rows(step * B + p, j), :] for j in range(H)]
        for z in range(H):
            add = sum((2.0 * OFF[k - 1]) * low[z - k + H] for k in range(z + 1, H + 1))
            halo_ref[p, stride_rows(z), :] = add
            add = sum((2.0 * OFF[H + j - z - 1]) * high[j] for j in range(z + 1))
            halo_ref[p, stride_rows(C - H + z), :] = add

    w_high, w_low = split(w_ref[...])
    gram = jnp.zeros((S, S), F32)
    cross = jnp.zeros((S, S), F32)
    for p in range(B):
        g_high, g_low = gg_high_ref[0, p], gg_low_ref[0, p]
        value = base_ref[p] + halo_ref[p] + (mm(g_high, w_high) + (mm(g_high, w_low) + mm(g_low, w_high)))
        second_ref[p] = value
        s_high, s_low = split(value)
        turned = s_high.T
        gram += mm(turned, s_high)
        cross += mm(turned, s_low)
    gram_ref[...] += gram
    cross_ref[...] += cross

    @pl.when(step == STEPS - 1)
    def _():
        cross = cross_ref[...]
        gram_ref[...] += cross + cross.T


def make_second(base, low, high, gg, weighted):
    shares = pl.BlockSpec((3, NEAR, S), lambda i: (0, 0, 0))
    return pl.pallas_call(
        second_kernel,
        grid=(STEPS,),
        in_specs=[plane_spec(), whole(MESSAGE.shape[0]), whole(MESSAGE.shape[0]), part_spec(0), part_spec(1)]
        + [shares, shares, whole(NEAR)],
        out_specs=[plane_spec(), whole()],
        out_shape=[FULL, sds((S, S))],
        scratch_shapes=[pltpu.VMEM((S, S), F32), pltpu.VMEM((S, S), F32), pltpu.VMEM((B, ROWS, S), F32)],
        compiler_params=params(16),
        cost_estimate=cost(1 << 27, 8 << 20),
        name="second",
    )(base, low, high, gg, gg, *weighted)


def exact(a, b):
    return jnp.dot(a, b, precision=lax.Precision.HIGHEST, preferred_element_type=F32)


def inverse_factor(gram_ref, a_ref, x_ref, state_ref):
    row = lax.broadcasted_iota(jnp.int32, (S, S), 0)
    column = lax.broadcasted_iota(jnp.int32, (S, S), 1)
    unit = jnp.where(row == column, 1.0, 0.0)
    gram = gram_ref[...]
    diagonal = jnp.where(row == column, gram, 0.0)
    down = lax.rsqrt(jnp.sum(diagonal, axis=1, keepdims=True))
    across = lax.rsqrt(jnp.sum(diagonal, axis=0, keepdims=True))
    a_ref[...] = gram * down * across
    x_ref[...] = unit

    def residual():
        x = x_ref[...]
        return unit - exact(exact(x, a_ref[...]), x.T)

    def size(e):
        return jnp.sum(e * e)

    def improve(e):
        lower = jnp.where(row > column, e, jnp.where(row == column, 0.5 * e, 0.0))
        x_ref[...] += exact(lower, x_ref[...])

    state_ref[0] = 0
    start = unit - a_ref[...]
    start_size = size(start)

    @pl.when(start_size < 0.16)
    def _():
        improve(start)
        state_ref[0] = jnp.where(start_size < 1e-6, 2, 1)

    for _ in range(5):

        @pl.when(state_ref[0] == 1)
        def _():
            e = residual()
            e_size = size(e)
            improve(e)
            state_ref[0] = jnp.where(e_size < 1e-6, 2, 1)

    @pl.when(state_ref[0] != 2)
    def _():
        x_ref[...] = unit
        lanes = lax.broadcasted_iota(jnp.int32, (1, S), 1)

        def step(j, _):
            line = a_ref[pl.ds(j, 1), :]
            scale = lax.rsqrt(jnp.sum(jnp.where(lanes == j, line, 0.0), axis=1, keepdims=True))
            a = a_ref[...]
            factor = jnp.sum(jnp.where(column == j, a, 0.0), axis=1, keepdims=True) * scale
            factor = jnp.where(row[:, :1] > j, factor, 0.0)
            x_line = x_ref[pl.ds(j, 1), :] * scale
            a_ref[...] = a - factor * (line * scale)
            x_ref[...] = jnp.where(row == j, x_line, x_ref[...] - factor * x_line)
            return 0

        lax.fori_loop(0, S, step, 0)

    x_ref[...] = x_ref[...] * across


def turn_kernel(second_ref, gram_ref, out_ref, a_ref, x_ref, i_high_ref, i_low_ref, state_ref):
    @pl.when(pl.program_id(0) == 0)
    def _():
        inverse_factor(gram_ref, a_ref, x_ref, state_ref)
        i_high, i_low = split(x_ref[...].T)
        i_high_ref[...] = i_high
        i_low_ref[...] = i_low

    i_high, i_low = i_high_ref[...], i_low_ref[...]

    for p in range(B):
        high, low = split(second_ref[p])
        out_ref[p] = mm(high, i_high) + (mm(high, i_low) + mm(low, i_high))


def turn(second, gram):
    return pl.pallas_call(
        turn_kernel,
        grid=(STEPS,),
        in_specs=[plane_spec(), whole()],
        out_specs=plane_spec(),
        out_shape=FULL,
        scratch_shapes=[pltpu.VMEM((S, S), F32)] * 2 + [pltpu.VMEM((S, S), BF16)] * 2 + [pltpu.SMEM((1,), jnp.int32)],
        compiler_params=params(16),
        cost_estimate=cost(1 << 28, 4 << 20),
        name="turn",
    )(second, gram)


def per_device(states, potential, atom_sites, projectors, energies):
    gx, gy = lax.axis_index("gx"), lax.axis_index("gy")
    depth = lax.axis_size("gzs")
    count = 4 * depth
    barrier = lax.optimization_barrier

    def send(value, flip=0, move=0):
        def target(d):
            return (d // depth * depth ^ flip) + (d + move) % depth

        return lax.ppermute(value, AXES, [(d, target(d)) for d in range(count)])

    over_x, over_y = 2 * depth, depth
    inner_ones = [d for d in range(count) if d % 4 in (1, 2)]
    outer_ones = [d for d in range(count) if d % 4 in (0, 3)]
    inner = ((lax.axis_index("gzs") + 1) // 2 % 2).astype(jnp.int32).reshape(1)
    s = states.reshape(C, ROWS, S)
    pot = potential.reshape(32, 128)

    atoms = jnp.concatenate(
        [projectors.reshape(4, TAPS), atom_sites.astype(F32), energies[:, None], jnp.zeros((4, 768 - TAPS - 4), F32)],
        axis=1,
    ).reshape(24, 128)
    mate = send(s, over_x)
    below, above = send(atoms, 0, 1), send(atoms, 0, -1)
    one_edge, head, tail = pack(s)
    one_edge = send(one_edge, over_y)
    head, tail, below, above = barrier((head, tail, below, above))
    parcel = stack(below, atoms, above, pot)
    parcel_y = send(parcel, over_y)
    parcel_x = send(parcel, over_x)
    low, high = send(tail, 0, 1), send(head, 0, -1)
    two_edge, three_edge, mid = pack_rest(s)
    vb = spread(parcel)
    beside = side_x(s, mate)
    parcel_y, one_edge, two_edge, three_edge, beside = barrier((parcel_y, one_edge, two_edge, three_edge, beside))
    relayed = lax.ppermute(three_edge, AXES, [(d, d ^ over_y ^ 1) for d in outer_ones])
    two_edge = send(two_edge, over_y)
    parcel_xy = send(parcel_y, over_x)
    corner = jnp.stack([gx * C, gy * C]).astype(jnp.int32)
    gg, part, energy = prep([parcel, parcel_x, parcel_y, parcel_xy], corner, vb, s)

    part, relayed, three_edge = barrier((part, relayed, three_edge))
    relayed = lax.ppermute(relayed, AXES, [(d, d ^ 1) for d in inner_ones])
    three_edge = lax.ppermute(three_edge, AXES, [(d, d ^ over_y) for d in inner_ones])
    part = part + send(part, over_x)
    part_mate = send(part, over_y)
    side_part = side_z(s, beside, low, high)
    edges = [one_edge, two_edge, three_edge, relayed]
    vb = vb.reshape(C, ROWS, S)
    q, mix, head, tail = make_first(s, side_part, vb, edges, inner, part, part_mate)
    low, high = send(tail, 0, 1), send(head, 0, -1)
    mate = send(mix, over_x)
    mid, part_mate = barrier((mid, part_mate))
    mid = send(mid, over_y)
    vb_mate = spread(parcel_y).reshape(C, ROWS, S)
    part_two = side_again(mix, mate)
    base = make_base(s, mid, vb, vb_mate, q, side_part, part_two, edges, inner)
    second, gram = make_second(base, low, high, gg.reshape(2, C, ROWS, S), [part, part_mate, energy])

    for flip in (64, 32, 36, 1, 3, 8, 24):
        gram = gram + lax.ppermute(gram, AXES, [(d, d ^ flip) for d in range(count)])
    gram = gram * (1.0 / (CELLS * count))
    return turn(second, gram).reshape(C, C, C, S)


def solution(mesh):
    return jax.shard_map(
        per_device,
        mesh=mesh,
        in_specs=(
            P("gx", "gy", "gzs", None),
            P("gx", "gy", "gzs"),
            P(("gx", "gy", "gzs"), None),
            P(("gx", "gy", "gzs"), None, None, None),
            P(("gx", "gy", "gzs")),
        ),
        out_specs=P("gx", "gy", "gzs", None),
        check_vma=False,
    )
```

```python
import math

import jax
import jax.numpy as jnp
from jax import lax
from jax.experimental import pallas as pl
from jax.experimental.pallas import tpu as pltpu
from jax.sharding import PartitionSpec as P

AXES = ("gx", "gy", "gzs")
H = 6
C = 16
ROWS = C * C
CELLS = C * C * C
S = 128
W = 9
R = 4
NEAR = 48
TAPS = W * W * W
F32 = jnp.float32
BF16 = jnp.bfloat16

grid_step = 0.6
filter_centre = 36.0
filter_half = 26.0


def weights():
    taps = []
    for k in range(1, 7):
        top = 2.0 * (-1) ** (k + 1) * math.factorial(6) ** 2
        under = k * k * math.factorial(6 - k) * math.factorial(6 + k)
        taps.append(top / under)
    scale = -0.5 / (grid_step * grid_step)
    off = [scale * t / filter_half for t in taps]
    diagonal = 3.0 * scale * (-2.0 * sum(taps))
    return off, diagonal


OFF, DIAGONAL = weights()


def params(mib):
    return pltpu.CompilerParams(vmem_limit_bytes=mib * 1024 * 1024)


def cost(flops, nbytes):
    return pl.CostEstimate(flops=flops, bytes_accessed=nbytes, transcendentals=0)


def sds(shape, dtype=F32):
    return jax.ShapeDtypeStruct(shape, dtype)


def split(value):
    high = value.astype(BF16)
    low = (value - high.astype(F32)).astype(BF16)
    return high, low


def mm(a, b):
    return jnp.dot(a, b, preferred_element_type=F32)


def tap_sum(at, index):
    total = None
    for k in range(1, 7):
        term = OFF[k - 1] * (at(index + k) + at(index - k))
        total = term if total is None else total + term
    return total


B = 4
STEPS = C // B
N = 2
FIRST = 6
MIDDLE = 10
EDGE = 192
MID = 64
MID_START = (MIDDLE - FIRST) * EDGE


def stride_rows(z):
    return pl.ds(z, C, stride=C)


def plane_spec(rows=ROWS, planes=B):
    return pl.BlockSpec((planes, rows, S), lambda i: (i, 0, 0))


def halo_spec(planes=B):
    return pl.BlockSpec((H, planes, C, S), lambda i: (0, i, 0, 0))


def part_spec(part):
    return pl.BlockSpec((1, B, ROWS, S), lambda i: (part, i, 0, 0))


def whole(rows=S):
    return pl.BlockSpec((rows, S), lambda i: (0, 0))


def edge_spec(start, stop):
    return pl.BlockSpec((N, EDGE, S), lambda i: (jnp.clip(i - start // N, 0, (stop - start) // N - 1), 0, 0))


def edge_specs():
    return [edge_spec(0, FIRST), edge_spec(FIRST, C), edge_spec(MIDDLE, C)]


def for_piece(edges, inner_ref, body):
    step = pl.program_id(0)
    direct = (inner_ref[0] == 1) | (step < MIDDLE // N)

    @pl.when(step < FIRST // N)
    def _():
        body(edges[0])

    @pl.when((step >= FIRST // N) & direct)
    def _():
        body(edges[1])

    @pl.when(jnp.logical_not(direct))
    def _():
        body(edges[2])


SCALARS = pl.BlockSpec(memory_space=pltpu.SMEM)
FULL = sds((C, ROWS, S))
FULL_ROWS = sds((CELLS, S))
HALO_ROWS = H * ROWS
MESSAGE = sds((HALO_ROWS + 2 * NEAR, S))
HALO = sds((H, C, C, S))
EDGES = [sds((FIRST, EDGE, S)), sds((C - FIRST, EDGE, S)), sds((C - MIDDLE, EDGE, S))]


def halo_rows(x, z):
    return pl.ds(pl.multiple_of(z * ROWS + x * C, C), C)


def halves(y, half):
    return slice(y * C + half * 8, y * C + half * 8 + 8)


def pack_edges(s_ref, out_ref):
    out_ref[:, 0:96, :] = s_ref[:, 0:96, :]
    out_ref[:, 96:192, :] = s_ref[:, 160:256, :]


def pack_kernel(s_ref, edge_ref, head_ref, tail_ref):
    @pl.when(pl.program_id(0) < FIRST // N)
    def _():
        pack_edges(s_ref, edge_ref)

    for p in range(N):
        for z in range(H):
            head_ref[z, p] = s_ref[p, stride_rows(z), :]
            tail_ref[z, p] = s_ref[p, stride_rows(C - H + z), :]


def pack(s):
    return pl.pallas_call(
        pack_kernel,
        grid=(C // N,),
        in_specs=[plane_spec(ROWS, N)],
        out_specs=edge_specs()[:1] + [halo_spec(N), halo_spec(N)],
        out_shape=EDGES[:1] + [HALO, HALO],
        compiler_params=params(12),
        cost_estimate=cost(1 << 32, 6 << 20),
        name="pack",
    )(s)


def pack_rest_kernel(s_ref, inner_ref, message_ref, relay_ref, mid_ref):
    step = pl.program_id(0)
    inner = inner_ref[0] == 1
    mid_ref[...] = s_ref[:, 96:160, :]

    @pl.when(step >= MIDDLE // N)
    def _():
        pack_edges(s_ref, relay_ref)

    @pl.when((step >= FIRST // N) & (inner | (step < MIDDLE // N)))
    def _():
        for p in range(N):
            row = pl.multiple_of((step * N + p - FIRST) * EDGE, MID)
            message_ref[pl.ds(row, 96), :] = s_ref[p, 0:96, :]
            message_ref[pl.ds(row + 96, 96), :] = s_ref[p, 160:256, :]

    @pl.when(jnp.logical_not(inner))
    def _():
        for p in range(N):
            row = pl.multiple_of(MID_START + (step * N + p) * MID, MID)
            message_ref[pl.ds(row, MID), :] = s_ref[p, 96:160, :]


def pack_rest(s, inner):
    rows = (C - FIRST) * EDGE
    message, relay, mid = pl.pallas_call(
        pack_rest_kernel,
        grid=(C // N,),
        in_specs=[plane_spec(ROWS, N), SCALARS],
        out_specs=[whole(rows), edge_spec(MIDDLE, C), plane_spec(MID, N)],
        out_shape=[sds((rows, S)), EDGES[2], sds((C, MID, S))],
        compiler_params=params(12),
        cost_estimate=cost(1 << 31, 4 << 20),
        name="pack_rest",
    )(s, inner)
    return message, relay, mid


def stack_kernel(*refs):
    start = 0
    for ref in refs[:-1]:
        refs[-1][start : start + ref.shape[0], :] = ref[...]
        start += ref.shape[0]


def stack(*arrays):
    rows = sum(a.shape[0] for a in arrays)
    return pl.pallas_call(stack_kernel, out_shape=sds((rows, S)), compiler_params=params(4), name="stack")(*arrays)


def along_x(s_ref, mate_ref, out_ref, add):
    def column(block, _):
        rows = pl.ds(pl.multiple_of(block * 8, 8), 8)
        ring = [mate_ref[C - H + i, rows, :] for i in range(H)]
        ring += [s_ref[x, rows, :] for x in range(C)]
        ring += [mate_ref[i, rows, :] for i in range(H)]
        for x in range(C):
            value = tap_sum(lambda i: ring[H + i], x)
            if add:
                value = value + out_ref[x, rows, :]
            out_ref[x, rows, :] = value
        return 0

    lax.fori_loop(0, ROWS // 8, column, 0)


def z_taps(ext_ref, y):
    return tap_sum(lambda k: ext_ref[y * 32 + 8 + k : y * 32 + 24 + k, :], 0)


def side_x_kernel(s_ref, mate_ref, out_ref):
    along_x(s_ref, mate_ref, out_ref, False)


def side_x(s, mate):
    return pl.pallas_call(
        side_x_kernel,
        out_shape=FULL,
        compiler_params=params(12),
        cost_estimate=cost(1 << 24, 6 << 20),
        name="side_x",
    )(s, mate)


def side_z_kernel(s_ref, part_ref, low_ref, high_ref, out_ref, ext_ref):
    def plane(x, _):
        for y in range(C):
            ext_ref[y * 32 + 8 : y * 32 + 24, :] = s_ref[x, y * C : (y + 1) * C, :]
        for z in range(H):
            ext_ref[pl.ds(2 + z, C, stride=32), :] = low_ref[z, x]
            ext_ref[pl.ds(24 + z, C, stride=32), :] = high_ref[z, x]
        for y in range(C):
            rows = slice(y * C, (y + 1) * C)
            out_ref[x, rows, :] = part_ref[x, rows, :] + z_taps(ext_ref, y)
        return 0

    lax.fori_loop(0, C, plane, 0)


def side_z(s, part, low, high):
    return pl.pallas_call(
        side_z_kernel,
        out_shape=FULL,
        scratch_shapes=[pltpu.VMEM((C * 32, S), F32)],
        compiler_params=params(14),
        cost_estimate=cost(1 << 24, 8 << 20),
        name="side_z",
    )(s, part, low, high)


def side_again_kernel(s_ref, mate_ref, out_ref, ext_ref):
    for y in range(C):
        ext_ref[y * 32 : y * 32 + 8, :] = jnp.zeros((8, S), F32)
        ext_ref[y * 32 + 24 : y * 32 + 32, :] = jnp.zeros((8, S), F32)

    def plane(x, _):
        for y in range(C):
            ext_ref[y * 32 + 8 : y * 32 + 24, :] = s_ref[x, y * C : (y + 1) * C, :]
        for y in range(C):
            out_ref[x, y * C : (y + 1) * C, :] = z_taps(ext_ref, y)
        return 0

    lax.fori_loop(0, C, plane, 0)
    along_x(s_ref, mate_ref, out_ref, True)


def side_again(s, mate):
    return pl.pallas_call(
        side_again_kernel,
        out_shape=FULL,
        scratch_shapes=[pltpu.VMEM((C * 32, S), F32)],
        compiler_params=params(12),
        cost_estimate=cost(1 << 25, 6 << 20),
        name="side_again",
    )(s, mate)


def tap_weight(distance):
    value = jnp.zeros(distance.shape, F32)
    for k in range(1, 7):
        value = jnp.where(distance == k, OFF[k - 1], value)
    return value


def ring_tables(coordinate):
    masks, factors = [], []
    for t in range(W):
        away = (coordinate - t) & 31
        masks.append(away == 0)
        factors.append(tap_weight(jnp.minimum(away, 32 - away)))
    return masks, factors


def spread_kernel(parcel_ref, vb_ref):
    def spread_row(row, _):
        line = (parcel_ref[pl.ds(72 + row, 1), :] + (DIAGONAL - filter_centre)) * (1.0 / filter_half)
        start = pl.multiple_of(row * 128, 128)
        vb_ref[pl.ds(start, 128), :] = jnp.broadcast_to(line, (128, 128)).T
        return 0

    lax.fori_loop(0, CELLS // 128, spread_row, 0, unroll=8)


def spread(parcel):
    return pl.pallas_call(
        spread_kernel,
        out_shape=FULL_ROWS,
        compiler_params=params(8),
        cost_estimate=cost(1 << 20, 2 << 20),
        name="spread",
    )(parcel)


def prep_kernel(*refs):
    parcels = refs[:4]
    corner_ref, vb_ref, s_ref, gg_ref, coef_ref, energy_ref, near_ref, table_ref, a1_ref, a1z_ref, a2_ref, a2s_ref = refs[4:]
    upper_x, upper_y = corner_ref[0] > 0, corner_ref[1] > 0
    for slab in range(3):
        own, over_x, over_y, over_xy = [parcel[slab * 24 : slab * 24 + 24, :] for parcel in parcels]
        same_x = [jnp.where(upper_y, over_y, own), jnp.where(upper_y, own, over_y)]
        other_x = [jnp.where(upper_y, over_xy, over_x), jnp.where(upper_y, over_x, over_xy)]
        ordered = [jnp.where(upper_x, o, m) for m, o in zip(same_x, other_x)]
        ordered += [jnp.where(upper_x, m, o) for m, o in zip(same_x, other_x)]
        for j in range(4):
            near_ref[slab * 96 + j * 24 : slab * 96 + j * 24 + 24, :] = ordered[j]
    blank = jnp.zeros((16, 128), F32)
    for block in range(6):
        rows = near_ref[pl.ds(block, NEAR, stride=6), :]
        table_ref[block * 128 : block * 128 + 128, :] = jnp.concatenate([rows, blank, rows, blank]).T
    at = TAPS + 3 - 640
    energy_ref[...] = jnp.broadcast_to(rows[:, at : at + 1] * (1.0 / filter_half), (NEAR, S))

    shape = (8, 128)
    sub = lax.broadcasted_iota(jnp.int32, shape, 0)
    lane = lax.broadcasted_iota(jnp.int32, shape, 1)
    first_lanes = lane < 64
    sites = [jnp.broadcast_to(table_ref[TAPS + d : TAPS + d + 1, :], shape).astype(jnp.int32) for d in range(3)]
    px = sites[0] - corner_ref[0]
    py = sites[1] - corner_ref[1]
    pz = (sites[2] & 15) + (((lane & 63) >> 4) - 1) * C
    zero = jnp.zeros(shape, F32)

    dz = sub + (lane >> 6) * 8 - pz + R
    z_masks = [dz == t for t in range(W)]
    z_factors = [tap_weight(jnp.abs(dz - t)) for t in range(W)]

    def place_z(ij, _):
        acc = zero
        along = zero
        for t in range(W):
            row = jnp.broadcast_to(table_ref[pl.ds(ij * W + t, 1), :], shape)
            acc = jnp.where(z_masks[t], row, acc)
            along = along + z_factors[t] * row
        a1_ref[ij] = acc
        a1z_ref[ij] = along
        return 0

    lax.fori_loop(0, W * W, place_z, 0, unroll=3)

    def place_y(y, _):
        masks, factors = ring_tables(y - py + R)
        for i in range(W):
            acc = zero
            along = zero
            moved = zero
            for t in range(W):
                value = a1_ref[i * W + t]
                acc = jnp.where(masks[t], value, acc)
                along = along + factors[t] * value
                moved = jnp.where(masks[t], a1z_ref[i * W + t], moved)
            a2_ref[i, y] = acc
            a2s_ref[i, y] = along + moved
        return 0

    lax.fori_loop(0, C, place_y, 0)

    def place_x(x, _):
        masks, factors = ring_tables(x - px + R)

        def per_y(y, _):
            row = pl.multiple_of(x * ROWS + y * C, C)
            acc = zero
            along = zero
            moved = zero
            for t in range(W):
                value = a2_ref[t, y]
                acc = jnp.where(masks[t], value, acc)
                along = along + factors[t] * value
                moved = jnp.where(masks[t], a2s_ref[t, y], moved)
            v = vb_ref[pl.ds(row, C), :]
            moved = along + moved + jnp.where(first_lanes, v[:8], v[8:]) * acc
            lower = jnp.where(first_lanes, acc, pltpu.roll(moved, 64, 1))
            upper = jnp.where(first_lanes, pltpu.roll(acc, 64, 1), moved)
            high, low = split(jnp.concatenate([lower, upper], axis=0))
            gg_ref[0, pl.ds(row, C), :] = high
            gg_ref[1, pl.ds(row, C), :] = low
            return 0

        lax.fori_loop(0, C, per_y, 0, unroll=16)
        return 0

    lax.fori_loop(0, C, place_x, 0)

    coef_ref[...] = jnp.zeros((3, NEAR, S), F32)

    def contract(x, _):
        rows = pl.ds(pl.multiple_of(x * 2 * ROWS, ROWS), 2 * ROWS)
        g_high, g_low = gg_ref[0, rows, :], gg_ref[1, rows, :]
        t_high, t_low = g_high.T, g_low.T
        high, low = split(s_ref[rows, :])
        got = mm(t_high, high) + (mm(t_high, low) + mm(t_low, high))
        t_high, t_low = t_high[:NEAR], t_low[:NEAR]
        pair = mm(t_high, g_high) + (mm(t_high, g_low) + mm(t_low, g_high))
        for slab in range(3):
            rows = slice(slab * C, slab * C + C)
            coef_ref[slab, 0:16] += got[rows]
            coef_ref[slab, 16:32] += got[64 + slab * C : 80 + slab * C]
            coef_ref[slab, 32:48] += pair[rows]
        return 0

    lax.fori_loop(0, C // 2, contract, 0, unroll=2)


def prep(parcels, corner, vb, s):
    vmem = pl.BlockSpec(memory_space=pltpu.VMEM)
    return pl.pallas_call(
        prep_kernel,
        in_specs=[vmem] * 4 + [pl.BlockSpec(memory_space=pltpu.SMEM), vmem, vmem],
        out_shape=[sds((2, CELLS, S), BF16), sds((3, NEAR, S)), sds((NEAR, S))],
        scratch_shapes=[
            pltpu.VMEM((288, 128), F32),
            pltpu.VMEM((768, 128), F32),
            pltpu.VMEM((W * W, 8, 128), F32),
            pltpu.VMEM((W * W, 8, 128), F32),
            pltpu.VMEM((W, C, 8, 128), F32),
            pltpu.VMEM((W, C, 8, 128), F32),
        ],
        compiler_params=params(16),
        cost_estimate=cost(1 << 27, 10 << 20),
        name="prep",
    )(*parcels, corner, vb, s.reshape(CELLS, S))


def move_pair(shares, away):
    lane = lax.broadcasted_iota(jnp.int32, (16, 128), 1)
    keep = (lane < 32) if away < 0 else (lane >= 16) & (lane < 48)
    pair = jnp.where(keep, pltpu.roll(shares[32:48], (away * 16) % 128, 1), 0.0)
    return jnp.concatenate([shares[0:32], pair])


def first_kernel(s_ref, side_ref, vb_ref, *refs):
    inner_ref, part_ref, mate_ref, q_ref, mix_ref, head_ref, tail_ref = refs[3:]
    step = pl.program_id(0)

    @pl.when(step == 0)
    def _():
        for j in range(2):
            rows = slice(HALO_ROWS + j * NEAR, HALO_ROWS + (j + 1) * NEAR)
            head_ref[rows, :] = part_ref[j] + mate_ref[j]
            tail_ref[rows, :] = part_ref[j + 1] + mate_ref[j + 1]

    def planes(edge_ref):
        for p in range(N):
            for half in range(2):
                ring = {y: s_ref[p, halves(y, half), :] for y in range(C)}
                for y in range(H):
                    ring[C + y] = edge_ref[p, halves(y, half), :]
                    ring[y - H] = edge_ref[p, halves(H + y, half), :]
                for y in range(C):
                    rows = halves(y, half)
                    dy = tap_sum(lambda i: ring[i], y)
                    q = dy + vb_ref[p, rows, :] * ring[y]
                    q_ref[p, rows, :] = q
                    mix_ref[p, rows, :] = side_ref[p, rows, :] + q + dy
            for z in range(H):
                rows = halo_rows(step * N + p, z)
                head_ref[rows, :] = mix_ref[p, stride_rows(z), :]
                tail_ref[rows, :] = mix_ref[p, stride_rows(C - H + z), :]

    for_piece(refs[:3], inner_ref, planes)


def make_first(s, side_part, vb, edges, inner, part, part_mate):
    shares = pl.BlockSpec((3, NEAR, S), lambda i: (0, 0, 0))
    return pl.pallas_call(
        first_kernel,
        grid=(C // N,),
        in_specs=[plane_spec(ROWS, N)] * 3 + edge_specs() + [SCALARS] + [shares] * 2,
        out_specs=[plane_spec(ROWS, N), plane_spec(ROWS, N), whole(MESSAGE.shape[0]), whole(MESSAGE.shape[0])],
        out_shape=[FULL, FULL, MESSAGE, MESSAGE],
        compiler_params=params(16),
        cost_estimate=cost(1 << 24, 14 << 20),
        name="first",
    )(s, side_part, vb, *edges, inner, part, part_mate)


def base_kernel(s_ref, mid_ref, vb_ref, vb_mate_ref, q_ref, side_ref, part_ref, *refs):
    inner_ref, message_ref, out_ref, middle_ref = refs[3:]
    step = pl.program_id(0)
    inner = inner_ref[0] == 1

    @pl.when(inner)
    def _():
        middle_ref[...] = mid_ref[...]

    @pl.when(jnp.logical_not(inner))
    def _():
        for p in range(N):
            middle_ref[p] = message_ref[pl.ds(pl.multiple_of(MID_START + (step * N + p) * MID, MID), MID), :]

    def planes(edge_ref):
        for p in range(N):
            for half in range(2):

                def other(y, p=p, half=half):
                    if y < H:
                        return edge_ref[p, halves(y, half), :]
                    if y < C - H:
                        return middle_ref[p, halves(y - H, half), :]
                    return edge_ref[p, halves(y - 4, half), :]

                ring = [s_ref[p, halves(y, half), :] for y in range(C)] + [other(y) for y in range(C)]
                q = {y: q_ref[p, halves(y, half), :] for y in range(C)}
                for y in list(range(H)) + list(range(C - H, C)):
                    v = vb_mate_ref[p, halves(y, half), :]
                    q[C + y] = tap_sum(lambda i: ring[i % 32], C + y) + v * ring[C + y]
                for y in range(C):
                    rows = halves(y, half)
                    total = tap_sum(lambda i: q[i % 32], y)
                    total = total + vb_ref[p, rows, :] * (side_ref[p, rows, :] + q[y])
                    out_ref[p, rows, :] = 2.0 * (total + part_ref[p, rows, :]) - ring[y]

    for_piece(refs[:3], inner_ref, planes)


def make_base(s, mid, vb, vb_mate, q, side_part, part, edges, inner):
    return pl.pallas_call(
        base_kernel,
        grid=(C // N,),
        in_specs=[plane_spec(ROWS, N), plane_spec(MID, N)]
        + [plane_spec(ROWS, N)] * 5
        + edge_specs()
        + [SCALARS, whole((C - FIRST) * EDGE)],
        out_specs=plane_spec(ROWS, N),
        out_shape=FULL,
        scratch_shapes=[pltpu.VMEM((N, MID, S), F32)],
        compiler_params=params(16),
        cost_estimate=cost(1 << 25, 16 << 20),
        name="base",
    )(s, mid, vb, vb_mate, q, side_part, part, *edges, inner, edges[1].reshape(-1, S))


def second_kernel(base_ref, low_ref, high_ref, gg_high_ref, gg_low_ref, *rest):
    part_ref, mate_ref, energy_ref, second_ref, gram_ref, cross_ref, w_ref, halo_ref = rest
    step = pl.program_id(0)

    @pl.when(step == 0)
    def _():
        gram_ref[...] = jnp.zeros((S, S), F32)
        cross_ref[...] = jnp.zeros((S, S), F32)
        w_ref[...] = jnp.zeros((S, S), F32)
        halo_ref[...] = jnp.zeros((B, ROWS, S), F32)
        mine = [part_ref[j] + mate_ref[j] for j in range(3)]
        below = [move_pair(low_ref[HALO_ROWS + j * NEAR : HALO_ROWS + (j + 1) * NEAR, :], -1) for j in range(2)]
        above = [move_pair(high_ref[HALO_ROWS + j * NEAR : HALO_ROWS + (j + 1) * NEAR, :], 1) for j in range(2)]
        slabs = [mine[0] + below[0], mine[1] + below[1] + above[0], mine[2] + above[1]]
        near = jnp.concatenate([slab[0:16] for slab in slabs]) * energy_ref[...]
        lane = lax.broadcasted_iota(jnp.int32, (NEAR, S), 1)
        pair = jnp.where(lane < NEAR, jnp.concatenate([slab[32:48] for slab in slabs]), 0.0)
        two = jnp.concatenate([slab[16:32] for slab in slabs])
        two = two + exact(pair, jnp.concatenate([near, jnp.zeros((S - NEAR, S), F32)]))
        w_ref[0:NEAR, :] = 2.0 * energy_ref[...] * two
        w_ref[64 : 64 + NEAR, :] = 2.0 * near

    for p in range(B):
        low = [low_ref[halo_rows(step * B + p, j), :] for j in range(H)]
        high = [high_ref[halo_rows(step * B + p, j), :] for j in range(H)]
        for z in range(H):
            add = sum((2.0 * OFF[k - 1]) * low[z - k + H] for k in range(z + 1, H + 1))
            halo_ref[p, stride_rows(z), :] = add
            add = sum((2.0 * OFF[H + j - z - 1]) * high[j] for j in range(z + 1))
            halo_ref[p, stride_rows(C - H + z), :] = add

    w_high, w_low = split(w_ref[...])
    gram = jnp.zeros((S, S), F32)
    cross = jnp.zeros((S, S), F32)
    for p in range(B):
        g_high, g_low = gg_high_ref[0, p], gg_low_ref[0, p]
        value = base_ref[p] + halo_ref[p] + (mm(g_high, w_high) + (mm(g_high, w_low) + mm(g_low, w_high)))
        second_ref[p] = value
        s_high, s_low = split(value)
        turned = s_high.T
        gram += mm(turned, s_high)
        cross += mm(turned, s_low)
    gram_ref[...] += gram
    cross_ref[...] += cross

    @pl.when(step == STEPS - 1)
    def _():
        cross = cross_ref[...]
        gram_ref[...] += cross + cross.T


def make_second(base, low, high, gg, weighted):
    shares = pl.BlockSpec((3, NEAR, S), lambda i: (0, 0, 0))
    return pl.pallas_call(
        second_kernel,
        grid=(STEPS,),
        in_specs=[plane_spec(), whole(MESSAGE.shape[0]), whole(MESSAGE.shape[0]), part_spec(0), part_spec(1)]
        + [shares, shares, whole(NEAR)],
        out_specs=[plane_spec(), whole()],
        out_shape=[FULL, sds((S, S))],
        scratch_shapes=[pltpu.VMEM((S, S), F32), pltpu.VMEM((S, S), F32), pltpu.VMEM((B, ROWS, S), F32)],
        compiler_params=params(16),
        cost_estimate=cost(1 << 27, 8 << 20),
        name="second",
    )(base, low, high, gg, gg, *weighted)


def exact(a, b):
    return jnp.dot(a, b, precision=lax.Precision.HIGHEST, preferred_element_type=F32)


def inverse_factor(gram_ref, a_ref, x_ref, state_ref):
    row = lax.broadcasted_iota(jnp.int32, (S, S), 0)
    column = lax.broadcasted_iota(jnp.int32, (S, S), 1)
    unit = jnp.where(row == column, 1.0, 0.0)
    gram = gram_ref[...]
    diagonal = jnp.where(row == column, gram, 0.0)
    down = lax.rsqrt(jnp.sum(diagonal, axis=1, keepdims=True))
    across = lax.rsqrt(jnp.sum(diagonal, axis=0, keepdims=True))
    a_ref[...] = gram * down * across
    x_ref[...] = unit

    def residual():
        x = x_ref[...]
        return unit - exact(exact(x, a_ref[...]), x.T)

    def size(e):
        return jnp.sum(e * e)

    def improve(e):
        lower = jnp.where(row > column, e, jnp.where(row == column, 0.5 * e, 0.0))
        x_ref[...] += exact(lower, x_ref[...])

    state_ref[0] = 0
    start = unit - a_ref[...]
    start_size = size(start)

    @pl.when(start_size < 0.16)
    def _():
        improve(start)
        state_ref[0] = jnp.where(start_size < 1e-6, 2, 1)

    for _ in range(5):

        @pl.when(state_ref[0] == 1)
        def _():
            e = residual()
            e_size = size(e)
            improve(e)
            state_ref[0] = jnp.where(e_size < 1e-6, 2, 1)

    @pl.when(state_ref[0] != 2)
    def _():
        x_ref[...] = unit
        lanes = lax.broadcasted_iota(jnp.int32, (1, S), 1)

        def step(j, _):
            line = a_ref[pl.ds(j, 1), :]
            scale = lax.rsqrt(jnp.sum(jnp.where(lanes == j, line, 0.0), axis=1, keepdims=True))
            a = a_ref[...]
            factor = jnp.sum(jnp.where(column == j, a, 0.0), axis=1, keepdims=True) * scale
            factor = jnp.where(row[:, :1] > j, factor, 0.0)
            x_line = x_ref[pl.ds(j, 1), :] * scale
            a_ref[...] = a - factor * (line * scale)
            x_ref[...] = jnp.where(row == j, x_line, x_ref[...] - factor * x_line)
            return 0

        lax.fori_loop(0, S, step, 0)

    x_ref[...] = x_ref[...] * across


def turn_kernel(second_ref, gram_ref, out_ref, a_ref, x_ref, i_high_ref, i_low_ref, state_ref):
    @pl.when(pl.program_id(0) == 0)
    def _():
        inverse_factor(gram_ref, a_ref, x_ref, state_ref)
        i_high, i_low = split(x_ref[...].T)
        i_high_ref[...] = i_high
        i_low_ref[...] = i_low

    i_high, i_low = i_high_ref[...], i_low_ref[...]

    for p in range(B):
        high, low = split(second_ref[p])
        out_ref[p] = mm(high, i_high) + (mm(high, i_low) + mm(low, i_high))


def turn(second, gram):
    return pl.pallas_call(
        turn_kernel,
        grid=(STEPS,),
        in_specs=[plane_spec(), whole()],
        out_specs=plane_spec(),
        out_shape=FULL,
        scratch_shapes=[pltpu.VMEM((S, S), F32)] * 2 + [pltpu.VMEM((S, S), BF16)] * 2 + [pltpu.SMEM((1,), jnp.int32)],
        compiler_params=params(16),
        cost_estimate=cost(1 << 28, 4 << 20),
        name="turn",
    )(second, gram)


def per_device(states, potential, atom_sites, projectors, energies):
    gx, gy = lax.axis_index("gx"), lax.axis_index("gy")
    depth = lax.axis_size("gzs")
    count = 4 * depth
    barrier = lax.optimization_barrier

    def send(value, flip=0, move=0):
        def target(d):
            return (d // depth * depth ^ flip) + (d + move) % depth

        return lax.ppermute(value, AXES, [(d, target(d)) for d in range(count)])

    over_x, over_y = 2 * depth, depth
    inner_ones = [d for d in range(count) if d % 4 in (1, 2)]
    outer_ones = [d for d in range(count) if d % 4 in (0, 3)]
    inner = ((lax.axis_index("gzs") + 1) // 2 % 2).astype(jnp.int32).reshape(1)
    s = states.reshape(C, ROWS, S)
    pot = potential.reshape(32, 128)

    atoms = jnp.concatenate(
        [projectors.reshape(4, TAPS), atom_sites.astype(F32), energies[:, None], jnp.zeros((4, 768 - TAPS - 4), F32)],
        axis=1,
    ).reshape(24, 128)
    mate = send(s, over_x)
    below, above = send(atoms, 0, 1), send(atoms, 0, -1)
    one_edge, head, tail = pack(s)
    one_edge = send(one_edge, over_y)
    head, tail, below, above = barrier((head, tail, below, above))
    parcel = stack(below, atoms, above, pot)
    parcel_y = send(parcel, over_y)
    parcel_x = send(parcel, over_x)
    low, high = send(tail, 0, 1), send(head, 0, -1)
    message, relay, mid = pack_rest(s, inner)
    vb = spread(parcel)
    beside = side_x(s, mate)
    parcel_y, one_edge, message, relay, beside = barrier((parcel_y, one_edge, message, relay, beside))
    relayed = lax.ppermute(relay, AXES, [(d, d ^ over_y ^ 1) for d in outer_ones])
    message = send(message, over_y)
    parcel_xy = send(parcel_y, over_x)
    corner = jnp.stack([gx * C, gy * C]).astype(jnp.int32)
    gg, part, energy = prep([parcel, parcel_x, parcel_y, parcel_xy], corner, vb, s)

    part, relayed = barrier((part, relayed))
    relayed = lax.ppermute(relayed, AXES, [(d, d ^ 1) for d in inner_ones])
    part = part + send(part, over_x)
    part_mate = send(part, over_y)
    side_part = side_z(s, beside, low, high)
    edges = [one_edge, message.reshape(C - FIRST, EDGE, S), relayed]
    vb = vb.reshape(C, ROWS, S)
    q, mix, head, tail = make_first(s, side_part, vb, edges, inner, part, part_mate)
    low, high = send(tail, 0, 1), send(head, 0, -1)
    mate = send(mix, over_x)
    mid, part_mate = barrier((mid, part_mate))
    mid = lax.ppermute(mid, AXES, [(d, d ^ over_y) for d in inner_ones])
    vb_mate = spread(parcel_y).reshape(C, ROWS, S)
    part_two = side_again(mix, mate)
    base = make_base(s, mid, vb, vb_mate, q, side_part, part_two, edges, inner)
    second, gram = make_second(base, low, high, gg.reshape(2, C, ROWS, S), [part, part_mate, energy])

    for flip in (64, 32, 36, 1, 3, 8, 24):
        gram = gram + lax.ppermute(gram, AXES, [(d, d ^ flip) for d in range(count)])
    gram = gram * (1.0 / (CELLS * count))
    return turn(second, gram).reshape(C, C, C, S)


def solution(mesh):
    return jax.shard_map(
        per_device,
        mesh=mesh,
        in_specs=(
            P("gx", "gy", "gzs", None),
            P("gx", "gy", "gzs"),
            P(("gx", "gy", "gzs"), None),
            P(("gx", "gy", "gzs"), None, None, None),
            P(("gx", "gy", "gzs")),
        ),
        out_specs=P("gx", "gy", "gzs", None),
        check_vma=False,
    )
```

```python
import math

import jax
import jax.numpy as jnp
from jax import lax
from jax.experimental import pallas as pl
from jax.experimental.pallas import tpu as pltpu
from jax.sharding import PartitionSpec as P

AXES = ("gx", "gy", "gzs")
H = 6
C = 16
ROWS = C * C
CELLS = C * C * C
NCELLS = 32 * 32 * 512
S = 128
W = 9
R = 4
NEAR = 48
TAPS = W * W * W
F32 = jnp.float32
BF16 = jnp.bfloat16

grid_step = 0.6
filter_centre = 36.0
filter_half = 26.0


def weights():
    taps = []
    for k in range(1, 7):
        top = 2.0 * (-1) ** (k + 1) * math.factorial(6) ** 2
        under = k * k * math.factorial(6 - k) * math.factorial(6 + k)
        taps.append(top / under)
    scale = -0.5 / (grid_step * grid_step)
    off = [scale * t / filter_half for t in taps]
    diagonal = 3.0 * scale * (-2.0 * sum(taps))
    return off, diagonal


OFF, DIAGONAL = weights()


def params(mib):
    return pltpu.CompilerParams(vmem_limit_bytes=mib * 1024 * 1024)


def cost(flops, nbytes):
    return pl.CostEstimate(flops=flops, bytes_accessed=nbytes, transcendentals=0)


def sds(shape, dtype=F32):
    return jax.ShapeDtypeStruct(shape, dtype)


def split(value):
    high = value.astype(BF16)
    low = (value - high.astype(F32)).astype(BF16)
    return high, low


def mm(a, b):
    return jnp.dot(a, b, preferred_element_type=F32)


def tap_sum(at, index):
    total = None
    for k in range(1, 7):
        term = OFF[k - 1] * (at(index + k) + at(index - k))
        total = term if total is None else total + term
    return total


B = 4
STEPS = C // B
N = 2
FIRST = 8
MIDDLE = 10
EDGE = 192
MID = 64
MID_START = (MIDDLE - FIRST) * EDGE


def stride_rows(z):
    return pl.ds(z, C, stride=C)


def plane_spec(rows=ROWS, planes=B):
    return pl.BlockSpec((planes, rows, S), lambda i: (i, 0, 0))


def halo_spec(planes=B):
    return pl.BlockSpec((H, planes, C, S), lambda i: (0, i, 0, 0))


def part_spec(part):
    return pl.BlockSpec((1, B, ROWS, S), lambda i: (part, i, 0, 0))


def whole(rows=S):
    return pl.BlockSpec((rows, S), lambda i: (0, 0))


def edge_spec(start, stop):
    return pl.BlockSpec((N, EDGE, S), lambda i: (jnp.clip(i - start // N, 0, (stop - start) // N - 1), 0, 0))


def edge_specs():
    return [edge_spec(0, FIRST), edge_spec(FIRST, C), edge_spec(MIDDLE, C)]


def for_piece(edges, inner_ref, body):
    step = pl.program_id(0)
    direct = (inner_ref[0] == 1) | (step < MIDDLE // N)

    @pl.when(step < FIRST // N)
    def _():
        body(edges[0])

    @pl.when((step >= FIRST // N) & direct)
    def _():
        body(edges[1])

    @pl.when(jnp.logical_not(direct))
    def _():
        body(edges[2])


SCALARS = pl.BlockSpec(memory_space=pltpu.SMEM)
FULL = sds((C, ROWS, S))
FULL_ROWS = sds((CELLS, S))
HALO_ROWS = H * FIRST * C
SHARES = 2 * NEAR
HALO = sds((H, C, C, S))
EDGES = [sds((FIRST, EDGE, S)), sds((C - FIRST, EDGE, S)), sds((C - MIDDLE, EDGE, S))]


def halo_rows(x, z):
    return pl.ds(pl.multiple_of(z * FIRST * C + x * C, C), C)


def halves(y, half):
    return slice(y * C + half * 8, y * C + half * 8 + 8)


def pack_edges(s_ref, out_ref):
    out_ref[:, 0:96, :] = s_ref[:, 0:96, :]
    out_ref[:, 96:192, :] = s_ref[:, 160:256, :]


def pack_kernel(s_ref, edge_ref, head_ref, tail_ref):
    @pl.when(pl.program_id(0) < FIRST // N)
    def _():
        pack_edges(s_ref, edge_ref)

    for p in range(N):
        for z in range(H):
            head_ref[z, p] = s_ref[p, stride_rows(z), :]
            tail_ref[z, p] = s_ref[p, stride_rows(C - H + z), :]


def pack(s):
    return pl.pallas_call(
        pack_kernel,
        grid=(C // N,),
        in_specs=[plane_spec(ROWS, N)],
        out_specs=edge_specs()[:1] + [halo_spec(N), halo_spec(N)],
        out_shape=EDGES[:1] + [HALO, HALO],
        compiler_params=params(12),
        cost_estimate=cost(1 << 32, 6 << 20),
        name="pack",
    )(s)


def pack_rest_kernel(s_ref, inner_ref, message_ref, relay_ref, mid_ref):
    step = pl.program_id(0)
    inner = inner_ref[0] == 1
    mid_ref[...] = s_ref[:, 96:160, :]

    @pl.when(step >= MIDDLE // N)
    def _():
        pack_edges(s_ref, relay_ref)

    @pl.when((step >= FIRST // N) & (inner | (step < MIDDLE // N)))
    def _():
        for p in range(N):
            row = pl.multiple_of((step * N + p - FIRST) * EDGE, MID)
            message_ref[pl.ds(row, 96), :] = s_ref[p, 0:96, :]
            message_ref[pl.ds(row + 96, 96), :] = s_ref[p, 160:256, :]

    @pl.when(jnp.logical_not(inner))
    def _():
        for p in range(N):
            row = pl.multiple_of(MID_START + (step * N + p) * MID, MID)
            message_ref[pl.ds(row, MID), :] = s_ref[p, 96:160, :]


def pack_rest(s, inner):
    rows = (C - FIRST) * EDGE
    message, relay, mid = pl.pallas_call(
        pack_rest_kernel,
        grid=(C // N,),
        in_specs=[plane_spec(ROWS, N), SCALARS],
        out_specs=[whole(rows), edge_spec(MIDDLE, C), plane_spec(MID, N)],
        out_shape=[sds((rows, S)), EDGES[2], sds((C, MID, S))],
        compiler_params=params(12),
        cost_estimate=cost(1 << 31, 4 << 20),
        name="pack_rest",
    )(s, inner)
    return message, relay, mid


def stack_kernel(*refs):
    start = 0
    for ref in refs[:-1]:
        refs[-1][start : start + ref.shape[0], :] = ref[...]
        start += ref.shape[0]


def stack(*arrays):
    rows = sum(a.shape[0] for a in arrays)
    return pl.pallas_call(stack_kernel, out_shape=sds((rows, S)), compiler_params=params(4), name="stack")(*arrays)


def along_x(s_ref, mate_ref, out_ref, add):
    def column(block, _):
        rows = pl.ds(pl.multiple_of(block * 8, 8), 8)
        ring = [mate_ref[C - H + i, rows, :] for i in range(H)]
        ring += [s_ref[x, rows, :] for x in range(C)]
        ring += [mate_ref[i, rows, :] for i in range(H)]
        for x in range(C):
            value = tap_sum(lambda i: ring[H + i], x)
            if add:
                value = value + out_ref[x, rows, :]
            out_ref[x, rows, :] = value
        return 0

    lax.fori_loop(0, ROWS // 8, column, 0)


def z_taps(ext_ref, y):
    return tap_sum(lambda k: ext_ref[y * 32 + 8 + k : y * 32 + 24 + k, :], 0)


def side_x_kernel(s_ref, mate_ref, out_ref):
    along_x(s_ref, mate_ref, out_ref, False)


def side_x(s, mate):
    return pl.pallas_call(
        side_x_kernel,
        out_shape=FULL,
        compiler_params=params(12),
        cost_estimate=cost(1 << 24, 6 << 20),
        name="side_x",
    )(s, mate)


def side_z_kernel(s_ref, part_ref, low_ref, high_ref, out_ref, ext_ref):
    def plane(x, _):
        for y in range(C):
            ext_ref[y * 32 + 8 : y * 32 + 24, :] = s_ref[x, y * C : (y + 1) * C, :]
        for z in range(H):
            ext_ref[pl.ds(2 + z, C, stride=32), :] = low_ref[z, x]
            ext_ref[pl.ds(24 + z, C, stride=32), :] = high_ref[z, x]
        for y in range(C):
            rows = slice(y * C, (y + 1) * C)
            out_ref[x, rows, :] = part_ref[x, rows, :] + z_taps(ext_ref, y)
        return 0

    lax.fori_loop(0, C, plane, 0)


def side_z(s, part, low, high):
    return pl.pallas_call(
        side_z_kernel,
        out_shape=FULL,
        scratch_shapes=[pltpu.VMEM((C * 32, S), F32)],
        compiler_params=params(14),
        cost_estimate=cost(1 << 24, 8 << 20),
        name="side_z",
    )(s, part, low, high)


def side_again_kernel(s_ref, mate_ref, out_ref, ext_ref):
    for y in range(C):
        ext_ref[y * 32 : y * 32 + 8, :] = jnp.zeros((8, S), F32)
        ext_ref[y * 32 + 24 : y * 32 + 32, :] = jnp.zeros((8, S), F32)

    def plane(x, _):
        for y in range(C):
            ext_ref[y * 32 + 8 : y * 32 + 24, :] = s_ref[x, y * C : (y + 1) * C, :]
        for y in range(C):
            out_ref[x, y * C : (y + 1) * C, :] = z_taps(ext_ref, y)
        return 0

    lax.fori_loop(0, C, plane, 0)
    along_x(s_ref, mate_ref, out_ref, True)


def side_again(s, mate):
    return pl.pallas_call(
        side_again_kernel,
        out_shape=FULL,
        scratch_shapes=[pltpu.VMEM((C * 32, S), F32)],
        compiler_params=params(12),
        cost_estimate=cost(1 << 25, 6 << 20),
        name="side_again",
    )(s, mate)


def tap_weight(distance):
    value = jnp.zeros(distance.shape, F32)
    for k in range(1, 7):
        value = jnp.where(distance == k, OFF[k - 1], value)
    return value


def ring_tables(coordinate):
    masks, factors = [], []
    for t in range(W):
        away = (coordinate - t) & 31
        masks.append(away == 0)
        factors.append(tap_weight(jnp.minimum(away, 32 - away)))
    return masks, factors


def spread_kernel(parcel_ref, vb_ref):
    def spread_row(row, _):
        line = (parcel_ref[pl.ds(72 + row, 1), :] + (DIAGONAL - filter_centre)) * (1.0 / filter_half)
        start = pl.multiple_of(row * 128, 128)
        vb_ref[pl.ds(start, 128), :] = jnp.broadcast_to(line, (128, 128)).T
        return 0

    lax.fori_loop(0, CELLS // 128, spread_row, 0, unroll=8)


def spread(parcel):
    return pl.pallas_call(
        spread_kernel,
        out_shape=FULL_ROWS,
        compiler_params=params(8),
        cost_estimate=cost(1 << 20, 2 << 20),
        name="spread",
    )(parcel)


def prep_kernel(*refs):
    parcels = refs[:4]
    corner_ref, vb_ref, s_ref, gg_ref, coef_ref, energy_ref, near_ref, table_ref, a1_ref, a1z_ref, a2_ref, a2s_ref = refs[4:]
    upper_x, upper_y = corner_ref[0] > 0, corner_ref[1] > 0
    for slab in range(3):
        own, over_x, over_y, over_xy = [parcel[slab * 24 : slab * 24 + 24, :] for parcel in parcels]
        same_x = [jnp.where(upper_y, over_y, own), jnp.where(upper_y, own, over_y)]
        other_x = [jnp.where(upper_y, over_xy, over_x), jnp.where(upper_y, over_x, over_xy)]
        ordered = [jnp.where(upper_x, o, m) for m, o in zip(same_x, other_x)]
        ordered += [jnp.where(upper_x, m, o) for m, o in zip(same_x, other_x)]
        for j in range(4):
            near_ref[slab * 96 + j * 24 : slab * 96 + j * 24 + 24, :] = ordered[j]
    blank = jnp.zeros((16, 128), F32)
    for block in range(6):
        rows = near_ref[pl.ds(block, NEAR, stride=6), :]
        table_ref[block * 128 : block * 128 + 128, :] = jnp.concatenate([rows, blank, rows, blank]).T
    at = TAPS + 3 - 640
    energy_ref[...] = jnp.broadcast_to(rows[:, at : at + 1] * (1.0 / filter_half), (NEAR, S))

    shape = (8, 128)
    sub = lax.broadcasted_iota(jnp.int32, shape, 0)
    lane = lax.broadcasted_iota(jnp.int32, shape, 1)
    first_lanes = lane < 64
    sites = [jnp.broadcast_to(table_ref[TAPS + d : TAPS + d + 1, :], shape).astype(jnp.int32) for d in range(3)]
    px = sites[0] - corner_ref[0]
    py = sites[1] - corner_ref[1]
    pz = (sites[2] & 15) + (((lane & 63) >> 4) - 1) * C
    zero = jnp.zeros(shape, F32)

    dz = sub + (lane >> 6) * 8 - pz + R
    z_masks = [dz == t for t in range(W)]
    z_factors = [tap_weight(jnp.abs(dz - t)) for t in range(W)]

    def place_z(ij, _):
        acc = zero
        along = zero
        for t in range(W):
            row = jnp.broadcast_to(table_ref[pl.ds(ij * W + t, 1), :], shape)
            acc = jnp.where(z_masks[t], row, acc)
            along = along + z_factors[t] * row
        a1_ref[ij] = acc
        a1z_ref[ij] = along
        return 0

    lax.fori_loop(0, W * W, place_z, 0, unroll=3)

    def place_y(y, _):
        masks, factors = ring_tables(y - py + R)
        for i in range(W):
            acc = zero
            along = zero
            moved = zero
            for t in range(W):
                value = a1_ref[i * W + t]
                acc = jnp.where(masks[t], value, acc)
                along = along + factors[t] * value
                moved = jnp.where(masks[t], a1z_ref[i * W + t], moved)
            a2_ref[i, y] = acc
            a2s_ref[i, y] = along + moved
        return 0

    lax.fori_loop(0, C, place_y, 0)

    def place_x(x, _):
        masks, factors = ring_tables(x - px + R)

        def per_y(y, _):
            row = pl.multiple_of(x * ROWS + y * C, C)
            acc = zero
            along = zero
            moved = zero
            for t in range(W):
                value = a2_ref[t, y]
                acc = jnp.where(masks[t], value, acc)
                along = along + factors[t] * value
                moved = jnp.where(masks[t], a2s_ref[t, y], moved)
            v = vb_ref[pl.ds(row, C), :]
            moved = along + moved + jnp.where(first_lanes, v[:8], v[8:]) * acc
            lower = jnp.where(first_lanes, acc, pltpu.roll(moved, 64, 1))
            upper = jnp.where(first_lanes, pltpu.roll(acc, 64, 1), moved)
            high, low = split(jnp.concatenate([lower, upper], axis=0))
            gg_ref[0, pl.ds(row, C), :] = high
            gg_ref[1, pl.ds(row, C), :] = low
            return 0

        lax.fori_loop(0, C, per_y, 0, unroll=16)
        return 0

    lax.fori_loop(0, C, place_x, 0)

    coef_ref[...] = jnp.zeros((3, NEAR, S), F32)

    def contract(x, _):
        rows = pl.ds(pl.multiple_of(x * 2 * ROWS, ROWS), 2 * ROWS)
        g_high, g_low = gg_ref[0, rows, :], gg_ref[1, rows, :]
        t_high, t_low = g_high.T, g_low.T
        high, low = split(s_ref[rows, :])
        got = mm(t_high, high) + (mm(t_high, low) + mm(t_low, high))
        t_high, t_low = t_high[:NEAR], t_low[:NEAR]
        pair = mm(t_high, g_high) + (mm(t_high, g_low) + mm(t_low, g_high))
        for slab in range(3):
            rows = slice(slab * C, slab * C + C)
            coef_ref[slab, 0:16] += got[rows]
            coef_ref[slab, 16:32] += got[64 + slab * C : 80 + slab * C]
            coef_ref[slab, 32:48] += pair[rows]
        return 0

    lax.fori_loop(0, C // 2, contract, 0, unroll=2)


def prep(parcels, corner, vb, s):
    vmem = pl.BlockSpec(memory_space=pltpu.VMEM)
    return pl.pallas_call(
        prep_kernel,
        in_specs=[vmem] * 4 + [pl.BlockSpec(memory_space=pltpu.SMEM), vmem, vmem],
        out_shape=[sds((2, CELLS, S), BF16), sds((3, NEAR, S)), sds((NEAR, S))],
        scratch_shapes=[
            pltpu.VMEM((288, 128), F32),
            pltpu.VMEM((768, 128), F32),
            pltpu.VMEM((W * W, 8, 128), F32),
            pltpu.VMEM((W * W, 8, 128), F32),
            pltpu.VMEM((W, C, 8, 128), F32),
            pltpu.VMEM((W, C, 8, 128), F32),
        ],
        compiler_params=params(16),
        cost_estimate=cost(1 << 27, 10 << 20),
        name="prep",
    )(*parcels, corner, vb, s.reshape(CELLS, S))


def move_pair(shares, away):
    lane = lax.broadcasted_iota(jnp.int32, (16, 128), 1)
    keep = (lane < 32) if away < 0 else (lane >= 16) & (lane < 48)
    pair = jnp.where(keep, pltpu.roll(shares[32:48], (away * 16) % 128, 1), 0.0)
    return jnp.concatenate([shares[0:32], pair])


def first_planes(s_ref, side_ref, vb_ref, edge_ref, q_ref, mix_ref, head_ref, tail_ref):
    for p in range(N):
        for half in range(2):
            ring = {y: s_ref[p, halves(y, half), :] for y in range(C)}
            for y in range(H):
                ring[C + y] = edge_ref[p, halves(y, half), :]
                ring[y - H] = edge_ref[p, halves(H + y, half), :]
            for y in range(C):
                rows = halves(y, half)
                dy = tap_sum(lambda i: ring[i], y)
                q = dy + vb_ref[p, rows, :] * ring[y]
                q_ref[p, rows, :] = q
                mix_ref[p, rows, :] = side_ref[p, rows, :] + q + dy
        for z in range(H):
            rows = halo_rows(pl.program_id(0) * N + p, z)
            head_ref[rows, :] = mix_ref[p, stride_rows(z), :]
            tail_ref[rows, :] = mix_ref[p, stride_rows(C - H + z), :]


def half_spec(start):
    return pl.BlockSpec((N, ROWS, S), lambda i: (i + start // N, 0, 0))


def first_half(s, side_part, vb, edge):
    return pl.pallas_call(
        first_planes,
        grid=(FIRST // N,),
        in_specs=[half_spec(0)] * 3 + [edge_spec(0, FIRST)],
        out_specs=[half_spec(0)] * 2 + [whole(HALO_ROWS)] * 2,
        out_shape=[FULL, FULL, sds((HALO_ROWS, S)), sds((HALO_ROWS, S))],
        compiler_params=params(16),
        cost_estimate=cost(1 << 23, 7 << 20),
        name="first_half",
    )(s, side_part, vb, edge)


def other_half_kernel(s_ref, side_ref, vb_ref, edge_ref, relay_ref, inner_ref, part_ref, mate_ref, _, __, *out):
    q_ref, mix_ref, head_ref, tail_ref = out

    @pl.when(pl.program_id(0) == 0)
    def _():
        for j in range(2):
            rows = slice(HALO_ROWS + j * NEAR, HALO_ROWS + (j + 1) * NEAR)
            head_ref[rows, :] = part_ref[j] + mate_ref[j]
            tail_ref[rows, :] = part_ref[j + 1] + mate_ref[j + 1]

    direct = (inner_ref[0] == 1) | (pl.program_id(0) < (MIDDLE - FIRST) // N)

    @pl.when(direct)
    def _():
        first_planes(s_ref, side_ref, vb_ref, edge_ref, *out)

    @pl.when(jnp.logical_not(direct))
    def _():
        first_planes(s_ref, side_ref, vb_ref, relay_ref, *out)


def other_half(s, side_part, vb, message, relayed, inner, part, part_mate, q, mix):
    shares = pl.BlockSpec((3, NEAR, S), lambda i: (0, 0, 0))
    anywhere = pl.BlockSpec(memory_space=pl.ANY)
    relay_spec = pl.BlockSpec((N, EDGE, S), lambda i: (jnp.maximum(i - (MIDDLE - FIRST) // N, 0), 0, 0))
    return pl.pallas_call(
        other_half_kernel,
        grid=((C - FIRST) // N,),
        in_specs=[half_spec(FIRST)] * 3
        + [pl.BlockSpec((N, EDGE, S), lambda i: (i, 0, 0)), relay_spec, SCALARS, shares, shares, anywhere, anywhere],
        out_specs=[half_spec(FIRST)] * 2 + [whole(HALO_ROWS + SHARES)] * 2,
        out_shape=[FULL, FULL, sds((HALO_ROWS + SHARES, S)), sds((HALO_ROWS + SHARES, S))],
        input_output_aliases={8: 0, 9: 1},
        compiler_params=params(16),
        cost_estimate=cost(1 << 23, 7 << 20),
        name="other_half",
    )(s, side_part, vb, message, relayed, inner, part, part_mate, q, mix)


def base_kernel(s_ref, mid_ref, vb_ref, vb_mate_ref, q_ref, side_ref, part_ref, *refs):
    inner_ref, message_ref, out_ref, middle_ref = refs[3:]
    step = pl.program_id(0)
    inner = inner_ref[0] == 1

    @pl.when(inner)
    def _():
        middle_ref[...] = mid_ref[...]

    @pl.when(jnp.logical_not(inner))
    def _():
        for p in range(N):
            middle_ref[p] = message_ref[pl.ds(pl.multiple_of(MID_START + (step * N + p) * MID, MID), MID), :]

    def planes(edge_ref):
        for p in range(N):
            for half in range(2):

                def other(y, p=p, half=half):
                    if y < H:
                        return edge_ref[p, halves(y, half), :]
                    if y < C - H:
                        return middle_ref[p, halves(y - H, half), :]
                    return edge_ref[p, halves(y - 4, half), :]

                ring = [s_ref[p, halves(y, half), :] for y in range(C)] + [other(y) for y in range(C)]
                q = {y: q_ref[p, halves(y, half), :] for y in range(C)}
                for y in list(range(H)) + list(range(C - H, C)):
                    v = vb_mate_ref[p, halves(y, half), :]
                    q[C + y] = tap_sum(lambda i: ring[i % 32], C + y) + v * ring[C + y]
                for y in range(C):
                    rows = halves(y, half)
                    total = tap_sum(lambda i: q[i % 32], y)
                    total = total + vb_ref[p, rows, :] * (side_ref[p, rows, :] + q[y])
                    out_ref[p, rows, :] = 2.0 * (total + part_ref[p, rows, :]) - ring[y]

    for_piece(refs[:3], inner_ref, planes)


def make_base(s, mid, vb, vb_mate, q, side_part, part, edges, inner):
    return pl.pallas_call(
        base_kernel,
        grid=(C // N,),
        in_specs=[plane_spec(ROWS, N), plane_spec(MID, N)]
        + [plane_spec(ROWS, N)] * 5
        + edge_specs()
        + [SCALARS, whole((C - FIRST) * EDGE)],
        out_specs=plane_spec(ROWS, N),
        out_shape=FULL,
        scratch_shapes=[pltpu.VMEM((N, MID, S), F32)],
        compiler_params=params(16),
        cost_estimate=cost(1 << 25, 16 << 20),
        name="base",
    )(s, mid, vb, vb_mate, q, side_part, part, *edges, inner, edges[1].reshape(-1, S))


def second_kernel(base_ref, low_one_ref, high_one_ref, low_ref, high_ref, gg_high_ref, gg_low_ref, *rest):
    part_ref, mate_ref, energy_ref, upper_ref, second_ref, keep_ref, give_ref, gram_ref, cross_ref, w_ref, halo_ref = rest
    step = pl.program_id(0)

    @pl.when(step == 0)
    def _():
        gram_ref[...] = jnp.zeros((S, S), F32)
        cross_ref[...] = jnp.zeros((S, S), F32)
        w_ref[...] = jnp.zeros((S, S), F32)
        halo_ref[...] = jnp.zeros((B, ROWS, S), F32)
        mine = [part_ref[j] + mate_ref[j] for j in range(3)]
        below = [move_pair(low_ref[HALO_ROWS + j * NEAR : HALO_ROWS + (j + 1) * NEAR, :], -1) for j in range(2)]
        above = [move_pair(high_ref[HALO_ROWS + j * NEAR : HALO_ROWS + (j + 1) * NEAR, :], 1) for j in range(2)]
        slabs = [mine[0] + below[0], mine[1] + below[1] + above[0], mine[2] + above[1]]
        near = jnp.concatenate([slab[0:16] for slab in slabs]) * energy_ref[...]
        lane = lax.broadcasted_iota(jnp.int32, (NEAR, S), 1)
        pair = jnp.where(lane < NEAR, jnp.concatenate([slab[32:48] for slab in slabs]), 0.0)
        two = jnp.concatenate([slab[16:32] for slab in slabs])
        two = two + exact(pair, jnp.concatenate([near, jnp.zeros((S - NEAR, S), F32)]))
        w_ref[0:NEAR, :] = 2.0 * energy_ref[...] * two
        w_ref[64 : 64 + NEAR, :] = 2.0 * near

    def halo_part(below_ref, above_ref, first_plane):
        for p in range(B):
            low = [below_ref[halo_rows(step * B + p - first_plane, j), :] for j in range(H)]
            high = [above_ref[halo_rows(step * B + p - first_plane, j), :] for j in range(H)]
            for z in range(H):
                add = sum((2.0 * OFF[k - 1]) * low[z - k + H] for k in range(z + 1, H + 1))
                halo_ref[p, stride_rows(z), :] = add
                add = sum((2.0 * OFF[H + j - z - 1]) * high[j] for j in range(z + 1))
                halo_ref[p, stride_rows(C - H + z), :] = add

    @pl.when(step < FIRST // B)
    def _():
        halo_part(low_one_ref, high_one_ref, 0)

    @pl.when(step >= FIRST // B)
    def _():
        halo_part(low_ref, high_ref, FIRST)

    w_high, w_low = split(w_ref[...])
    gram = jnp.zeros((S, S), F32)
    cross = jnp.zeros((S, S), F32)
    for p in range(B):
        g_high, g_low = gg_high_ref[0, p], gg_low_ref[0, p]
        value = base_ref[p] + halo_ref[p] + (mm(g_high, w_high) + (mm(g_high, w_low) + mm(g_low, w_high)))
        second_ref[p] = value
        s_high, s_low = split(value)
        turned = s_high.T
        gram += mm(turned, s_high)
        cross += mm(turned, s_low)
    gram_ref[...] += gram
    cross_ref[...] += cross

    @pl.when(step == STEPS - 1)
    def _():
        cross = cross_ref[...]
        gram = (gram_ref[...] + (cross + cross.T)) * (1.0 / NCELLS)
        upper = upper_ref[0] == 1
        keep_ref[...] = jnp.where(upper, gram[S // 2 :], gram[: S // 2])
        give_ref[...] = jnp.where(upper, gram[: S // 2], gram[S // 2 :])


def make_second(base, halos, gg, shares, upper):
    three = pl.BlockSpec((3, NEAR, S), lambda i: (0, 0, 0))
    return pl.pallas_call(
        second_kernel,
        grid=(STEPS,),
        in_specs=[plane_spec()]
        + [whole(HALO_ROWS)] * 2
        + [whole(HALO_ROWS + SHARES)] * 2
        + [part_spec(0), part_spec(1), three, three, whole(NEAR), SCALARS],
        out_specs=[plane_spec(), whole(S // 2), whole(S // 2)],
        out_shape=[FULL, sds((S // 2, S)), sds((S // 2, S))],
        scratch_shapes=[pltpu.VMEM((S, S), F32)] * 3 + [pltpu.VMEM((B, ROWS, S), F32)],
        compiler_params=params(16),
        cost_estimate=cost(1 << 27, 8 << 20),
        name="second",
    )(base, *halos, gg, gg, *shares, upper)


def exact(a, b):
    return jnp.dot(a, b, precision=lax.Precision.HIGHEST, preferred_element_type=F32)


def inverse_factor(gram_ref, a_ref, x_ref, state_ref):
    row = lax.broadcasted_iota(jnp.int32, (S, S), 0)
    column = lax.broadcasted_iota(jnp.int32, (S, S), 1)
    unit = jnp.where(row == column, 1.0, 0.0)
    gram = gram_ref[...]
    diagonal = jnp.where(row == column, gram, 0.0)
    down = lax.rsqrt(jnp.sum(diagonal, axis=1, keepdims=True))
    across = lax.rsqrt(jnp.sum(diagonal, axis=0, keepdims=True))
    a_ref[...] = gram * down * across
    x_ref[...] = unit

    def residual():
        x = x_ref[...]
        return unit - exact(exact(x, a_ref[...]), x.T)

    def size(e):
        return jnp.sum(e * e)

    def improve(e):
        lower = jnp.where(row > column, e, jnp.where(row == column, 0.5 * e, 0.0))
        x_ref[...] += exact(lower, x_ref[...])

    state_ref[0] = 0
    start = unit - a_ref[...]
    start_size = size(start)

    @pl.when(start_size < 0.16)
    def _():
        improve(start)
        state_ref[0] = jnp.where(start_size < 1e-6, 2, 1)

    for _ in range(5):

        @pl.when(state_ref[0] == 1)
        def _():
            e = residual()
            e_size = size(e)
            improve(e)
            state_ref[0] = jnp.where(e_size < 1e-6, 2, 1)

    @pl.when(state_ref[0] != 2)
    def _():
        x_ref[...] = unit
        lanes = lax.broadcasted_iota(jnp.int32, (1, S), 1)

        def step(j, _):
            line = a_ref[pl.ds(j, 1), :]
            scale = lax.rsqrt(jnp.sum(jnp.where(lanes == j, line, 0.0), axis=1, keepdims=True))
            a = a_ref[...]
            factor = jnp.sum(jnp.where(column == j, a, 0.0), axis=1, keepdims=True) * scale
            factor = jnp.where(row[:, :1] > j, factor, 0.0)
            x_line = x_ref[pl.ds(j, 1), :] * scale
            a_ref[...] = a - factor * (line * scale)
            x_ref[...] = jnp.where(row == j, x_line, x_ref[...] - factor * x_line)
            return 0

        lax.fori_loop(0, S, step, 0)

    x_ref[...] = x_ref[...] * across


def turn_kernel(second_ref, own_ref, other_ref, upper_ref, out_ref, gram_ref, a_ref, x_ref, i_high_ref, i_low_ref, state_ref):
    @pl.when(pl.program_id(0) == 0)
    def _():
        upper = upper_ref[0] == 1
        gram_ref[: S // 2, :] = jnp.where(upper, other_ref[...], own_ref[...])
        gram_ref[S // 2 :, :] = jnp.where(upper, own_ref[...], other_ref[...])
        inverse_factor(gram_ref, a_ref, x_ref, state_ref)
        i_high, i_low = split(x_ref[...].T)
        i_high_ref[...] = i_high
        i_low_ref[...] = i_low

    i_high, i_low = i_high_ref[...], i_low_ref[...]

    for p in range(B):
        high, low = split(second_ref[p])
        out_ref[p] = mm(high, i_high) + (mm(high, i_low) + mm(low, i_high))


def turn(second, own, other, upper):
    return pl.pallas_call(
        turn_kernel,
        grid=(STEPS,),
        in_specs=[plane_spec(), whole(S // 2), whole(S // 2), SCALARS],
        out_specs=plane_spec(),
        out_shape=FULL,
        scratch_shapes=[pltpu.VMEM((S, S), F32)] * 3 + [pltpu.VMEM((S, S), BF16)] * 2 + [pltpu.SMEM((1,), jnp.int32)],
        compiler_params=params(16),
        cost_estimate=cost(1 << 28, 4 << 20),
        name="turn",
    )(second, own, other, upper)


def per_device(states, potential, atom_sites, projectors, energies):
    gx, gy = lax.axis_index("gx"), lax.axis_index("gy")
    depth = lax.axis_size("gzs")
    count = 4 * depth
    barrier = lax.optimization_barrier

    def send(value, flip=0, move=0):
        def target(d):
            return (d // depth * depth ^ flip) + (d + move) % depth

        return lax.ppermute(value, AXES, [(d, target(d)) for d in range(count)])

    over_x, over_y = 2 * depth, depth
    inner_ones = [d for d in range(count) if d % 4 in (1, 2)]
    outer_ones = [d for d in range(count) if d % 4 in (0, 3)]
    inner = ((lax.axis_index("gzs") + 1) // 2 % 2).astype(jnp.int32).reshape(1)
    s = states.reshape(C, ROWS, S)
    pot = potential.reshape(32, 128)

    atoms = jnp.concatenate(
        [projectors.reshape(4, TAPS), atom_sites.astype(F32), energies[:, None], jnp.zeros((4, 768 - TAPS - 4), F32)],
        axis=1,
    ).reshape(24, 128)
    mate = send(s, over_x)
    below, above = send(atoms, 0, 1), send(atoms, 0, -1)
    one_edge, head, tail = pack(s)
    one_edge = send(one_edge, over_y)
    head, tail, below, above = barrier((head, tail, below, above))
    parcel = stack(below, atoms, above, pot)
    parcel_y = send(parcel, over_y)
    parcel_x = send(parcel, over_x)
    low, high = send(tail, 0, 1), send(head, 0, -1)
    message, relay, mid = pack_rest(s, inner)
    vb = spread(parcel)
    beside = side_x(s, mate)
    parcel_y, one_edge, message, relay, beside = barrier((parcel_y, one_edge, message, relay, beside))
    relayed = lax.ppermute(relay, AXES, [(d, d ^ over_y ^ 1) for d in outer_ones])
    message = send(message, over_y)
    parcel_xy = send(parcel_y, over_x)
    corner = jnp.stack([gx * C, gy * C]).astype(jnp.int32)
    upper = gx.astype(jnp.int32).reshape(1)
    planes = vb.reshape(C, ROWS, S)
    side_part = side_z(s, beside, low, high)
    q, mix, head, tail = first_half(s, side_part, planes, one_edge)
    low_one, high_one = send(tail, 0, 1), send(head, 0, -1)
    parcel_xy, head, tail, relayed = barrier((parcel_xy, head, tail, relayed))
    relayed = lax.ppermute(relayed, AXES, [(d, d ^ 1) for d in inner_ones])
    gg, part, energy = prep([parcel, parcel_x, parcel_y, parcel_xy], corner, vb, s)

    part = part + send(part, over_x)
    part_mate = send(part, over_y)
    part_mate, low_one, high_one = barrier((part_mate, low_one, high_one))
    message = message.reshape(C - FIRST, EDGE, S)
    q, mix, head, tail = other_half(s, side_part, planes, message, relayed, inner, part, part_mate, q, mix)
    halos = [low_one, high_one, send(tail, 0, 1), send(head, 0, -1)]
    mate = send(mix, over_x)
    mid, part_mate = barrier((mid, part_mate))
    mid = lax.ppermute(mid, AXES, [(d, d ^ over_y) for d in inner_ones])
    planes_mate = spread(parcel_y).reshape(C, ROWS, S)
    part_two = side_again(mix, mate)
    base = make_base(s, mid, planes, planes_mate, q, side_part, part_two, [one_edge, message, relayed], inner)
    gg = gg.reshape(2, C, ROWS, S)
    second, own, give = make_second(base, halos, gg, [part, part_mate, energy], upper)

    own = own + send(give, over_x)
    for flip in (32, 36, 1, 3, 8, 24):
        own = own + lax.ppermute(own, AXES, [(d, d ^ flip) for d in range(count)])
    return turn(second, own, send(own, over_x), upper).reshape(C, C, C, S)


def solution(mesh):
    return jax.shard_map(
        per_device,
        mesh=mesh,
        in_specs=(
            P("gx", "gy", "gzs", None),
            P("gx", "gy", "gzs"),
            P(("gx", "gy", "gzs"), None),
            P(("gx", "gy", "gzs"), None, None, None),
            P(("gx", "gy", "gzs")),
        ),
        out_specs=P("gx", "gy", "gzs", None),
        check_vma=False,
    )
```

```python
import math

import jax
import jax.numpy as jnp
from jax import lax
from jax.experimental import pallas as pl
from jax.experimental.pallas import tpu as pltpu
from jax.sharding import PartitionSpec as P

AXES = ("gx", "gy", "gzs")
H = 6
C = 16
ROWS = C * C
CELLS = C * C * C
NCELLS = 32 * 32 * 512
S = 128
W = 9
R = 4
NEAR = 48
TAPS = W * W * W
F32 = jnp.float32
BF16 = jnp.bfloat16

grid_step = 0.6
filter_centre = 36.0
filter_half = 26.0


def weights():
    taps = []
    for k in range(1, 7):
        top = 2.0 * (-1) ** (k + 1) * math.factorial(6) ** 2
        under = k * k * math.factorial(6 - k) * math.factorial(6 + k)
        taps.append(top / under)
    scale = -0.5 / (grid_step * grid_step)
    off = [scale * t / filter_half for t in taps]
    diagonal = 3.0 * scale * (-2.0 * sum(taps))
    return off, diagonal


OFF, DIAGONAL = weights()


def params(mib):
    return pltpu.CompilerParams(vmem_limit_bytes=mib * 1024 * 1024)


def cost(flops, nbytes):
    return pl.CostEstimate(flops=flops, bytes_accessed=nbytes, transcendentals=0)


def sds(shape, dtype=F32):
    return jax.ShapeDtypeStruct(shape, dtype)


def split(value):
    high = value.astype(BF16)
    low = (value - high.astype(F32)).astype(BF16)
    return high, low


def mm(a, b):
    return jnp.dot(a, b, preferred_element_type=F32)


def tap_sum(at, index):
    total = None
    for k in range(1, 7):
        term = OFF[k - 1] * (at(index + k) + at(index - k))
        total = term if total is None else total + term
    return total


B = 4
STEPS = C // B
N = 2
FIRST = 8
MIDDLE = 10
EDGE = 192
MID = 64
MID_START = (MIDDLE - FIRST) * EDGE


def stride_rows(z):
    return pl.ds(z, C, stride=C)


def plane_spec(rows=ROWS, planes=B):
    return pl.BlockSpec((planes, rows, S), lambda i: (i, 0, 0))


def halo_spec(planes=B):
    return pl.BlockSpec((H, planes, C, S), lambda i: (0, i, 0, 0))


def part_spec(part):
    return pl.BlockSpec((1, B, ROWS, S), lambda i: (part, i, 0, 0))


def whole(rows=S):
    return pl.BlockSpec((rows, S), lambda i: (0, 0))


def edge_spec(start, stop):
    return pl.BlockSpec((N, EDGE, S), lambda i: (jnp.clip(i - start // N, 0, (stop - start) // N - 1), 0, 0))


def edge_specs():
    return [edge_spec(0, FIRST), edge_spec(FIRST, C), edge_spec(MIDDLE, C)]


def for_piece(edges, inner_ref, body):
    step = pl.program_id(0)
    direct = (inner_ref[0] == 1) | (step < MIDDLE // N)

    @pl.when(step < FIRST // N)
    def _():
        body(edges[0])

    @pl.when((step >= FIRST // N) & direct)
    def _():
        body(edges[1])

    @pl.when(jnp.logical_not(direct))
    def _():
        body(edges[2])


SCALARS = pl.BlockSpec(memory_space=pltpu.SMEM)
FULL = sds((C, ROWS, S))
FULL_ROWS = sds((CELLS, S))
HALO_ROWS = H * FIRST * C
SHARES = 2 * NEAR
HALO = sds((H, C, C, S))
EDGES = [sds((FIRST, EDGE, S)), sds((C - FIRST, EDGE, S)), sds((C - MIDDLE, EDGE, S))]


def halo_rows(x, z):
    return pl.ds(pl.multiple_of(z * FIRST * C + x * C, C), C)


def halves(y, half):
    return slice(y * C + half * 8, y * C + half * 8 + 8)


def pack_edges(s_ref, out_ref):
    out_ref[:, 0:96, :] = s_ref[:, 0:96, :]
    out_ref[:, 96:192, :] = s_ref[:, 160:256, :]


def pack_kernel(s_ref, edge_ref, head_ref, tail_ref):
    @pl.when(pl.program_id(0) < FIRST // N)
    def _():
        pack_edges(s_ref, edge_ref)

    for p in range(N):
        for z in range(H):
            head_ref[z, p] = s_ref[p, stride_rows(z), :]
            tail_ref[z, p] = s_ref[p, stride_rows(C - H + z), :]


def pack(s):
    return pl.pallas_call(
        pack_kernel,
        grid=(C // N,),
        in_specs=[plane_spec(ROWS, N)],
        out_specs=edge_specs()[:1] + [halo_spec(N), halo_spec(N)],
        out_shape=EDGES[:1] + [HALO, HALO],
        compiler_params=params(12),
        cost_estimate=cost(1 << 32, 6 << 20),
        name="pack",
    )(s)


def pack_rest_kernel(s_ref, inner_ref, message_ref, relay_ref, mid_ref):
    step = pl.program_id(0)
    inner = inner_ref[0] == 1
    mid_ref[...] = s_ref[:, 96:160, :]

    @pl.when(step >= MIDDLE // N)
    def _():
        pack_edges(s_ref, relay_ref)

    @pl.when((step >= FIRST // N) & (inner | (step < MIDDLE // N)))
    def _():
        for p in range(N):
            row = pl.multiple_of((step * N + p - FIRST) * EDGE, MID)
            message_ref[pl.ds(row, 96), :] = s_ref[p, 0:96, :]
            message_ref[pl.ds(row + 96, 96), :] = s_ref[p, 160:256, :]

    @pl.when(jnp.logical_not(inner))
    def _():
        for p in range(N):
            row = pl.multiple_of(MID_START + (step * N + p) * MID, MID)
            message_ref[pl.ds(row, MID), :] = s_ref[p, 96:160, :]


def pack_rest(s, inner):
    rows = (C - FIRST) * EDGE
    message, relay, mid = pl.pallas_call(
        pack_rest_kernel,
        grid=(C // N,),
        in_specs=[plane_spec(ROWS, N), SCALARS],
        out_specs=[whole(rows), edge_spec(MIDDLE, C), plane_spec(MID, N)],
        out_shape=[sds((rows, S)), EDGES[2], sds((C, MID, S))],
        compiler_params=params(12),
        cost_estimate=cost(1 << 31, 4 << 20),
        name="pack_rest",
    )(s, inner)
    return message, relay, mid


def stack(*pieces):
    def kernel(*refs):
        start = 0
        for ref, (_, rows) in zip(refs, pieces):
            refs[-1][start : start + rows, :] = ref[:rows, :]
            start += rows

    arrays = [array for array, _ in pieces]
    rows = sum(rows for _, rows in pieces)
    return pl.pallas_call(kernel, out_shape=sds((rows, S)), compiler_params=params(4), name="stack")(*arrays)


def along_x(s_ref, mate_ref, out_ref, add):
    def column(block, _):
        rows = pl.ds(pl.multiple_of(block * 8, 8), 8)
        ring = [mate_ref[C - H + i, rows, :] for i in range(H)]
        ring += [s_ref[x, rows, :] for x in range(C)]
        ring += [mate_ref[i, rows, :] for i in range(H)]
        for x in range(C):
            value = tap_sum(lambda i: ring[H + i], x)
            if add:
                value = value + out_ref[x, rows, :]
            out_ref[x, rows, :] = value
        return 0

    lax.fori_loop(0, ROWS // 8, column, 0)


def z_taps(ext_ref, y):
    return tap_sum(lambda k: ext_ref[y * 32 + 8 + k : y * 32 + 24 + k, :], 0)


def side_x_kernel(s_ref, mate_ref, out_ref):
    along_x(s_ref, mate_ref, out_ref, False)


def side_x(s, mate):
    return pl.pallas_call(
        side_x_kernel,
        out_shape=FULL,
        compiler_params=params(12),
        cost_estimate=cost(1 << 24, 6 << 20),
        name="side_x",
    )(s, mate)


def side_z_kernel(s_ref, part_ref, low_ref, high_ref, out_ref, ext_ref):
    def plane(x, _):
        for y in range(C):
            ext_ref[y * 32 + 8 : y * 32 + 24, :] = s_ref[x, y * C : (y + 1) * C, :]
        for z in range(H):
            ext_ref[pl.ds(2 + z, C, stride=32), :] = low_ref[z, x]
            ext_ref[pl.ds(24 + z, C, stride=32), :] = high_ref[z, x]
        for y in range(C):
            rows = slice(y * C, (y + 1) * C)
            out_ref[x, rows, :] = part_ref[x, rows, :] + z_taps(ext_ref, y)
        return 0

    lax.fori_loop(0, C, plane, 0)


def side_z(s, part, low, high):
    return pl.pallas_call(
        side_z_kernel,
        out_shape=FULL,
        scratch_shapes=[pltpu.VMEM((C * 32, S), F32)],
        compiler_params=params(14),
        cost_estimate=cost(1 << 24, 8 << 20),
        name="side_z",
    )(s, part, low, high)


def side_again_kernel(s_ref, mate_ref, out_ref, ext_ref):
    for y in range(C):
        ext_ref[y * 32 : y * 32 + 8, :] = jnp.zeros((8, S), F32)
        ext_ref[y * 32 + 24 : y * 32 + 32, :] = jnp.zeros((8, S), F32)

    def plane(x, _):
        for y in range(C):
            ext_ref[y * 32 + 8 : y * 32 + 24, :] = s_ref[x, y * C : (y + 1) * C, :]
        for y in range(C):
            out_ref[x, y * C : (y + 1) * C, :] = z_taps(ext_ref, y)
        return 0

    lax.fori_loop(0, C, plane, 0)
    along_x(s_ref, mate_ref, out_ref, True)


def side_again(s, mate):
    return pl.pallas_call(
        side_again_kernel,
        out_shape=FULL,
        scratch_shapes=[pltpu.VMEM((C * 32, S), F32)],
        compiler_params=params(12),
        cost_estimate=cost(1 << 25, 6 << 20),
        name="side_again",
    )(s, mate)


def tap_weight(distance):
    value = jnp.zeros(distance.shape, F32)
    for k in range(1, 7):
        value = jnp.where(distance == k, OFF[k - 1], value)
    return value


def ring_tables(coordinate):
    masks, factors = [], []
    for t in range(W):
        away = (coordinate - t) & 31
        masks.append(away == 0)
        factors.append(tap_weight(jnp.minimum(away, 32 - away)))
    return masks, factors


def spread_kernel(parcel_ref, vb_ref):
    def spread_row(row, _):
        line = (parcel_ref[pl.ds(24 + row, 1), :] + (DIAGONAL - filter_centre)) * (1.0 / filter_half)
        start = pl.multiple_of(row * 128, 128)
        vb_ref[pl.ds(start, 128), :] = jnp.broadcast_to(line, (128, 128)).T
        return 0

    lax.fori_loop(0, CELLS // 128, spread_row, 0, unroll=8)


def spread(parcel):
    return pl.pallas_call(
        spread_kernel,
        out_shape=FULL_ROWS,
        compiler_params=params(8),
        cost_estimate=cost(1 << 20, 2 << 20),
        name="spread",
    )(parcel)


def prep_kernel(*refs):
    own_ref, other_ref, corner_ref, vb_ref, s_ref, gg_ref, coef_ref, energy_ref, near_ref, table_ref = refs[:10]
    a1_ref, a1z_ref, a2_ref, a2s_ref = refs[10:]
    upper_x, upper_y = corner_ref[0] > 0, corner_ref[1] > 0
    for slab in range(3):
        own = [own_ref[slab * 48 + j * 24 : slab * 48 + j * 24 + 24, :] for j in range(2)]
        other = [other_ref[slab * 48 + j * 24 : slab * 48 + j * 24 + 24, :] for j in range(2)]
        lower = [jnp.where(upper_x, o, m) for m, o in zip(own, other)]
        higher = [jnp.where(upper_x, m, o) for m, o in zip(own, other)]
        ordered = []
        for pair in (lower, higher):
            ordered += [jnp.where(upper_y, pair[1], pair[0]), jnp.where(upper_y, pair[0], pair[1])]
        for j in range(4):
            near_ref[slab * 96 + j * 24 : slab * 96 + j * 24 + 24, :] = ordered[j]
    blank = jnp.zeros((16, 128), F32)
    for block in range(6):
        rows = near_ref[pl.ds(block, NEAR, stride=6), :]
        table_ref[block * 128 : block * 128 + 128, :] = jnp.concatenate([rows, blank, rows, blank]).T
    at = TAPS + 3 - 640
    energy_ref[...] = jnp.broadcast_to(rows[:, at : at + 1] * (1.0 / filter_half), (NEAR, S))

    shape = (8, 128)
    sub = lax.broadcasted_iota(jnp.int32, shape, 0)
    lane = lax.broadcasted_iota(jnp.int32, shape, 1)
    first_lanes = lane < 64
    sites = [jnp.broadcast_to(table_ref[TAPS + d : TAPS + d + 1, :], shape).astype(jnp.int32) for d in range(3)]
    px = sites[0] - corner_ref[0]
    py = sites[1] - corner_ref[1]
    pz = (sites[2] & 15) + (((lane & 63) >> 4) - 1) * C
    zero = jnp.zeros(shape, F32)

    dz = sub + (lane >> 6) * 8 - pz + R
    z_masks = [dz == t for t in range(W)]
    z_factors = [tap_weight(jnp.abs(dz - t)) for t in range(W)]

    def place_z(ij, _):
        acc = zero
        along = zero
        for t in range(W):
            row = jnp.broadcast_to(table_ref[pl.ds(ij * W + t, 1), :], shape)
            acc = jnp.where(z_masks[t], row, acc)
            along = along + z_factors[t] * row
        a1_ref[ij] = acc
        a1z_ref[ij] = along
        return 0

    lax.fori_loop(0, W * W, place_z, 0, unroll=3)

    def place_y(y, _):
        masks, factors = ring_tables(y - py + R)
        for i in range(W):
            acc = zero
            along = zero
            moved = zero
            for t in range(W):
                value = a1_ref[i * W + t]
                acc = jnp.where(masks[t], value, acc)
                along = along + factors[t] * value
                moved = jnp.where(masks[t], a1z_ref[i * W + t], moved)
            a2_ref[i, y] = acc
            a2s_ref[i, y] = along + moved
        return 0

    lax.fori_loop(0, C, place_y, 0)

    def place_x(x, _):
        masks, factors = ring_tables(x - px + R)

        def per_y(y, _):
            row = pl.multiple_of(x * ROWS + y * C, C)
            acc = zero
            along = zero
            moved = zero
            for t in range(W):
                value = a2_ref[t, y]
                acc = jnp.where(masks[t], value, acc)
                along = along + factors[t] * value
                moved = jnp.where(masks[t], a2s_ref[t, y], moved)
            v = vb_ref[pl.ds(row, C), :]
            moved = along + moved + jnp.where(first_lanes, v[:8], v[8:]) * acc
            lower = jnp.where(first_lanes, acc, pltpu.roll(moved, 64, 1))
            upper = jnp.where(first_lanes, pltpu.roll(acc, 64, 1), moved)
            high, low = split(jnp.concatenate([lower, upper], axis=0))
            gg_ref[0, pl.ds(row, C), :] = high
            gg_ref[1, pl.ds(row, C), :] = low
            return 0

        lax.fori_loop(0, C, per_y, 0, unroll=16)
        return 0

    lax.fori_loop(0, C, place_x, 0)

    coef_ref[...] = jnp.zeros((3, NEAR, S), F32)

    def contract(x, _):
        rows = pl.ds(pl.multiple_of(x * 2 * ROWS, ROWS), 2 * ROWS)
        g_high, g_low = gg_ref[0, rows, :], gg_ref[1, rows, :]
        t_high, t_low = g_high.T, g_low.T
        high, low = split(s_ref[rows, :])
        got = mm(t_high, high) + (mm(t_high, low) + mm(t_low, high))
        t_high, t_low = t_high[:NEAR], t_low[:NEAR]
        pair = mm(t_high, g_high) + (mm(t_high, g_low) + mm(t_low, g_high))
        for slab in range(3):
            rows = slice(slab * C, slab * C + C)
            coef_ref[slab, 0:16] += got[rows]
            coef_ref[slab, 16:32] += got[64 + slab * C : 80 + slab * C]
            coef_ref[slab, 32:48] += pair[rows]
        return 0

    lax.fori_loop(0, C // 2, contract, 0, unroll=2)


def prep(parcels, corner, vb, s):
    vmem = pl.BlockSpec(memory_space=pltpu.VMEM)
    return pl.pallas_call(
        prep_kernel,
        in_specs=[vmem] * 2 + [pl.BlockSpec(memory_space=pltpu.SMEM), vmem, vmem],
        out_shape=[sds((2, CELLS, S), BF16), sds((3, NEAR, S)), sds((NEAR, S))],
        scratch_shapes=[
            pltpu.VMEM((288, 128), F32),
            pltpu.VMEM((768, 128), F32),
            pltpu.VMEM((W * W, 8, 128), F32),
            pltpu.VMEM((W * W, 8, 128), F32),
            pltpu.VMEM((W, C, 8, 128), F32),
            pltpu.VMEM((W, C, 8, 128), F32),
        ],
        compiler_params=params(16),
        cost_estimate=cost(1 << 27, 10 << 20),
        name="prep",
    )(*parcels, corner, vb, s.reshape(CELLS, S))


def move_pair(shares, away):
    lane = lax.broadcasted_iota(jnp.int32, (16, 128), 1)
    keep = (lane < 32) if away < 0 else (lane >= 16) & (lane < 48)
    pair = jnp.where(keep, pltpu.roll(shares[32:48], (away * 16) % 128, 1), 0.0)
    return jnp.concatenate([shares[0:32], pair])


def first_planes(s_ref, side_ref, vb_ref, edge_ref, q_ref, mix_ref, head_ref, tail_ref):
    for p in range(N):
        for half in range(2):
            ring = {y: s_ref[p, halves(y, half), :] for y in range(C)}
            for y in range(H):
                ring[C + y] = edge_ref[p, halves(y, half), :]
                ring[y - H] = edge_ref[p, halves(H + y, half), :]
            for y in range(C):
                rows = halves(y, half)
                dy = tap_sum(lambda i: ring[i], y)
                q = dy + vb_ref[p, rows, :] * ring[y]
                q_ref[p, rows, :] = q
                mix_ref[p, rows, :] = side_ref[p, rows, :] + q + dy
        for z in range(H):
            rows = halo_rows(pl.program_id(0) * N + p, z)
            head_ref[rows, :] = mix_ref[p, stride_rows(z), :]
            tail_ref[rows, :] = mix_ref[p, stride_rows(C - H + z), :]


def half_spec(start):
    return pl.BlockSpec((N, ROWS, S), lambda i: (i + start // N, 0, 0))


def first_half(s, side_part, vb, edge):
    return pl.pallas_call(
        first_planes,
        grid=(FIRST // N,),
        in_specs=[half_spec(0)] * 3 + [edge_spec(0, FIRST)],
        out_specs=[half_spec(0)] * 2 + [whole(HALO_ROWS)] * 2,
        out_shape=[FULL, FULL, sds((HALO_ROWS, S)), sds((HALO_ROWS, S))],
        compiler_params=params(16),
        cost_estimate=cost(1 << 23, 7 << 20),
        name="first_half",
    )(s, side_part, vb, edge)


def other_half_kernel(s_ref, side_ref, vb_ref, edge_ref, relay_ref, inner_ref, part_ref, mate_ref, _, __, *out):
    q_ref, mix_ref, head_ref, tail_ref = out

    @pl.when(pl.program_id(0) == 0)
    def _():
        for j in range(2):
            rows = slice(HALO_ROWS + j * NEAR, HALO_ROWS + (j + 1) * NEAR)
            head_ref[rows, :] = part_ref[j] + mate_ref[j]
            tail_ref[rows, :] = part_ref[j + 1] + mate_ref[j + 1]

    direct = (inner_ref[0] == 1) | (pl.program_id(0) < (MIDDLE - FIRST) // N)

    @pl.when(direct)
    def _():
        first_planes(s_ref, side_ref, vb_ref, edge_ref, *out)

    @pl.when(jnp.logical_not(direct))
    def _():
        first_planes(s_ref, side_ref, vb_ref, relay_ref, *out)


def other_half(s, side_part, vb, message, relayed, inner, part, part_mate, q, mix):
    shares = pl.BlockSpec((3, NEAR, S), lambda i: (0, 0, 0))
    anywhere = pl.BlockSpec(memory_space=pl.ANY)
    relay_spec = pl.BlockSpec((N, EDGE, S), lambda i: (jnp.maximum(i - (MIDDLE - FIRST) // N, 0), 0, 0))
    return pl.pallas_call(
        other_half_kernel,
        grid=((C - FIRST) // N,),
        in_specs=[half_spec(FIRST)] * 3
        + [pl.BlockSpec((N, EDGE, S), lambda i: (i, 0, 0)), relay_spec, SCALARS, shares, shares, anywhere, anywhere],
        out_specs=[half_spec(FIRST)] * 2 + [whole(HALO_ROWS + SHARES)] * 2,
        out_shape=[FULL, FULL, sds((HALO_ROWS + SHARES, S)), sds((HALO_ROWS + SHARES, S))],
        input_output_aliases={8: 0, 9: 1},
        compiler_params=params(16),
        cost_estimate=cost(1 << 23, 7 << 20),
        name="other_half",
    )(s, side_part, vb, message, relayed, inner, part, part_mate, q, mix)


def base_kernel(s_ref, mid_ref, vb_ref, vb_mate_ref, q_ref, side_ref, part_ref, *refs):
    inner_ref, message_ref, out_ref, middle_ref = refs[3:]
    step = pl.program_id(0)
    inner = inner_ref[0] == 1

    @pl.when(inner)
    def _():
        middle_ref[...] = mid_ref[...]

    @pl.when(jnp.logical_not(inner))
    def _():
        for p in range(N):
            middle_ref[p] = message_ref[pl.ds(pl.multiple_of(MID_START + (step * N + p) * MID, MID), MID), :]

    def planes(edge_ref):
        for p in range(N):
            for half in range(2):

                def other(y, p=p, half=half):
                    if y < H:
                        return edge_ref[p, halves(y, half), :]
                    if y < C - H:
                        return middle_ref[p, halves(y - H, half), :]
                    return edge_ref[p, halves(y - 4, half), :]

                ring = [s_ref[p, halves(y, half), :] for y in range(C)] + [other(y) for y in range(C)]
                q = {y: q_ref[p, halves(y, half), :] for y in range(C)}
                for y in list(range(H)) + list(range(C - H, C)):
                    v = vb_mate_ref[p, halves(y, half), :]
                    q[C + y] = tap_sum(lambda i: ring[i % 32], C + y) + v * ring[C + y]
                for y in range(C):
                    rows = halves(y, half)
                    total = tap_sum(lambda i: q[i % 32], y)
                    total = total + vb_ref[p, rows, :] * (side_ref[p, rows, :] + q[y])
                    out_ref[p, rows, :] = 2.0 * (total + part_ref[p, rows, :]) - ring[y]

    for_piece(refs[:3], inner_ref, planes)


def make_base(s, mid, vb, vb_mate, q, side_part, part, edges, inner):
    return pl.pallas_call(
        base_kernel,
        grid=(C // N,),
        in_specs=[plane_spec(ROWS, N), plane_spec(MID, N)]
        + [plane_spec(ROWS, N)] * 5
        + edge_specs()
        + [SCALARS, whole((C - FIRST) * EDGE)],
        out_specs=plane_spec(ROWS, N),
        out_shape=FULL,
        scratch_shapes=[pltpu.VMEM((N, MID, S), F32)],
        compiler_params=params(16),
        cost_estimate=cost(1 << 25, 16 << 20),
        name="base",
    )(s, mid, vb, vb_mate, q, side_part, part, *edges, inner, edges[1].reshape(-1, S))


def second_kernel(base_ref, low_one_ref, high_one_ref, low_ref, high_ref, gg_high_ref, gg_low_ref, *rest):
    part_ref, mate_ref, energy_ref, upper_ref, second_ref, keep_ref, give_ref, gram_ref, cross_ref, w_ref, halo_ref = rest
    step = pl.program_id(0)

    @pl.when(step == 0)
    def _():
        gram_ref[...] = jnp.zeros((S, S), F32)
        cross_ref[...] = jnp.zeros((S, S), F32)
        w_ref[...] = jnp.zeros((S, S), F32)
        halo_ref[...] = jnp.zeros((B, ROWS, S), F32)
        mine = [part_ref[j] + mate_ref[j] for j in range(3)]
        below = [move_pair(low_ref[HALO_ROWS + j * NEAR : HALO_ROWS + (j + 1) * NEAR, :], -1) for j in range(2)]
        above = [move_pair(high_ref[HALO_ROWS + j * NEAR : HALO_ROWS + (j + 1) * NEAR, :], 1) for j in range(2)]
        slabs = [mine[0] + below[0], mine[1] + below[1] + above[0], mine[2] + above[1]]
        near = jnp.concatenate([slab[0:16] for slab in slabs]) * energy_ref[...]
        lane = lax.broadcasted_iota(jnp.int32, (NEAR, S), 1)
        pair = jnp.where(lane < NEAR, jnp.concatenate([slab[32:48] for slab in slabs]), 0.0)
        two = jnp.concatenate([slab[16:32] for slab in slabs])
        two = two + exact(pair, jnp.concatenate([near, jnp.zeros((S - NEAR, S), F32)]))
        w_ref[0:NEAR, :] = 2.0 * energy_ref[...] * two
        w_ref[64 : 64 + NEAR, :] = 2.0 * near

    def halo_part(below_ref, above_ref, first_plane):
        for p in range(B):
            low = [below_ref[halo_rows(step * B + p - first_plane, j), :] for j in range(H)]
            high = [above_ref[halo_rows(step * B + p - first_plane, j), :] for j in range(H)]
            for z in range(H):
                add = sum((2.0 * OFF[k - 1]) * low[z - k + H] for k in range(z + 1, H + 1))
                halo_ref[p, stride_rows(z), :] = add
                add = sum((2.0 * OFF[H + j - z - 1]) * high[j] for j in range(z + 1))
                halo_ref[p, stride_rows(C - H + z), :] = add

    @pl.when(step < FIRST // B)
    def _():
        halo_part(low_one_ref, high_one_ref, 0)

    @pl.when(step >= FIRST // B)
    def _():
        halo_part(low_ref, high_ref, FIRST)

    w_high, w_low = split(w_ref[...])
    gram = jnp.zeros((S, S), F32)
    cross = jnp.zeros((S, S), F32)
    for p in range(B):
        g_high, g_low = gg_high_ref[0, p], gg_low_ref[0, p]
        value = base_ref[p] + halo_ref[p] + (mm(g_high, w_high) + (mm(g_high, w_low) + mm(g_low, w_high)))
        second_ref[p] = value
        s_high, s_low = split(value)
        turned = s_high.T
        gram += mm(turned, s_high)
        cross += mm(turned, s_low)
    gram_ref[...] += gram
    cross_ref[...] += cross

    @pl.when(step == STEPS - 1)
    def _():
        cross = cross_ref[...]
        gram = (gram_ref[...] + (cross + cross.T)) * (1.0 / NCELLS)
        upper = upper_ref[0] == 1
        keep_ref[...] = jnp.where(upper, gram[S // 2 :], gram[: S // 2])
        give_ref[...] = jnp.where(upper, gram[: S // 2], gram[S // 2 :])


def make_second(base, halos, gg, shares, upper):
    three = pl.BlockSpec((3, NEAR, S), lambda i: (0, 0, 0))
    return pl.pallas_call(
        second_kernel,
        grid=(STEPS,),
        in_specs=[plane_spec()]
        + [whole(HALO_ROWS)] * 2
        + [whole(HALO_ROWS + SHARES)] * 2
        + [part_spec(0), part_spec(1), three, three, whole(NEAR), SCALARS],
        out_specs=[plane_spec(), whole(S // 2), whole(S // 2)],
        out_shape=[FULL, sds((S // 2, S)), sds((S // 2, S))],
        scratch_shapes=[pltpu.VMEM((S, S), F32)] * 3 + [pltpu.VMEM((B, ROWS, S), F32)],
        compiler_params=params(16),
        cost_estimate=cost(1 << 27, 8 << 20),
        name="second",
    )(base, *halos, gg, gg, *shares, upper)


def exact(a, b):
    return jnp.dot(a, b, precision=lax.Precision.HIGHEST, preferred_element_type=F32)


def inverse_factor(gram_ref, a_ref, x_ref, state_ref):
    row = lax.broadcasted_iota(jnp.int32, (S, S), 0)
    column = lax.broadcasted_iota(jnp.int32, (S, S), 1)
    unit = jnp.where(row == column, 1.0, 0.0)
    gram = gram_ref[...]
    diagonal = jnp.where(row == column, gram, 0.0)
    down = lax.rsqrt(jnp.sum(diagonal, axis=1, keepdims=True))
    across = lax.rsqrt(jnp.sum(diagonal, axis=0, keepdims=True))
    a_ref[...] = gram * down * across
    x_ref[...] = unit

    def residual():
        x = x_ref[...]
        return unit - exact(exact(x, a_ref[...]), x.T)

    def size(e):
        return jnp.sum(e * e)

    def improve(e):
        lower = jnp.where(row > column, e, jnp.where(row == column, 0.5 * e, 0.0))
        x_ref[...] += exact(lower, x_ref[...])

    state_ref[0] = 0
    start = unit - a_ref[...]
    start_size = size(start)

    @pl.when(start_size < 0.16)
    def _():
        improve(start)
        state_ref[0] = jnp.where(start_size < 1e-6, 2, 1)

    for _ in range(5):

        @pl.when(state_ref[0] == 1)
        def _():
            e = residual()
            e_size = size(e)
            improve(e)
            state_ref[0] = jnp.where(e_size < 1e-6, 2, 1)

    @pl.when(state_ref[0] != 2)
    def _():
        x_ref[...] = unit
        lanes = lax.broadcasted_iota(jnp.int32, (1, S), 1)

        def step(j, _):
            line = a_ref[pl.ds(j, 1), :]
            scale = lax.rsqrt(jnp.sum(jnp.where(lanes == j, line, 0.0), axis=1, keepdims=True))
            a = a_ref[...]
            factor = jnp.sum(jnp.where(column == j, a, 0.0), axis=1, keepdims=True) * scale
            factor = jnp.where(row[:, :1] > j, factor, 0.0)
            x_line = x_ref[pl.ds(j, 1), :] * scale
            a_ref[...] = a - factor * (line * scale)
            x_ref[...] = jnp.where(row == j, x_line, x_ref[...] - factor * x_line)
            return 0

        lax.fori_loop(0, S, step, 0)

    x_ref[...] = x_ref[...] * across


def turn_kernel(second_ref, own_ref, other_ref, upper_ref, out_ref, gram_ref, a_ref, x_ref, i_high_ref, i_low_ref, state_ref):
    @pl.when(pl.program_id(0) == 0)
    def _():
        upper = upper_ref[0] == 1
        gram_ref[: S // 2, :] = jnp.where(upper, other_ref[...], own_ref[...])
        gram_ref[S // 2 :, :] = jnp.where(upper, own_ref[...], other_ref[...])
        inverse_factor(gram_ref, a_ref, x_ref, state_ref)
        i_high, i_low = split(x_ref[...].T)
        i_high_ref[...] = i_high
        i_low_ref[...] = i_low

    i_high, i_low = i_high_ref[...], i_low_ref[...]

    for p in range(B):
        high, low = split(second_ref[p])
        out_ref[p] = mm(high, i_high) + (mm(high, i_low) + mm(low, i_high))


def turn(second, own, other, upper):
    return pl.pallas_call(
        turn_kernel,
        grid=(STEPS,),
        in_specs=[plane_spec(), whole(S // 2), whole(S // 2), SCALARS],
        out_specs=plane_spec(),
        out_shape=FULL,
        scratch_shapes=[pltpu.VMEM((S, S), F32)] * 3 + [pltpu.VMEM((S, S), BF16)] * 2 + [pltpu.SMEM((1,), jnp.int32)],
        compiler_params=params(16),
        cost_estimate=cost(1 << 28, 4 << 20),
        name="turn",
    )(second, own, other, upper)


def per_device(states, potential, atom_sites, projectors, energies):
    gx, gy = lax.axis_index("gx"), lax.axis_index("gy")
    depth = lax.axis_size("gzs")
    count = 4 * depth
    barrier = lax.optimization_barrier

    def send(value, flip=0, move=0):
        def target(d):
            return (d // depth * depth ^ flip) + (d + move) % depth

        return lax.ppermute(value, AXES, [(d, target(d)) for d in range(count)])

    over_x, over_y = 2 * depth, depth
    inner_ones = [d for d in range(count) if d % 4 in (1, 2)]
    outer_ones = [d for d in range(count) if d % 4 in (0, 3)]
    inner = ((lax.axis_index("gzs") + 1) // 2 % 2).astype(jnp.int32).reshape(1)
    s = states.reshape(C, ROWS, S)
    mate = send(s, over_x)
    pot = potential.reshape(32, 128)
    corner = jnp.stack([gx * C, gy * C]).astype(jnp.int32)
    upper = gx.astype(jnp.int32).reshape(1)
    atoms = jnp.concatenate(
        [projectors.reshape(4, TAPS), atom_sites.astype(F32), energies[:, None], jnp.zeros((4, 768 - TAPS - 4), F32)],
        axis=1,
    ).reshape(24, 128)
    to_pack, pot, corner, upper, inner, atoms = barrier((s, pot, corner, upper, inner, atoms))

    parcel = stack((atoms, 24), (pot, 32))
    parcel_mate = send(parcel, over_y)
    one_edge, head, tail = pack(to_pack)
    one_edge = send(one_edge, over_y)
    pair = stack((parcel, 24), (parcel_mate, 24))
    column = stack((send(pair, 0, 1), 48), (pair, 48), (send(pair, 0, -1), 48))
    column_mate = send(column, over_x)
    message, relay, mid = pack_rest(s, inner)
    vb = spread(parcel)
    beside = side_x(s, mate)
    column_mate, head, tail, message, relay, beside = barrier((column_mate, head, tail, message, relay, beside))
    low, high = send(tail, 0, 1), send(head, 0, -1)
    relayed = lax.ppermute(relay, AXES, [(d, d ^ over_y ^ 1) for d in outer_ones])
    message = send(message, over_y)
    gg, part, energy = prep([column, column_mate], corner, vb, s)
    part, relayed, one_edge = barrier((part, relayed, one_edge))
    relayed = lax.ppermute(relayed, AXES, [(d, d ^ 1) for d in inner_ones])
    planes = vb.reshape(C, ROWS, S)
    side_part = side_z(s, beside, low, high)
    q, mix, head, tail = first_half(s, side_part, planes, one_edge)
    low_one, high_one = send(tail, 0, 1), send(head, 0, -1)

    part = part + send(part, over_x)
    part_mate = send(part, over_y)
    part_mate, low_one, high_one = barrier((part_mate, low_one, high_one))
    message = message.reshape(C - FIRST, EDGE, S)
    q, mix, head, tail = other_half(s, side_part, planes, message, relayed, inner, part, part_mate, q, mix)
    halos = [low_one, high_one, send(tail, 0, 1), send(head, 0, -1)]
    mate = send(mix, over_x)
    mid, part_mate = barrier((mid, part_mate))
    mid = lax.ppermute(mid, AXES, [(d, d ^ over_y) for d in inner_ones])
    planes_mate = spread(parcel_mate).reshape(C, ROWS, S)
    part_two = side_again(mix, mate)
    base = make_base(s, mid, planes, planes_mate, q, side_part, part_two, [one_edge, message, relayed], inner)
    gg = gg.reshape(2, C, ROWS, S)
    second, own, give = make_second(base, halos, gg, [part, part_mate, energy], upper)

    own = own + send(give, over_x)
    for flip in (32, 36, 1, 3, 8, 24):
        own = own + lax.ppermute(own, AXES, [(d, d ^ flip) for d in range(count)])
    return turn(second, own, send(own, over_x), upper).reshape(C, C, C, S)


def solution(mesh):
    return jax.shard_map(
        per_device,
        mesh=mesh,
        in_specs=(
            P("gx", "gy", "gzs", None),
            P("gx", "gy", "gzs"),
            P(("gx", "gy", "gzs"), None),
            P(("gx", "gy", "gzs"), None, None, None),
            P(("gx", "gy", "gzs")),
        ),
        out_specs=P("gx", "gy", "gzs", None),
        check_vma=False,
    )
```

```python
import math

import jax
import jax.numpy as jnp
from jax import lax
from jax.experimental import pallas as pl
from jax.experimental.pallas import tpu as pltpu
from jax.sharding import PartitionSpec as P

AXES = ("gx", "gy", "gzs")
H = 6
C = 16
ROWS = C * C
CELLS = C * C * C
NCELLS = 32 * 32 * 512
S = 128
W = 9
R = 4
NEAR = 48
TAPS = W * W * W
F32 = jnp.float32
BF16 = jnp.bfloat16

grid_step = 0.6
filter_centre = 36.0
filter_half = 26.0


def weights():
    taps = []
    for k in range(1, 7):
        top = 2.0 * (-1) ** (k + 1) * math.factorial(6) ** 2
        under = k * k * math.factorial(6 - k) * math.factorial(6 + k)
        taps.append(top / under)
    scale = -0.5 / (grid_step * grid_step)
    off = [scale * t / filter_half for t in taps]
    diagonal = 3.0 * scale * (-2.0 * sum(taps))
    return off, diagonal


OFF, DIAGONAL = weights()


def params(mib):
    return pltpu.CompilerParams(vmem_limit_bytes=mib * 1024 * 1024)


def cost(flops, nbytes):
    return pl.CostEstimate(flops=flops, bytes_accessed=nbytes, transcendentals=0)


def sds(shape, dtype=F32):
    return jax.ShapeDtypeStruct(shape, dtype)


def split(value):
    high = value.astype(BF16)
    low = (value - high.astype(F32)).astype(BF16)
    return high, low


def mm(a, b):
    return jnp.dot(a, b, preferred_element_type=F32)


def tap_sum(at, index):
    total = None
    for k in range(1, 7):
        term = OFF[k - 1] * (at(index + k) + at(index - k))
        total = term if total is None else total + term
    return total


B = 4
STEPS = C // B
N = 2
FIRST = 8
MIDDLE = 10
EDGE = 192
MID = 64
MID_START = (MIDDLE - FIRST) * EDGE


def stride_rows(z):
    return pl.ds(z, C, stride=C)


def plane_spec(rows=ROWS, planes=B):
    return pl.BlockSpec((planes, rows, S), lambda i: (i, 0, 0))


def halo_spec(planes=B):
    return pl.BlockSpec((H, planes, C, S), lambda i: (0, i, 0, 0))


def part_spec(part):
    return pl.BlockSpec((1, B, ROWS, S), lambda i: (part, i, 0, 0))


def whole(rows=S):
    return pl.BlockSpec((rows, S), lambda i: (0, 0))


def edge_spec(start, stop):
    return pl.BlockSpec((N, EDGE, S), lambda i: (jnp.clip(i - start // N, 0, (stop - start) // N - 1), 0, 0))


def edge_specs():
    return [edge_spec(0, FIRST), edge_spec(FIRST, C), edge_spec(MIDDLE, C)]


def for_piece(edges, inner_ref, body):
    step = pl.program_id(0)
    direct = (inner_ref[0] == 1) | (step < MIDDLE // N)

    @pl.when(step < FIRST // N)
    def _():
        body(edges[0])

    @pl.when((step >= FIRST // N) & direct)
    def _():
        body(edges[1])

    @pl.when(jnp.logical_not(direct))
    def _():
        body(edges[2])


SCALARS = pl.BlockSpec(memory_space=pltpu.SMEM)
FULL = sds((C, ROWS, S))
FULL_ROWS = sds((CELLS, S))
HALO_ROWS = H * FIRST * C
SHARES = 2 * NEAR
HALO = sds((H, C, C, S))
EDGES = [sds((FIRST, EDGE, S)), sds((C - FIRST, EDGE, S)), sds((C - MIDDLE, EDGE, S))]


def halo_rows(x, z):
    return pl.ds(pl.multiple_of(z * FIRST * C + x * C, C), C)


def halves(y, half):
    return slice(y * C + half * 8, y * C + half * 8 + 8)


def pack_edges(s_ref, out_ref):
    out_ref[:, 0:96, :] = s_ref[:, 0:96, :]
    out_ref[:, 96:192, :] = s_ref[:, 160:256, :]


def pack_kernel(s_ref, edge_ref, relay_ref, head_ref, tail_ref):
    @pl.when(pl.program_id(0) >= MIDDLE // N)
    def _():
        pack_edges(s_ref, relay_ref)

    @pl.when(pl.program_id(0) < FIRST // N)
    def _():
        pack_edges(s_ref, edge_ref)

    for p in range(N):
        for z in range(H):
            head_ref[z, p] = s_ref[p, stride_rows(z), :]
            tail_ref[z, p] = s_ref[p, stride_rows(C - H + z), :]


def pack(s):
    return pl.pallas_call(
        pack_kernel,
        grid=(C // N,),
        in_specs=[plane_spec(ROWS, N)],
        out_specs=[edge_spec(0, FIRST), edge_spec(MIDDLE, C), halo_spec(N), halo_spec(N)],
        out_shape=[EDGES[0], EDGES[2], HALO, HALO],
        compiler_params=params(12),
        cost_estimate=cost(1 << 32, 6 << 20),
        name="pack",
    )(s)


def pack_rest_kernel(s_ref, inner_ref, message_ref, mid_ref):
    step = pl.program_id(0)
    inner = inner_ref[0] == 1
    mid_ref[...] = s_ref[:, 96:160, :]

    @pl.when((step >= FIRST // N) & (inner | (step < MIDDLE // N)))
    def _():
        for p in range(N):
            row = pl.multiple_of((step * N + p - FIRST) * EDGE, MID)
            message_ref[pl.ds(row, 96), :] = s_ref[p, 0:96, :]
            message_ref[pl.ds(row + 96, 96), :] = s_ref[p, 160:256, :]

    @pl.when(jnp.logical_not(inner))
    def _():
        for p in range(N):
            row = pl.multiple_of(MID_START + (step * N + p) * MID, MID)
            message_ref[pl.ds(row, MID), :] = s_ref[p, 96:160, :]


def pack_rest(s, inner):
    rows = (C - FIRST) * EDGE
    return pl.pallas_call(
        pack_rest_kernel,
        grid=(C // N,),
        in_specs=[plane_spec(ROWS, N), SCALARS],
        out_specs=[whole(rows), plane_spec(MID, N)],
        out_shape=[sds((rows, S)), sds((C, MID, S))],
        compiler_params=params(12),
        cost_estimate=cost(1 << 31, 4 << 20),
        name="pack_rest",
    )(s, inner)


def stack(*pieces):
    def kernel(*refs):
        start = 0
        for ref, (_, rows) in zip(refs, pieces):
            refs[-1][start : start + rows, :] = ref[:rows, :]
            start += rows

    arrays = [array for array, _ in pieces]
    rows = sum(rows for _, rows in pieces)
    return pl.pallas_call(kernel, out_shape=sds((rows, S)), compiler_params=params(4), name="stack")(*arrays)


def along_x(s_ref, mate_ref, out_ref, add):
    def column(block, _):
        rows = pl.ds(pl.multiple_of(block * 8, 8), 8)
        ring = [mate_ref[C - H + i, rows, :] for i in range(H)]
        ring += [s_ref[x, rows, :] for x in range(C)]
        ring += [mate_ref[i, rows, :] for i in range(H)]
        for x in range(C):
            value = tap_sum(lambda i: ring[H + i], x)
            if add:
                value = value + out_ref[x, rows, :]
            out_ref[x, rows, :] = value
        return 0

    lax.fori_loop(0, ROWS // 8, column, 0)


def z_taps(ext_ref, y):
    return tap_sum(lambda k: ext_ref[y * 32 + 8 + k : y * 32 + 24 + k, :], 0)


def side_x_kernel(s_ref, mate_ref, out_ref):
    along_x(s_ref, mate_ref, out_ref, False)


def side_x(s, mate):
    return pl.pallas_call(
        side_x_kernel,
        out_shape=FULL,
        compiler_params=params(12),
        cost_estimate=cost(1 << 24, 6 << 20),
        name="side_x",
    )(s, mate)


def side_z_kernel(s_ref, part_ref, low_ref, high_ref, out_ref, ext_ref):
    def plane(x, _):
        for y in range(C):
            ext_ref[y * 32 + 8 : y * 32 + 24, :] = s_ref[x, y * C : (y + 1) * C, :]
        for z in range(H):
            ext_ref[pl.ds(2 + z, C, stride=32), :] = low_ref[z, x]
            ext_ref[pl.ds(24 + z, C, stride=32), :] = high_ref[z, x]
        for y in range(C):
            rows = slice(y * C, (y + 1) * C)
            out_ref[x, rows, :] = part_ref[x, rows, :] + z_taps(ext_ref, y)
        return 0

    lax.fori_loop(0, C, plane, 0)


def side_z(s, part, low, high):
    return pl.pallas_call(
        side_z_kernel,
        out_shape=FULL,
        scratch_shapes=[pltpu.VMEM((C * 32, S), F32)],
        compiler_params=params(14),
        cost_estimate=cost(1 << 24, 8 << 20),
        name="side_z",
    )(s, part, low, high)


def side_again_kernel(s_ref, mate_ref, out_ref, ext_ref):
    for y in range(C):
        ext_ref[y * 32 : y * 32 + 8, :] = jnp.zeros((8, S), F32)
        ext_ref[y * 32 + 24 : y * 32 + 32, :] = jnp.zeros((8, S), F32)

    def plane(x, _):
        for y in range(C):
            ext_ref[y * 32 + 8 : y * 32 + 24, :] = s_ref[x, y * C : (y + 1) * C, :]
        for y in range(C):
            out_ref[x, y * C : (y + 1) * C, :] = z_taps(ext_ref, y)
        return 0

    lax.fori_loop(0, C, plane, 0)
    along_x(s_ref, mate_ref, out_ref, True)


def side_again(s, mate):
    return pl.pallas_call(
        side_again_kernel,
        out_shape=FULL,
        scratch_shapes=[pltpu.VMEM((C * 32, S), F32)],
        compiler_params=params(12),
        cost_estimate=cost(1 << 25, 6 << 20),
        name="side_again",
    )(s, mate)


def tap_weight(distance):
    value = jnp.zeros(distance.shape, F32)
    for k in range(1, 7):
        value = jnp.where(distance == k, OFF[k - 1], value)
    return value


def ring_tables(coordinate):
    masks, factors = [], []
    for t in range(W):
        away = (coordinate - t) & 31
        masks.append(away == 0)
        factors.append(tap_weight(jnp.minimum(away, 32 - away)))
    return masks, factors


def spread_kernel(parcel_ref, vb_ref):
    def spread_row(row, _):
        line = (parcel_ref[pl.ds(24 + row, 1), :] + (DIAGONAL - filter_centre)) * (1.0 / filter_half)
        start = pl.multiple_of(row * 128, 128)
        vb_ref[pl.ds(start, 128), :] = jnp.broadcast_to(line, (128, 128)).T
        return 0

    lax.fori_loop(0, CELLS // 128, spread_row, 0, unroll=8)


def spread(parcel):
    return pl.pallas_call(
        spread_kernel,
        out_shape=FULL_ROWS,
        compiler_params=params(8),
        cost_estimate=cost(1 << 20, 2 << 20),
        name="spread",
    )(parcel)


def prep_kernel(*refs):
    own_ref, other_ref, corner_ref, vb_ref, s_ref, gg_ref, coef_ref, energy_ref, near_ref, table_ref = refs[:10]
    a1_ref, a1z_ref, a2_ref, a2s_ref = refs[10:]
    upper_x, upper_y = corner_ref[0] > 0, corner_ref[1] > 0
    for slab in range(3):
        own = [own_ref[slab * 48 + j * 24 : slab * 48 + j * 24 + 24, :] for j in range(2)]
        other = [other_ref[slab * 48 + j * 24 : slab * 48 + j * 24 + 24, :] for j in range(2)]
        lower = [jnp.where(upper_x, o, m) for m, o in zip(own, other)]
        higher = [jnp.where(upper_x, m, o) for m, o in zip(own, other)]
        ordered = []
        for pair in (lower, higher):
            ordered += [jnp.where(upper_y, pair[1], pair[0]), jnp.where(upper_y, pair[0], pair[1])]
        for j in range(4):
            near_ref[slab * 96 + j * 24 : slab * 96 + j * 24 + 24, :] = ordered[j]
    blank = jnp.zeros((16, 128), F32)
    for block in range(6):
        rows = near_ref[pl.ds(block, NEAR, stride=6), :]
        table_ref[block * 128 : block * 128 + 128, :] = jnp.concatenate([rows, blank, rows, blank]).T
    at = TAPS + 3 - 640
    energy_ref[...] = jnp.broadcast_to(rows[:, at : at + 1] * (1.0 / filter_half), (NEAR, S))

    shape = (8, 128)
    sub = lax.broadcasted_iota(jnp.int32, shape, 0)
    lane = lax.broadcasted_iota(jnp.int32, shape, 1)
    first_lanes = lane < 64
    sites = [jnp.broadcast_to(table_ref[TAPS + d : TAPS + d + 1, :], shape).astype(jnp.int32) for d in range(3)]
    px = sites[0] - corner_ref[0]
    py = sites[1] - corner_ref[1]
    pz = (sites[2] & 15) + (((lane & 63) >> 4) - 1) * C
    zero = jnp.zeros(shape, F32)

    dz = sub + (lane >> 6) * 8 - pz + R
    z_masks = [dz == t for t in range(W)]
    z_factors = [tap_weight(jnp.abs(dz - t)) for t in range(W)]

    def place_z(ij, _):
        acc = zero
        along = zero
        for t in range(W):
            row = jnp.broadcast_to(table_ref[pl.ds(ij * W + t, 1), :], shape)
            acc = jnp.where(z_masks[t], row, acc)
            along = along + z_factors[t] * row
        a1_ref[ij] = acc
        a1z_ref[ij] = along
        return 0

    lax.fori_loop(0, W * W, place_z, 0, unroll=3)

    def place_y(y, _):
        masks, factors = ring_tables(y - py + R)
        for i in range(W):
            acc = zero
            along = zero
            moved = zero
            for t in range(W):
                value = a1_ref[i * W + t]
                acc = jnp.where(masks[t], value, acc)
                along = along + factors[t] * value
                moved = jnp.where(masks[t], a1z_ref[i * W + t], moved)
            a2_ref[i, y] = acc
            a2s_ref[i, y] = along + moved
        return 0

    lax.fori_loop(0, C, place_y, 0)

    def place_x(x, _):
        masks, factors = ring_tables(x - px + R)

        def per_y(y, _):
            row = pl.multiple_of(x * ROWS + y * C, C)
            acc = zero
            along = zero
            moved = zero
            for t in range(W):
                value = a2_ref[t, y]
                acc = jnp.where(masks[t], value, acc)
                along = along + factors[t] * value
                moved = jnp.where(masks[t], a2s_ref[t, y], moved)
            v = vb_ref[pl.ds(row, C), :]
            moved = along + moved + jnp.where(first_lanes, v[:8], v[8:]) * acc
            lower = jnp.where(first_lanes, acc, pltpu.roll(moved, 64, 1))
            upper = jnp.where(first_lanes, pltpu.roll(acc, 64, 1), moved)
            high, low = split(jnp.concatenate([lower, upper], axis=0))
            gg_ref[0, pl.ds(row, C), :] = high
            gg_ref[1, pl.ds(row, C), :] = low
            return 0

        lax.fori_loop(0, C, per_y, 0, unroll=16)
        return 0

    lax.fori_loop(0, C, place_x, 0)

    coef_ref[...] = jnp.zeros((3, NEAR, S), F32)

    def contract(x, _):
        rows = pl.ds(pl.multiple_of(x * 2 * ROWS, ROWS), 2 * ROWS)
        g_high, g_low = gg_ref[0, rows, :], gg_ref[1, rows, :]
        t_high, t_low = g_high.T, g_low.T
        high, low = split(s_ref[rows, :])
        got = mm(t_high, high) + (mm(t_high, low) + mm(t_low, high))
        t_high, t_low = t_high[:NEAR], t_low[:NEAR]
        pair = mm(t_high, g_high) + (mm(t_high, g_low) + mm(t_low, g_high))
        for slab in range(3):
            rows = slice(slab * C, slab * C + C)
            coef_ref[slab, 0:16] += got[rows]
            coef_ref[slab, 16:32] += got[64 + slab * C : 80 + slab * C]
            coef_ref[slab, 32:48] += pair[rows]
        return 0

    lax.fori_loop(0, C // 2, contract, 0, unroll=2)


def prep(parcels, corner, vb, s):
    vmem = pl.BlockSpec(memory_space=pltpu.VMEM)
    return pl.pallas_call(
        prep_kernel,
        in_specs=[vmem] * 2 + [pl.BlockSpec(memory_space=pltpu.SMEM), vmem, vmem],
        out_shape=[sds((2, CELLS, S), BF16), sds((3, NEAR, S)), sds((NEAR, S))],
        scratch_shapes=[
            pltpu.VMEM((288, 128), F32),
            pltpu.VMEM((768, 128), F32),
            pltpu.VMEM((W * W, 8, 128), F32),
            pltpu.VMEM((W * W, 8, 128), F32),
            pltpu.VMEM((W, C, 8, 128), F32),
            pltpu.VMEM((W, C, 8, 128), F32),
        ],
        compiler_params=params(16),
        cost_estimate=cost(1 << 27, 10 << 20),
        name="prep",
    )(*parcels, corner, vb, s.reshape(CELLS, S))


def move_pair(shares, away):
    lane = lax.broadcasted_iota(jnp.int32, (16, 128), 1)
    keep = (lane < 32) if away < 0 else (lane >= 16) & (lane < 48)
    pair = jnp.where(keep, pltpu.roll(shares[32:48], (away * 16) % 128, 1), 0.0)
    return jnp.concatenate([shares[0:32], pair])


def first_planes(s_ref, side_ref, vb_ref, edge_ref, q_ref, mix_ref, head_ref, tail_ref):
    for p in range(N):
        for half in range(2):
            ring = {y: s_ref[p, halves(y, half), :] for y in range(C)}
            for y in range(H):
                ring[C + y] = edge_ref[p, halves(y, half), :]
                ring[y - H] = edge_ref[p, halves(H + y, half), :]
            for y in range(C):
                rows = halves(y, half)
                dy = tap_sum(lambda i: ring[i], y)
                q = dy + vb_ref[p, rows, :] * ring[y]
                q_ref[p, rows, :] = q
                mix_ref[p, rows, :] = side_ref[p, rows, :] + q + dy
        for z in range(H):
            rows = halo_rows(pl.program_id(0) * N + p, z)
            head_ref[rows, :] = mix_ref[p, stride_rows(z), :]
            tail_ref[rows, :] = mix_ref[p, stride_rows(C - H + z), :]


def half_spec(start):
    return pl.BlockSpec((N, ROWS, S), lambda i: (i + start // N, 0, 0))


def first_half(s, side_part, vb, edge):
    return pl.pallas_call(
        first_planes,
        grid=(FIRST // N,),
        in_specs=[half_spec(0)] * 3 + [edge_spec(0, FIRST)],
        out_specs=[half_spec(0)] * 2 + [whole(HALO_ROWS)] * 2,
        out_shape=[FULL, FULL, sds((HALO_ROWS, S)), sds((HALO_ROWS, S))],
        compiler_params=params(16),
        cost_estimate=cost(1 << 23, 7 << 20),
        name="first_half",
    )(s, side_part, vb, edge)


def other_half_kernel(s_ref, side_ref, vb_ref, edge_ref, relay_ref, inner_ref, part_ref, mate_ref, _, __, *out):
    q_ref, mix_ref, head_ref, tail_ref = out

    @pl.when(pl.program_id(0) == 0)
    def _():
        for j in range(2):
            rows = slice(HALO_ROWS + j * NEAR, HALO_ROWS + (j + 1) * NEAR)
            head_ref[rows, :] = part_ref[j] + mate_ref[j]
            tail_ref[rows, :] = part_ref[j + 1] + mate_ref[j + 1]

    direct = (inner_ref[0] == 1) | (pl.program_id(0) < (MIDDLE - FIRST) // N)

    @pl.when(direct)
    def _():
        first_planes(s_ref, side_ref, vb_ref, edge_ref, *out)

    @pl.when(jnp.logical_not(direct))
    def _():
        first_planes(s_ref, side_ref, vb_ref, relay_ref, *out)


def other_half(s, side_part, vb, message, relayed, inner, part, part_mate, q, mix):
    shares = pl.BlockSpec((3, NEAR, S), lambda i: (0, 0, 0))
    anywhere = pl.BlockSpec(memory_space=pl.ANY)
    relay_spec = pl.BlockSpec((N, EDGE, S), lambda i: (jnp.maximum(i - (MIDDLE - FIRST) // N, 0), 0, 0))
    return pl.pallas_call(
        other_half_kernel,
        grid=((C - FIRST) // N,),
        in_specs=[half_spec(FIRST)] * 3
        + [pl.BlockSpec((N, EDGE, S), lambda i: (i, 0, 0)), relay_spec, SCALARS, shares, shares, anywhere, anywhere],
        out_specs=[half_spec(FIRST)] * 2 + [whole(HALO_ROWS + SHARES)] * 2,
        out_shape=[FULL, FULL, sds((HALO_ROWS + SHARES, S)), sds((HALO_ROWS + SHARES, S))],
        input_output_aliases={8: 0, 9: 1},
        compiler_params=params(16),
        cost_estimate=cost(1 << 23, 7 << 20),
        name="other_half",
    )(s, side_part, vb, message, relayed, inner, part, part_mate, q, mix)


def base_kernel(s_ref, mid_ref, vb_ref, vb_mate_ref, q_ref, side_ref, part_ref, *refs):
    inner_ref, message_ref, out_ref, middle_ref = refs[3:]
    step = pl.program_id(0)
    inner = inner_ref[0] == 1

    @pl.when(inner)
    def _():
        middle_ref[...] = mid_ref[...]

    @pl.when(jnp.logical_not(inner))
    def _():
        for p in range(N):
            middle_ref[p] = message_ref[pl.ds(pl.multiple_of(MID_START + (step * N + p) * MID, MID), MID), :]

    def planes(edge_ref):
        for p in range(N):
            for half in range(2):

                def other(y, p=p, half=half):
                    if y < H:
                        return edge_ref[p, halves(y, half), :]
                    if y < C - H:
                        return middle_ref[p, halves(y - H, half), :]
                    return edge_ref[p, halves(y - 4, half), :]

                ring = [s_ref[p, halves(y, half), :] for y in range(C)] + [other(y) for y in range(C)]
                q = {y: q_ref[p, halves(y, half), :] for y in range(C)}
                for y in list(range(H)) + list(range(C - H, C)):
                    v = vb_mate_ref[p, halves(y, half), :]
                    q[C + y] = tap_sum(lambda i: ring[i % 32], C + y) + v * ring[C + y]
                for y in range(C):
                    rows = halves(y, half)
                    total = tap_sum(lambda i: q[i % 32], y)
                    total = total + vb_ref[p, rows, :] * (side_ref[p, rows, :] + q[y])
                    out_ref[p, rows, :] = 2.0 * (total + part_ref[p, rows, :]) - ring[y]

    for_piece(refs[:3], inner_ref, planes)


def make_base(s, mid, vb, vb_mate, q, side_part, part, edges, inner):
    return pl.pallas_call(
        base_kernel,
        grid=(C // N,),
        in_specs=[plane_spec(ROWS, N), plane_spec(MID, N)]
        + [plane_spec(ROWS, N)] * 5
        + edge_specs()
        + [SCALARS, whole((C - FIRST) * EDGE)],
        out_specs=plane_spec(ROWS, N),
        out_shape=FULL,
        scratch_shapes=[pltpu.VMEM((N, MID, S), F32)],
        compiler_params=params(16),
        cost_estimate=cost(1 << 25, 16 << 20),
        name="base",
    )(s, mid, vb, vb_mate, q, side_part, part, *edges, inner, edges[1].reshape(-1, S))


def second_kernel(base_ref, low_one_ref, high_one_ref, low_ref, high_ref, gg_high_ref, gg_low_ref, *rest):
    part_ref, mate_ref, energy_ref, upper_ref, second_ref, keep_ref, give_ref, gram_ref, cross_ref, w_ref, halo_ref = rest
    step = pl.program_id(0)

    @pl.when(step == 0)
    def _():
        gram_ref[...] = jnp.zeros((S, S), F32)
        cross_ref[...] = jnp.zeros((S, S), F32)
        w_ref[...] = jnp.zeros((S, S), F32)
        halo_ref[...] = jnp.zeros((B, ROWS, S), F32)
        mine = [part_ref[j] + mate_ref[j] for j in range(3)]
        below = [move_pair(low_ref[HALO_ROWS + j * NEAR : HALO_ROWS + (j + 1) * NEAR, :], -1) for j in range(2)]
        above = [move_pair(high_ref[HALO_ROWS + j * NEAR : HALO_ROWS + (j + 1) * NEAR, :], 1) for j in range(2)]
        slabs = [mine[0] + below[0], mine[1] + below[1] + above[0], mine[2] + above[1]]
        near = jnp.concatenate([slab[0:16] for slab in slabs]) * energy_ref[...]
        lane = lax.broadcasted_iota(jnp.int32, (NEAR, S), 1)
        pair = jnp.where(lane < NEAR, jnp.concatenate([slab[32:48] for slab in slabs]), 0.0)
        two = jnp.concatenate([slab[16:32] for slab in slabs])
        two = two + exact(pair, jnp.concatenate([near, jnp.zeros((S - NEAR, S), F32)]))
        w_ref[0:NEAR, :] = 2.0 * energy_ref[...] * two
        w_ref[64 : 64 + NEAR, :] = 2.0 * near

    def halo_part(below_ref, above_ref, first_plane):
        for p in range(B):
            low = [below_ref[halo_rows(step * B + p - first_plane, j), :] for j in range(H)]
            high = [above_ref[halo_rows(step * B + p - first_plane, j), :] for j in range(H)]
            for z in range(H):
                add = sum((2.0 * OFF[k - 1]) * low[z - k + H] for k in range(z + 1, H + 1))
                halo_ref[p, stride_rows(z), :] = add
                add = sum((2.0 * OFF[H + j - z - 1]) * high[j] for j in range(z + 1))
                halo_ref[p, stride_rows(C - H + z), :] = add

    @pl.when(step < FIRST // B)
    def _():
        halo_part(low_one_ref, high_one_ref, 0)

    @pl.when(step >= FIRST // B)
    def _():
        halo_part(low_ref, high_ref, FIRST)

    w_high, w_low = split(w_ref[...])
    gram = jnp.zeros((S, S), F32)
    cross = jnp.zeros((S, S), F32)
    for p in range(B):
        g_high, g_low = gg_high_ref[0, p], gg_low_ref[0, p]
        value = base_ref[p] + halo_ref[p] + (mm(g_high, w_high) + (mm(g_high, w_low) + mm(g_low, w_high)))
        second_ref[p] = value
        s_high, s_low = split(value)
        turned = s_high.T
        gram += mm(turned, s_high)
        cross += mm(turned, s_low)
    gram_ref[...] += gram
    cross_ref[...] += cross

    @pl.when(step == STEPS - 1)
    def _():
        cross = cross_ref[...]
        gram = (gram_ref[...] + (cross + cross.T)) * (1.0 / NCELLS)
        upper = upper_ref[0] == 1
        keep_ref[...] = jnp.where(upper, gram[S // 2 :], gram[: S // 2])
        give_ref[...] = jnp.where(upper, gram[: S // 2], gram[S // 2 :])


def make_second(base, halos, gg, shares, upper):
    three = pl.BlockSpec((3, NEAR, S), lambda i: (0, 0, 0))
    return pl.pallas_call(
        second_kernel,
        grid=(STEPS,),
        in_specs=[plane_spec()]
        + [whole(HALO_ROWS)] * 2
        + [whole(HALO_ROWS + SHARES)] * 2
        + [part_spec(0), part_spec(1), three, three, whole(NEAR), SCALARS],
        out_specs=[plane_spec(), whole(S // 2), whole(S // 2)],
        out_shape=[FULL, sds((S // 2, S)), sds((S // 2, S))],
        scratch_shapes=[pltpu.VMEM((S, S), F32)] * 3 + [pltpu.VMEM((B, ROWS, S), F32)],
        compiler_params=params(16),
        cost_estimate=cost(1 << 27, 8 << 20),
        name="second",
    )(base, *halos, gg, gg, *shares, upper)


def exact(a, b):
    return jnp.dot(a, b, precision=lax.Precision.HIGHEST, preferred_element_type=F32)


def inverse_factor(gram_ref, a_ref, x_ref, state_ref):
    row = lax.broadcasted_iota(jnp.int32, (S, S), 0)
    column = lax.broadcasted_iota(jnp.int32, (S, S), 1)
    unit = jnp.where(row == column, 1.0, 0.0)
    gram = gram_ref[...]
    diagonal = jnp.where(row == column, gram, 0.0)
    down = lax.rsqrt(jnp.sum(diagonal, axis=1, keepdims=True))
    across = lax.rsqrt(jnp.sum(diagonal, axis=0, keepdims=True))
    a_ref[...] = gram * down * across
    x_ref[...] = unit

    def residual():
        x = x_ref[...]
        return unit - exact(exact(x, a_ref[...]), x.T)

    def size(e):
        return jnp.sum(e * e)

    def improve(e):
        lower = jnp.where(row > column, e, jnp.where(row == column, 0.5 * e, 0.0))
        x_ref[...] += exact(lower, x_ref[...])

    state_ref[0] = 0
    start = unit - a_ref[...]
    start_size = size(start)

    @pl.when(start_size < 0.16)
    def _():
        improve(start)
        state_ref[0] = jnp.where(start_size < 1e-6, 2, 1)

    for _ in range(5):

        @pl.when(state_ref[0] == 1)
        def _():
            e = residual()
            e_size = size(e)
            improve(e)
            state_ref[0] = jnp.where(e_size < 1e-6, 2, 1)

    @pl.when(state_ref[0] != 2)
    def _():
        x_ref[...] = unit
        lanes = lax.broadcasted_iota(jnp.int32, (1, S), 1)

        def step(j, _):
            line = a_ref[pl.ds(j, 1), :]
            scale = lax.rsqrt(jnp.sum(jnp.where(lanes == j, line, 0.0), axis=1, keepdims=True))
            a = a_ref[...]
            factor = jnp.sum(jnp.where(column == j, a, 0.0), axis=1, keepdims=True) * scale
            factor = jnp.where(row[:, :1] > j, factor, 0.0)
            x_line = x_ref[pl.ds(j, 1), :] * scale
            a_ref[...] = a - factor * (line * scale)
            x_ref[...] = jnp.where(row == j, x_line, x_ref[...] - factor * x_line)
            return 0

        lax.fori_loop(0, S, step, 0)

    x_ref[...] = x_ref[...] * across


def turn_kernel(second_ref, own_ref, other_ref, upper_ref, out_ref, gram_ref, a_ref, x_ref, i_high_ref, i_low_ref, state_ref):
    @pl.when(pl.program_id(0) == 0)
    def _():
        upper = upper_ref[0] == 1
        gram_ref[: S // 2, :] = jnp.where(upper, other_ref[...], own_ref[...])
        gram_ref[S // 2 :, :] = jnp.where(upper, own_ref[...], other_ref[...])
        inverse_factor(gram_ref, a_ref, x_ref, state_ref)
        i_high, i_low = split(x_ref[...].T)
        i_high_ref[...] = i_high
        i_low_ref[...] = i_low

    i_high, i_low = i_high_ref[...], i_low_ref[...]

    for p in range(B):
        high, low = split(second_ref[p])
        out_ref[p] = mm(high, i_high) + (mm(high, i_low) + mm(low, i_high))


def turn(second, own, other, upper):
    return pl.pallas_call(
        turn_kernel,
        grid=(STEPS,),
        in_specs=[plane_spec(), whole(S // 2), whole(S // 2), SCALARS],
        out_specs=plane_spec(),
        out_shape=FULL,
        scratch_shapes=[pltpu.VMEM((S, S), F32)] * 3 + [pltpu.VMEM((S, S), BF16)] * 2 + [pltpu.SMEM((1,), jnp.int32)],
        compiler_params=params(16),
        cost_estimate=cost(1 << 28, 4 << 20),
        name="turn",
    )(second, own, other, upper)


def per_device(states, potential, atom_sites, projectors, energies):
    gx, gy = lax.axis_index("gx"), lax.axis_index("gy")
    depth = lax.axis_size("gzs")
    count = 4 * depth
    barrier = lax.optimization_barrier

    def send(value, flip=0, move=0):
        def target(d):
            return (d // depth * depth ^ flip) + (d + move) % depth

        return lax.ppermute(value, AXES, [(d, target(d)) for d in range(count)])

    over_x, over_y = 2 * depth, depth
    inner_ones = [d for d in range(count) if d % 4 in (1, 2)]
    outer_ones = [d for d in range(count) if d % 4 in (0, 3)]
    inner = ((lax.axis_index("gzs") + 1) // 2 % 2).astype(jnp.int32).reshape(1)
    s = states.reshape(C, ROWS, S)
    mate = send(s, over_x)
    pot = potential.reshape(32, 128)
    corner = jnp.stack([gx * C, gy * C]).astype(jnp.int32)
    upper = gx.astype(jnp.int32).reshape(1)
    atoms = jnp.concatenate(
        [projectors.reshape(4, TAPS), atom_sites.astype(F32), energies[:, None], jnp.zeros((4, 768 - TAPS - 4), F32)],
        axis=1,
    ).reshape(24, 128)
    to_pack, pot, corner, upper, inner, atoms = barrier((s, pot, corner, upper, inner, atoms))

    parcel = stack((atoms, 24), (pot, 32))
    parcel_mate = send(parcel, over_y)
    one_edge, relay, head, tail = pack(to_pack)
    relayed = lax.ppermute(relay, AXES, [(d, d ^ over_y ^ 1) for d in outer_ones])
    one_edge = send(one_edge, over_y)
    parcel_mate, relay = barrier((parcel_mate, relay))
    pair = stack((parcel, 24), (parcel_mate, 24))
    column = stack((send(pair, 0, 1), 48), (pair, 48), (send(pair, 0, -1), 48))
    column, head, tail = barrier((column, head, tail))
    column, relayed = barrier((column, relayed))
    column_mate = send(column, over_x)
    message, mid = pack_rest(s, inner)
    vb = spread(parcel)
    beside = side_x(s, mate)
    low, high = send(tail, 0, 1), send(head, 0, -1)
    column_mate, message, beside = barrier((column_mate, message, beside))
    message = send(message, over_y)
    gg, part, energy = prep([column, column_mate], corner, vb, s)
    part, low, one_edge, relayed = barrier((part, low, one_edge, relayed))
    relayed = lax.ppermute(relayed, AXES, [(d, d ^ 1) for d in inner_ones])
    planes = vb.reshape(C, ROWS, S)
    side_part = side_z(s, beside, low, high)
    q, mix, head, tail = first_half(s, side_part, planes, one_edge)
    low_one, high_one = send(tail, 0, 1), send(head, 0, -1)

    part = part + send(part, over_x)
    part_mate = send(part, over_y)
    part_mate, low_one, high_one = barrier((part_mate, low_one, high_one))
    message = message.reshape(C - FIRST, EDGE, S)
    q, mix, head, tail = other_half(s, side_part, planes, message, relayed, inner, part, part_mate, q, mix)
    mate = send(mix, over_x)
    halos = [send(tail, 0, 1), send(head, 0, -1)]
    mid, part_mate = barrier((mid, part_mate))
    mid = lax.ppermute(mid, AXES, [(d, d ^ over_y) for d in inner_ones])
    planes_mate = spread(parcel_mate).reshape(C, ROWS, S)
    part_two = side_again(mix, mate)
    base = make_base(s, mid, planes, planes_mate, q, side_part, part_two, [one_edge, message, relayed], inner)
    gg = gg.reshape(2, C, ROWS, S)
    second, own, give = make_second(base, [low_one, high_one] + halos, gg, [part, part_mate, energy], upper)

    own = own + send(give, over_x)
    for flip in (32, 36, 1, 3, 8, 24):
        own = own + lax.ppermute(own, AXES, [(d, d ^ flip) for d in range(count)])
    return turn(second, own, send(own, over_x), upper).reshape(C, C, C, S)


def solution(mesh):
    return jax.shard_map(
        per_device,
        mesh=mesh,
        in_specs=(
            P("gx", "gy", "gzs", None),
            P("gx", "gy", "gzs"),
            P(("gx", "gy", "gzs"), None),
            P(("gx", "gy", "gzs"), None, None, None),
            P(("gx", "gy", "gzs")),
        ),
        out_specs=P("gx", "gy", "gzs", None),
        check_vma=False,
    )
```

```python
import math

import jax
import jax.numpy as jnp
from jax import lax
from jax.experimental import pallas as pl
from jax.experimental.pallas import tpu as pltpu
from jax.sharding import PartitionSpec as P

AXES = ("gx", "gy", "gzs")
H = 6
C = 16
ROWS = C * C
CELLS = C * C * C
NCELLS = 32 * 32 * 512
S = 128
W = 9
R = 4
NEAR = 48
TAPS = W * W * W
F32 = jnp.float32
BF16 = jnp.bfloat16

grid_step = 0.6
filter_centre = 36.0
filter_half = 26.0


def weights():
    taps = []
    for k in range(1, 7):
        top = 2.0 * (-1) ** (k + 1) * math.factorial(6) ** 2
        under = k * k * math.factorial(6 - k) * math.factorial(6 + k)
        taps.append(top / under)
    scale = -0.5 / (grid_step * grid_step)
    off = [scale * t / filter_half for t in taps]
    diagonal = 3.0 * scale * (-2.0 * sum(taps))
    return off, diagonal


OFF, DIAGONAL = weights()


def params(mib):
    return pltpu.CompilerParams(vmem_limit_bytes=mib * 1024 * 1024)


def cost(flops, nbytes):
    return pl.CostEstimate(flops=flops, bytes_accessed=nbytes, transcendentals=0)


def sds(shape, dtype=F32):
    return jax.ShapeDtypeStruct(shape, dtype)


def split(value):
    high = value.astype(BF16)
    low = (value - high.astype(F32)).astype(BF16)
    return high, low


def mm(a, b):
    return jnp.dot(a, b, preferred_element_type=F32)


def tap_sum(at, index):
    total = None
    for k in range(1, 7):
        term = OFF[k - 1] * (at(index + k) + at(index - k))
        total = term if total is None else total + term
    return total


B = 4
STEPS = C // B
N = 2
FIRST = 8
MIDDLE = 10
EDGE = 192
MID = 64
MID_START = (MIDDLE - FIRST) * EDGE


def stride_rows(z):
    return pl.ds(z, C, stride=C)


def plane_spec(rows=ROWS, planes=B):
    return pl.BlockSpec((planes, rows, S), lambda i: (i, 0, 0))


def halo_spec(planes=B):
    return pl.BlockSpec((H, planes, C, S), lambda i: (0, i, 0, 0))


def part_spec(part):
    return pl.BlockSpec((1, B, ROWS, S), lambda i: (part, i, 0, 0))


def whole(rows=S):
    return pl.BlockSpec((rows, S), lambda i: (0, 0))


def edge_spec(start, stop):
    return pl.BlockSpec((N, EDGE, S), lambda i: (jnp.clip(i - start // N, 0, (stop - start) // N - 1), 0, 0))


def edge_specs():
    return [edge_spec(0, FIRST), edge_spec(FIRST, C), edge_spec(MIDDLE, C)]


def for_piece(edges, inner_ref, body):
    step = pl.program_id(0)
    direct = (inner_ref[0] == 1) | (step < MIDDLE // N)

    @pl.when(step < FIRST // N)
    def _():
        body(edges[0])

    @pl.when((step >= FIRST // N) & direct)
    def _():
        body(edges[1])

    @pl.when(jnp.logical_not(direct))
    def _():
        body(edges[2])


SCALARS = pl.BlockSpec(memory_space=pltpu.SMEM)
FULL = sds((C, ROWS, S))
FULL_ROWS = sds((CELLS, S))
HALO_ROWS = H * ROWS
MESSAGE = sds((HALO_ROWS + 2 * NEAR, S))
HALO = sds((H, C, C, S))
EDGES = [sds((FIRST, EDGE, S)), sds((C - FIRST, EDGE, S)), sds((C - MIDDLE, EDGE, S))]


def halo_rows(x, z):
    return pl.ds(pl.multiple_of(z * ROWS + x * C, C), C)


def halves(y, half):
    return slice(y * C + half * 8, y * C + half * 8 + 8)


def pack_edges(s_ref, out_ref):
    out_ref[:, 0:96, :] = s_ref[:, 0:96, :]
    out_ref[:, 96:192, :] = s_ref[:, 160:256, :]


def pack_kernel(s_ref, edge_ref, head_ref, tail_ref):
    @pl.when(pl.program_id(0) < FIRST // N)
    def _():
        pack_edges(s_ref, edge_ref)

    for p in range(N):
        for z in range(H):
            head_ref[z, p] = s_ref[p, stride_rows(z), :]
            tail_ref[z, p] = s_ref[p, stride_rows(C - H + z), :]


def pack(s):
    return pl.pallas_call(
        pack_kernel,
        grid=(C // N,),
        in_specs=[plane_spec(ROWS, N)],
        out_specs=edge_specs()[:1] + [halo_spec(N), halo_spec(N)],
        out_shape=EDGES[:1] + [HALO, HALO],
        compiler_params=params(12),
        cost_estimate=cost(1 << 32, 6 << 20),
        name="pack",
    )(s)


def pack_rest_kernel(s_ref, inner_ref, message_ref, relay_ref, mid_ref):
    step = pl.program_id(0)
    inner = inner_ref[0] == 1
    mid_ref[...] = s_ref[:, 96:160, :]

    @pl.when(step >= MIDDLE // N)
    def _():
        pack_edges(s_ref, relay_ref)

    @pl.when((step >= FIRST // N) & (inner | (step < MIDDLE // N)))
    def _():
        for p in range(N):
            row = pl.multiple_of((step * N + p - FIRST) * EDGE, MID)
            message_ref[pl.ds(row, 96), :] = s_ref[p, 0:96, :]
            message_ref[pl.ds(row + 96, 96), :] = s_ref[p, 160:256, :]

    @pl.when(jnp.logical_not(inner))
    def _():
        for p in range(N):
            row = pl.multiple_of(MID_START + (step * N + p) * MID, MID)
            message_ref[pl.ds(row, MID), :] = s_ref[p, 96:160, :]


def pack_rest(s, inner):
    rows = (C - FIRST) * EDGE
    message, relay, mid = pl.pallas_call(
        pack_rest_kernel,
        grid=(C // N,),
        in_specs=[plane_spec(ROWS, N), SCALARS],
        out_specs=[whole(rows), edge_spec(MIDDLE, C), plane_spec(MID, N)],
        out_shape=[sds((rows, S)), EDGES[2], sds((C, MID, S))],
        compiler_params=params(12),
        cost_estimate=cost(1 << 31, 4 << 20),
        name="pack_rest",
    )(s, inner)
    return message, relay, mid


def stack(*pieces):
    def kernel(*refs):
        start = 0
        for ref, (_, rows) in zip(refs, pieces):
            refs[-1][start : start + rows, :] = ref[:rows, :]
            start += rows

    arrays = [array for array, _ in pieces]
    rows = sum(rows for _, rows in pieces)
    return pl.pallas_call(kernel, out_shape=sds((rows, S)), compiler_params=params(4), name="stack")(*arrays)


def along_x(s_ref, mate_ref, out_ref, add):
    def column(block, _):
        rows = pl.ds(pl.multiple_of(block * 8, 8), 8)
        ring = [mate_ref[C - H + i, rows, :] for i in range(H)]
        ring += [s_ref[x, rows, :] for x in range(C)]
        ring += [mate_ref[i, rows, :] for i in range(H)]
        for x in range(C):
            value = tap_sum(lambda i: ring[H + i], x)
            if add:
                value = value + out_ref[x, rows, :]
            out_ref[x, rows, :] = value
        return 0

    lax.fori_loop(0, ROWS // 8, column, 0)


def z_taps(ext_ref, y):
    return tap_sum(lambda k: ext_ref[y * 32 + 8 + k : y * 32 + 24 + k, :], 0)


def side_x_kernel(s_ref, mate_ref, out_ref):
    along_x(s_ref, mate_ref, out_ref, False)


def side_x(s, mate):
    return pl.pallas_call(
        side_x_kernel,
        out_shape=FULL,
        compiler_params=params(12),
        cost_estimate=cost(1 << 24, 6 << 20),
        name="side_x",
    )(s, mate)


def side_z_kernel(s_ref, part_ref, low_ref, high_ref, out_ref, ext_ref):
    def plane(x, _):
        for y in range(C):
            ext_ref[y * 32 + 8 : y * 32 + 24, :] = s_ref[x, y * C : (y + 1) * C, :]
        for z in range(H):
            ext_ref[pl.ds(2 + z, C, stride=32), :] = low_ref[z, x]
            ext_ref[pl.ds(24 + z, C, stride=32), :] = high_ref[z, x]
        for y in range(C):
            rows = slice(y * C, (y + 1) * C)
            out_ref[x, rows, :] = part_ref[x, rows, :] + z_taps(ext_ref, y)
        return 0

    lax.fori_loop(0, C, plane, 0)


def side_z(s, part, low, high):
    return pl.pallas_call(
        side_z_kernel,
        out_shape=FULL,
        scratch_shapes=[pltpu.VMEM((C * 32, S), F32)],
        compiler_params=params(14),
        cost_estimate=cost(1 << 24, 8 << 20),
        name="side_z",
    )(s, part, low, high)


def side_again_kernel(s_ref, mate_ref, out_ref, ext_ref):
    for y in range(C):
        ext_ref[y * 32 : y * 32 + 8, :] = jnp.zeros((8, S), F32)
        ext_ref[y * 32 + 24 : y * 32 + 32, :] = jnp.zeros((8, S), F32)

    def plane(x, _):
        for y in range(C):
            ext_ref[y * 32 + 8 : y * 32 + 24, :] = s_ref[x, y * C : (y + 1) * C, :]
        for y in range(C):
            out_ref[x, y * C : (y + 1) * C, :] = z_taps(ext_ref, y)
        return 0

    lax.fori_loop(0, C, plane, 0)
    along_x(s_ref, mate_ref, out_ref, True)


def side_again(s, mate):
    return pl.pallas_call(
        side_again_kernel,
        out_shape=FULL,
        scratch_shapes=[pltpu.VMEM((C * 32, S), F32)],
        compiler_params=params(12),
        cost_estimate=cost(1 << 25, 6 << 20),
        name="side_again",
    )(s, mate)


def tap_weight(distance):
    value = jnp.zeros(distance.shape, F32)
    for k in range(1, 7):
        value = jnp.where(distance == k, OFF[k - 1], value)
    return value


def ring_tables(coordinate):
    masks, factors = [], []
    for t in range(W):
        away = (coordinate - t) & 31
        masks.append(away == 0)
        factors.append(tap_weight(jnp.minimum(away, 32 - away)))
    return masks, factors


def spread_kernel(parcel_ref, vb_ref):
    def spread_row(row, _):
        line = (parcel_ref[pl.ds(24 + row, 1), :] + (DIAGONAL - filter_centre)) * (1.0 / filter_half)
        start = pl.multiple_of(row * 128, 128)
        vb_ref[pl.ds(start, 128), :] = jnp.broadcast_to(line, (128, 128)).T
        return 0

    lax.fori_loop(0, CELLS // 128, spread_row, 0, unroll=8)


def spread(parcel):
    return pl.pallas_call(
        spread_kernel,
        out_shape=FULL_ROWS,
        compiler_params=params(8),
        cost_estimate=cost(1 << 20, 2 << 20),
        name="spread",
    )(parcel)


def prep_kernel(*refs):
    own_ref, other_ref, corner_ref, vb_ref, s_ref, gg_ref, coef_ref, energy_ref, near_ref, table_ref = refs[:10]
    a1_ref, a1z_ref, a2_ref, a2s_ref = refs[10:]
    upper_x, upper_y = corner_ref[0] > 0, corner_ref[1] > 0
    for slab in range(3):
        own = [own_ref[slab * 48 + j * 24 : slab * 48 + j * 24 + 24, :] for j in range(2)]
        other = [other_ref[slab * 48 + j * 24 : slab * 48 + j * 24 + 24, :] for j in range(2)]
        lower = [jnp.where(upper_x, o, m) for m, o in zip(own, other)]
        higher = [jnp.where(upper_x, m, o) for m, o in zip(own, other)]
        ordered = []
        for pair in (lower, higher):
            ordered += [jnp.where(upper_y, pair[1], pair[0]), jnp.where(upper_y, pair[0], pair[1])]
        for j in range(4):
            near_ref[slab * 96 + j * 24 : slab * 96 + j * 24 + 24, :] = ordered[j]
    blank = jnp.zeros((16, 128), F32)
    for block in range(6):
        rows = near_ref[pl.ds(block, NEAR, stride=6), :]
        table_ref[block * 128 : block * 128 + 128, :] = jnp.concatenate([rows, blank, rows, blank]).T
    at = TAPS + 3 - 640
    energy_ref[...] = jnp.broadcast_to(rows[:, at : at + 1] * (1.0 / filter_half), (NEAR, S))

    shape = (8, 128)
    sub = lax.broadcasted_iota(jnp.int32, shape, 0)
    lane = lax.broadcasted_iota(jnp.int32, shape, 1)
    first_lanes = lane < 64
    sites = [jnp.broadcast_to(table_ref[TAPS + d : TAPS + d + 1, :], shape).astype(jnp.int32) for d in range(3)]
    px = sites[0] - corner_ref[0]
    py = sites[1] - corner_ref[1]
    pz = (sites[2] & 15) + (((lane & 63) >> 4) - 1) * C
    zero = jnp.zeros(shape, F32)

    dz = sub + (lane >> 6) * 8 - pz + R
    z_masks = [dz == t for t in range(W)]
    z_factors = [tap_weight(jnp.abs(dz - t)) for t in range(W)]

    def place_z(ij, _):
        acc = zero
        along = zero
        for t in range(W):
            row = jnp.broadcast_to(table_ref[pl.ds(ij * W + t, 1), :], shape)
            acc = jnp.where(z_masks[t], row, acc)
            along = along + z_factors[t] * row
        a1_ref[ij] = acc
        a1z_ref[ij] = along
        return 0

    lax.fori_loop(0, W * W, place_z, 0, unroll=3)

    def place_y(y, _):
        masks, factors = ring_tables(y - py + R)
        for i in range(W):
            acc = zero
            along = zero
            moved = zero
            for t in range(W):
                value = a1_ref[i * W + t]
                acc = jnp.where(masks[t], value, acc)
                along = along + factors[t] * value
                moved = jnp.where(masks[t], a1z_ref[i * W + t], moved)
            a2_ref[i, y] = acc
            a2s_ref[i, y] = along + moved
        return 0

    lax.fori_loop(0, C, place_y, 0)

    def place_x(x, _):
        masks, factors = ring_tables(x - px + R)

        def per_y(y, _):
            row = pl.multiple_of(x * ROWS + y * C, C)
            acc = zero
            along = zero
            moved = zero
            for t in range(W):
                value = a2_ref[t, y]
                acc = jnp.where(masks[t], value, acc)
                along = along + factors[t] * value
                moved = jnp.where(masks[t], a2s_ref[t, y], moved)
            v = vb_ref[pl.ds(row, C), :]
            moved = along + moved + jnp.where(first_lanes, v[:8], v[8:]) * acc
            lower = jnp.where(first_lanes, acc, pltpu.roll(moved, 64, 1))
            upper = jnp.where(first_lanes, pltpu.roll(acc, 64, 1), moved)
            high, low = split(jnp.concatenate([lower, upper], axis=0))
            gg_ref[0, pl.ds(row, C), :] = high
            gg_ref[1, pl.ds(row, C), :] = low
            return 0

        lax.fori_loop(0, C, per_y, 0, unroll=16)
        return 0

    lax.fori_loop(0, C, place_x, 0)

    coef_ref[...] = jnp.zeros((3, NEAR, S), F32)

    def contract(x, _):
        rows = pl.ds(pl.multiple_of(x * 2 * ROWS, ROWS), 2 * ROWS)
        g_high, g_low = gg_ref[0, rows, :], gg_ref[1, rows, :]
        t_high, t_low = g_high.T, g_low.T
        high, low = split(s_ref[rows, :])
        got = mm(t_high, high) + (mm(t_high, low) + mm(t_low, high))
        t_high, t_low = t_high[:NEAR], t_low[:NEAR]
        pair = mm(t_high, g_high) + (mm(t_high, g_low) + mm(t_low, g_high))
        for slab in range(3):
            rows = slice(slab * C, slab * C + C)
            coef_ref[slab, 0:16] += got[rows]
            coef_ref[slab, 16:32] += got[64 + slab * C : 80 + slab * C]
            coef_ref[slab, 32:48] += pair[rows]
        return 0

    lax.fori_loop(0, C // 2, contract, 0, unroll=2)


def prep(parcels, corner, vb, s):
    vmem = pl.BlockSpec(memory_space=pltpu.VMEM)
    return pl.pallas_call(
        prep_kernel,
        in_specs=[vmem] * 2 + [pl.BlockSpec(memory_space=pltpu.SMEM), vmem, vmem],
        out_shape=[sds((2, CELLS, S), BF16), sds((3, NEAR, S)), sds((NEAR, S))],
        scratch_shapes=[
            pltpu.VMEM((288, 128), F32),
            pltpu.VMEM((768, 128), F32),
            pltpu.VMEM((W * W, 8, 128), F32),
            pltpu.VMEM((W * W, 8, 128), F32),
            pltpu.VMEM((W, C, 8, 128), F32),
            pltpu.VMEM((W, C, 8, 128), F32),
        ],
        compiler_params=params(16),
        cost_estimate=cost(1 << 27, 10 << 20),
        name="prep",
    )(*parcels, corner, vb, s.reshape(CELLS, S))


def move_pair(shares, away):
    lane = lax.broadcasted_iota(jnp.int32, (16, 128), 1)
    keep = (lane < 32) if away < 0 else (lane >= 16) & (lane < 48)
    pair = jnp.where(keep, pltpu.roll(shares[32:48], (away * 16) % 128, 1), 0.0)
    return jnp.concatenate([shares[0:32], pair])


def first_kernel(s_ref, side_ref, vb_ref, *refs):
    inner_ref, part_ref, mate_ref, q_ref, mix_ref, head_ref, tail_ref = refs[3:]
    step = pl.program_id(0)

    @pl.when(step == 0)
    def _():
        for j in range(2):
            rows = slice(HALO_ROWS + j * NEAR, HALO_ROWS + (j + 1) * NEAR)
            head_ref[rows, :] = part_ref[j] + mate_ref[j]
            tail_ref[rows, :] = part_ref[j + 1] + mate_ref[j + 1]

    def planes(edge_ref):
        for p in range(N):
            for half in range(2):
                ring = {y: s_ref[p, halves(y, half), :] for y in range(C)}
                for y in range(H):
                    ring[C + y] = edge_ref[p, halves(y, half), :]
                    ring[y - H] = edge_ref[p, halves(H + y, half), :]
                for y in range(C):
                    rows = halves(y, half)
                    dy = tap_sum(lambda i: ring[i], y)
                    q = dy + vb_ref[p, rows, :] * ring[y]
                    q_ref[p, rows, :] = q
                    mix_ref[p, rows, :] = side_ref[p, rows, :] + q + dy
            for z in range(H):
                rows = halo_rows(step * N + p, z)
                head_ref[rows, :] = mix_ref[p, stride_rows(z), :]
                tail_ref[rows, :] = mix_ref[p, stride_rows(C - H + z), :]

    for_piece(refs[:3], inner_ref, planes)


def make_first(s, side_part, vb, edges, inner, part, part_mate):
    shares = pl.BlockSpec((3, NEAR, S), lambda i: (0, 0, 0))
    return pl.pallas_call(
        first_kernel,
        grid=(C // N,),
        in_specs=[plane_spec(ROWS, N)] * 3 + edge_specs() + [SCALARS] + [shares] * 2,
        out_specs=[plane_spec(ROWS, N), plane_spec(ROWS, N), whole(MESSAGE.shape[0]), whole(MESSAGE.shape[0])],
        out_shape=[FULL, FULL, MESSAGE, MESSAGE],
        compiler_params=params(16),
        cost_estimate=cost(1 << 24, 14 << 20),
        name="first",
    )(s, side_part, vb, *edges, inner, part, part_mate)


def base_kernel(s_ref, mid_ref, vb_ref, vb_mate_ref, q_ref, side_ref, part_ref, *refs):
    inner_ref, message_ref, out_ref, middle_ref = refs[3:]
    step = pl.program_id(0)
    inner = inner_ref[0] == 1

    @pl.when(inner)
    def _():
        middle_ref[...] = mid_ref[...]

    @pl.when(jnp.logical_not(inner))
    def _():
        for p in range(N):
            middle_ref[p] = message_ref[pl.ds(pl.multiple_of(MID_START + (step * N + p) * MID, MID), MID), :]

    def planes(edge_ref):
        for p in range(N):
            for half in range(2):

                def other(y, p=p, half=half):
                    if y < H:
                        return edge_ref[p, halves(y, half), :]
                    if y < C - H:
                        return middle_ref[p, halves(y - H, half), :]
                    return edge_ref[p, halves(y - 4, half), :]

                ring = [s_ref[p, halves(y, half), :] for y in range(C)] + [other(y) for y in range(C)]
                q = {y: q_ref[p, halves(y, half), :] for y in range(C)}
                for y in list(range(H)) + list(range(C - H, C)):
                    v = vb_mate_ref[p, halves(y, half), :]
                    q[C + y] = tap_sum(lambda i: ring[i % 32], C + y) + v * ring[C + y]
                for y in range(C):
                    rows = halves(y, half)
                    total = tap_sum(lambda i: q[i % 32], y)
                    total = total + vb_ref[p, rows, :] * (side_ref[p, rows, :] + q[y])
                    out_ref[p, rows, :] = 2.0 * (total + part_ref[p, rows, :]) - ring[y]

    for_piece(refs[:3], inner_ref, planes)


def make_base(s, mid, vb, vb_mate, q, side_part, part, edges, inner):
    return pl.pallas_call(
        base_kernel,
        grid=(C // N,),
        in_specs=[plane_spec(ROWS, N), plane_spec(MID, N)]
        + [plane_spec(ROWS, N)] * 5
        + edge_specs()
        + [SCALARS, whole((C - FIRST) * EDGE)],
        out_specs=plane_spec(ROWS, N),
        out_shape=FULL,
        scratch_shapes=[pltpu.VMEM((N, MID, S), F32)],
        compiler_params=params(16),
        cost_estimate=cost(1 << 25, 16 << 20),
        name="base",
    )(s, mid, vb, vb_mate, q, side_part, part, *edges, inner, edges[1].reshape(-1, S))


def second_kernel(base_ref, low_ref, high_ref, gg_high_ref, gg_low_ref, *rest):
    part_ref, mate_ref, energy_ref, upper_ref, second_ref, keep_ref, give_ref, gram_ref, cross_ref, w_ref, halo_ref = rest
    step = pl.program_id(0)

    @pl.when(step == 0)
    def _():
        gram_ref[...] = jnp.zeros((S, S), F32)
        cross_ref[...] = jnp.zeros((S, S), F32)
        w_ref[...] = jnp.zeros((S, S), F32)
        halo_ref[...] = jnp.zeros((B, ROWS, S), F32)
        mine = [part_ref[j] + mate_ref[j] for j in range(3)]
        below = [move_pair(low_ref[HALO_ROWS + j * NEAR : HALO_ROWS + (j + 1) * NEAR, :], -1) for j in range(2)]
        above = [move_pair(high_ref[HALO_ROWS + j * NEAR : HALO_ROWS + (j + 1) * NEAR, :], 1) for j in range(2)]
        slabs = [mine[0] + below[0], mine[1] + below[1] + above[0], mine[2] + above[1]]
        near = jnp.concatenate([slab[0:16] for slab in slabs]) * energy_ref[...]
        lane = lax.broadcasted_iota(jnp.int32, (NEAR, S), 1)
        pair = jnp.where(lane < NEAR, jnp.concatenate([slab[32:48] for slab in slabs]), 0.0)
        two = jnp.concatenate([slab[16:32] for slab in slabs])
        two = two + exact(pair, jnp.concatenate([near, jnp.zeros((S - NEAR, S), F32)]))
        w_ref[0:NEAR, :] = 2.0 * energy_ref[...] * two
        w_ref[64 : 64 + NEAR, :] = 2.0 * near

    for p in range(B):
        low = [low_ref[halo_rows(step * B + p, j), :] for j in range(H)]
        high = [high_ref[halo_rows(step * B + p, j), :] for j in range(H)]
        for z in range(H):
            add = sum((2.0 * OFF[k - 1]) * low[z - k + H] for k in range(z + 1, H + 1))
            halo_ref[p, stride_rows(z), :] = add
            add = sum((2.0 * OFF[H + j - z - 1]) * high[j] for j in range(z + 1))
            halo_ref[p, stride_rows(C - H + z), :] = add

    w_high, w_low = split(w_ref[...])
    w_twice = jnp.concatenate([w_high, w_high])
    gram = jnp.zeros((S, 2 * S), F32)
    for p in range(B):
        g_high, g_low = gg_high_ref[0, p], gg_low_ref[0, p]
        near = mm(jnp.concatenate([g_high, g_low], axis=1), w_twice) + mm(g_high, w_low)
        value = base_ref[p] + halo_ref[p] + near
        second_ref[p] = value
        s_high, s_low = split(value)
        gram += mm(s_high.T, jnp.concatenate([s_high, s_low], axis=1))
    gram_ref[...] += gram[:, :S]
    cross_ref[...] += gram[:, S:]

    @pl.when(step == STEPS - 1)
    def _():
        cross = cross_ref[...]
        gram = (gram_ref[...] + (cross + cross.T)) * (1.0 / NCELLS)
        upper = upper_ref[0] == 1
        keep_ref[...] = jnp.where(upper, gram[S // 2 :], gram[: S // 2])
        give_ref[...] = jnp.where(upper, gram[: S // 2], gram[S // 2 :])


def make_second(base, halos, gg, shares, upper):
    three = pl.BlockSpec((3, NEAR, S), lambda i: (0, 0, 0))
    return pl.pallas_call(
        second_kernel,
        grid=(STEPS,),
        in_specs=[plane_spec()]
        + [whole(MESSAGE.shape[0])] * 2
        + [part_spec(0), part_spec(1), three, three, whole(NEAR), SCALARS],
        out_specs=[plane_spec(), whole(S // 2), whole(S // 2)],
        out_shape=[FULL, sds((S // 2, S)), sds((S // 2, S))],
        scratch_shapes=[pltpu.VMEM((S, S), F32)] * 3 + [pltpu.VMEM((B, ROWS, S), F32)],
        compiler_params=params(16),
        cost_estimate=cost(1 << 27, 8 << 20),
        name="second",
    )(base, *halos, gg, gg, *shares, upper)


def exact(a, b):
    return jnp.dot(a, b, precision=lax.Precision.HIGHEST, preferred_element_type=F32)


def inverse_factor(gram_ref, a_ref, x_ref, state_ref):
    row = lax.broadcasted_iota(jnp.int32, (S, S), 0)
    column = lax.broadcasted_iota(jnp.int32, (S, S), 1)
    unit = jnp.where(row == column, 1.0, 0.0)
    gram = gram_ref[...]
    diagonal = jnp.where(row == column, gram, 0.0)
    down = lax.rsqrt(jnp.sum(diagonal, axis=1, keepdims=True))
    across = lax.rsqrt(jnp.sum(diagonal, axis=0, keepdims=True))
    a_ref[...] = gram * down * across
    x_ref[...] = unit

    def residual():
        x = x_ref[...]
        return unit - exact(exact(x, a_ref[...]), x.T)

    def size(e):
        return jnp.sum(e * e)

    def improve(e):
        lower = jnp.where(row > column, e, jnp.where(row == column, 0.5 * e, 0.0))
        x_ref[...] += exact(lower, x_ref[...])

    state_ref[0] = 0
    start = unit - a_ref[...]
    start_size = size(start)

    @pl.when(start_size < 0.16)
    def _():
        improve(start)
        state_ref[0] = jnp.where(start_size < 1e-6, 2, 1)

    for _ in range(5):

        @pl.when(state_ref[0] == 1)
        def _():
            e = residual()
            e_size = size(e)
            improve(e)
            state_ref[0] = jnp.where(e_size < 1e-6, 2, 1)

    @pl.when(state_ref[0] != 2)
    def _():
        x_ref[...] = unit
        lanes = lax.broadcasted_iota(jnp.int32, (1, S), 1)

        def step(j, _):
            line = a_ref[pl.ds(j, 1), :]
            scale = lax.rsqrt(jnp.sum(jnp.where(lanes == j, line, 0.0), axis=1, keepdims=True))
            a = a_ref[...]
            factor = jnp.sum(jnp.where(column == j, a, 0.0), axis=1, keepdims=True) * scale
            factor = jnp.where(row[:, :1] > j, factor, 0.0)
            x_line = x_ref[pl.ds(j, 1), :] * scale
            a_ref[...] = a - factor * (line * scale)
            x_ref[...] = jnp.where(row == j, x_line, x_ref[...] - factor * x_line)
            return 0

        lax.fori_loop(0, S, step, 0)

    x_ref[...] = x_ref[...] * across


def turn_kernel(second_ref, own_ref, other_ref, upper_ref, out_ref, gram_ref, a_ref, x_ref, i_high_ref, i_low_ref, state_ref):
    @pl.when(pl.program_id(0) == 0)
    def _():
        upper = upper_ref[0] == 1
        gram_ref[: S // 2, :] = jnp.where(upper, other_ref[...], own_ref[...])
        gram_ref[S // 2 :, :] = jnp.where(upper, own_ref[...], other_ref[...])
        inverse_factor(gram_ref, a_ref, x_ref, state_ref)
        i_high, i_low = split(x_ref[...].T)
        i_high_ref[...] = i_high
        i_low_ref[...] = i_low

    i_high, i_low = i_high_ref[...], i_low_ref[...]
    i_twice = jnp.concatenate([i_high, i_high])
    for p in range(B):
        high, low = split(second_ref[p])
        out_ref[p] = mm(jnp.concatenate([high, low], axis=1), i_twice) + mm(high, i_low)


def turn(second, own, other, upper):
    return pl.pallas_call(
        turn_kernel,
        grid=(STEPS,),
        in_specs=[plane_spec(), whole(S // 2), whole(S // 2), SCALARS],
        out_specs=plane_spec(),
        out_shape=FULL,
        scratch_shapes=[pltpu.VMEM((S, S), F32)] * 3 + [pltpu.VMEM((S, S), BF16)] * 2 + [pltpu.SMEM((1,), jnp.int32)],
        compiler_params=params(16),
        cost_estimate=cost(1 << 28, 4 << 20),
        name="turn",
    )(second, own, other, upper)


def per_device(states, potential, atom_sites, projectors, energies):
    gx, gy = lax.axis_index("gx"), lax.axis_index("gy")
    depth = lax.axis_size("gzs")
    count = 4 * depth
    barrier = lax.optimization_barrier

    def send(value, flip=0, move=0):
        def target(d):
            return (d // depth * depth ^ flip) + (d + move) % depth

        return lax.ppermute(value, AXES, [(d, target(d)) for d in range(count)])

    over_x, over_y = 2 * depth, depth
    inner_ones = [d for d in range(count) if d % 4 in (1, 2)]
    outer_ones = [d for d in range(count) if d % 4 in (0, 3)]
    inner = ((lax.axis_index("gzs") + 1) // 2 % 2).astype(jnp.int32).reshape(1)
    s = states.reshape(C, ROWS, S)
    mate = send(s, over_x)
    pot = potential.reshape(32, 128)
    corner = jnp.stack([gx * C, gy * C]).astype(jnp.int32)
    upper = gx.astype(jnp.int32).reshape(1)
    atoms = jnp.concatenate(
        [projectors.reshape(4, TAPS), atom_sites.astype(F32), energies[:, None], jnp.zeros((4, 768 - TAPS - 4), F32)],
        axis=1,
    ).reshape(24, 128)
    to_pack, pot, corner, upper, inner, atoms = barrier((s, pot, corner, upper, inner, atoms))

    parcel = stack((atoms, 24), (pot, 32))
    parcel_mate = send(parcel, over_y)
    one_edge, head, tail = pack(to_pack)
    one_edge = send(one_edge, over_y)
    pair = stack((parcel, 24), (parcel_mate, 24))
    column = stack((send(pair, 0, 1), 48), (pair, 48), (send(pair, 0, -1), 48))
    column_mate = send(column, over_x)
    message, relay, mid = pack_rest(s, inner)
    vb = spread(parcel)
    beside = side_x(s, mate)
    column_mate, head, tail, relay, beside = barrier((column_mate, head, tail, relay, beside))
    low, high = send(tail, 0, 1), send(head, 0, -1)
    relayed = lax.ppermute(relay, AXES, [(d, d ^ over_y ^ 1) for d in outer_ones])
    column_mate, one_edge = barrier((column_mate, one_edge))
    gg, part, energy = prep([column, column_mate], corner, vb, s)
    part, message = barrier((part, message))
    message = send(message, over_y)
    side_part = side_z(s, beside, low, high)
    side_part, relayed = barrier((side_part, relayed))
    relayed = lax.ppermute(relayed, AXES, [(d, d ^ 1) for d in inner_ones])
    planes = vb.reshape(C, ROWS, S)

    part = part + send(part, over_x)
    part_mate = send(part, over_y)
    message = message.reshape(C - FIRST, EDGE, S)
    edges = [one_edge, message, relayed]
    q, mix, head, tail = make_first(s, side_part, planes, edges, inner, part, part_mate)
    halos = [send(tail, 0, 1), send(head, 0, -1)]
    mate = send(mix, over_x)
    mid, part_mate = barrier((mid, part_mate))
    mid = lax.ppermute(mid, AXES, [(d, d ^ over_y) for d in inner_ones])
    planes_mate = spread(parcel_mate).reshape(C, ROWS, S)
    part_two = side_again(mix, mate)
    base = make_base(s, mid, planes, planes_mate, q, side_part, part_two, edges, inner)
    gg = gg.reshape(2, C, ROWS, S)
    second, own, give = make_second(base, halos, gg, [part, part_mate, energy], upper)

    own = own + send(give, over_x)
    for flip in (32, 36, 1, 3, 8, 24):
        own = own + lax.ppermute(own, AXES, [(d, d ^ flip) for d in range(count)])
    return turn(second, own, send(own, over_x), upper).reshape(C, C, C, S)


def solution(mesh):
    return jax.shard_map(
        per_device,
        mesh=mesh,
        in_specs=(
            P("gx", "gy", "gzs", None),
            P("gx", "gy", "gzs"),
            P(("gx", "gy", "gzs"), None),
            P(("gx", "gy", "gzs"), None, None, None),
            P(("gx", "gy", "gzs")),
        ),
        out_specs=P("gx", "gy", "gzs", None),
        check_vma=False,
    )
```

```python
import math

import jax
import jax.numpy as jnp
from jax import lax
from jax.experimental import pallas as pl
from jax.experimental.pallas import tpu as pltpu
from jax.sharding import PartitionSpec as P

AXES = ("gx", "gy", "gzs")
H = 6
C = 16
ROWS = C * C
CELLS = C * C * C
NCELLS = 32 * 32 * 512
S = 128
W = 9
R = 4
NEAR = 48
TAPS = W * W * W
F32 = jnp.float32
BF16 = jnp.bfloat16

grid_step = 0.6
filter_centre = 36.0
filter_half = 26.0


def weights():
    taps = []
    for k in range(1, 7):
        top = 2.0 * (-1) ** (k + 1) * math.factorial(6) ** 2
        under = k * k * math.factorial(6 - k) * math.factorial(6 + k)
        taps.append(top / under)
    scale = -0.5 / (grid_step * grid_step)
    off = [scale * t / filter_half for t in taps]
    diagonal = 3.0 * scale * (-2.0 * sum(taps))
    return off, diagonal


OFF, DIAGONAL = weights()


def params(mib):
    return pltpu.CompilerParams(vmem_limit_bytes=mib * 1024 * 1024)


def cost(flops, nbytes):
    return pl.CostEstimate(flops=flops, bytes_accessed=nbytes, transcendentals=0)


def sds(shape, dtype=F32):
    return jax.ShapeDtypeStruct(shape, dtype)


def split(value):
    high = value.astype(BF16)
    low = (value - high.astype(F32)).astype(BF16)
    return high, low


def mm(a, b):
    return jnp.dot(a, b, preferred_element_type=F32)


def tap_sum(at, index):
    total = None
    for k in range(1, 7):
        term = OFF[k - 1] * (at(index + k) + at(index - k))
        total = term if total is None else total + term
    return total


B = 4
STEPS = C // B
N = 2
FIRST = 8
MIDDLE = 10
EDGE = 192
MID = 64
MID_START = (MIDDLE - FIRST) * EDGE


def stride_rows(z):
    return pl.ds(z, C, stride=C)


def plane_spec(rows=ROWS, planes=B):
    return pl.BlockSpec((planes, rows, S), lambda i: (i, 0, 0))


def halo_spec(planes=B):
    return pl.BlockSpec((H, planes, C, S), lambda i: (0, i, 0, 0))


def part_spec(part):
    return pl.BlockSpec((1, B, ROWS, S), lambda i: (part, i, 0, 0))


def whole(rows=S):
    return pl.BlockSpec((rows, S), lambda i: (0, 0))


def edge_spec(start, stop):
    return pl.BlockSpec((N, EDGE, S), lambda i: (jnp.clip(i - start // N, 0, (stop - start) // N - 1), 0, 0))


def edge_specs():
    return [edge_spec(0, FIRST), edge_spec(FIRST, C), edge_spec(MIDDLE, C)]


def for_piece(edges, inner_ref, body):
    step = pl.program_id(0)
    direct = (inner_ref[0] == 1) | (step < MIDDLE // N)

    @pl.when(step < FIRST // N)
    def _():
        body(edges[0])

    @pl.when((step >= FIRST // N) & direct)
    def _():
        body(edges[1])

    @pl.when(jnp.logical_not(direct))
    def _():
        body(edges[2])


SCALARS = pl.BlockSpec(memory_space=pltpu.SMEM)
FULL = sds((C, ROWS, S))
FULL_ROWS = sds((CELLS, S))
HALO_ROWS = H * ROWS
MESSAGE = sds((HALO_ROWS + 2 * NEAR, S))
HALO = sds((H, C, C, S))
EDGES = [sds((FIRST, EDGE, S)), sds((C - FIRST, EDGE, S)), sds((C - MIDDLE, EDGE, S))]


def halo_rows(x, z):
    return pl.ds(pl.multiple_of(z * ROWS + x * C, C), C)


def halves(y, half):
    return slice(y * C + half * 8, y * C + half * 8 + 8)


def pack_edges(s_ref, out_ref):
    out_ref[:, 0:96, :] = s_ref[:, 0:96, :]
    out_ref[:, 96:192, :] = s_ref[:, 160:256, :]


def pack_kernel(s_ref, edge_ref, head_ref, tail_ref):
    @pl.when(pl.program_id(0) < FIRST // N)
    def _():
        pack_edges(s_ref, edge_ref)

    for p in range(N):
        for z in range(H):
            head_ref[z, p] = s_ref[p, stride_rows(z), :]
            tail_ref[z, p] = s_ref[p, stride_rows(C - H + z), :]


def pack(s):
    return pl.pallas_call(
        pack_kernel,
        grid=(C // N,),
        in_specs=[plane_spec(ROWS, N)],
        out_specs=edge_specs()[:1] + [halo_spec(N), halo_spec(N)],
        out_shape=EDGES[:1] + [HALO, HALO],
        compiler_params=params(12),
        cost_estimate=cost(1 << 32, 6 << 20),
        name="pack",
    )(s)


def pack_rest_kernel(s_ref, inner_ref, message_ref, relay_ref, mid_ref):
    step = pl.program_id(0)
    inner = inner_ref[0] == 1
    mid_ref[...] = s_ref[:, 96:160, :]

    @pl.when(step >= MIDDLE // N)
    def _():
        pack_edges(s_ref, relay_ref)

    @pl.when((step >= FIRST // N) & (inner | (step < MIDDLE // N)))
    def _():
        for p in range(N):
            row = pl.multiple_of((step * N + p - FIRST) * EDGE, MID)
            message_ref[pl.ds(row, 96), :] = s_ref[p, 0:96, :]
            message_ref[pl.ds(row + 96, 96), :] = s_ref[p, 160:256, :]

    @pl.when(jnp.logical_not(inner))
    def _():
        for p in range(N):
            row = pl.multiple_of(MID_START + (step * N + p) * MID, MID)
            message_ref[pl.ds(row, MID), :] = s_ref[p, 96:160, :]


def pack_rest(s, inner):
    rows = (C - FIRST) * EDGE
    message, relay, mid = pl.pallas_call(
        pack_rest_kernel,
        grid=(C // N,),
        in_specs=[plane_spec(ROWS, N), SCALARS],
        out_specs=[whole(rows), edge_spec(MIDDLE, C), plane_spec(MID, N)],
        out_shape=[sds((rows, S)), EDGES[2], sds((C, MID, S))],
        compiler_params=params(12),
        cost_estimate=cost(1 << 31, 4 << 20),
        name="pack_rest",
    )(s, inner)
    return message, relay, mid


def stack(*pieces):
    def kernel(*refs):
        start = 0
        for ref, (_, rows) in zip(refs, pieces):
            refs[-1][start : start + rows, :] = ref[:rows, :]
            start += rows

    arrays = [array for array, _ in pieces]
    rows = sum(rows for _, rows in pieces)
    return pl.pallas_call(kernel, out_shape=sds((rows, S)), compiler_params=params(4), name="stack")(*arrays)


def along_x(s_ref, mate_ref, out_ref, add):
    def column(block, _):
        rows = pl.ds(pl.multiple_of(block * 8, 8), 8)
        ring = [mate_ref[C - H + i, rows, :] for i in range(H)]
        ring += [s_ref[x, rows, :] for x in range(C)]
        ring += [mate_ref[i, rows, :] for i in range(H)]
        for x in range(C):
            value = tap_sum(lambda i: ring[H + i], x)
            if add:
                value = value + out_ref[x, rows, :]
            out_ref[x, rows, :] = value
        return 0

    lax.fori_loop(0, ROWS // 8, column, 0)


def z_taps(ext_ref, y):
    return tap_sum(lambda k: ext_ref[y * 32 + 8 + k : y * 32 + 24 + k, :], 0)


def side_x_kernel(s_ref, mate_ref, out_ref):
    along_x(s_ref, mate_ref, out_ref, False)


def side_x(s, mate):
    return pl.pallas_call(
        side_x_kernel,
        out_shape=FULL,
        compiler_params=params(12),
        cost_estimate=cost(1 << 24, 6 << 20),
        name="side_x",
    )(s, mate)


def side_z_kernel(s_ref, part_ref, low_ref, high_ref, out_ref, ext_ref):
    def plane(x, _):
        for y in range(C):
            ext_ref[y * 32 + 8 : y * 32 + 24, :] = s_ref[x, y * C : (y + 1) * C, :]
        for z in range(H):
            ext_ref[pl.ds(2 + z, C, stride=32), :] = low_ref[z, x]
            ext_ref[pl.ds(24 + z, C, stride=32), :] = high_ref[z, x]
        for y in range(C):
            rows = slice(y * C, (y + 1) * C)
            out_ref[x, rows, :] = part_ref[x, rows, :] + z_taps(ext_ref, y)
        return 0

    lax.fori_loop(0, C, plane, 0)


def side_z(s, part, low, high):
    return pl.pallas_call(
        side_z_kernel,
        out_shape=FULL,
        scratch_shapes=[pltpu.VMEM((C * 32, S), F32)],
        compiler_params=params(14),
        cost_estimate=cost(1 << 24, 8 << 20),
        name="side_z",
    )(s, part, low, high)


def side_again_kernel(s_ref, mate_ref, out_ref, ext_ref):
    for y in range(C):
        ext_ref[y * 32 : y * 32 + 8, :] = jnp.zeros((8, S), F32)
        ext_ref[y * 32 + 24 : y * 32 + 32, :] = jnp.zeros((8, S), F32)

    def plane(x, _):
        for y in range(C):
            ext_ref[y * 32 + 8 : y * 32 + 24, :] = s_ref[x, y * C : (y + 1) * C, :]
        for y in range(C):
            out_ref[x, y * C : (y + 1) * C, :] = z_taps(ext_ref, y)
        return 0

    lax.fori_loop(0, C, plane, 0)
    along_x(s_ref, mate_ref, out_ref, True)


def side_again(s, mate):
    return pl.pallas_call(
        side_again_kernel,
        out_shape=FULL,
        scratch_shapes=[pltpu.VMEM((C * 32, S), F32)],
        compiler_params=params(12),
        cost_estimate=cost(1 << 25, 6 << 20),
        name="side_again",
    )(s, mate)


def tap_weight(distance):
    value = jnp.zeros(distance.shape, F32)
    for k in range(1, 7):
        value = jnp.where(distance == k, OFF[k - 1], value)
    return value


def ring_tables(coordinate):
    masks, factors = [], []
    for t in range(W):
        away = (coordinate - t) & 31
        masks.append(away == 0)
        factors.append(tap_weight(jnp.minimum(away, 32 - away)))
    return masks, factors


def spread_kernel(parcel_ref, vb_ref):
    def spread_row(row, _):
        line = (parcel_ref[pl.ds(24 + row, 1), :] + (DIAGONAL - filter_centre)) * (1.0 / filter_half)
        start = pl.multiple_of(row * 128, 128)
        vb_ref[pl.ds(start, 128), :] = jnp.broadcast_to(line, (128, 128)).T
        return 0

    lax.fori_loop(0, CELLS // 128, spread_row, 0, unroll=8)


def spread(parcel):
    return pl.pallas_call(
        spread_kernel,
        out_shape=FULL_ROWS,
        compiler_params=params(8),
        cost_estimate=cost(1 << 20, 2 << 20),
        name="spread",
    )(parcel)


def prep_kernel(*refs):
    own_ref, other_ref, corner_ref, vb_ref, s_ref, gg_ref, coef_ref, energy_ref, near_ref, table_ref = refs[:10]
    a1_ref, a1z_ref, a2_ref, a2s_ref = refs[10:]
    upper_x, upper_y = corner_ref[0] > 0, corner_ref[1] > 0
    for slab in range(3):
        own = [own_ref[slab * 48 + j * 24 : slab * 48 + j * 24 + 24, :] for j in range(2)]
        other = [other_ref[slab * 48 + j * 24 : slab * 48 + j * 24 + 24, :] for j in range(2)]
        lower = [jnp.where(upper_x, o, m) for m, o in zip(own, other)]
        higher = [jnp.where(upper_x, m, o) for m, o in zip(own, other)]
        ordered = []
        for pair in (lower, higher):
            ordered += [jnp.where(upper_y, pair[1], pair[0]), jnp.where(upper_y, pair[0], pair[1])]
        for j in range(4):
            near_ref[slab * 96 + j * 24 : slab * 96 + j * 24 + 24, :] = ordered[j]
    blank = jnp.zeros((16, 128), F32)
    for block in range(6):
        rows = near_ref[pl.ds(block, NEAR, stride=6), :]
        table_ref[block * 128 : block * 128 + 128, :] = jnp.concatenate([rows, blank, rows, blank]).T
    at = TAPS + 3 - 640
    energy_ref[...] = jnp.broadcast_to(rows[:, at : at + 1] * (1.0 / filter_half), (NEAR, S))

    shape = (8, 128)
    sub = lax.broadcasted_iota(jnp.int32, shape, 0)
    lane = lax.broadcasted_iota(jnp.int32, shape, 1)
    first_lanes = lane < 64
    sites = [jnp.broadcast_to(table_ref[TAPS + d : TAPS + d + 1, :], shape).astype(jnp.int32) for d in range(3)]
    px = sites[0] - corner_ref[0]
    py = sites[1] - corner_ref[1]
    pz = (sites[2] & 15) + (((lane & 63) >> 4) - 1) * C
    zero = jnp.zeros(shape, F32)

    dz = sub + (lane >> 6) * 8 - pz + R
    z_masks = [dz == t for t in range(W)]
    z_factors = [tap_weight(jnp.abs(dz - t)) for t in range(W)]

    def place_z(ij, _):
        acc = zero
        along = zero
        for t in range(W):
            row = jnp.broadcast_to(table_ref[pl.ds(ij * W + t, 1), :], shape)
            acc = jnp.where(z_masks[t], row, acc)
            along = along + z_factors[t] * row
        a1_ref[ij] = acc
        a1z_ref[ij] = along
        return 0

    lax.fori_loop(0, W * W, place_z, 0, unroll=3)

    def place_y(y, _):
        masks, factors = ring_tables(y - py + R)
        for i in range(W):
            acc = zero
            along = zero
            moved = zero
            for t in range(W):
                value = a1_ref[i * W + t]
                acc = jnp.where(masks[t], value, acc)
                along = along + factors[t] * value
                moved = jnp.where(masks[t], a1z_ref[i * W + t], moved)
            a2_ref[i, y] = acc
            a2s_ref[i, y] = along + moved
        return 0

    lax.fori_loop(0, C, place_y, 0)

    def place_x(x, _):
        masks, factors = ring_tables(x - px + R)

        def per_y(y, _):
            row = pl.multiple_of(x * ROWS + y * C, C)
            acc = zero
            along = zero
            moved = zero
            for t in range(W):
                value = a2_ref[t, y]
                acc = jnp.where(masks[t], value, acc)
                along = along + factors[t] * value
                moved = jnp.where(masks[t], a2s_ref[t, y], moved)
            v = vb_ref[pl.ds(row, C), :]
            moved = along + moved + jnp.where(first_lanes, v[:8], v[8:]) * acc
            lower = jnp.where(first_lanes, acc, pltpu.roll(moved, 64, 1))
            upper = jnp.where(first_lanes, pltpu.roll(acc, 64, 1), moved)
            high, low = split(jnp.concatenate([lower, upper], axis=0))
            gg_ref[0, pl.ds(row, C), :] = high
            gg_ref[1, pl.ds(row, C), :] = low
            return 0

        lax.fori_loop(0, C, per_y, 0, unroll=16)
        return 0

    lax.fori_loop(0, C, place_x, 0)

    coef_ref[...] = jnp.zeros((3, NEAR, S), F32)

    def contract(x, _):
        rows = pl.ds(pl.multiple_of(x * 2 * ROWS, ROWS), 2 * ROWS)
        g_high, g_low = gg_ref[0, rows, :], gg_ref[1, rows, :]
        t_high, t_low = g_high.T, g_low.T
        high, low = split(s_ref[rows, :])
        got = mm(t_high, high) + (mm(t_high, low) + mm(t_low, high))
        t_high, t_low = t_high[:NEAR], t_low[:NEAR]
        pair = mm(t_high, g_high) + (mm(t_high, g_low) + mm(t_low, g_high))
        for slab in range(3):
            rows = slice(slab * C, slab * C + C)
            coef_ref[slab, 0:16] += got[rows]
            coef_ref[slab, 16:32] += got[64 + slab * C : 80 + slab * C]
            coef_ref[slab, 32:48] += pair[rows]
        return 0

    lax.fori_loop(0, C // 2, contract, 0, unroll=2)


def prep(parcels, corner, vb, s):
    vmem = pl.BlockSpec(memory_space=pltpu.VMEM)
    return pl.pallas_call(
        prep_kernel,
        in_specs=[vmem] * 2 + [pl.BlockSpec(memory_space=pltpu.SMEM), vmem, vmem],
        out_shape=[sds((2, CELLS, S), BF16), sds((3, NEAR, S)), sds((NEAR, S))],
        scratch_shapes=[
            pltpu.VMEM((288, 128), F32),
            pltpu.VMEM((768, 128), F32),
            pltpu.VMEM((W * W, 8, 128), F32),
            pltpu.VMEM((W * W, 8, 128), F32),
            pltpu.VMEM((W, C, 8, 128), F32),
            pltpu.VMEM((W, C, 8, 128), F32),
        ],
        compiler_params=params(16),
        cost_estimate=cost(1 << 27, 10 << 20),
        name="prep",
    )(*parcels, corner, vb, s.reshape(CELLS, S))


def move_pair(shares, away):
    lane = lax.broadcasted_iota(jnp.int32, (16, 128), 1)
    keep = (lane < 32) if away < 0 else (lane >= 16) & (lane < 48)
    pair = jnp.where(keep, pltpu.roll(shares[32:48], (away * 16) % 128, 1), 0.0)
    return jnp.concatenate([shares[0:32], pair])


def first_kernel(s_ref, side_ref, vb_ref, *refs):
    inner_ref, part_ref, mate_ref, q_ref, mix_ref, head_ref, tail_ref = refs[3:]
    step = pl.program_id(0)

    @pl.when(step == 0)
    def _():
        for j in range(2):
            rows = slice(HALO_ROWS + j * NEAR, HALO_ROWS + (j + 1) * NEAR)
            head_ref[rows, :] = part_ref[j] + mate_ref[j]
            tail_ref[rows, :] = part_ref[j + 1] + mate_ref[j + 1]

    def planes(edge_ref):
        for p in range(N):
            for half in range(2):
                ring = {y: s_ref[p, halves(y, half), :] for y in range(C)}
                for y in range(H):
                    ring[C + y] = edge_ref[p, halves(y, half), :]
                    ring[y - H] = edge_ref[p, halves(H + y, half), :]
                for y in range(C):
                    rows = halves(y, half)
                    dy = tap_sum(lambda i: ring[i], y)
                    q = dy + vb_ref[p, rows, :] * ring[y]
                    q_ref[p, rows, :] = q
                    mix_ref[p, rows, :] = side_ref[p, rows, :] + q + dy
            for z in range(H):
                rows = halo_rows(step * N + p, z)
                head_ref[rows, :] = mix_ref[p, stride_rows(z), :]
                tail_ref[rows, :] = mix_ref[p, stride_rows(C - H + z), :]

    for_piece(refs[:3], inner_ref, planes)


def make_first(s, side_part, vb, edges, inner, part, part_mate):
    shares = pl.BlockSpec((3, NEAR, S), lambda i: (0, 0, 0))
    return pl.pallas_call(
        first_kernel,
        grid=(C // N,),
        in_specs=[plane_spec(ROWS, N)] * 3 + edge_specs() + [SCALARS] + [shares] * 2,
        out_specs=[plane_spec(ROWS, N), plane_spec(ROWS, N), whole(MESSAGE.shape[0]), whole(MESSAGE.shape[0])],
        out_shape=[FULL, FULL, MESSAGE, MESSAGE],
        compiler_params=params(16),
        cost_estimate=cost(1 << 24, 14 << 20),
        name="first",
    )(s, side_part, vb, *edges, inner, part, part_mate)


def base_kernel(s_ref, mid_ref, vb_ref, vb_mate_ref, q_ref, side_ref, part_ref, *refs):
    inner_ref, message_ref, out_ref, middle_ref = refs[3:]
    step = pl.program_id(0)
    inner = inner_ref[0] == 1

    @pl.when(inner)
    def _():
        middle_ref[...] = mid_ref[...]

    @pl.when(jnp.logical_not(inner))
    def _():
        for p in range(N):
            middle_ref[p] = message_ref[pl.ds(pl.multiple_of(MID_START + (step * N + p) * MID, MID), MID), :]

    def planes(edge_ref):
        for p in range(N):
            for half in range(2):

                def other(y, p=p, half=half):
                    if y < H:
                        return edge_ref[p, halves(y, half), :]
                    if y < C - H:
                        return middle_ref[p, halves(y - H, half), :]
                    return edge_ref[p, halves(y - 4, half), :]

                ring = [s_ref[p, halves(y, half), :] for y in range(C)] + [other(y) for y in range(C)]
                q = {y: q_ref[p, halves(y, half), :] for y in range(C)}
                for y in list(range(H)) + list(range(C - H, C)):
                    v = vb_mate_ref[p, halves(y, half), :]
                    q[C + y] = tap_sum(lambda i: ring[i % 32], C + y) + v * ring[C + y]
                for y in range(C):
                    rows = halves(y, half)
                    total = tap_sum(lambda i: q[i % 32], y)
                    total = total + vb_ref[p, rows, :] * (side_ref[p, rows, :] + q[y])
                    out_ref[p, rows, :] = 2.0 * (total + part_ref[p, rows, :]) - ring[y]

    for_piece(refs[:3], inner_ref, planes)


def make_base(s, mid, vb, vb_mate, q, side_part, part, edges, inner):
    return pl.pallas_call(
        base_kernel,
        grid=(C // N,),
        in_specs=[plane_spec(ROWS, N), plane_spec(MID, N)]
        + [plane_spec(ROWS, N)] * 5
        + edge_specs()
        + [SCALARS, whole((C - FIRST) * EDGE)],
        out_specs=plane_spec(ROWS, N),
        out_shape=FULL,
        scratch_shapes=[pltpu.VMEM((N, MID, S), F32)],
        compiler_params=params(16),
        cost_estimate=cost(1 << 25, 16 << 20),
        name="base",
    )(s, mid, vb, vb_mate, q, side_part, part, *edges, inner, edges[1].reshape(-1, S))


def second_kernel(base_ref, low_ref, high_ref, gg_high_ref, gg_low_ref, *rest):
    part_ref, mate_ref, energy_ref, upper_ref, second_ref, keep_ref, give_ref, gram_ref, cross_ref, w_ref, halo_ref = rest
    step = pl.program_id(0)

    @pl.when(step == 0)
    def _():
        gram_ref[...] = jnp.zeros((S, S), F32)
        cross_ref[...] = jnp.zeros((S, S), F32)
        w_ref[...] = jnp.zeros((S, S), F32)
        halo_ref[...] = jnp.zeros((B, ROWS, S), F32)
        mine = [part_ref[j] + mate_ref[j] for j in range(3)]
        below = [move_pair(low_ref[HALO_ROWS + j * NEAR : HALO_ROWS + (j + 1) * NEAR, :], -1) for j in range(2)]
        above = [move_pair(high_ref[HALO_ROWS + j * NEAR : HALO_ROWS + (j + 1) * NEAR, :], 1) for j in range(2)]
        slabs = [mine[0] + below[0], mine[1] + below[1] + above[0], mine[2] + above[1]]
        near = jnp.concatenate([slab[0:16] for slab in slabs]) * energy_ref[...]
        lane = lax.broadcasted_iota(jnp.int32, (NEAR, S), 1)
        pair = jnp.where(lane < NEAR, jnp.concatenate([slab[32:48] for slab in slabs]), 0.0)
        two = jnp.concatenate([slab[16:32] for slab in slabs])
        two = two + exact(pair, jnp.concatenate([near, jnp.zeros((S - NEAR, S), F32)]))
        w_ref[0:NEAR, :] = 2.0 * energy_ref[...] * two
        w_ref[64 : 64 + NEAR, :] = 2.0 * near

    for p in range(B):
        low = [low_ref[halo_rows(step * B + p, j), :] for j in range(H)]
        high = [high_ref[halo_rows(step * B + p, j), :] for j in range(H)]
        for z in range(H):
            add = sum((2.0 * OFF[k - 1]) * low[z - k + H] for k in range(z + 1, H + 1))
            halo_ref[p, stride_rows(z), :] = add
            add = sum((2.0 * OFF[H + j - z - 1]) * high[j] for j in range(z + 1))
            halo_ref[p, stride_rows(C - H + z), :] = add

    w_high, w_low = split(w_ref[...])
    w_twice = jnp.concatenate([w_high, w_high])
    gram = jnp.zeros((S, 2 * S), F32)
    for p in range(B):
        g_high, g_low = gg_high_ref[0, p], gg_low_ref[0, p]
        near = mm(jnp.concatenate([g_high, g_low], axis=1), w_twice) + mm(g_high, w_low)
        value = base_ref[p] + halo_ref[p] + near
        second_ref[p] = value
        s_high, s_low = split(value)
        gram += mm(s_high.T, jnp.concatenate([s_high, s_low], axis=1))
    gram_ref[...] += gram[:, :S]
    cross_ref[...] += gram[:, S:]

    @pl.when(step == STEPS - 1)
    def _():
        cross = cross_ref[...]
        gram = (gram_ref[...] + (cross + cross.T)) * (1.0 / NCELLS)
        upper = upper_ref[0] == 1
        keep_ref[...] = jnp.where(upper, gram[S // 2 :], gram[: S // 2])
        give_ref[...] = jnp.where(upper, gram[: S // 2], gram[S // 2 :])


def make_second(base, halos, gg, shares, upper):
    three = pl.BlockSpec((3, NEAR, S), lambda i: (0, 0, 0))
    return pl.pallas_call(
        second_kernel,
        grid=(STEPS,),
        in_specs=[plane_spec()]
        + [whole(MESSAGE.shape[0])] * 2
        + [part_spec(0), part_spec(1), three, three, whole(NEAR), SCALARS],
        out_specs=[plane_spec(), whole(S // 2), whole(S // 2)],
        out_shape=[FULL, sds((S // 2, S)), sds((S // 2, S))],
        scratch_shapes=[pltpu.VMEM((S, S), F32)] * 3 + [pltpu.VMEM((B, ROWS, S), F32)],
        compiler_params=params(16),
        cost_estimate=cost(1 << 27, 8 << 20),
        name="second",
    )(base, *halos, gg, gg, *shares, upper)


def exact(a, b):
    return jnp.dot(a, b, precision=lax.Precision.HIGHEST, preferred_element_type=F32)


def inverse_factor(gram_ref, a_ref, x_ref, state_ref):
    row = lax.broadcasted_iota(jnp.int32, (S, S), 0)
    column = lax.broadcasted_iota(jnp.int32, (S, S), 1)
    unit = jnp.where(row == column, 1.0, 0.0)
    gram = gram_ref[...]
    diagonal = jnp.where(row == column, gram, 0.0)
    down = lax.rsqrt(jnp.sum(diagonal, axis=1, keepdims=True))
    across = lax.rsqrt(jnp.sum(diagonal, axis=0, keepdims=True))
    a_ref[...] = gram * down * across
    x_ref[...] = unit

    def residual():
        x = x_ref[...]
        return unit - exact(exact(x, a_ref[...]), x.T)

    def size(e):
        return jnp.sum(e * e)

    def improve(e):
        lower = jnp.where(row > column, e, jnp.where(row == column, 0.5 * e, 0.0))
        x_ref[...] += exact(lower, x_ref[...])

    state_ref[0] = 0
    start = unit - a_ref[...]
    start_size = size(start)

    @pl.when(start_size < 0.16)
    def _():
        improve(start)
        state_ref[0] = jnp.where(start_size < 1e-6, 2, 1)

    for _ in range(5):

        @pl.when(state_ref[0] == 1)
        def _():
            e = residual()
            e_size = size(e)
            improve(e)
            state_ref[0] = jnp.where(e_size < 1e-6, 2, 1)

    @pl.when(state_ref[0] != 2)
    def _():
        x_ref[...] = unit
        lanes = lax.broadcasted_iota(jnp.int32, (1, S), 1)

        def step(j, _):
            line = a_ref[pl.ds(j, 1), :]
            scale = lax.rsqrt(jnp.sum(jnp.where(lanes == j, line, 0.0), axis=1, keepdims=True))
            a = a_ref[...]
            factor = jnp.sum(jnp.where(column == j, a, 0.0), axis=1, keepdims=True) * scale
            factor = jnp.where(row[:, :1] > j, factor, 0.0)
            x_line = x_ref[pl.ds(j, 1), :] * scale
            a_ref[...] = a - factor * (line * scale)
            x_ref[...] = jnp.where(row == j, x_line, x_ref[...] - factor * x_line)
            return 0

        lax.fori_loop(0, S, step, 0)

    x_ref[...] = x_ref[...] * across


def turn_kernel(second_ref, own_ref, other_ref, upper_ref, out_ref, gram_ref, a_ref, x_ref, i_high_ref, i_low_ref, state_ref):
    @pl.when(pl.program_id(0) == 0)
    def _():
        upper = upper_ref[0] == 1
        gram_ref[: S // 2, :] = jnp.where(upper, other_ref[...], own_ref[...])
        gram_ref[S // 2 :, :] = jnp.where(upper, own_ref[...], other_ref[...])
        inverse_factor(gram_ref, a_ref, x_ref, state_ref)
        i_high, i_low = split(x_ref[...].T)
        i_high_ref[...] = i_high
        i_low_ref[...] = i_low

    i_high, i_low = i_high_ref[...], i_low_ref[...]
    i_twice = jnp.concatenate([i_high, i_high])
    for p in range(B):
        high, low = split(second_ref[p])
        out_ref[p] = mm(jnp.concatenate([high, low], axis=1), i_twice) + mm(high, i_low)


def turn(second, own, other, upper):
    return pl.pallas_call(
        turn_kernel,
        grid=(STEPS,),
        in_specs=[plane_spec(), whole(S // 2), whole(S // 2), SCALARS],
        out_specs=plane_spec(),
        out_shape=FULL,
        scratch_shapes=[pltpu.VMEM((S, S), F32)] * 3 + [pltpu.VMEM((S, S), BF16)] * 2 + [pltpu.SMEM((1,), jnp.int32)],
        compiler_params=params(16),
        cost_estimate=cost(1 << 28, 4 << 20),
        name="turn",
    )(second, own, other, upper)


def per_device(states, potential, atom_sites, projectors, energies):
    gx, gy = lax.axis_index("gx"), lax.axis_index("gy")
    depth = lax.axis_size("gzs")
    count = 4 * depth
    barrier = lax.optimization_barrier

    def send(value, flip=0, move=0):
        def target(d):
            return (d // depth * depth ^ flip) + (d + move) % depth

        return lax.ppermute(value, AXES, [(d, target(d)) for d in range(count)])

    over_x, over_y = 2 * depth, depth
    inner_ones = [d for d in range(count) if d % 4 in (1, 2)]
    outer_ones = [d for d in range(count) if d % 4 in (0, 3)]
    inner = ((lax.axis_index("gzs") + 1) // 2 % 2).astype(jnp.int32).reshape(1)
    s = states.reshape(C, ROWS, S)
    mate = send(s, over_x)
    pot = potential.reshape(32, 128)
    corner = jnp.stack([gx * C, gy * C]).astype(jnp.int32)
    upper = gx.astype(jnp.int32).reshape(1)
    atoms = jnp.concatenate(
        [projectors.reshape(4, TAPS), atom_sites.astype(F32), energies[:, None], jnp.zeros((4, 768 - TAPS - 4), F32)],
        axis=1,
    ).reshape(24, 128)
    to_pack, pot, corner, upper, inner, atoms = barrier((s, pot, corner, upper, inner, atoms))

    parcel = stack((atoms, 24), (pot, 32))
    parcel_mate = send(parcel, over_y)
    one_edge, head, tail = pack(to_pack)
    one_edge = send(one_edge, over_y)
    parcel_mate, head = barrier((parcel_mate, head))
    pair = stack((parcel, 24), (parcel_mate, 24))
    column = stack((send(pair, 0, 1), 48), (pair, 48), (send(pair, 0, -1), 48))
    column_mate = send(column, over_x)
    message, relay, mid = pack_rest(s, inner)
    vb = spread(parcel)
    beside = side_x(s, mate)
    column_mate, head, tail, relay, message, beside = barrier((column_mate, head, tail, relay, message, beside))
    low, high = send(tail, 0, 1), send(head, 0, -1)
    relayed = lax.ppermute(relay, AXES, [(d, d ^ over_y ^ 1) for d in outer_ones])
    message = send(message, over_y)
    column_mate, one_edge = barrier((column_mate, one_edge))
    gg, part, energy = prep([column, column_mate], corner, vb, s)
    part, relayed = barrier((part, relayed))
    side_part = side_z(s, beside, low, high)
    relayed = lax.ppermute(relayed, AXES, [(d, d ^ 1) for d in inner_ones])
    planes = vb.reshape(C, ROWS, S)

    part = part + send(part, over_x)
    part_mate = send(part, over_y)
    message = message.reshape(C - FIRST, EDGE, S)
    edges = [one_edge, message, relayed]
    q, mix, head, tail = make_first(s, side_part, planes, edges, inner, part, part_mate)
    halos = [send(tail, 0, 1), send(head, 0, -1)]
    mate = send(mix, over_x)
    mid, part_mate = barrier((mid, part_mate))
    mid = lax.ppermute(mid, AXES, [(d, d ^ over_y) for d in inner_ones])
    planes_mate = spread(parcel_mate).reshape(C, ROWS, S)
    part_two = side_again(mix, mate)
    base = make_base(s, mid, planes, planes_mate, q, side_part, part_two, edges, inner)
    gg = gg.reshape(2, C, ROWS, S)
    second, own, give = make_second(base, halos, gg, [part, part_mate, energy], upper)

    own = own + send(give, over_x)
    for flip in (32, 36, 1, 3, 8, 24):
        own = own + lax.ppermute(own, AXES, [(d, d ^ flip) for d in range(count)])
    return turn(second, own, send(own, over_x), upper).reshape(C, C, C, S)


def solution(mesh):
    return jax.shard_map(
        per_device,
        mesh=mesh,
        in_specs=(
            P("gx", "gy", "gzs", None),
            P("gx", "gy", "gzs"),
            P(("gx", "gy", "gzs"), None),
            P(("gx", "gy", "gzs"), None, None, None),
            P(("gx", "gy", "gzs")),
        ),
        out_specs=P("gx", "gy", "gzs", None),
        check_vma=False,
    )
```

```python
import math

import jax
import jax.numpy as jnp
from jax import lax
from jax.experimental import pallas as pl
from jax.experimental.pallas import tpu as pltpu
from jax.sharding import PartitionSpec as P

AXES = ("gx", "gy", "gzs")
H = 6
C = 16
ROWS = C * C
CELLS = C * C * C
NCELLS = 32 * 32 * 512
S = 128
W = 9
R = 4
NEAR = 48
TAPS = W * W * W
F32 = jnp.float32
BF16 = jnp.bfloat16

grid_step = 0.6
filter_centre = 36.0
filter_half = 26.0


def weights():
    taps = []
    for k in range(1, 7):
        top = 2.0 * (-1) ** (k + 1) * math.factorial(6) ** 2
        under = k * k * math.factorial(6 - k) * math.factorial(6 + k)
        taps.append(top / under)
    scale = -0.5 / (grid_step * grid_step)
    off = [scale * t / filter_half for t in taps]
    diagonal = 3.0 * scale * (-2.0 * sum(taps))
    return off, diagonal


OFF, DIAGONAL = weights()


def params(mib):
    return pltpu.CompilerParams(vmem_limit_bytes=mib * 1024 * 1024)


def cost(flops, nbytes):
    return pl.CostEstimate(flops=flops, bytes_accessed=nbytes, transcendentals=0)


def sds(shape, dtype=F32):
    return jax.ShapeDtypeStruct(shape, dtype)


def split(value):
    high = value.astype(BF16)
    low = (value - high.astype(F32)).astype(BF16)
    return high, low


def mm(a, b):
    return jnp.dot(a, b, preferred_element_type=F32)


def tap_sum(at, index):
    total = None
    for k in range(1, 7):
        term = OFF[k - 1] * (at(index + k) + at(index - k))
        total = term if total is None else total + term
    return total


B = 4
STEPS = C // B
N = 2
FIRST = 4
MIDDLE = 10
EDGE = 192
MID = 64
MID_START = (MIDDLE - FIRST) * EDGE


def stride_rows(z):
    return pl.ds(z, C, stride=C)


def plane_spec(rows=ROWS, planes=B):
    return pl.BlockSpec((planes, rows, S), lambda i: (i, 0, 0))


def halo_spec(planes=B):
    return pl.BlockSpec((H, planes, C, S), lambda i: (0, i, 0, 0))


def part_spec(part):
    return pl.BlockSpec((1, B, ROWS, S), lambda i: (part, i, 0, 0))


def whole(rows=S):
    return pl.BlockSpec((rows, S), lambda i: (0, 0))


def edge_spec(start, stop):
    return pl.BlockSpec((N, EDGE, S), lambda i: (jnp.clip(i - start // N, 0, (stop - start) // N - 1), 0, 0))


def edge_specs():
    return [edge_spec(0, FIRST), edge_spec(FIRST, C), edge_spec(MIDDLE, C)]


def for_piece(edges, inner_ref, body):
    step = pl.program_id(0)
    direct = (inner_ref[0] == 1) | (step < MIDDLE // N)

    @pl.when(step < FIRST // N)
    def _():
        body(edges[0])

    @pl.when((step >= FIRST // N) & direct)
    def _():
        body(edges[1])

    @pl.when(jnp.logical_not(direct))
    def _():
        body(edges[2])


SCALARS = pl.BlockSpec(memory_space=pltpu.SMEM)
FULL = sds((C, ROWS, S))
FULL_ROWS = sds((CELLS, S))
HALO_ROWS = H * ROWS
MESSAGE = sds((HALO_ROWS + 2 * NEAR, S))
HALO = sds((H, C, C, S))
EDGES = [sds((FIRST, EDGE, S)), sds((C - FIRST, EDGE, S)), sds((C - MIDDLE, EDGE, S))]


def halo_rows(x, z):
    return pl.ds(pl.multiple_of(z * ROWS + x * C, C), C)


def halves(y, half):
    return slice(y * C + half * 8, y * C + half * 8 + 8)


def pack_edges(s_ref, out_ref):
    out_ref[:, 0:96, :] = s_ref[:, 0:96, :]
    out_ref[:, 96:192, :] = s_ref[:, 160:256, :]


def pack_kernel(s_ref, edge_ref, relay_ref, head_ref, tail_ref):
    @pl.when(pl.program_id(0) >= MIDDLE // N)
    def _():
        pack_edges(s_ref, relay_ref)

    @pl.when(pl.program_id(0) < FIRST // N)
    def _():
        pack_edges(s_ref, edge_ref)

    for p in range(N):
        for z in range(H):
            head_ref[z, p] = s_ref[p, stride_rows(z), :]
            tail_ref[z, p] = s_ref[p, stride_rows(C - H + z), :]


def pack(s):
    return pl.pallas_call(
        pack_kernel,
        grid=(C // N,),
        in_specs=[plane_spec(ROWS, N)],
        out_specs=[edge_spec(0, FIRST), edge_spec(MIDDLE, C), halo_spec(N), halo_spec(N)],
        out_shape=[EDGES[0], EDGES[2], HALO, HALO],
        compiler_params=params(12),
        cost_estimate=cost(1 << 32, 6 << 20),
        name="pack",
    )(s)


def pack_rest_kernel(s_ref, inner_ref, message_ref, mid_ref):
    step = pl.program_id(0)
    inner = inner_ref[0] == 1
    mid_ref[...] = s_ref[:, 96:160, :]

    @pl.when((step >= FIRST // N) & (inner | (step < MIDDLE // N)))
    def _():
        for p in range(N):
            row = pl.multiple_of((step * N + p - FIRST) * EDGE, MID)
            message_ref[pl.ds(row, 96), :] = s_ref[p, 0:96, :]
            message_ref[pl.ds(row + 96, 96), :] = s_ref[p, 160:256, :]

    @pl.when(jnp.logical_not(inner))
    def _():
        for p in range(N):
            row = pl.multiple_of(MID_START + (step * N + p) * MID, MID)
            message_ref[pl.ds(row, MID), :] = s_ref[p, 96:160, :]


def pack_rest(s, inner):
    rows = (C - FIRST) * EDGE
    return pl.pallas_call(
        pack_rest_kernel,
        grid=(C // N,),
        in_specs=[plane_spec(ROWS, N), SCALARS],
        out_specs=[whole(rows), plane_spec(MID, N)],
        out_shape=[sds((rows, S)), sds((C, MID, S))],
        compiler_params=params(12),
        cost_estimate=cost(1 << 31, 4 << 20),
        name="pack_rest",
    )(s, inner)


def stack(*pieces):
    def kernel(*refs):
        start = 0
        for ref, (_, rows) in zip(refs, pieces):
            refs[-1][start : start + rows, :] = ref[:rows, :]
            start += rows

    arrays = [array for array, _ in pieces]
    rows = sum(rows for _, rows in pieces)
    return pl.pallas_call(kernel, out_shape=sds((rows, S)), compiler_params=params(4), name="stack")(*arrays)


def along_x(s_ref, mate_ref, out_ref, add):
    def column(block, _):
        rows = pl.ds(pl.multiple_of(block * 8, 8), 8)
        ring = [mate_ref[C - H + i, rows, :] for i in range(H)]
        ring += [s_ref[x, rows, :] for x in range(C)]
        ring += [mate_ref[i, rows, :] for i in range(H)]
        for x in range(C):
            value = tap_sum(lambda i: ring[H + i], x)
            if add:
                value = value + out_ref[x, rows, :]
            out_ref[x, rows, :] = value
        return 0

    lax.fori_loop(0, ROWS // 8, column, 0)


def z_taps(ext_ref, y):
    return tap_sum(lambda k: ext_ref[y * 32 + 8 + k : y * 32 + 24 + k, :], 0)


def side_x_kernel(s_ref, mate_ref, out_ref):
    along_x(s_ref, mate_ref, out_ref, False)


def side_x(s, mate):
    return pl.pallas_call(
        side_x_kernel,
        out_shape=FULL,
        compiler_params=params(12),
        cost_estimate=cost(1 << 24, 6 << 20),
        name="side_x",
    )(s, mate)


def side_z_kernel(s_ref, part_ref, low_ref, high_ref, out_ref, ext_ref):
    def plane(x, _):
        for y in range(C):
            ext_ref[y * 32 + 8 : y * 32 + 24, :] = s_ref[x, y * C : (y + 1) * C, :]
        for z in range(H):
            ext_ref[pl.ds(2 + z, C, stride=32), :] = low_ref[z, x]
            ext_ref[pl.ds(24 + z, C, stride=32), :] = high_ref[z, x]
        for y in range(C):
            rows = slice(y * C, (y + 1) * C)
            out_ref[x, rows, :] = part_ref[x, rows, :] + z_taps(ext_ref, y)
        return 0

    lax.fori_loop(0, C, plane, 0)


def side_z(s, part, low, high):
    return pl.pallas_call(
        side_z_kernel,
        out_shape=FULL,
        scratch_shapes=[pltpu.VMEM((C * 32, S), F32)],
        compiler_params=params(14),
        cost_estimate=cost(1 << 24, 8 << 20),
        name="side_z",
    )(s, part, low, high)


def side_again_kernel(s_ref, mate_ref, out_ref, ext_ref):
    for y in range(C):
        ext_ref[y * 32 : y * 32 + 8, :] = jnp.zeros((8, S), F32)
        ext_ref[y * 32 + 24 : y * 32 + 32, :] = jnp.zeros((8, S), F32)

    def plane(x, _):
        for y in range(C):
            ext_ref[y * 32 + 8 : y * 32 + 24, :] = s_ref[x, y * C : (y + 1) * C, :]
        for y in range(C):
            out_ref[x, y * C : (y + 1) * C, :] = z_taps(ext_ref, y)
        return 0

    lax.fori_loop(0, C, plane, 0)
    along_x(s_ref, mate_ref, out_ref, True)


def side_again(s, mate):
    return pl.pallas_call(
        side_again_kernel,
        out_shape=FULL,
        scratch_shapes=[pltpu.VMEM((C * 32, S), F32)],
        compiler_params=params(12),
        cost_estimate=cost(1 << 25, 6 << 20),
        name="side_again",
    )(s, mate)


def tap_weight(distance):
    value = jnp.zeros(distance.shape, F32)
    for k in range(1, 7):
        value = jnp.where(distance == k, OFF[k - 1], value)
    return value


def ring_tables(coordinate):
    masks, factors = [], []
    for t in range(W):
        away = (coordinate - t) & 31
        masks.append(away == 0)
        factors.append(tap_weight(jnp.minimum(away, 32 - away)))
    return masks, factors


def spread_kernel(parcel_ref, vb_ref):
    def spread_row(row, _):
        line = (parcel_ref[pl.ds(24 + row, 1), :] + (DIAGONAL - filter_centre)) * (1.0 / filter_half)
        start = pl.multiple_of(row * 128, 128)
        vb_ref[pl.ds(start, 128), :] = jnp.broadcast_to(line, (128, 128)).T
        return 0

    lax.fori_loop(0, CELLS // 128, spread_row, 0, unroll=8)


def spread(parcel):
    return pl.pallas_call(
        spread_kernel,
        out_shape=FULL_ROWS,
        compiler_params=params(8),
        cost_estimate=cost(1 << 20, 2 << 20),
        name="spread",
    )(parcel)


def prep_kernel(*refs):
    own_ref, other_ref, corner_ref, vb_ref, s_ref, gg_ref, coef_ref, energy_ref, near_ref, table_ref = refs[:10]
    a1_ref, a1z_ref, a2_ref, a2s_ref = refs[10:]
    upper_x, upper_y = corner_ref[0] > 0, corner_ref[1] > 0
    for slab in range(3):
        own = [own_ref[slab * 48 + j * 24 : slab * 48 + j * 24 + 24, :] for j in range(2)]
        other = [other_ref[slab * 48 + j * 24 : slab * 48 + j * 24 + 24, :] for j in range(2)]
        lower = [jnp.where(upper_x, o, m) for m, o in zip(own, other)]
        higher = [jnp.where(upper_x, m, o) for m, o in zip(own, other)]
        ordered = []
        for pair in (lower, higher):
            ordered += [jnp.where(upper_y, pair[1], pair[0]), jnp.where(upper_y, pair[0], pair[1])]
        for j in range(4):
            near_ref[slab * 96 + j * 24 : slab * 96 + j * 24 + 24, :] = ordered[j]
    blank = jnp.zeros((16, 128), F32)
    for block in range(6):
        rows = near_ref[pl.ds(block, NEAR, stride=6), :]
        table_ref[block * 128 : block * 128 + 128, :] = jnp.concatenate([rows, blank, rows, blank]).T
    at = TAPS + 3 - 640
    energy_ref[...] = jnp.broadcast_to(rows[:, at : at + 1] * (1.0 / filter_half), (NEAR, S))

    shape = (8, 128)
    sub = lax.broadcasted_iota(jnp.int32, shape, 0)
    lane = lax.broadcasted_iota(jnp.int32, shape, 1)
    first_lanes = lane < 64
    sites = [jnp.broadcast_to(table_ref[TAPS + d : TAPS + d + 1, :], shape).astype(jnp.int32) for d in range(3)]
    px = sites[0] - corner_ref[0]
    py = sites[1] - corner_ref[1]
    pz = (sites[2] & 15) + (((lane & 63) >> 4) - 1) * C
    zero = jnp.zeros(shape, F32)

    dz = sub + (lane >> 6) * 8 - pz + R
    z_masks = [dz == t for t in range(W)]
    z_factors = [tap_weight(jnp.abs(dz - t)) for t in range(W)]

    def place_z(ij, _):
        acc = zero
        along = zero
        for t in range(W):
            row = jnp.broadcast_to(table_ref[pl.ds(ij * W + t, 1), :], shape)
            acc = jnp.where(z_masks[t], row, acc)
            along = along + z_factors[t] * row
        a1_ref[ij] = acc
        a1z_ref[ij] = along
        return 0

    lax.fori_loop(0, W * W, place_z, 0, unroll=3)

    def place_y(y, _):
        masks, factors = ring_tables(y - py + R)
        for i in range(W):
            acc = zero
            along = zero
            moved = zero
            for t in range(W):
                value = a1_ref[i * W + t]
                acc = jnp.where(masks[t], value, acc)
                along = along + factors[t] * value
                moved = jnp.where(masks[t], a1z_ref[i * W + t], moved)
            a2_ref[i, y] = acc
            a2s_ref[i, y] = along + moved
        return 0

    lax.fori_loop(0, C, place_y, 0)

    def place_x(x, _):
        masks, factors = ring_tables(x - px + R)

        def per_y(y, _):
            row = pl.multiple_of(x * ROWS + y * C, C)
            acc = zero
            along = zero
            moved = zero
            for t in range(W):
                value = a2_ref[t, y]
                acc = jnp.where(masks[t], value, acc)
                along = along + factors[t] * value
                moved = jnp.where(masks[t], a2s_ref[t, y], moved)
            v = vb_ref[pl.ds(row, C), :]
            moved = along + moved + jnp.where(first_lanes, v[:8], v[8:]) * acc
            lower = jnp.where(first_lanes, acc, pltpu.roll(moved, 64, 1))
            upper = jnp.where(first_lanes, pltpu.roll(acc, 64, 1), moved)
            high, low = split(jnp.concatenate([lower, upper], axis=0))
            gg_ref[0, pl.ds(row, C), :] = high
            gg_ref[1, pl.ds(row, C), :] = low
            return 0

        lax.fori_loop(0, C, per_y, 0, unroll=16)
        return 0

    lax.fori_loop(0, C, place_x, 0)

    coef_ref[...] = jnp.zeros((3, NEAR, S), F32)

    def contract(x, _):
        rows = pl.ds(pl.multiple_of(x * 2 * ROWS, ROWS), 2 * ROWS)
        g_high, g_low = gg_ref[0, rows, :], gg_ref[1, rows, :]
        t_high, t_low = g_high.T, g_low.T
        high, low = split(s_ref[rows, :])
        got = mm(t_high, high) + (mm(t_high, low) + mm(t_low, high))
        t_high, t_low = t_high[:NEAR], t_low[:NEAR]
        pair = mm(t_high, g_high) + (mm(t_high, g_low) + mm(t_low, g_high))
        for slab in range(3):
            rows = slice(slab * C, slab * C + C)
            coef_ref[slab, 0:16] += got[rows]
            coef_ref[slab, 16:32] += got[64 + slab * C : 80 + slab * C]
            coef_ref[slab, 32:48] += pair[rows]
        return 0

    lax.fori_loop(0, C // 2, contract, 0, unroll=2)


def prep(parcels, corner, vb, s):
    vmem = pl.BlockSpec(memory_space=pltpu.VMEM)
    return pl.pallas_call(
        prep_kernel,
        in_specs=[vmem] * 2 + [pl.BlockSpec(memory_space=pltpu.SMEM), vmem, vmem],
        out_shape=[sds((2, CELLS, S), BF16), sds((3, NEAR, S)), sds((NEAR, S))],
        scratch_shapes=[
            pltpu.VMEM((288, 128), F32),
            pltpu.VMEM((768, 128), F32),
            pltpu.VMEM((W * W, 8, 128), F32),
            pltpu.VMEM((W * W, 8, 128), F32),
            pltpu.VMEM((W, C, 8, 128), F32),
            pltpu.VMEM((W, C, 8, 128), F32),
        ],
        compiler_params=params(16),
        cost_estimate=cost(1 << 27, 10 << 20),
        name="prep",
    )(*parcels, corner, vb, s.reshape(CELLS, S))


def move_pair(shares, away):
    lane = lax.broadcasted_iota(jnp.int32, (16, 128), 1)
    keep = (lane < 32) if away < 0 else (lane >= 16) & (lane < 48)
    pair = jnp.where(keep, pltpu.roll(shares[32:48], (away * 16) % 128, 1), 0.0)
    return jnp.concatenate([shares[0:32], pair])


def first_kernel(s_ref, side_ref, vb_ref, *refs):
    inner_ref, part_ref, mate_ref, q_ref, mix_ref, head_ref, tail_ref = refs[3:]
    step = pl.program_id(0)

    @pl.when(step == 0)
    def _():
        for j in range(2):
            rows = slice(HALO_ROWS + j * NEAR, HALO_ROWS + (j + 1) * NEAR)
            head_ref[rows, :] = part_ref[j] + mate_ref[j]
            tail_ref[rows, :] = part_ref[j + 1] + mate_ref[j + 1]

    def planes(edge_ref):
        for p in range(N):
            for half in range(2):
                ring = {y: s_ref[p, halves(y, half), :] for y in range(C)}
                for y in range(H):
                    ring[C + y] = edge_ref[p, halves(y, half), :]
                    ring[y - H] = edge_ref[p, halves(H + y, half), :]
                for y in range(C):
                    rows = halves(y, half)
                    dy = tap_sum(lambda i: ring[i], y)
                    q = dy + vb_ref[p, rows, :] * ring[y]
                    q_ref[p, rows, :] = q
                    mix_ref[p, rows, :] = side_ref[p, rows, :] + q + dy
            for z in range(H):
                rows = halo_rows(step * N + p, z)
                head_ref[rows, :] = mix_ref[p, stride_rows(z), :]
                tail_ref[rows, :] = mix_ref[p, stride_rows(C - H + z), :]

    for_piece(refs[:3], inner_ref, planes)


def make_first(s, side_part, vb, edges, inner, part, part_mate):
    shares = pl.BlockSpec((3, NEAR, S), lambda i: (0, 0, 0))
    return pl.pallas_call(
        first_kernel,
        grid=(C // N,),
        in_specs=[plane_spec(ROWS, N)] * 3 + edge_specs() + [SCALARS] + [shares] * 2,
        out_specs=[plane_spec(ROWS, N), plane_spec(ROWS, N), whole(MESSAGE.shape[0]), whole(MESSAGE.shape[0])],
        out_shape=[FULL, FULL, MESSAGE, MESSAGE],
        compiler_params=params(16),
        cost_estimate=cost(1 << 24, 14 << 20),
        name="first",
    )(s, side_part, vb, *edges, inner, part, part_mate)


def base_kernel(s_ref, mid_ref, vb_ref, vb_mate_ref, q_ref, side_ref, part_ref, *refs):
    inner_ref, message_ref, out_ref, middle_ref = refs[3:]
    step = pl.program_id(0)
    inner = inner_ref[0] == 1

    @pl.when(inner)
    def _():
        middle_ref[...] = mid_ref[...]

    @pl.when(jnp.logical_not(inner))
    def _():
        for p in range(N):
            middle_ref[p] = message_ref[pl.ds(pl.multiple_of(MID_START + (step * N + p) * MID, MID), MID), :]

    def planes(edge_ref):
        for p in range(N):
            for half in range(2):

                def other(y, p=p, half=half):
                    if y < H:
                        return edge_ref[p, halves(y, half), :]
                    if y < C - H:
                        return middle_ref[p, halves(y - H, half), :]
                    return edge_ref[p, halves(y - 4, half), :]

                ring = [s_ref[p, halves(y, half), :] for y in range(C)] + [other(y) for y in range(C)]
                q = {y: q_ref[p, halves(y, half), :] for y in range(C)}
                for y in list(range(H)) + list(range(C - H, C)):
                    v = vb_mate_ref[p, halves(y, half), :]
                    q[C + y] = tap_sum(lambda i: ring[i % 32], C + y) + v * ring[C + y]
                for y in range(C):
                    rows = halves(y, half)
                    total = tap_sum(lambda i: q[i % 32], y)
                    total = total + vb_ref[p, rows, :] * (side_ref[p, rows, :] + q[y])
                    out_ref[p, rows, :] = 2.0 * (total + part_ref[p, rows, :]) - ring[y]

    for_piece(refs[:3], inner_ref, planes)


def make_base(s, mid, vb, vb_mate, q, side_part, part, edges, inner):
    return pl.pallas_call(
        base_kernel,
        grid=(C // N,),
        in_specs=[plane_spec(ROWS, N), plane_spec(MID, N)]
        + [plane_spec(ROWS, N)] * 5
        + edge_specs()
        + [SCALARS, whole((C - FIRST) * EDGE)],
        out_specs=plane_spec(ROWS, N),
        out_shape=FULL,
        scratch_shapes=[pltpu.VMEM((N, MID, S), F32)],
        compiler_params=params(16),
        cost_estimate=cost(1 << 25, 16 << 20),
        name="base",
    )(s, mid, vb, vb_mate, q, side_part, part, *edges, inner, edges[1].reshape(-1, S))


def second_kernel(base_ref, low_ref, high_ref, gg_high_ref, gg_low_ref, *rest):
    part_ref, mate_ref, energy_ref, upper_ref, second_ref, keep_ref, give_ref, gram_ref, cross_ref, w_ref, halo_ref = rest
    step = pl.program_id(0)

    @pl.when(step == 0)
    def _():
        gram_ref[...] = jnp.zeros((S, S), F32)
        cross_ref[...] = jnp.zeros((S, S), F32)
        w_ref[...] = jnp.zeros((S, S), F32)
        halo_ref[...] = jnp.zeros((B, ROWS, S), F32)
        mine = [part_ref[j] + mate_ref[j] for j in range(3)]
        below = [move_pair(low_ref[HALO_ROWS + j * NEAR : HALO_ROWS + (j + 1) * NEAR, :], -1) for j in range(2)]
        above = [move_pair(high_ref[HALO_ROWS + j * NEAR : HALO_ROWS + (j + 1) * NEAR, :], 1) for j in range(2)]
        slabs = [mine[0] + below[0], mine[1] + below[1] + above[0], mine[2] + above[1]]
        near = jnp.concatenate([slab[0:16] for slab in slabs]) * energy_ref[...]
        lane = lax.broadcasted_iota(jnp.int32, (NEAR, S), 1)
        pair = jnp.where(lane < NEAR, jnp.concatenate([slab[32:48] for slab in slabs]), 0.0)
        two = jnp.concatenate([slab[16:32] for slab in slabs])
        two = two + exact(pair, jnp.concatenate([near, jnp.zeros((S - NEAR, S), F32)]))
        w_ref[0:NEAR, :] = 2.0 * energy_ref[...] * two
        w_ref[64 : 64 + NEAR, :] = 2.0 * near

    for p in range(B):
        low = [low_ref[halo_rows(step * B + p, j), :] for j in range(H)]
        high = [high_ref[halo_rows(step * B + p, j), :] for j in range(H)]
        for z in range(H):
            add = sum((2.0 * OFF[k - 1]) * low[z - k + H] for k in range(z + 1, H + 1))
            halo_ref[p, stride_rows(z), :] = add
            add = sum((2.0 * OFF[H + j - z - 1]) * high[j] for j in range(z + 1))
            halo_ref[p, stride_rows(C - H + z), :] = add

    w_high, w_low = split(w_ref[...])
    w_twice = jnp.concatenate([w_high, w_high])
    gram = jnp.zeros((S, 2 * S), F32)
    for p in range(B):
        g_high, g_low = gg_high_ref[0, p], gg_low_ref[0, p]
        near = mm(jnp.concatenate([g_high, g_low], axis=1), w_twice) + mm(g_high, w_low)
        value = base_ref[p] + halo_ref[p] + near
        second_ref[p] = value
        s_high, s_low = split(value)
        gram += mm(s_high.T, jnp.concatenate([s_high, s_low], axis=1))
    gram_ref[...] += gram[:, :S]
    cross_ref[...] += gram[:, S:]

    @pl.when(step == STEPS - 1)
    def _():
        cross = cross_ref[...]
        gram = (gram_ref[...] + (cross + cross.T)) * (1.0 / NCELLS)
        upper = upper_ref[0] == 1
        keep_ref[...] = jnp.where(upper, gram[S // 2 :], gram[: S // 2])
        give_ref[...] = jnp.where(upper, gram[: S // 2], gram[S // 2 :])


def make_second(base, halos, gg, shares, upper):
    three = pl.BlockSpec((3, NEAR, S), lambda i: (0, 0, 0))
    return pl.pallas_call(
        second_kernel,
        grid=(STEPS,),
        in_specs=[plane_spec()]
        + [whole(MESSAGE.shape[0])] * 2
        + [part_spec(0), part_spec(1), three, three, whole(NEAR), SCALARS],
        out_specs=[plane_spec(), whole(S // 2), whole(S // 2)],
        out_shape=[FULL, sds((S // 2, S)), sds((S // 2, S))],
        scratch_shapes=[pltpu.VMEM((S, S), F32)] * 3 + [pltpu.VMEM((B, ROWS, S), F32)],
        compiler_params=params(16),
        cost_estimate=cost(1 << 27, 8 << 20),
        name="second",
    )(base, *halos, gg, gg, *shares, upper)


def exact(a, b):
    return jnp.dot(a, b, precision=lax.Precision.HIGHEST, preferred_element_type=F32)


def inverse_factor(gram_ref, a_ref, x_ref, state_ref):
    row = lax.broadcasted_iota(jnp.int32, (S, S), 0)
    column = lax.broadcasted_iota(jnp.int32, (S, S), 1)
    unit = jnp.where(row == column, 1.0, 0.0)
    gram = gram_ref[...]
    diagonal = jnp.where(row == column, gram, 0.0)
    down = lax.rsqrt(jnp.sum(diagonal, axis=1, keepdims=True))
    across = lax.rsqrt(jnp.sum(diagonal, axis=0, keepdims=True))
    a_ref[...] = gram * down * across
    x_ref[...] = unit

    def residual():
        x = x_ref[...]
        return unit - exact(exact(x, a_ref[...]), x.T)

    def size(e):
        return jnp.sum(e * e)

    def improve(e):
        lower = jnp.where(row > column, e, jnp.where(row == column, 0.5 * e, 0.0))
        x_ref[...] += exact(lower, x_ref[...])

    state_ref[0] = 0
    start = unit - a_ref[...]
    start_size = size(start)

    @pl.when(start_size < 0.16)
    def _():
        improve(start)
        state_ref[0] = jnp.where(start_size < 1e-6, 2, 1)

    for _ in range(5):

        @pl.when(state_ref[0] == 1)
        def _():
            e = residual()
            e_size = size(e)
            improve(e)
            state_ref[0] = jnp.where(e_size < 1e-6, 2, 1)

    @pl.when(state_ref[0] != 2)
    def _():
        x_ref[...] = unit
        lanes = lax.broadcasted_iota(jnp.int32, (1, S), 1)

        def step(j, _):
            line = a_ref[pl.ds(j, 1), :]
            scale = lax.rsqrt(jnp.sum(jnp.where(lanes == j, line, 0.0), axis=1, keepdims=True))
            a = a_ref[...]
            factor = jnp.sum(jnp.where(column == j, a, 0.0), axis=1, keepdims=True) * scale
            factor = jnp.where(row[:, :1] > j, factor, 0.0)
            x_line = x_ref[pl.ds(j, 1), :] * scale
            a_ref[...] = a - factor * (line * scale)
            x_ref[...] = jnp.where(row == j, x_line, x_ref[...] - factor * x_line)
            return 0

        lax.fori_loop(0, S, step, 0)

    x_ref[...] = x_ref[...] * across


def turn_kernel(second_ref, own_ref, other_ref, upper_ref, out_ref, gram_ref, a_ref, x_ref, i_high_ref, i_low_ref, state_ref):
    @pl.when(pl.program_id(0) == 0)
    def _():
        upper = upper_ref[0] == 1
        gram_ref[: S // 2, :] = jnp.where(upper, other_ref[...], own_ref[...])
        gram_ref[S // 2 :, :] = jnp.where(upper, own_ref[...], other_ref[...])
        inverse_factor(gram_ref, a_ref, x_ref, state_ref)
        i_high, i_low = split(x_ref[...].T)
        i_high_ref[...] = i_high
        i_low_ref[...] = i_low

    i_high, i_low = i_high_ref[...], i_low_ref[...]
    i_twice = jnp.concatenate([i_high, i_high])
    for p in range(B):
        high, low = split(second_ref[p])
        out_ref[p] = mm(jnp.concatenate([high, low], axis=1), i_twice) + mm(high, i_low)


def turn(second, own, other, upper):
    return pl.pallas_call(
        turn_kernel,
        grid=(STEPS,),
        in_specs=[plane_spec(), whole(S // 2), whole(S // 2), SCALARS],
        out_specs=plane_spec(),
        out_shape=FULL,
        scratch_shapes=[pltpu.VMEM((S, S), F32)] * 3 + [pltpu.VMEM((S, S), BF16)] * 2 + [pltpu.SMEM((1,), jnp.int32)],
        compiler_params=params(16),
        cost_estimate=cost(1 << 28, 4 << 20),
        name="turn",
    )(second, own, other, upper)


def per_device(states, potential, atom_sites, projectors, energies):
    gx, gy = lax.axis_index("gx"), lax.axis_index("gy")
    depth = lax.axis_size("gzs")
    count = 4 * depth
    barrier = lax.optimization_barrier

    def send(value, flip=0, move=0):
        def target(d):
            return (d // depth * depth ^ flip) + (d + move) % depth

        return lax.ppermute(value, AXES, [(d, target(d)) for d in range(count)])

    over_x, over_y = 2 * depth, depth
    inner_ones = [d for d in range(count) if d % 4 in (1, 2)]
    outer_ones = [d for d in range(count) if d % 4 in (0, 3)]
    inner = ((lax.axis_index("gzs") + 1) // 2 % 2).astype(jnp.int32).reshape(1)
    s = states.reshape(C, ROWS, S)
    mate = send(s, over_x)
    corner = jnp.stack([gx * C, gy * C]).astype(jnp.int32)
    upper = gx.astype(jnp.int32).reshape(1)
    to_pack, corner, upper, inner = barrier((s, corner, upper, inner))
    one_edge, relay, head, tail = pack(to_pack)
    one_edge = send(one_edge, over_y)
    relayed = lax.ppermute(relay, AXES, [(d, d ^ over_y ^ 1) for d in outer_ones])

    pot = potential.reshape(32, 128)
    atoms = jnp.concatenate(
        [projectors.reshape(4, TAPS), atom_sites.astype(F32), energies[:, None], jnp.zeros((4, 768 - TAPS - 4), F32)],
        axis=1,
    ).reshape(24, 128)
    parcel = stack((atoms, 24), (pot, 32))
    parcel_mate = send(parcel, over_y)
    message, mid = pack_rest(s, inner)
    parcel_mate, one_edge, message = barrier((parcel_mate, one_edge, message))
    message = send(message, over_y)
    pair = stack((parcel, 24), (parcel_mate, 24))
    column = stack((send(pair, 0, 1), 48), (pair, 48), (send(pair, 0, -1), 48))
    column, head, tail = barrier((column, head, tail))
    low, high = send(tail, 0, 1), send(head, 0, -1)
    column, relayed = barrier((column, relayed))
    column_mate = send(column, over_x)
    vb = spread(parcel)
    beside = side_x(s, mate)
    column_mate, beside = barrier((column_mate, beside))
    gg, part, energy = prep([column, column_mate], corner, vb, s)
    part, relayed = barrier((part, relayed))
    relayed = lax.ppermute(relayed, AXES, [(d, d ^ 1) for d in inner_ones])
    side_part = side_z(s, beside, low, high)
    planes = vb.reshape(C, ROWS, S)

    part = part + send(part, over_x)
    part_mate = send(part, over_y)
    message = message.reshape(C - FIRST, EDGE, S)
    edges = [one_edge, message, relayed]
    q, mix, head, tail = make_first(s, side_part, planes, edges, inner, part, part_mate)
    halos = [send(tail, 0, 1), send(head, 0, -1)]
    mate = send(mix, over_x)
    mid, part_mate = barrier((mid, part_mate))
    mid = lax.ppermute(mid, AXES, [(d, d ^ over_y) for d in inner_ones])
    planes_mate = spread(parcel_mate).reshape(C, ROWS, S)
    part_two = side_again(mix, mate)
    base = make_base(s, mid, planes, planes_mate, q, side_part, part_two, edges, inner)
    gg = gg.reshape(2, C, ROWS, S)
    second, own, give = make_second(base, halos, gg, [part, part_mate, energy], upper)

    own = own + send(give, over_x)
    for flip in (32, 36, 1, 3, 8, 24):
        own = own + lax.ppermute(own, AXES, [(d, d ^ flip) for d in range(count)])
    return turn(second, own, send(own, over_x), upper).reshape(C, C, C, S)


def solution(mesh):
    return jax.shard_map(
        per_device,
        mesh=mesh,
        in_specs=(
            P("gx", "gy", "gzs", None),
            P("gx", "gy", "gzs"),
            P(("gx", "gy", "gzs"), None),
            P(("gx", "gy", "gzs"), None, None, None),
            P(("gx", "gy", "gzs")),
        ),
        out_specs=P("gx", "gy", "gzs", None),
        check_vma=False,
    )
```

```python
import math

import jax
import jax.numpy as jnp
from jax import lax
from jax.experimental import pallas as pl
from jax.experimental.pallas import tpu as pltpu
from jax.sharding import PartitionSpec as P

AXES = ("gx", "gy", "gzs")
H = 6
C = 16
ROWS = C * C
CELLS = C * C * C
NCELLS = 32 * 32 * 512
S = 128
W = 9
R = 4
NEAR = 48
TAPS = W * W * W
F32 = jnp.float32
BF16 = jnp.bfloat16

grid_step = 0.6
filter_centre = 36.0
filter_half = 26.0


def weights():
    taps = []
    for k in range(1, 7):
        top = 2.0 * (-1) ** (k + 1) * math.factorial(6) ** 2
        under = k * k * math.factorial(6 - k) * math.factorial(6 + k)
        taps.append(top / under)
    scale = -0.5 / (grid_step * grid_step)
    off = [scale * t / filter_half for t in taps]
    diagonal = 3.0 * scale * (-2.0 * sum(taps))
    return off, diagonal


OFF, DIAGONAL = weights()


def params(mib):
    return pltpu.CompilerParams(vmem_limit_bytes=mib * 1024 * 1024)


def cost(flops, nbytes):
    return pl.CostEstimate(flops=flops, bytes_accessed=nbytes, transcendentals=0)


def sds(shape, dtype=F32):
    return jax.ShapeDtypeStruct(shape, dtype)


def split(value):
    high = value.astype(BF16)
    low = (value - high.astype(F32)).astype(BF16)
    return high, low


def mm(a, b):
    return jnp.dot(a, b, preferred_element_type=F32)


def tap_sum(at, index):
    total = None
    for k in range(1, 7):
        term = OFF[k - 1] * (at(index + k) + at(index - k))
        total = term if total is None else total + term
    return total


B = 4
STEPS = C // B
N = 2
FIRST = 6
MIDDLE = 10
EDGE = 192
MID = 64
MID_START = (MIDDLE - FIRST) * EDGE


def stride_rows(z):
    return pl.ds(z, C, stride=C)


def plane_spec(rows=ROWS, planes=B):
    return pl.BlockSpec((planes, rows, S), lambda i: (i, 0, 0))


def halo_spec(planes=B):
    return pl.BlockSpec((H, planes, C, S), lambda i: (0, i, 0, 0))


def part_spec(part):
    return pl.BlockSpec((1, B, ROWS, S), lambda i: (part, i, 0, 0))


def whole(rows=S):
    return pl.BlockSpec((rows, S), lambda i: (0, 0))


def edge_spec(start, stop):
    return pl.BlockSpec((N, EDGE, S), lambda i: (jnp.clip(i - start // N, 0, (stop - start) // N - 1), 0, 0))


def edge_specs():
    return [edge_spec(0, FIRST), edge_spec(FIRST, C), edge_spec(MIDDLE, C)]


def for_piece(edges, inner_ref, body):
    step = pl.program_id(0)
    direct = (inner_ref[0] == 1) | (step < MIDDLE // N)

    @pl.when(step < FIRST // N)
    def _():
        body(edges[0])

    @pl.when((step >= FIRST // N) & direct)
    def _():
        body(edges[1])

    @pl.when(jnp.logical_not(direct))
    def _():
        body(edges[2])


SCALARS = pl.BlockSpec(memory_space=pltpu.SMEM)
FULL = sds((C, ROWS, S))
FULL_ROWS = sds((CELLS, S))
HALO_ROWS = H * ROWS
MESSAGE = sds((HALO_ROWS + 2 * NEAR, S))
HALO = sds((H, C, C, S))
EDGES = [sds((FIRST, EDGE, S)), sds((C - FIRST, EDGE, S)), sds((C - MIDDLE, EDGE, S))]


def halo_rows(x, z):
    return pl.ds(pl.multiple_of(z * ROWS + x * C, C), C)


def halves(y, half):
    return slice(y * C + half * 8, y * C + half * 8 + 8)


def pack_edges(s_ref, out_ref):
    out_ref[:, 0:96, :] = s_ref[:, 0:96, :]
    out_ref[:, 96:192, :] = s_ref[:, 160:256, :]


def pack_kernel(s_ref, edge_ref, head_ref, tail_ref):
    @pl.when(pl.program_id(0) < FIRST // N)
    def _():
        pack_edges(s_ref, edge_ref)

    for p in range(N):
        for z in range(H):
            head_ref[z, p] = s_ref[p, stride_rows(z), :]
            tail_ref[z, p] = s_ref[p, stride_rows(C - H + z), :]


def pack(s):
    return pl.pallas_call(
        pack_kernel,
        grid=(C // N,),
        in_specs=[plane_spec(ROWS, N)],
        out_specs=edge_specs()[:1] + [halo_spec(N), halo_spec(N)],
        out_shape=EDGES[:1] + [HALO, HALO],
        compiler_params=params(12),
        cost_estimate=cost(1 << 32, 6 << 20),
        name="pack",
    )(s)


def pack_rest_kernel(s_ref, inner_ref, message_ref, relay_ref, mid_ref):
    step = pl.program_id(0)
    inner = inner_ref[0] == 1
    mid_ref[...] = s_ref[:, 96:160, :]

    @pl.when(step >= MIDDLE // N)
    def _():
        pack_edges(s_ref, relay_ref)

    @pl.when((step >= FIRST // N) & (inner | (step < MIDDLE // N)))
    def _():
        for p in range(N):
            row = pl.multiple_of((step * N + p - FIRST) * EDGE, MID)
            message_ref[pl.ds(row, 96), :] = s_ref[p, 0:96, :]
            message_ref[pl.ds(row + 96, 96), :] = s_ref[p, 160:256, :]

    @pl.when(jnp.logical_not(inner))
    def _():
        for p in range(N):
            row = pl.multiple_of(MID_START + (step * N + p) * MID, MID)
            message_ref[pl.ds(row, MID), :] = s_ref[p, 96:160, :]


def pack_rest(s, inner):
    rows = (C - FIRST) * EDGE
    message, relay, mid = pl.pallas_call(
        pack_rest_kernel,
        grid=(C // N,),
        in_specs=[plane_spec(ROWS, N), SCALARS],
        out_specs=[whole(rows), edge_spec(MIDDLE, C), plane_spec(MID, N)],
        out_shape=[sds((rows, S)), EDGES[2], sds((C, MID, S))],
        compiler_params=params(12),
        cost_estimate=cost(1 << 31, 4 << 20),
        name="pack_rest",
    )(s, inner)
    return message, relay, mid


def stack_kernel(*refs):
    start = 0
    for ref in refs[:-1]:
        refs[-1][start : start + ref.shape[0], :] = ref[...]
        start += ref.shape[0]


def stack(*arrays):
    rows = sum(a.shape[0] for a in arrays)
    return pl.pallas_call(stack_kernel, out_shape=sds((rows, S)), compiler_params=params(4), name="stack")(*arrays)


def along_x(s_ref, mate_ref, out_ref, add):
    def column(block, _):
        rows = pl.ds(pl.multiple_of(block * 8, 8), 8)
        ring = [mate_ref[C - H + i, rows, :] for i in range(H)]
        ring += [s_ref[x, rows, :] for x in range(C)]
        ring += [mate_ref[i, rows, :] for i in range(H)]
        for x in range(C):
            value = tap_sum(lambda i: ring[H + i], x)
            if add:
                value = value + out_ref[x, rows, :]
            out_ref[x, rows, :] = value
        return 0

    lax.fori_loop(0, ROWS // 8, column, 0)


def z_taps(ext_ref, y):
    return tap_sum(lambda k: ext_ref[y * 32 + 8 + k : y * 32 + 24 + k, :], 0)


def side_x_kernel(s_ref, mate_ref, out_ref):
    along_x(s_ref, mate_ref, out_ref, False)


def side_x(s, mate):
    return pl.pallas_call(
        side_x_kernel,
        out_shape=FULL,
        compiler_params=params(12),
        cost_estimate=cost(1 << 24, 6 << 20),
        name="side_x",
    )(s, mate)


def side_z_kernel(s_ref, part_ref, low_ref, high_ref, out_ref, ext_ref):
    def plane(x, _):
        for y in range(C):
            ext_ref[y * 32 + 8 : y * 32 + 24, :] = s_ref[x, y * C : (y + 1) * C, :]
        for z in range(H):
            ext_ref[pl.ds(2 + z, C, stride=32), :] = low_ref[z, x]
            ext_ref[pl.ds(24 + z, C, stride=32), :] = high_ref[z, x]
        for y in range(C):
            rows = slice(y * C, (y + 1) * C)
            out_ref[x, rows, :] = part_ref[x, rows, :] + z_taps(ext_ref, y)
        return 0

    lax.fori_loop(0, C, plane, 0)


def side_z(s, part, low, high):
    return pl.pallas_call(
        side_z_kernel,
        out_shape=FULL,
        scratch_shapes=[pltpu.VMEM((C * 32, S), F32)],
        compiler_params=params(14),
        cost_estimate=cost(1 << 24, 8 << 20),
        name="side_z",
    )(s, part, low, high)


def side_again_kernel(s_ref, mate_ref, out_ref, ext_ref):
    for y in range(C):
        ext_ref[y * 32 : y * 32 + 8, :] = jnp.zeros((8, S), F32)
        ext_ref[y * 32 + 24 : y * 32 + 32, :] = jnp.zeros((8, S), F32)

    def plane(x, _):
        for y in range(C):
            ext_ref[y * 32 + 8 : y * 32 + 24, :] = s_ref[x, y * C : (y + 1) * C, :]
        for y in range(C):
            out_ref[x, y * C : (y + 1) * C, :] = z_taps(ext_ref, y)
        return 0

    lax.fori_loop(0, C, plane, 0)
    along_x(s_ref, mate_ref, out_ref, True)


def side_again(s, mate):
    return pl.pallas_call(
        side_again_kernel,
        out_shape=FULL,
        scratch_shapes=[pltpu.VMEM((C * 32, S), F32)],
        compiler_params=params(12),
        cost_estimate=cost(1 << 25, 6 << 20),
        name="side_again",
    )(s, mate)


def tap_weight(distance):
    value = jnp.zeros(distance.shape, F32)
    for k in range(1, 7):
        value = jnp.where(distance == k, OFF[k - 1], value)
    return value


def ring_tables(coordinate):
    masks, factors = [], []
    for t in range(W):
        away = (coordinate - t) & 31
        masks.append(away == 0)
        factors.append(tap_weight(jnp.minimum(away, 32 - away)))
    return masks, factors


def spread_kernel(parcel_ref, vb_ref):
    def spread_row(row, _):
        line = (parcel_ref[pl.ds(72 + row, 1), :] + (DIAGONAL - filter_centre)) * (1.0 / filter_half)
        start = pl.multiple_of(row * 128, 128)
        vb_ref[pl.ds(start, 128), :] = jnp.broadcast_to(line, (128, 128)).T
        return 0

    lax.fori_loop(0, CELLS // 128, spread_row, 0, unroll=8)


def spread(parcel):
    return pl.pallas_call(
        spread_kernel,
        out_shape=FULL_ROWS,
        compiler_params=params(8),
        cost_estimate=cost(1 << 20, 2 << 20),
        name="spread",
    )(parcel)


def prep_kernel(*refs):
    parcels = refs[:4]
    corner_ref, vb_ref, s_ref, gg_ref, coef_ref, energy_ref, near_ref, table_ref, a1_ref, a1z_ref, a2_ref, a2s_ref = refs[4:]
    upper_x, upper_y = corner_ref[0] > 0, corner_ref[1] > 0
    for slab in range(3):
        own, over_x, over_y, over_xy = [parcel[slab * 24 : slab * 24 + 24, :] for parcel in parcels]
        same_x = [jnp.where(upper_y, over_y, own), jnp.where(upper_y, own, over_y)]
        other_x = [jnp.where(upper_y, over_xy, over_x), jnp.where(upper_y, over_x, over_xy)]
        ordered = [jnp.where(upper_x, o, m) for m, o in zip(same_x, other_x)]
        ordered += [jnp.where(upper_x, m, o) for m, o in zip(same_x, other_x)]
        for j in range(4):
            near_ref[slab * 96 + j * 24 : slab * 96 + j * 24 + 24, :] = ordered[j]
    blank = jnp.zeros((16, 128), F32)
    for block in range(6):
        rows = near_ref[pl.ds(block, NEAR, stride=6), :]
        table_ref[block * 128 : block * 128 + 128, :] = jnp.concatenate([rows, blank, rows, blank]).T
    at = TAPS + 3 - 640
    energy_ref[...] = jnp.broadcast_to(rows[:, at : at + 1] * (1.0 / filter_half), (NEAR, S))

    shape = (8, 128)
    sub = lax.broadcasted_iota(jnp.int32, shape, 0)
    lane = lax.broadcasted_iota(jnp.int32, shape, 1)
    first_lanes = lane < 64
    sites = [jnp.broadcast_to(table_ref[TAPS + d : TAPS + d + 1, :], shape).astype(jnp.int32) for d in range(3)]
    px = sites[0] - corner_ref[0]
    py = sites[1] - corner_ref[1]
    pz = (sites[2] & 15) + (((lane & 63) >> 4) - 1) * C
    zero = jnp.zeros(shape, F32)

    dz = sub + (lane >> 6) * 8 - pz + R
    z_masks = [dz == t for t in range(W)]
    z_factors = [tap_weight(jnp.abs(dz - t)) for t in range(W)]

    def place_z(ij, _):
        acc = zero
        along = zero
        for t in range(W):
            row = jnp.broadcast_to(table_ref[pl.ds(ij * W + t, 1), :], shape)
            acc = jnp.where(z_masks[t], row, acc)
            along = along + z_factors[t] * row
        a1_ref[ij] = acc
        a1z_ref[ij] = along
        return 0

    lax.fori_loop(0, W * W, place_z, 0, unroll=3)

    def place_y(y, _):
        masks, factors = ring_tables(y - py + R)
        for i in range(W):
            acc = zero
            along = zero
            moved = zero
            for t in range(W):
                value = a1_ref[i * W + t]
                acc = jnp.where(masks[t], value, acc)
                along = along + factors[t] * value
                moved = jnp.where(masks[t], a1z_ref[i * W + t], moved)
            a2_ref[i, y] = acc
            a2s_ref[i, y] = along + moved
        return 0

    lax.fori_loop(0, C, place_y, 0)

    def place_x(x, _):
        masks, factors = ring_tables(x - px + R)

        def per_y(y, _):
            row = pl.multiple_of(x * ROWS + y * C, C)
            acc = zero
            along = zero
            moved = zero
            for t in range(W):
                value = a2_ref[t, y]
                acc = jnp.where(masks[t], value, acc)
                along = along + factors[t] * value
                moved = jnp.where(masks[t], a2s_ref[t, y], moved)
            v = vb_ref[pl.ds(row, C), :]
            moved = along + moved + jnp.where(first_lanes, v[:8], v[8:]) * acc
            lower = jnp.where(first_lanes, acc, pltpu.roll(moved, 64, 1))
            upper = jnp.where(first_lanes, pltpu.roll(acc, 64, 1), moved)
            high, low = split(jnp.concatenate([lower, upper], axis=0))
            gg_ref[0, pl.ds(row, C), :] = high
            gg_ref[1, pl.ds(row, C), :] = low
            return 0

        lax.fori_loop(0, C, per_y, 0, unroll=16)
        return 0

    lax.fori_loop(0, C, place_x, 0)

    coef_ref[...] = jnp.zeros((3, NEAR, S), F32)

    def contract(x, _):
        rows = pl.ds(pl.multiple_of(x * 2 * ROWS, ROWS), 2 * ROWS)
        g_high, g_low = gg_ref[0, rows, :], gg_ref[1, rows, :]
        t_high, t_low = g_high.T, g_low.T
        high, low = split(s_ref[rows, :])
        got = mm(t_high, high) + (mm(t_high, low) + mm(t_low, high))
        t_high, t_low = t_high[:NEAR], t_low[:NEAR]
        pair = mm(t_high, g_high) + (mm(t_high, g_low) + mm(t_low, g_high))
        for slab in range(3):
            rows = slice(slab * C, slab * C + C)
            coef_ref[slab, 0:16] += got[rows]
            coef_ref[slab, 16:32] += got[64 + slab * C : 80 + slab * C]
            coef_ref[slab, 32:48] += pair[rows]
        return 0

    lax.fori_loop(0, C // 2, contract, 0, unroll=2)


def prep(parcels, corner, vb, s):
    vmem = pl.BlockSpec(memory_space=pltpu.VMEM)
    return pl.pallas_call(
        prep_kernel,
        in_specs=[vmem] * 4 + [pl.BlockSpec(memory_space=pltpu.SMEM), vmem, vmem],
        out_shape=[sds((2, CELLS, S), BF16), sds((3, NEAR, S)), sds((NEAR, S))],
        scratch_shapes=[
            pltpu.VMEM((288, 128), F32),
            pltpu.VMEM((768, 128), F32),
            pltpu.VMEM((W * W, 8, 128), F32),
            pltpu.VMEM((W * W, 8, 128), F32),
            pltpu.VMEM((W, C, 8, 128), F32),
            pltpu.VMEM((W, C, 8, 128), F32),
        ],
        compiler_params=params(16),
        cost_estimate=cost(1 << 27, 10 << 20),
        name="prep",
    )(*parcels, corner, vb, s.reshape(CELLS, S))


def move_pair(shares, away):
    lane = lax.broadcasted_iota(jnp.int32, (16, 128), 1)
    keep = (lane < 32) if away < 0 else (lane >= 16) & (lane < 48)
    pair = jnp.where(keep, pltpu.roll(shares[32:48], (away * 16) % 128, 1), 0.0)
    return jnp.concatenate([shares[0:32], pair])


def first_kernel(s_ref, side_ref, vb_ref, *refs):
    inner_ref, part_ref, mate_ref, q_ref, mix_ref, head_ref, tail_ref = refs[3:]
    step = pl.program_id(0)

    @pl.when(step == 0)
    def _():
        for j in range(2):
            rows = slice(HALO_ROWS + j * NEAR, HALO_ROWS + (j + 1) * NEAR)
            head_ref[rows, :] = part_ref[j] + mate_ref[j]
            tail_ref[rows, :] = part_ref[j + 1] + mate_ref[j + 1]

    def planes(edge_ref):
        for p in range(N):
            for half in range(2):
                ring = {y: s_ref[p, halves(y, half), :] for y in range(C)}
                for y in range(H):
                    ring[C + y] = edge_ref[p, halves(y, half), :]
                    ring[y - H] = edge_ref[p, halves(H + y, half), :]
                for y in range(C):
                    rows = halves(y, half)
                    dy = tap_sum(lambda i: ring[i], y)
                    q = dy + vb_ref[p, rows, :] * ring[y]
                    q_ref[p, rows, :] = q
                    mix_ref[p, rows, :] = side_ref[p, rows, :] + q + dy
            for z in range(H):
                rows = halo_rows(step * N + p, z)
                head_ref[rows, :] = mix_ref[p, stride_rows(z), :]
                tail_ref[rows, :] = mix_ref[p, stride_rows(C - H + z), :]

    for_piece(refs[:3], inner_ref, planes)


def make_first(s, side_part, vb, edges, inner, part, part_mate):
    shares = pl.BlockSpec((3, NEAR, S), lambda i: (0, 0, 0))
    return pl.pallas_call(
        first_kernel,
        grid=(C // N,),
        in_specs=[plane_spec(ROWS, N)] * 3 + edge_specs() + [SCALARS] + [shares] * 2,
        out_specs=[plane_spec(ROWS, N), plane_spec(ROWS, N), whole(MESSAGE.shape[0]), whole(MESSAGE.shape[0])],
        out_shape=[FULL, FULL, MESSAGE, MESSAGE],
        compiler_params=params(16),
        cost_estimate=cost(1 << 24, 14 << 20),
        name="first",
    )(s, side_part, vb, *edges, inner, part, part_mate)


def base_kernel(s_ref, mid_ref, vb_ref, vb_mate_ref, q_ref, side_ref, part_ref, *refs):
    inner_ref, message_ref, out_ref, middle_ref = refs[3:]
    step = pl.program_id(0)
    inner = inner_ref[0] == 1

    @pl.when(inner)
    def _():
        middle_ref[...] = mid_ref[...]

    @pl.when(jnp.logical_not(inner))
    def _():
        for p in range(N):
            middle_ref[p] = message_ref[pl.ds(pl.multiple_of(MID_START + (step * N + p) * MID, MID), MID), :]

    def planes(edge_ref):
        for p in range(N):
            for half in range(2):

                def other(y, p=p, half=half):
                    if y < H:
                        return edge_ref[p, halves(y, half), :]
                    if y < C - H:
                        return middle_ref[p, halves(y - H, half), :]
                    return edge_ref[p, halves(y - 4, half), :]

                ring = [s_ref[p, halves(y, half), :] for y in range(C)] + [other(y) for y in range(C)]
                q = {y: q_ref[p, halves(y, half), :] for y in range(C)}
                for y in list(range(H)) + list(range(C - H, C)):
                    v = vb_mate_ref[p, halves(y, half), :]
                    q[C + y] = tap_sum(lambda i: ring[i % 32], C + y) + v * ring[C + y]
                for y in range(C):
                    rows = halves(y, half)
                    total = tap_sum(lambda i: q[i % 32], y)
                    total = total + vb_ref[p, rows, :] * (side_ref[p, rows, :] + q[y])
                    out_ref[p, rows, :] = 2.0 * (total + part_ref[p, rows, :]) - ring[y]

    for_piece(refs[:3], inner_ref, planes)


def make_base(s, mid, vb, vb_mate, q, side_part, part, edges, inner):
    return pl.pallas_call(
        base_kernel,
        grid=(C // N,),
        in_specs=[plane_spec(ROWS, N), plane_spec(MID, N)]
        + [plane_spec(ROWS, N)] * 5
        + edge_specs()
        + [SCALARS, whole((C - FIRST) * EDGE)],
        out_specs=plane_spec(ROWS, N),
        out_shape=FULL,
        scratch_shapes=[pltpu.VMEM((N, MID, S), F32)],
        compiler_params=params(16),
        cost_estimate=cost(1 << 25, 16 << 20),
        name="base",
    )(s, mid, vb, vb_mate, q, side_part, part, *edges, inner, edges[1].reshape(-1, S))


def second_kernel(base_ref, low_ref, high_ref, gg_high_ref, gg_low_ref, *rest):
    part_ref, mate_ref, energy_ref, upper_ref, second_ref, keep_ref, give_ref, gram_ref, cross_ref, w_ref, halo_ref = rest
    step = pl.program_id(0)

    @pl.when(step == 0)
    def _():
        gram_ref[...] = jnp.zeros((S, S), F32)
        cross_ref[...] = jnp.zeros((S, S), F32)
        w_ref[...] = jnp.zeros((S, S), F32)
        halo_ref[...] = jnp.zeros((B, ROWS, S), F32)
        mine = [part_ref[j] + mate_ref[j] for j in range(3)]
        below = [move_pair(low_ref[HALO_ROWS + j * NEAR : HALO_ROWS + (j + 1) * NEAR, :], -1) for j in range(2)]
        above = [move_pair(high_ref[HALO_ROWS + j * NEAR : HALO_ROWS + (j + 1) * NEAR, :], 1) for j in range(2)]
        slabs = [mine[0] + below[0], mine[1] + below[1] + above[0], mine[2] + above[1]]
        near = jnp.concatenate([slab[0:16] for slab in slabs]) * energy_ref[...]
        lane = lax.broadcasted_iota(jnp.int32, (NEAR, S), 1)
        pair = jnp.where(lane < NEAR, jnp.concatenate([slab[32:48] for slab in slabs]), 0.0)
        two = jnp.concatenate([slab[16:32] for slab in slabs])
        two = two + exact(pair, jnp.concatenate([near, jnp.zeros((S - NEAR, S), F32)]))
        w_ref[0:NEAR, :] = 2.0 * energy_ref[...] * two
        w_ref[64 : 64 + NEAR, :] = 2.0 * near

    for p in range(B):
        low = [low_ref[halo_rows(step * B + p, j), :] for j in range(H)]
        high = [high_ref[halo_rows(step * B + p, j), :] for j in range(H)]
        for z in range(H):
            add = sum((2.0 * OFF[k - 1]) * low[z - k + H] for k in range(z + 1, H + 1))
            halo_ref[p, stride_rows(z), :] = add
            add = sum((2.0 * OFF[H + j - z - 1]) * high[j] for j in range(z + 1))
            halo_ref[p, stride_rows(C - H + z), :] = add

    w_high, w_low = split(w_ref[...])
    w_twice = jnp.concatenate([w_high, w_high])
    gram = jnp.zeros((S, 2 * S), F32)
    for p in range(B):
        g_high, g_low = gg_high_ref[0, p], gg_low_ref[0, p]
        near = mm(jnp.concatenate([g_high, g_low], axis=1), w_twice) + mm(g_high, w_low)
        value = base_ref[p] + halo_ref[p] + near
        second_ref[p] = value
        s_high, s_low = split(value)
        gram += mm(s_high.T, jnp.concatenate([s_high, s_low], axis=1))
    gram_ref[...] += gram[:, :S]
    cross_ref[...] += gram[:, S:]

    @pl.when(step == STEPS - 1)
    def _():
        cross = cross_ref[...]
        gram = (gram_ref[...] + (cross + cross.T)) * (1.0 / NCELLS)
        upper = upper_ref[0] == 1
        keep_ref[...] = jnp.where(upper, gram[S // 2 :], gram[: S // 2])
        give_ref[...] = jnp.where(upper, gram[: S // 2], gram[S // 2 :])


def make_second(base, halos, gg, shares, upper):
    three = pl.BlockSpec((3, NEAR, S), lambda i: (0, 0, 0))
    return pl.pallas_call(
        second_kernel,
        grid=(STEPS,),
        in_specs=[plane_spec()]
        + [whole(MESSAGE.shape[0])] * 2
        + [part_spec(0), part_spec(1), three, three, whole(NEAR), SCALARS],
        out_specs=[plane_spec(), whole(S // 2), whole(S // 2)],
        out_shape=[FULL, sds((S // 2, S)), sds((S // 2, S))],
        scratch_shapes=[pltpu.VMEM((S, S), F32)] * 3 + [pltpu.VMEM((B, ROWS, S), F32)],
        compiler_params=params(16),
        cost_estimate=cost(1 << 27, 8 << 20),
        name="second",
    )(base, *halos, gg, gg, *shares, upper)


def exact(a, b):
    return jnp.dot(a, b, precision=lax.Precision.HIGHEST, preferred_element_type=F32)


def inverse_factor(gram_ref, a_ref, x_ref, state_ref):
    row = lax.broadcasted_iota(jnp.int32, (S, S), 0)
    column = lax.broadcasted_iota(jnp.int32, (S, S), 1)
    unit = jnp.where(row == column, 1.0, 0.0)
    gram = gram_ref[...]
    diagonal = jnp.where(row == column, gram, 0.0)
    down = lax.rsqrt(jnp.sum(diagonal, axis=1, keepdims=True))
    across = lax.rsqrt(jnp.sum(diagonal, axis=0, keepdims=True))
    a_ref[...] = gram * down * across
    x_ref[...] = unit

    def residual():
        x = x_ref[...]
        return unit - exact(exact(x, a_ref[...]), x.T)

    def size(e):
        return jnp.sum(e * e)

    def improve(e):
        lower = jnp.where(row > column, e, jnp.where(row == column, 0.5 * e, 0.0))
        x_ref[...] += exact(lower, x_ref[...])

    state_ref[0] = 0
    start = unit - a_ref[...]
    start_size = size(start)

    @pl.when(start_size < 0.16)
    def _():
        improve(start)
        state_ref[0] = jnp.where(start_size < 1e-6, 2, 1)

    for _ in range(5):

        @pl.when(state_ref[0] == 1)
        def _():
            e = residual()
            e_size = size(e)
            improve(e)
            state_ref[0] = jnp.where(e_size < 1e-6, 2, 1)

    @pl.when(state_ref[0] != 2)
    def _():
        x_ref[...] = unit
        lanes = lax.broadcasted_iota(jnp.int32, (1, S), 1)

        def step(j, _):
            line = a_ref[pl.ds(j, 1), :]
            scale = lax.rsqrt(jnp.sum(jnp.where(lanes == j, line, 0.0), axis=1, keepdims=True))
            a = a_ref[...]
            factor = jnp.sum(jnp.where(column == j, a, 0.0), axis=1, keepdims=True) * scale
            factor = jnp.where(row[:, :1] > j, factor, 0.0)
            x_line = x_ref[pl.ds(j, 1), :] * scale
            a_ref[...] = a - factor * (line * scale)
            x_ref[...] = jnp.where(row == j, x_line, x_ref[...] - factor * x_line)
            return 0

        lax.fori_loop(0, S, step, 0)

    x_ref[...] = x_ref[...] * across


def turn_kernel(second_ref, own_ref, other_ref, upper_ref, out_ref, gram_ref, a_ref, x_ref, i_high_ref, i_low_ref, state_ref):
    @pl.when(pl.program_id(0) == 0)
    def _():
        upper = upper_ref[0] == 1
        gram_ref[: S // 2, :] = jnp.where(upper, other_ref[...], own_ref[...])
        gram_ref[S // 2 :, :] = jnp.where(upper, own_ref[...], other_ref[...])
        inverse_factor(gram_ref, a_ref, x_ref, state_ref)
        i_high, i_low = split(x_ref[...].T)
        i_high_ref[...] = i_high
        i_low_ref[...] = i_low

    i_high, i_low = i_high_ref[...], i_low_ref[...]
    i_twice = jnp.concatenate([i_high, i_high])
    for p in range(B):
        high, low = split(second_ref[p])
        out_ref[p] = mm(jnp.concatenate([high, low], axis=1), i_twice) + mm(high, i_low)


def turn(second, own, other, upper):
    return pl.pallas_call(
        turn_kernel,
        grid=(STEPS,),
        in_specs=[plane_spec(), whole(S // 2), whole(S // 2), SCALARS],
        out_specs=plane_spec(),
        out_shape=FULL,
        scratch_shapes=[pltpu.VMEM((S, S), F32)] * 3 + [pltpu.VMEM((S, S), BF16)] * 2 + [pltpu.SMEM((1,), jnp.int32)],
        compiler_params=params(16),
        cost_estimate=cost(1 << 28, 4 << 20),
        name="turn",
    )(second, own, other, upper)


def per_device(states, potential, atom_sites, projectors, energies):
    gx, gy = lax.axis_index("gx"), lax.axis_index("gy")
    depth = lax.axis_size("gzs")
    count = 4 * depth
    barrier = lax.optimization_barrier

    def send(value, flip=0, move=0):
        def target(d):
            return (d // depth * depth ^ flip) + (d + move) % depth

        return lax.ppermute(value, AXES, [(d, target(d)) for d in range(count)])

    over_x, over_y = 2 * depth, depth
    inner_ones = [d for d in range(count) if d % 4 in (1, 2)]
    outer_ones = [d for d in range(count) if d % 4 in (0, 3)]
    inner = ((lax.axis_index("gzs") + 1) // 2 % 2).astype(jnp.int32).reshape(1)
    s = states.reshape(C, ROWS, S)
    pot = potential.reshape(32, 128)

    atoms = jnp.concatenate(
        [projectors.reshape(4, TAPS), atom_sites.astype(F32), energies[:, None], jnp.zeros((4, 768 - TAPS - 4), F32)],
        axis=1,
    ).reshape(24, 128)
    mate = send(s, over_x)
    corner = jnp.stack([gx * C, gy * C]).astype(jnp.int32)
    upper = gx.astype(jnp.int32).reshape(1)
    to_pack, corner, upper, inner = barrier((s, corner, upper, inner))
    below, above = send(atoms, 0, 1), send(atoms, 0, -1)
    one_edge, head, tail = pack(to_pack)
    one_edge = send(one_edge, over_y)
    head, tail, below, above = barrier((head, tail, below, above))
    parcel = stack(below, atoms, above, pot)
    parcel_y = send(parcel, over_y)
    parcel_x = send(parcel, over_x)
    low, high = send(tail, 0, 1), send(head, 0, -1)
    message, relay, mid = pack_rest(s, inner)
    vb = spread(parcel)
    beside = side_x(s, mate)
    parcel_y, one_edge, message, relay, beside = barrier((parcel_y, one_edge, message, relay, beside))
    relayed = lax.ppermute(relay, AXES, [(d, d ^ over_y ^ 1) for d in outer_ones])
    message = send(message, over_y)
    parcel_xy = send(parcel_y, over_x)
    gg, part, energy = prep([parcel, parcel_x, parcel_y, parcel_xy], corner, vb, s)

    part, relayed = barrier((part, relayed))
    relayed = lax.ppermute(relayed, AXES, [(d, d ^ 1) for d in inner_ones])
    part = part + send(part, over_x)
    part_mate = send(part, over_y)
    side_part = side_z(s, beside, low, high)
    edges = [one_edge, message.reshape(C - FIRST, EDGE, S), relayed]
    vb = vb.reshape(C, ROWS, S)
    q, mix, head, tail = make_first(s, side_part, vb, edges, inner, part, part_mate)
    low, high = send(tail, 0, 1), send(head, 0, -1)
    mate = send(mix, over_x)
    mid, part_mate = barrier((mid, part_mate))
    mid = lax.ppermute(mid, AXES, [(d, d ^ over_y) for d in inner_ones])
    vb_mate = spread(parcel_y).reshape(C, ROWS, S)
    part_two = side_again(mix, mate)
    base = make_base(s, mid, vb, vb_mate, q, side_part, part_two, edges, inner)
    gg = gg.reshape(2, C, ROWS, S)
    second, own, give = make_second(base, [low, high], gg, [part, part_mate, energy], upper)

    own = own + send(give, over_x)
    for flip in (32, 36, 1, 3, 8, 24):
        own = own + lax.ppermute(own, AXES, [(d, d ^ flip) for d in range(count)])
    return turn(second, own, send(own, over_x), upper).reshape(C, C, C, S)


def solution(mesh):
    return jax.shard_map(
        per_device,
        mesh=mesh,
        in_specs=(
            P("gx", "gy", "gzs", None),
            P("gx", "gy", "gzs"),
            P(("gx", "gy", "gzs"), None),
            P(("gx", "gy", "gzs"), None, None, None),
            P(("gx", "gy", "gzs")),
        ),
        out_specs=P("gx", "gy", "gzs", None),
        check_vma=False,
    )
```

```python
import math

import jax
import jax.numpy as jnp
from jax import lax
from jax.experimental import pallas as pl
from jax.experimental.pallas import tpu as pltpu
from jax.sharding import PartitionSpec as P

AXES = ("gx", "gy", "gzs")
H = 6
C = 16
ROWS = C * C
CELLS = C * C * C
NCELLS = 32 * 32 * 512
S = 128
W = 9
R = 4
NEAR = 48
TAPS = W * W * W
F32 = jnp.float32
BF16 = jnp.bfloat16

grid_step = 0.6
filter_centre = 36.0
filter_half = 26.0


def weights():
    taps = []
    for k in range(1, 7):
        top = 2.0 * (-1) ** (k + 1) * math.factorial(6) ** 2
        under = k * k * math.factorial(6 - k) * math.factorial(6 + k)
        taps.append(top / under)
    scale = -0.5 / (grid_step * grid_step)
    off = [scale * t / filter_half for t in taps]
    diagonal = 3.0 * scale * (-2.0 * sum(taps))
    return off, diagonal


OFF, DIAGONAL = weights()


def params(mib):
    return pltpu.CompilerParams(vmem_limit_bytes=mib * 1024 * 1024)


def cost(flops, nbytes):
    return pl.CostEstimate(flops=flops, bytes_accessed=nbytes, transcendentals=0)


def sds(shape, dtype=F32):
    return jax.ShapeDtypeStruct(shape, dtype)


def split(value):
    high = value.astype(BF16)
    low = (value - high.astype(F32)).astype(BF16)
    return high, low


def mm(a, b):
    return jnp.dot(a, b, preferred_element_type=F32)


def tap_sum(at, index):
    total = None
    for k in range(1, 7):
        term = OFF[k - 1] * (at(index + k) + at(index - k))
        total = term if total is None else total + term
    return total


B = 4
STEPS = C // B
N = 2
FIRST = 6
MIDDLE = 10
EDGE = 192
MID = 64
MID_START = (MIDDLE - FIRST) * EDGE


def stride_rows(z):
    return pl.ds(z, C, stride=C)


def plane_spec(rows=ROWS, planes=B):
    return pl.BlockSpec((planes, rows, S), lambda i: (i, 0, 0))


def halo_spec(planes=B):
    return pl.BlockSpec((H, planes, C, S), lambda i: (0, i, 0, 0))


def part_spec(part):
    return pl.BlockSpec((1, B, ROWS, S), lambda i: (part, i, 0, 0))


def whole(rows=S):
    return pl.BlockSpec((rows, S), lambda i: (0, 0))


def edge_spec(start, stop):
    return pl.BlockSpec((N, EDGE, S), lambda i: (jnp.clip(i - start // N, 0, (stop - start) // N - 1), 0, 0))


def edge_specs():
    return [edge_spec(0, FIRST), edge_spec(FIRST, C), edge_spec(MIDDLE, C)]


def for_piece(edges, inner_ref, body):
    step = pl.program_id(0)
    direct = (inner_ref[0] == 1) | (step < MIDDLE // N)

    @pl.when(step < FIRST // N)
    def _():
        body(edges[0])

    @pl.when((step >= FIRST // N) & direct)
    def _():
        body(edges[1])

    @pl.when(jnp.logical_not(direct))
    def _():
        body(edges[2])


SCALARS = pl.BlockSpec(memory_space=pltpu.SMEM)
FULL = sds((C, ROWS, S))
FULL_ROWS = sds((CELLS, S))
HALO_ROWS = H * ROWS
MESSAGE = sds((HALO_ROWS + 2 * NEAR, S))
HALO = sds((H, C, C, S))
EDGES = [sds((FIRST, EDGE, S)), sds((C - FIRST, EDGE, S)), sds((C - MIDDLE, EDGE, S))]


def halo_rows(x, z):
    return pl.ds(pl.multiple_of(z * ROWS + x * C, C), C)


def halves(y, half):
    return slice(y * C + half * 8, y * C + half * 8 + 8)


def pack_edges(s_ref, out_ref):
    out_ref[:, 0:96, :] = s_ref[:, 0:96, :]
    out_ref[:, 96:192, :] = s_ref[:, 160:256, :]


def pack_kernel(s_ref, edge_ref, head_ref, tail_ref):
    @pl.when(pl.program_id(0) < FIRST // N)
    def _():
        pack_edges(s_ref, edge_ref)

    for p in range(N):
        for z in range(H):
            head_ref[z, p] = s_ref[p, stride_rows(z), :]
            tail_ref[z, p] = s_ref[p, stride_rows(C - H + z), :]


def pack(s):
    return pl.pallas_call(
        pack_kernel,
        grid=(C // N,),
        in_specs=[plane_spec(ROWS, N)],
        out_specs=edge_specs()[:1] + [halo_spec(N), halo_spec(N)],
        out_shape=EDGES[:1] + [HALO, HALO],
        compiler_params=params(12),
        cost_estimate=cost(1 << 32, 6 << 20),
        name="pack",
    )(s)


def pack_rest_kernel(s_ref, inner_ref, message_ref, relay_ref, mid_ref):
    step = pl.program_id(0)
    inner = inner_ref[0] == 1
    mid_ref[...] = s_ref[:, 96:160, :]

    @pl.when(step >= MIDDLE // N)
    def _():
        pack_edges(s_ref, relay_ref)

    @pl.when((step >= FIRST // N) & (inner | (step < MIDDLE // N)))
    def _():
        for p in range(N):
            row = pl.multiple_of((step * N + p - FIRST) * EDGE, MID)
            message_ref[pl.ds(row, 96), :] = s_ref[p, 0:96, :]
            message_ref[pl.ds(row + 96, 96), :] = s_ref[p, 160:256, :]

    @pl.when(jnp.logical_not(inner))
    def _():
        for p in range(N):
            row = pl.multiple_of(MID_START + (step * N + p) * MID, MID)
            message_ref[pl.ds(row, MID), :] = s_ref[p, 96:160, :]


def pack_rest(s, inner):
    rows = (C - FIRST) * EDGE
    message, relay, mid = pl.pallas_call(
        pack_rest_kernel,
        grid=(C // N,),
        in_specs=[plane_spec(ROWS, N), SCALARS],
        out_specs=[whole(rows), edge_spec(MIDDLE, C), plane_spec(MID, N)],
        out_shape=[sds((rows, S)), EDGES[2], sds((C, MID, S))],
        compiler_params=params(12),
        cost_estimate=cost(1 << 31, 4 << 20),
        name="pack_rest",
    )(s, inner)
    return message, relay, mid


def stack_kernel(*refs):
    start = 0
    for ref in refs[:-1]:
        refs[-1][start : start + ref.shape[0], :] = ref[...]
        start += ref.shape[0]


def stack(*arrays):
    rows = sum(a.shape[0] for a in arrays)
    return pl.pallas_call(stack_kernel, out_shape=sds((rows, S)), compiler_params=params(4), name="stack")(*arrays)


def along_x(s_ref, mate_ref, out_ref, add):
    def column(block, _):
        rows = pl.ds(pl.multiple_of(block * 8, 8), 8)
        ring = [mate_ref[C - H + i, rows, :] for i in range(H)]
        ring += [s_ref[x, rows, :] for x in range(C)]
        ring += [mate_ref[i, rows, :] for i in range(H)]
        for x in range(C):
            value = tap_sum(lambda i: ring[H + i], x)
            if add:
                value = value + out_ref[x, rows, :]
            out_ref[x, rows, :] = value
        return 0

    lax.fori_loop(0, ROWS // 8, column, 0)


def z_taps(ext_ref, y):
    return tap_sum(lambda k: ext_ref[y * 32 + 8 + k : y * 32 + 24 + k, :], 0)


def side_x_kernel(s_ref, mate_ref, out_ref):
    along_x(s_ref, mate_ref, out_ref, False)


def side_x(s, mate):
    return pl.pallas_call(
        side_x_kernel,
        out_shape=FULL,
        compiler_params=params(12),
        cost_estimate=cost(1 << 24, 6 << 20),
        name="side_x",
    )(s, mate)


def side_z_kernel(s_ref, part_ref, low_ref, high_ref, out_ref, ext_ref):
    def plane(x, _):
        for y in range(C):
            ext_ref[y * 32 + 8 : y * 32 + 24, :] = s_ref[x, y * C : (y + 1) * C, :]
        for z in range(H):
            ext_ref[pl.ds(2 + z, C, stride=32), :] = low_ref[z, x]
            ext_ref[pl.ds(24 + z, C, stride=32), :] = high_ref[z, x]
        for y in range(C):
            rows = slice(y * C, (y + 1) * C)
            out_ref[x, rows, :] = part_ref[x, rows, :] + z_taps(ext_ref, y)
        return 0

    lax.fori_loop(0, C, plane, 0)


def side_z(s, part, low, high):
    return pl.pallas_call(
        side_z_kernel,
        out_shape=FULL,
        scratch_shapes=[pltpu.VMEM((C * 32, S), F32)],
        compiler_params=params(14),
        cost_estimate=cost(1 << 24, 8 << 20),
        name="side_z",
    )(s, part, low, high)


def side_again_kernel(s_ref, mate_ref, out_ref, ext_ref):
    for y in range(C):
        ext_ref[y * 32 : y * 32 + 8, :] = jnp.zeros((8, S), F32)
        ext_ref[y * 32 + 24 : y * 32 + 32, :] = jnp.zeros((8, S), F32)

    def plane(x, _):
        for y in range(C):
            ext_ref[y * 32 + 8 : y * 32 + 24, :] = s_ref[x, y * C : (y + 1) * C, :]
        for y in range(C):
            out_ref[x, y * C : (y + 1) * C, :] = z_taps(ext_ref, y)
        return 0

    lax.fori_loop(0, C, plane, 0)
    along_x(s_ref, mate_ref, out_ref, True)


def side_again(s, mate):
    return pl.pallas_call(
        side_again_kernel,
        out_shape=FULL,
        scratch_shapes=[pltpu.VMEM((C * 32, S), F32)],
        compiler_params=params(12),
        cost_estimate=cost(1 << 25, 6 << 20),
        name="side_again",
    )(s, mate)


def tap_weight(distance):
    value = jnp.zeros(distance.shape, F32)
    for k in range(1, 7):
        value = jnp.where(distance == k, OFF[k - 1], value)
    return value


def ring_tables(coordinate):
    masks, factors = [], []
    for t in range(W):
        away = (coordinate - t) & 31
        masks.append(away == 0)
        factors.append(tap_weight(jnp.minimum(away, 32 - away)))
    return masks, factors


def spread_kernel(parcel_ref, vb_ref):
    def spread_row(row, _):
        line = (parcel_ref[pl.ds(72 + row, 1), :] + (DIAGONAL - filter_centre)) * (1.0 / filter_half)
        start = pl.multiple_of(row * 128, 128)
        vb_ref[pl.ds(start, 128), :] = jnp.broadcast_to(line, (128, 128)).T
        return 0

    lax.fori_loop(0, CELLS // 128, spread_row, 0, unroll=8)


def spread(parcel):
    return pl.pallas_call(
        spread_kernel,
        out_shape=FULL_ROWS,
        compiler_params=params(8),
        cost_estimate=cost(1 << 20, 2 << 20),
        name="spread",
    )(parcel)


def prep_kernel(*refs):
    parcels = refs[:4]
    corner_ref, vb_ref, s_ref, gg_ref, coef_ref, energy_ref, near_ref, table_ref, a1_ref, a1z_ref, a2_ref, a2s_ref = refs[4:]
    upper_x, upper_y = corner_ref[0] > 0, corner_ref[1] > 0
    for slab in range(3):
        own, over_x, over_y, over_xy = [parcel[slab * 24 : slab * 24 + 24, :] for parcel in parcels]
        same_x = [jnp.where(upper_y, over_y, own), jnp.where(upper_y, own, over_y)]
        other_x = [jnp.where(upper_y, over_xy, over_x), jnp.where(upper_y, over_x, over_xy)]
        ordered = [jnp.where(upper_x, o, m) for m, o in zip(same_x, other_x)]
        ordered += [jnp.where(upper_x, m, o) for m, o in zip(same_x, other_x)]
        for j in range(4):
            near_ref[slab * 96 + j * 24 : slab * 96 + j * 24 + 24, :] = ordered[j]
    blank = jnp.zeros((16, 128), F32)
    for block in range(6):
        rows = near_ref[pl.ds(block, NEAR, stride=6), :]
        table_ref[block * 128 : block * 128 + 128, :] = jnp.concatenate([rows, blank, rows, blank]).T
    at = TAPS + 3 - 640
    energy_ref[...] = jnp.broadcast_to(rows[:, at : at + 1] * (1.0 / filter_half), (NEAR, S))

    shape = (8, 128)
    sub = lax.broadcasted_iota(jnp.int32, shape, 0)
    lane = lax.broadcasted_iota(jnp.int32, shape, 1)
    first_lanes = lane < 64
    sites = [jnp.broadcast_to(table_ref[TAPS + d : TAPS + d + 1, :], shape).astype(jnp.int32) for d in range(3)]
    px = sites[0] - corner_ref[0]
    py = sites[1] - corner_ref[1]
    pz = (sites[2] & 15) + (((lane & 63) >> 4) - 1) * C
    zero = jnp.zeros(shape, F32)

    dz = sub + (lane >> 6) * 8 - pz + R
    z_masks = [dz == t for t in range(W)]
    z_factors = [tap_weight(jnp.abs(dz - t)) for t in range(W)]

    def place_z(ij, _):
        acc = zero
        along = zero
        for t in range(W):
            row = jnp.broadcast_to(table_ref[pl.ds(ij * W + t, 1), :], shape)
            acc = jnp.where(z_masks[t], row, acc)
            along = along + z_factors[t] * row
        a1_ref[ij] = acc
        a1z_ref[ij] = along
        return 0

    lax.fori_loop(0, W * W, place_z, 0, unroll=3)

    def place_y(y, _):
        masks, factors = ring_tables(y - py + R)
        for i in range(W):
            acc = zero
            along = zero
            moved = zero
            for t in range(W):
                value = a1_ref[i * W + t]
                acc = jnp.where(masks[t], value, acc)
                along = along + factors[t] * value
                moved = jnp.where(masks[t], a1z_ref[i * W + t], moved)
            a2_ref[i, y] = acc
            a2s_ref[i, y] = along + moved
        return 0

    lax.fori_loop(0, C, place_y, 0)

    def place_x(x, _):
        masks, factors = ring_tables(x - px + R)

        def per_y(y, _):
            row = pl.multiple_of(x * ROWS + y * C, C)
            acc = zero
            along = zero
            moved = zero
            for t in range(W):
                value = a2_ref[t, y]
                acc = jnp.where(masks[t], value, acc)
                along = along + factors[t] * value
                moved = jnp.where(masks[t], a2s_ref[t, y], moved)
            v = vb_ref[pl.ds(row, C), :]
            moved = along + moved + jnp.where(first_lanes, v[:8], v[8:]) * acc
            lower = jnp.where(first_lanes, acc, pltpu.roll(moved, 64, 1))
            upper = jnp.where(first_lanes, pltpu.roll(acc, 64, 1), moved)
            high, low = split(jnp.concatenate([lower, upper], axis=0))
            gg_ref[0, pl.ds(row, C), :] = high
            gg_ref[1, pl.ds(row, C), :] = low
            return 0

        lax.fori_loop(0, C, per_y, 0, unroll=16)
        return 0

    lax.fori_loop(0, C, place_x, 0)

    coef_ref[...] = jnp.zeros((3, NEAR, S), F32)

    def contract(x, _):
        rows = pl.ds(pl.multiple_of(x * 2 * ROWS, ROWS), 2 * ROWS)
        g_high, g_low = gg_ref[0, rows, :], gg_ref[1, rows, :]
        t_high, t_low = g_high.T, g_low.T
        high, low = split(s_ref[rows, :])
        got = mm(t_high, high) + (mm(t_high, low) + mm(t_low, high))
        t_high, t_low = t_high[:NEAR], t_low[:NEAR]
        pair = mm(t_high, g_high) + (mm(t_high, g_low) + mm(t_low, g_high))
        for slab in range(3):
            rows = slice(slab * C, slab * C + C)
            coef_ref[slab, 0:16] += got[rows]
            coef_ref[slab, 16:32] += got[64 + slab * C : 80 + slab * C]
            coef_ref[slab, 32:48] += pair[rows]
        return 0

    lax.fori_loop(0, C // 2, contract, 0, unroll=2)


def prep(parcels, corner, vb, s):
    vmem = pl.BlockSpec(memory_space=pltpu.VMEM)
    return pl.pallas_call(
        prep_kernel,
        in_specs=[vmem] * 4 + [pl.BlockSpec(memory_space=pltpu.SMEM), vmem, vmem],
        out_shape=[sds((2, CELLS, S), BF16), sds((3, NEAR, S)), sds((NEAR, S))],
        scratch_shapes=[
            pltpu.VMEM((288, 128), F32),
            pltpu.VMEM((768, 128), F32),
            pltpu.VMEM((W * W, 8, 128), F32),
            pltpu.VMEM((W * W, 8, 128), F32),
            pltpu.VMEM((W, C, 8, 128), F32),
            pltpu.VMEM((W, C, 8, 128), F32),
        ],
        compiler_params=params(16),
        cost_estimate=cost(1 << 27, 10 << 20),
        name="prep",
    )(*parcels, corner, vb, s.reshape(CELLS, S))


def move_pair(shares, away):
    lane = lax.broadcasted_iota(jnp.int32, (16, 128), 1)
    keep = (lane < 32) if away < 0 else (lane >= 16) & (lane < 48)
    pair = jnp.where(keep, pltpu.roll(shares[32:48], (away * 16) % 128, 1), 0.0)
    return jnp.concatenate([shares[0:32], pair])


def first_kernel(s_ref, side_ref, vb_ref, *refs):
    inner_ref, part_ref, mate_ref, q_ref, mix_ref, head_ref, tail_ref = refs[3:]
    step = pl.program_id(0)

    @pl.when(step == 0)
    def _():
        for j in range(2):
            rows = slice(HALO_ROWS + j * NEAR, HALO_ROWS + (j + 1) * NEAR)
            head_ref[rows, :] = part_ref[j] + mate_ref[j]
            tail_ref[rows, :] = part_ref[j + 1] + mate_ref[j + 1]

    def planes(edge_ref):
        for p in range(N):
            for half in range(2):
                ring = {y: s_ref[p, halves(y, half), :] for y in range(C)}
                for y in range(H):
                    ring[C + y] = edge_ref[p, halves(y, half), :]
                    ring[y - H] = edge_ref[p, halves(H + y, half), :]
                for y in range(C):
                    rows = halves(y, half)
                    dy = tap_sum(lambda i: ring[i], y)
                    q = dy + vb_ref[p, rows, :] * ring[y]
                    q_ref[p, rows, :] = q
                    mix_ref[p, rows, :] = side_ref[p, rows, :] + q + dy
            for z in range(H):
                rows = halo_rows(step * N + p, z)
                head_ref[rows, :] = mix_ref[p, stride_rows(z), :]
                tail_ref[rows, :] = mix_ref[p, stride_rows(C - H + z), :]

    for_piece(refs[:3], inner_ref, planes)


def make_first(s, side_part, vb, edges, inner, part, part_mate):
    shares = pl.BlockSpec((3, NEAR, S), lambda i: (0, 0, 0))
    return pl.pallas_call(
        first_kernel,
        grid=(C // N,),
        in_specs=[plane_spec(ROWS, N)] * 3 + edge_specs() + [SCALARS] + [shares] * 2,
        out_specs=[plane_spec(ROWS, N), plane_spec(ROWS, N), whole(MESSAGE.shape[0]), whole(MESSAGE.shape[0])],
        out_shape=[FULL, FULL, MESSAGE, MESSAGE],
        compiler_params=params(16),
        cost_estimate=cost(1 << 24, 14 << 20),
        name="first",
    )(s, side_part, vb, *edges, inner, part, part_mate)


def base_kernel(s_ref, mid_ref, vb_ref, vb_mate_ref, q_ref, side_ref, part_ref, *refs):
    inner_ref, message_ref, out_ref, middle_ref = refs[3:]
    step = pl.program_id(0)
    inner = inner_ref[0] == 1

    @pl.when(inner)
    def _():
        middle_ref[...] = mid_ref[...]

    @pl.when(jnp.logical_not(inner))
    def _():
        for p in range(N):
            middle_ref[p] = message_ref[pl.ds(pl.multiple_of(MID_START + (step * N + p) * MID, MID), MID), :]

    def planes(edge_ref):
        for p in range(N):
            for half in range(2):

                def other(y, p=p, half=half):
                    if y < H:
                        return edge_ref[p, halves(y, half), :]
                    if y < C - H:
                        return middle_ref[p, halves(y - H, half), :]
                    return edge_ref[p, halves(y - 4, half), :]

                ring = [s_ref[p, halves(y, half), :] for y in range(C)] + [other(y) for y in range(C)]
                q = {y: q_ref[p, halves(y, half), :] for y in range(C)}
                for y in list(range(H)) + list(range(C - H, C)):
                    v = vb_mate_ref[p, halves(y, half), :]
                    q[C + y] = tap_sum(lambda i: ring[i % 32], C + y) + v * ring[C + y]
                for y in range(C):
                    rows = halves(y, half)
                    total = tap_sum(lambda i: q[i % 32], y)
                    total = total + vb_ref[p, rows, :] * (side_ref[p, rows, :] + q[y])
                    out_ref[p, rows, :] = 2.0 * (total + part_ref[p, rows, :]) - ring[y]

    for_piece(refs[:3], inner_ref, planes)


def make_base(s, mid, vb, vb_mate, q, side_part, part, edges, inner):
    return pl.pallas_call(
        base_kernel,
        grid=(C // N,),
        in_specs=[plane_spec(ROWS, N), plane_spec(MID, N)]
        + [plane_spec(ROWS, N)] * 5
        + edge_specs()
        + [SCALARS, whole((C - FIRST) * EDGE)],
        out_specs=plane_spec(ROWS, N),
        out_shape=FULL,
        scratch_shapes=[pltpu.VMEM((N, MID, S), F32)],
        compiler_params=params(16),
        cost_estimate=cost(1 << 25, 16 << 20),
        name="base",
    )(s, mid, vb, vb_mate, q, side_part, part, *edges, inner, edges[1].reshape(-1, S))


def second_kernel(base_ref, low_ref, high_ref, gg_high_ref, gg_low_ref, *rest):
    part_ref, mate_ref, energy_ref, upper_ref, second_ref, keep_ref, give_ref, gram_ref, cross_ref, w_ref, halo_ref = rest
    step = pl.program_id(0)

    @pl.when(step == 0)
    def _():
        gram_ref[...] = jnp.zeros((S, S), F32)
        cross_ref[...] = jnp.zeros((S, S), F32)
        w_ref[...] = jnp.zeros((S, S), F32)
        halo_ref[...] = jnp.zeros((B, ROWS, S), F32)
        mine = [part_ref[j] + mate_ref[j] for j in range(3)]
        below = [move_pair(low_ref[HALO_ROWS + j * NEAR : HALO_ROWS + (j + 1) * NEAR, :], -1) for j in range(2)]
        above = [move_pair(high_ref[HALO_ROWS + j * NEAR : HALO_ROWS + (j + 1) * NEAR, :], 1) for j in range(2)]
        slabs = [mine[0] + below[0], mine[1] + below[1] + above[0], mine[2] + above[1]]
        near = jnp.concatenate([slab[0:16] for slab in slabs]) * energy_ref[...]
        lane = lax.broadcasted_iota(jnp.int32, (NEAR, S), 1)
        pair = jnp.where(lane < NEAR, jnp.concatenate([slab[32:48] for slab in slabs]), 0.0)
        two = jnp.concatenate([slab[16:32] for slab in slabs])
        two = two + exact(pair, jnp.concatenate([near, jnp.zeros((S - NEAR, S), F32)]))
        w_ref[0:NEAR, :] = 2.0 * energy_ref[...] * two
        w_ref[64 : 64 + NEAR, :] = 2.0 * near

    for p in range(B):
        low = [low_ref[halo_rows(step * B + p, j), :] for j in range(H)]
        high = [high_ref[halo_rows(step * B + p, j), :] for j in range(H)]
        for z in range(H):
            add = sum((2.0 * OFF[k - 1]) * low[z - k + H] for k in range(z + 1, H + 1))
            halo_ref[p, stride_rows(z), :] = add
            add = sum((2.0 * OFF[H + j - z - 1]) * high[j] for j in range(z + 1))
            halo_ref[p, stride_rows(C - H + z), :] = add

    w_high, w_low = split(w_ref[...])
    w_twice = jnp.concatenate([w_high, w_high])
    gram = jnp.zeros((S, 2 * S), F32)
    for p in range(B):
        g_high, g_low = gg_high_ref[0, p], gg_low_ref[0, p]
        near = mm(jnp.concatenate([g_high, g_low], axis=1), w_twice) + mm(g_high, w_low)
        value = base_ref[p] + halo_ref[p] + near
        second_ref[p] = value
        s_high, s_low = split(value)
        gram += mm(s_high.T, jnp.concatenate([s_high, s_low], axis=1))
    gram_ref[...] += gram[:, :S]
    cross_ref[...] += gram[:, S:]

    @pl.when(step == STEPS - 1)
    def _():
        cross = cross_ref[...]
        gram = (gram_ref[...] + (cross + cross.T)) * (1.0 / NCELLS)
        upper = upper_ref[0] == 1
        keep_ref[...] = jnp.where(upper, gram[S // 2 :], gram[: S // 2])
        give_ref[...] = jnp.where(upper, gram[: S // 2], gram[S // 2 :])


def make_second(base, halos, gg, shares, upper):
    three = pl.BlockSpec((3, NEAR, S), lambda i: (0, 0, 0))
    return pl.pallas_call(
        second_kernel,
        grid=(STEPS,),
        in_specs=[plane_spec()]
        + [whole(MESSAGE.shape[0])] * 2
        + [part_spec(0), part_spec(1), three, three, whole(NEAR), SCALARS],
        out_specs=[plane_spec(), whole(S // 2), whole(S // 2)],
        out_shape=[FULL, sds((S // 2, S)), sds((S // 2, S))],
        scratch_shapes=[pltpu.VMEM((S, S), F32)] * 3 + [pltpu.VMEM((B, ROWS, S), F32)],
        compiler_params=params(16),
        cost_estimate=cost(1 << 27, 8 << 20),
        name="second",
    )(base, *halos, gg, gg, *shares, upper)


def exact(a, b):
    return jnp.dot(a, b, precision=lax.Precision.HIGHEST, preferred_element_type=F32)


def inverse_factor(gram_ref, a_ref, x_ref, state_ref):
    row = lax.broadcasted_iota(jnp.int32, (S, S), 0)
    column = lax.broadcasted_iota(jnp.int32, (S, S), 1)
    unit = jnp.where(row == column, 1.0, 0.0)
    gram = gram_ref[...]
    diagonal = jnp.where(row == column, gram, 0.0)
    down = lax.rsqrt(jnp.sum(diagonal, axis=1, keepdims=True))
    across = lax.rsqrt(jnp.sum(diagonal, axis=0, keepdims=True))
    a_ref[...] = gram * down * across
    x_ref[...] = unit

    def residual():
        x = x_ref[...]
        return unit - exact(exact(x, a_ref[...]), x.T)

    def size(e):
        return jnp.sum(e * e)

    def improve(e):
        lower = jnp.where(row > column, e, jnp.where(row == column, 0.5 * e, 0.0))
        x_ref[...] += exact(lower, x_ref[...])

    state_ref[0] = 0
    start = unit - a_ref[...]
    start_size = size(start)

    @pl.when(start_size < 0.16)
    def _():
        improve(start)
        state_ref[0] = jnp.where(start_size < 1e-6, 2, 1)

    for _ in range(5):

        @pl.when(state_ref[0] == 1)
        def _():
            e = residual()
            e_size = size(e)
            improve(e)
            state_ref[0] = jnp.where(e_size < 1e-6, 2, 1)

    @pl.when(state_ref[0] != 2)
    def _():
        x_ref[...] = unit
        lanes = lax.broadcasted_iota(jnp.int32, (1, S), 1)

        def step(j, _):
            line = a_ref[pl.ds(j, 1), :]
            scale = lax.rsqrt(jnp.sum(jnp.where(lanes == j, line, 0.0), axis=1, keepdims=True))
            a = a_ref[...]
            factor = jnp.sum(jnp.where(column == j, a, 0.0), axis=1, keepdims=True) * scale
            factor = jnp.where(row[:, :1] > j, factor, 0.0)
            x_line = x_ref[pl.ds(j, 1), :] * scale
            a_ref[...] = a - factor * (line * scale)
            x_ref[...] = jnp.where(row == j, x_line, x_ref[...] - factor * x_line)
            return 0

        lax.fori_loop(0, S, step, 0)

    x_ref[...] = x_ref[...] * across


def turn_kernel(second_ref, own_ref, other_ref, upper_ref, out_ref, gram_ref, a_ref, x_ref, i_high_ref, i_low_ref, state_ref):
    @pl.when(pl.program_id(0) == 0)
    def _():
        upper = upper_ref[0] == 1
        gram_ref[: S // 2, :] = jnp.where(upper, other_ref[...], own_ref[...])
        gram_ref[S // 2 :, :] = jnp.where(upper, own_ref[...], other_ref[...])
        inverse_factor(gram_ref, a_ref, x_ref, state_ref)
        i_high, i_low = split(x_ref[...].T)
        i_high_ref[...] = i_high
        i_low_ref[...] = i_low

    i_high, i_low = i_high_ref[...], i_low_ref[...]
    i_twice = jnp.concatenate([i_high, i_high])
    for p in range(B):
        high, low = split(second_ref[p])
        out_ref[p] = mm(jnp.concatenate([high, low], axis=1), i_twice) + mm(high, i_low)


def turn(second, own, other, upper):
    return pl.pallas_call(
        turn_kernel,
        grid=(STEPS,),
        in_specs=[plane_spec(), whole(S // 2), whole(S // 2), SCALARS],
        out_specs=plane_spec(),
        out_shape=FULL,
        scratch_shapes=[pltpu.VMEM((S, S), F32)] * 3 + [pltpu.VMEM((S, S), BF16)] * 2 + [pltpu.SMEM((1,), jnp.int32)],
        compiler_params=params(16),
        cost_estimate=cost(1 << 28, 4 << 20),
        name="turn",
    )(second, own, other, upper)


def per_device(states, potential, atom_sites, projectors, energies):
    gx, gy = lax.axis_index("gx"), lax.axis_index("gy")
    depth = lax.axis_size("gzs")
    count = 4 * depth
    barrier = lax.optimization_barrier

    def send(value, flip=0, move=0):
        def target(d):
            return (d // depth * depth ^ flip) + (d + move) % depth

        return lax.ppermute(value, AXES, [(d, target(d)) for d in range(count)])

    over_x, over_y = 2 * depth, depth
    inner_ones = [d for d in range(count) if d % 4 in (1, 2)]
    outer_ones = [d for d in range(count) if d % 4 in (0, 3)]
    inner = ((lax.axis_index("gzs") + 1) // 2 % 2).astype(jnp.int32).reshape(1)
    s = states.reshape(C, ROWS, S)
    pot = potential.reshape(32, 128)

    atoms = jnp.concatenate(
        [projectors.reshape(4, TAPS), atom_sites.astype(F32), energies[:, None], jnp.zeros((4, 768 - TAPS - 4), F32)],
        axis=1,
    ).reshape(24, 128)
    mate = send(s, over_x)
    corner = jnp.stack([gx * C, gy * C]).astype(jnp.int32)
    upper = gx.astype(jnp.int32).reshape(1)
    to_pack, corner, upper, inner = barrier((s, corner, upper, inner))
    below, above = send(atoms, 0, 1), send(atoms, 0, -1)
    one_edge, head, tail = pack(to_pack)
    one_edge = send(one_edge, over_y)
    head, tail, below, above = barrier((head, tail, below, above))
    parcel = stack(below, atoms, above, pot)
    parcel_xy = send(parcel, over_x ^ over_y)
    parcel_x = send(parcel, over_x)
    low, high = send(tail, 0, 1), send(head, 0, -1)
    message, relay, mid = pack_rest(s, inner)
    vb = spread(parcel)
    beside = side_x(s, mate)
    parcel_xy, one_edge, message, relay, beside = barrier((parcel_xy, one_edge, message, relay, beside))
    relayed = lax.ppermute(relay, AXES, [(d, d ^ over_y ^ 1) for d in outer_ones])
    message = send(message, over_y)
    parcel_y = send(parcel_xy, over_x)
    gg, part, energy = prep([parcel, parcel_x, parcel_y, parcel_xy], corner, vb, s)

    part, relayed = barrier((part, relayed))
    relayed = lax.ppermute(relayed, AXES, [(d, d ^ 1) for d in inner_ones])
    part = part + send(part, over_x)
    part_mate = send(part, over_y)
    side_part = side_z(s, beside, low, high)
    edges = [one_edge, message.reshape(C - FIRST, EDGE, S), relayed]
    vb = vb.reshape(C, ROWS, S)
    q, mix, head, tail = make_first(s, side_part, vb, edges, inner, part, part_mate)
    low, high = send(tail, 0, 1), send(head, 0, -1)
    mate = send(mix, over_x)
    mid, part_mate = barrier((mid, part_mate))
    mid = lax.ppermute(mid, AXES, [(d, d ^ over_y) for d in inner_ones])
    vb_mate = spread(parcel_y).reshape(C, ROWS, S)
    part_two = side_again(mix, mate)
    base = make_base(s, mid, vb, vb_mate, q, side_part, part_two, edges, inner)
    gg = gg.reshape(2, C, ROWS, S)
    second, own, give = make_second(base, [low, high], gg, [part, part_mate, energy], upper)

    own = own + send(give, over_x)
    for flip in (32, 36, 1, 3, 8, 24):
        own = own + lax.ppermute(own, AXES, [(d, d ^ flip) for d in range(count)])
    return turn(second, own, send(own, over_x), upper).reshape(C, C, C, S)


def solution(mesh):
    return jax.shard_map(
        per_device,
        mesh=mesh,
        in_specs=(
            P("gx", "gy", "gzs", None),
            P("gx", "gy", "gzs"),
            P(("gx", "gy", "gzs"), None),
            P(("gx", "gy", "gzs"), None, None, None),
            P(("gx", "gy", "gzs")),
        ),
        out_specs=P("gx", "gy", "gzs", None),
        check_vma=False,
    )
```

```python
import math

import jax
import jax.numpy as jnp
from jax import lax
from jax.experimental import pallas as pl
from jax.experimental.pallas import tpu as pltpu
from jax.sharding import PartitionSpec as P

AXES = ("gx", "gy", "gzs")
H = 6
C = 16
ROWS = C * C
CELLS = C * C * C
NCELLS = 32 * 32 * 512
S = 128
W = 9
R = 4
NEAR = 48
TAPS = W * W * W
F32 = jnp.float32
BF16 = jnp.bfloat16

grid_step = 0.6
filter_centre = 36.0
filter_half = 26.0


def weights():
    taps = []
    for k in range(1, 7):
        top = 2.0 * (-1) ** (k + 1) * math.factorial(6) ** 2
        under = k * k * math.factorial(6 - k) * math.factorial(6 + k)
        taps.append(top / under)
    scale = -0.5 / (grid_step * grid_step)
    off = [scale * t / filter_half for t in taps]
    diagonal = 3.0 * scale * (-2.0 * sum(taps))
    return off, diagonal


OFF, DIAGONAL = weights()


def params(mib):
    return pltpu.CompilerParams(vmem_limit_bytes=mib * 1024 * 1024)


def cost(flops, nbytes):
    return pl.CostEstimate(flops=flops, bytes_accessed=nbytes, transcendentals=0)


def sds(shape, dtype=F32):
    return jax.ShapeDtypeStruct(shape, dtype)


def split(value):
    high = value.astype(BF16)
    low = (value - high.astype(F32)).astype(BF16)
    return high, low


def mm(a, b):
    return jnp.dot(a, b, preferred_element_type=F32)


def tap_sum(at, index):
    total = None
    for k in range(1, 7):
        term = OFF[k - 1] * (at(index + k) + at(index - k))
        total = term if total is None else total + term
    return total


B = 4
STEPS = C // B
N = 2
FIRST = 6
MIDDLE = 10
EDGE = 192
MID = 64
MID_START = (MIDDLE - FIRST) * EDGE


def stride_rows(z):
    return pl.ds(z, C, stride=C)


def plane_spec(rows=ROWS, planes=B):
    return pl.BlockSpec((planes, rows, S), lambda i: (i, 0, 0))


def halo_spec(planes=B):
    return pl.BlockSpec((H, planes, C, S), lambda i: (0, i, 0, 0))


def part_spec(part):
    return pl.BlockSpec((1, B, ROWS, S), lambda i: (part, i, 0, 0))


def whole(rows=S):
    return pl.BlockSpec((rows, S), lambda i: (0, 0))


def edge_spec(start, stop):
    return pl.BlockSpec((N, EDGE, S), lambda i: (jnp.clip(i - start // N, 0, (stop - start) // N - 1), 0, 0))


def edge_specs():
    return [edge_spec(0, FIRST), edge_spec(FIRST, C), edge_spec(MIDDLE, C)]


def for_piece(edges, inner_ref, body):
    step = pl.program_id(0)
    direct = (inner_ref[0] == 1) | (step < MIDDLE // N)

    @pl.when(step < FIRST // N)
    def _():
        body(edges[0])

    @pl.when((step >= FIRST // N) & direct)
    def _():
        body(edges[1])

    @pl.when(jnp.logical_not(direct))
    def _():
        body(edges[2])


SCALARS = pl.BlockSpec(memory_space=pltpu.SMEM)
FULL = sds((C, ROWS, S))
FULL_ROWS = sds((CELLS, S))
HALO_ROWS = H * ROWS
MESSAGE = sds((HALO_ROWS + 2 * NEAR, S))
HALO = sds((H, C, C, S))
EDGES = [sds((FIRST, EDGE, S)), sds((C - FIRST, EDGE, S)), sds((C - MIDDLE, EDGE, S))]


def halo_rows(x, z):
    return pl.ds(pl.multiple_of(z * ROWS + x * C, C), C)


def halves(y, half):
    return slice(y * C + half * 8, y * C + half * 8 + 8)


def pack_edges(s_ref, out_ref):
    out_ref[:, 0:96, :] = s_ref[:, 0:96, :]
    out_ref[:, 96:192, :] = s_ref[:, 160:256, :]


def by_side(odd_ref, body, one, two):
    odd = odd_ref[0] == 1

    @pl.when(odd)
    def _():
        body(one, two)

    @pl.when(jnp.logical_not(odd))
    def _():
        body(two, one)


def pack_kernel(s_ref, odd_ref, edge_ref, one_ref, two_ref):
    @pl.when(pl.program_id(0) < FIRST // N)
    def _():
        pack_edges(s_ref, edge_ref)

    def halos(head_ref, tail_ref):
        for p in range(N):
            for z in range(H):
                head_ref[z, p] = s_ref[p, stride_rows(z), :]
                tail_ref[z, p] = s_ref[p, stride_rows(C - H + z), :]

    by_side(odd_ref, halos, one_ref, two_ref)


def pack(s, odd):
    return pl.pallas_call(
        pack_kernel,
        grid=(C // N,),
        in_specs=[plane_spec(ROWS, N), SCALARS],
        out_specs=edge_specs()[:1] + [halo_spec(N), halo_spec(N)],
        out_shape=EDGES[:1] + [HALO, HALO],
        compiler_params=params(12),
        cost_estimate=cost(1 << 32, 6 << 20),
        name="pack",
    )(s, odd)


def pack_rest_kernel(s_ref, inner_ref, message_ref, relay_ref, mid_ref):
    step = pl.program_id(0)
    inner = inner_ref[0] == 1
    mid_ref[...] = s_ref[:, 96:160, :]

    @pl.when(step >= MIDDLE // N)
    def _():
        pack_edges(s_ref, relay_ref)

    @pl.when((step >= FIRST // N) & (inner | (step < MIDDLE // N)))
    def _():
        for p in range(N):
            row = pl.multiple_of((step * N + p - FIRST) * EDGE, MID)
            message_ref[pl.ds(row, 96), :] = s_ref[p, 0:96, :]
            message_ref[pl.ds(row + 96, 96), :] = s_ref[p, 160:256, :]

    @pl.when(jnp.logical_not(inner))
    def _():
        for p in range(N):
            row = pl.multiple_of(MID_START + (step * N + p) * MID, MID)
            message_ref[pl.ds(row, MID), :] = s_ref[p, 96:160, :]


def pack_rest(s, inner):
    rows = (C - FIRST) * EDGE
    message, relay, mid = pl.pallas_call(
        pack_rest_kernel,
        grid=(C // N,),
        in_specs=[plane_spec(ROWS, N), SCALARS],
        out_specs=[whole(rows), edge_spec(MIDDLE, C), plane_spec(MID, N)],
        out_shape=[sds((rows, S)), EDGES[2], sds((C, MID, S))],
        compiler_params=params(12),
        cost_estimate=cost(1 << 31, 4 << 20),
        name="pack_rest",
    )(s, inner)
    return message, relay, mid


def column_kernel(own_ref, one_ref, two_ref, pot_ref, odd_ref, out_ref):
    def beside(below_ref, above_ref):
        out_ref[0:24, :] = below_ref[...]
        out_ref[48:72, :] = above_ref[...]

    by_side(odd_ref, beside, one_ref, two_ref)
    out_ref[24:48, :] = own_ref[...]
    out_ref[72:104, :] = pot_ref[...]


def column(own, one, two, pot, odd):
    return pl.pallas_call(
        column_kernel,
        in_specs=[pl.BlockSpec(memory_space=pltpu.VMEM)] * 4 + [SCALARS],
        out_shape=sds((104, S)),
        compiler_params=params(4),
        name="column",
    )(own, one, two, pot, odd)


def along_x(s_ref, mate_ref, out_ref, add):
    def column(block, _):
        rows = pl.ds(pl.multiple_of(block * 8, 8), 8)
        ring = [mate_ref[C - H + i, rows, :] for i in range(H)]
        ring += [s_ref[x, rows, :] for x in range(C)]
        ring += [mate_ref[i, rows, :] for i in range(H)]
        for x in range(C):
            value = tap_sum(lambda i: ring[H + i], x)
            if add:
                value = value + out_ref[x, rows, :]
            out_ref[x, rows, :] = value
        return 0

    lax.fori_loop(0, ROWS // 8, column, 0)


def z_taps(ext_ref, y):
    return tap_sum(lambda k: ext_ref[y * 32 + 8 + k : y * 32 + 24 + k, :], 0)


def side_x_kernel(s_ref, mate_ref, out_ref):
    along_x(s_ref, mate_ref, out_ref, False)


def side_x(s, mate):
    return pl.pallas_call(
        side_x_kernel,
        out_shape=FULL,
        compiler_params=params(12),
        cost_estimate=cost(1 << 24, 6 << 20),
        name="side_x",
    )(s, mate)


def side_z_kernel(s_ref, part_ref, one_ref, two_ref, odd_ref, out_ref, ext_ref):
    def planes(low_ref, high_ref):
        def plane(x, _):
            for y in range(C):
                ext_ref[y * 32 + 8 : y * 32 + 24, :] = s_ref[x, y * C : (y + 1) * C, :]
            for z in range(H):
                ext_ref[pl.ds(2 + z, C, stride=32), :] = low_ref[z, x]
                ext_ref[pl.ds(24 + z, C, stride=32), :] = high_ref[z, x]
            for y in range(C):
                rows = slice(y * C, (y + 1) * C)
                out_ref[x, rows, :] = part_ref[x, rows, :] + z_taps(ext_ref, y)
            return 0

        lax.fori_loop(0, C, plane, 0)

    by_side(odd_ref, planes, one_ref, two_ref)


def side_z(s, part, halos, odd):
    return pl.pallas_call(
        side_z_kernel,
        in_specs=[pl.BlockSpec(memory_space=pltpu.VMEM)] * 4 + [SCALARS],
        out_shape=FULL,
        scratch_shapes=[pltpu.VMEM((C * 32, S), F32)],
        compiler_params=params(14),
        cost_estimate=cost(1 << 24, 8 << 20),
        name="side_z",
    )(s, part, *halos, odd)


def side_again_kernel(s_ref, mate_ref, out_ref, ext_ref):
    for y in range(C):
        ext_ref[y * 32 : y * 32 + 8, :] = jnp.zeros((8, S), F32)
        ext_ref[y * 32 + 24 : y * 32 + 32, :] = jnp.zeros((8, S), F32)

    def plane(x, _):
        for y in range(C):
            ext_ref[y * 32 + 8 : y * 32 + 24, :] = s_ref[x, y * C : (y + 1) * C, :]
        for y in range(C):
            out_ref[x, y * C : (y + 1) * C, :] = z_taps(ext_ref, y)
        return 0

    lax.fori_loop(0, C, plane, 0)
    along_x(s_ref, mate_ref, out_ref, True)


def side_again(s, mate):
    return pl.pallas_call(
        side_again_kernel,
        out_shape=FULL,
        scratch_shapes=[pltpu.VMEM((C * 32, S), F32)],
        compiler_params=params(12),
        cost_estimate=cost(1 << 25, 6 << 20),
        name="side_again",
    )(s, mate)


def tap_weight(distance):
    value = jnp.zeros(distance.shape, F32)
    for k in range(1, 7):
        value = jnp.where(distance == k, OFF[k - 1], value)
    return value


def ring_tables(coordinate):
    masks, factors = [], []
    for t in range(W):
        away = (coordinate - t) & 31
        masks.append(away == 0)
        factors.append(tap_weight(jnp.minimum(away, 32 - away)))
    return masks, factors


def spread_kernel(parcel_ref, vb_ref):
    def spread_row(row, _):
        line = (parcel_ref[pl.ds(72 + row, 1), :] + (DIAGONAL - filter_centre)) * (1.0 / filter_half)
        start = pl.multiple_of(row * 128, 128)
        vb_ref[pl.ds(start, 128), :] = jnp.broadcast_to(line, (128, 128)).T
        return 0

    lax.fori_loop(0, CELLS // 128, spread_row, 0, unroll=8)


def spread(parcel):
    return pl.pallas_call(
        spread_kernel,
        out_shape=FULL_ROWS,
        compiler_params=params(8),
        cost_estimate=cost(1 << 20, 2 << 20),
        name="spread",
    )(parcel)


def prep_kernel(*refs):
    parcels = refs[:4]
    corner_ref, vb_ref, s_ref, gg_ref, coef_ref, energy_ref, near_ref, table_ref, a1_ref, a1z_ref, a2_ref, a2s_ref = refs[4:]
    upper_x, upper_y = corner_ref[0] > 0, corner_ref[1] > 0
    for slab in range(3):
        own, over_x, over_y, over_xy = [parcel[slab * 24 : slab * 24 + 24, :] for parcel in parcels]
        same_x = [jnp.where(upper_y, over_y, own), jnp.where(upper_y, own, over_y)]
        other_x = [jnp.where(upper_y, over_xy, over_x), jnp.where(upper_y, over_x, over_xy)]
        ordered = [jnp.where(upper_x, o, m) for m, o in zip(same_x, other_x)]
        ordered += [jnp.where(upper_x, m, o) for m, o in zip(same_x, other_x)]
        for j in range(4):
            near_ref[slab * 96 + j * 24 : slab * 96 + j * 24 + 24, :] = ordered[j]
    blank = jnp.zeros((16, 128), F32)
    for block in range(6):
        rows = near_ref[pl.ds(block, NEAR, stride=6), :]
        table_ref[block * 128 : block * 128 + 128, :] = jnp.concatenate([rows, blank, rows, blank]).T
    at = TAPS + 3 - 640
    energy_ref[...] = jnp.broadcast_to(rows[:, at : at + 1] * (1.0 / filter_half), (NEAR, S))

    shape = (8, 128)
    sub = lax.broadcasted_iota(jnp.int32, shape, 0)
    lane = lax.broadcasted_iota(jnp.int32, shape, 1)
    first_lanes = lane < 64
    sites = [jnp.broadcast_to(table_ref[TAPS + d : TAPS + d + 1, :], shape).astype(jnp.int32) for d in range(3)]
    px = sites[0] - corner_ref[0]
    py = sites[1] - corner_ref[1]
    pz = (sites[2] & 15) + (((lane & 63) >> 4) - 1) * C
    zero = jnp.zeros(shape, F32)

    dz = sub + (lane >> 6) * 8 - pz + R
    z_masks = [dz == t for t in range(W)]
    z_factors = [tap_weight(jnp.abs(dz - t)) for t in range(W)]

    def place_z(ij, _):
        acc = zero
        along = zero
        for t in range(W):
            row = jnp.broadcast_to(table_ref[pl.ds(ij * W + t, 1), :], shape)
            acc = jnp.where(z_masks[t], row, acc)
            along = along + z_factors[t] * row
        a1_ref[ij] = acc
        a1z_ref[ij] = along
        return 0

    lax.fori_loop(0, W * W, place_z, 0, unroll=3)

    def place_y(y, _):
        masks, factors = ring_tables(y - py + R)
        for i in range(W):
            acc = zero
            along = zero
            moved = zero
            for t in range(W):
                value = a1_ref[i * W + t]
                acc = jnp.where(masks[t], value, acc)
                along = along + factors[t] * value
                moved = jnp.where(masks[t], a1z_ref[i * W + t], moved)
            a2_ref[i, y] = acc
            a2s_ref[i, y] = along + moved
        return 0

    lax.fori_loop(0, C, place_y, 0)

    def place_x(x, _):
        masks, factors = ring_tables(x - px + R)

        def per_y(y, _):
            row = pl.multiple_of(x * ROWS + y * C, C)
            acc = zero
            along = zero
            moved = zero
            for t in range(W):
                value = a2_ref[t, y]
                acc = jnp.where(masks[t], value, acc)
                along = along + factors[t] * value
                moved = jnp.where(masks[t], a2s_ref[t, y], moved)
            v = vb_ref[pl.ds(row, C), :]
            moved = along + moved + jnp.where(first_lanes, v[:8], v[8:]) * acc
            lower = jnp.where(first_lanes, acc, pltpu.roll(moved, 64, 1))
            upper = jnp.where(first_lanes, pltpu.roll(acc, 64, 1), moved)
            high, low = split(jnp.concatenate([lower, upper], axis=0))
            gg_ref[0, pl.ds(row, C), :] = high
            gg_ref[1, pl.ds(row, C), :] = low
            return 0

        lax.fori_loop(0, C, per_y, 0, unroll=16)
        return 0

    lax.fori_loop(0, C, place_x, 0)

    coef_ref[...] = jnp.zeros((3, NEAR, S), F32)

    def contract(x, _):
        rows = pl.ds(pl.multiple_of(x * 2 * ROWS, ROWS), 2 * ROWS)
        g_high, g_low = gg_ref[0, rows, :], gg_ref[1, rows, :]
        t_high, t_low = g_high.T, g_low.T
        high, low = split(s_ref[rows, :])
        got = mm(t_high, high) + (mm(t_high, low) + mm(t_low, high))
        t_high, t_low = t_high[:NEAR], t_low[:NEAR]
        pair = mm(t_high, g_high) + (mm(t_high, g_low) + mm(t_low, g_high))
        for slab in range(3):
            rows = slice(slab * C, slab * C + C)
            coef_ref[slab, 0:16] += got[rows]
            coef_ref[slab, 16:32] += got[64 + slab * C : 80 + slab * C]
            coef_ref[slab, 32:48] += pair[rows]
        return 0

    lax.fori_loop(0, C // 2, contract, 0, unroll=2)


def prep(parcels, corner, vb, s):
    vmem = pl.BlockSpec(memory_space=pltpu.VMEM)
    return pl.pallas_call(
        prep_kernel,
        in_specs=[vmem] * 4 + [pl.BlockSpec(memory_space=pltpu.SMEM), vmem, vmem],
        out_shape=[sds((2, CELLS, S), BF16), sds((3, NEAR, S)), sds((NEAR, S))],
        scratch_shapes=[
            pltpu.VMEM((288, 128), F32),
            pltpu.VMEM((768, 128), F32),
            pltpu.VMEM((W * W, 8, 128), F32),
            pltpu.VMEM((W * W, 8, 128), F32),
            pltpu.VMEM((W, C, 8, 128), F32),
            pltpu.VMEM((W, C, 8, 128), F32),
        ],
        compiler_params=params(16),
        cost_estimate=cost(1 << 27, 10 << 20),
        name="prep",
    )(*parcels, corner, vb, s.reshape(CELLS, S))


def move_pair(shares, away):
    lane = lax.broadcasted_iota(jnp.int32, (16, 128), 1)
    keep = (lane < 32) if away < 0 else (lane >= 16) & (lane < 48)
    pair = jnp.where(keep, pltpu.roll(shares[32:48], (away * 16) % 128, 1), 0.0)
    return jnp.concatenate([shares[0:32], pair])


def first_kernel(s_ref, side_ref, vb_ref, *refs):
    inner_ref, odd_ref, part_ref, mate_ref, q_ref, mix_ref, one_ref, two_ref = refs[3:]
    step = pl.program_id(0)

    @pl.when(step == 0)
    def _():
        def shares(head_ref, tail_ref):
            for j in range(2):
                rows = slice(HALO_ROWS + j * NEAR, HALO_ROWS + (j + 1) * NEAR)
                head_ref[rows, :] = part_ref[j] + mate_ref[j]
                tail_ref[rows, :] = part_ref[j + 1] + mate_ref[j + 1]

        by_side(odd_ref, shares, one_ref, two_ref)

    def planes(edge_ref):
        for p in range(N):
            for half in range(2):
                ring = {y: s_ref[p, halves(y, half), :] for y in range(C)}
                for y in range(H):
                    ring[C + y] = edge_ref[p, halves(y, half), :]
                    ring[y - H] = edge_ref[p, halves(H + y, half), :]
                for y in range(C):
                    rows = halves(y, half)
                    dy = tap_sum(lambda i: ring[i], y)
                    q = dy + vb_ref[p, rows, :] * ring[y]
                    q_ref[p, rows, :] = q
                    mix_ref[p, rows, :] = side_ref[p, rows, :] + q + dy

    for_piece(refs[:3], inner_ref, planes)

    def halos(head_ref, tail_ref):
        for p in range(N):
            for z in range(H):
                rows = halo_rows(step * N + p, z)
                head_ref[rows, :] = mix_ref[p, stride_rows(z), :]
                tail_ref[rows, :] = mix_ref[p, stride_rows(C - H + z), :]

    by_side(odd_ref, halos, one_ref, two_ref)


def make_first(s, side_part, vb, edges, inner, odd, part, part_mate):
    shares = pl.BlockSpec((3, NEAR, S), lambda i: (0, 0, 0))
    return pl.pallas_call(
        first_kernel,
        grid=(C // N,),
        in_specs=[plane_spec(ROWS, N)] * 3 + edge_specs() + [SCALARS] * 2 + [shares] * 2,
        out_specs=[plane_spec(ROWS, N), plane_spec(ROWS, N), whole(MESSAGE.shape[0]), whole(MESSAGE.shape[0])],
        out_shape=[FULL, FULL, MESSAGE, MESSAGE],
        compiler_params=params(16),
        cost_estimate=cost(1 << 24, 14 << 20),
        name="first",
    )(s, side_part, vb, *edges, inner, odd, part, part_mate)


def base_kernel(s_ref, mid_ref, vb_ref, vb_mate_ref, q_ref, side_ref, part_ref, *refs):
    inner_ref, message_ref, out_ref, middle_ref = refs[3:]
    step = pl.program_id(0)
    inner = inner_ref[0] == 1

    @pl.when(inner)
    def _():
        middle_ref[...] = mid_ref[...]

    @pl.when(jnp.logical_not(inner))
    def _():
        for p in range(N):
            middle_ref[p] = message_ref[pl.ds(pl.multiple_of(MID_START + (step * N + p) * MID, MID), MID), :]

    def planes(edge_ref):
        for p in range(N):
            for half in range(2):

                def other(y, p=p, half=half):
                    if y < H:
                        return edge_ref[p, halves(y, half), :]
                    if y < C - H:
                        return middle_ref[p, halves(y - H, half), :]
                    return edge_ref[p, halves(y - 4, half), :]

                ring = [s_ref[p, halves(y, half), :] for y in range(C)] + [other(y) for y in range(C)]
                q = {y: q_ref[p, halves(y, half), :] for y in range(C)}
                for y in list(range(H)) + list(range(C - H, C)):
                    v = vb_mate_ref[p, halves(y, half), :]
                    q[C + y] = tap_sum(lambda i: ring[i % 32], C + y) + v * ring[C + y]
                for y in range(C):
                    rows = halves(y, half)
                    total = tap_sum(lambda i: q[i % 32], y)
                    total = total + vb_ref[p, rows, :] * (side_ref[p, rows, :] + q[y])
                    out_ref[p, rows, :] = 2.0 * (total + part_ref[p, rows, :]) - ring[y]

    for_piece(refs[:3], inner_ref, planes)


def make_base(s, mid, vb, vb_mate, q, side_part, part, edges, inner):
    return pl.pallas_call(
        base_kernel,
        grid=(C // N,),
        in_specs=[plane_spec(ROWS, N), plane_spec(MID, N)]
        + [plane_spec(ROWS, N)] * 5
        + edge_specs()
        + [SCALARS, whole((C - FIRST) * EDGE)],
        out_specs=plane_spec(ROWS, N),
        out_shape=FULL,
        scratch_shapes=[pltpu.VMEM((N, MID, S), F32)],
        compiler_params=params(16),
        cost_estimate=cost(1 << 25, 16 << 20),
        name="base",
    )(s, mid, vb, vb_mate, q, side_part, part, *edges, inner, edges[1].reshape(-1, S))


def second_kernel(base_ref, one_ref, two_ref, gg_high_ref, gg_low_ref, *rest):
    part_ref, mate_ref, energy_ref, upper_ref, odd_ref, second_ref, keep_ref, give_ref, gram_ref, cross_ref, w_ref, halo_ref = rest
    step = pl.program_id(0)

    @pl.when(step == 0)
    def _():
        gram_ref[...] = jnp.zeros((S, S), F32)
        cross_ref[...] = jnp.zeros((S, S), F32)
        w_ref[...] = jnp.zeros((S, S), F32)
        halo_ref[...] = jnp.zeros((B, ROWS, S), F32)
        mine = [part_ref[j] + mate_ref[j] for j in range(3)]
        odd = odd_ref[0] == 1
        got = [[ref[HALO_ROWS + j * NEAR : HALO_ROWS + (j + 1) * NEAR, :] for j in range(2)] for ref in (one_ref, two_ref)]
        below = [move_pair(jnp.where(odd, a, b), -1) for a, b in zip(*got)]
        above = [move_pair(jnp.where(odd, b, a), 1) for a, b in zip(*got)]
        slabs = [mine[0] + below[0], mine[1] + below[1] + above[0], mine[2] + above[1]]
        near = jnp.concatenate([slab[0:16] for slab in slabs]) * energy_ref[...]
        lane = lax.broadcasted_iota(jnp.int32, (NEAR, S), 1)
        pair = jnp.where(lane < NEAR, jnp.concatenate([slab[32:48] for slab in slabs]), 0.0)
        two = jnp.concatenate([slab[16:32] for slab in slabs])
        two = two + exact(pair, jnp.concatenate([near, jnp.zeros((S - NEAR, S), F32)]))
        w_ref[0:NEAR, :] = 2.0 * energy_ref[...] * two
        w_ref[64 : 64 + NEAR, :] = 2.0 * near

    def halo_part(low_ref, high_ref):
        for p in range(B):
            low = [low_ref[halo_rows(step * B + p, j), :] for j in range(H)]
            high = [high_ref[halo_rows(step * B + p, j), :] for j in range(H)]
            for z in range(H):
                add = sum((2.0 * OFF[k - 1]) * low[z - k + H] for k in range(z + 1, H + 1))
                halo_ref[p, stride_rows(z), :] = add
                add = sum((2.0 * OFF[H + j - z - 1]) * high[j] for j in range(z + 1))
                halo_ref[p, stride_rows(C - H + z), :] = add

    by_side(odd_ref, halo_part, one_ref, two_ref)

    w_high, w_low = split(w_ref[...])
    w_twice = jnp.concatenate([w_high, w_high])
    gram = jnp.zeros((S, 2 * S), F32)
    for p in range(B):
        g_high, g_low = gg_high_ref[0, p], gg_low_ref[0, p]
        near = mm(jnp.concatenate([g_high, g_low], axis=1), w_twice) + mm(g_high, w_low)
        value = base_ref[p] + halo_ref[p] + near
        second_ref[p] = value
        s_high, s_low = split(value)
        gram += mm(s_high.T, jnp.concatenate([s_high, s_low], axis=1))
    gram_ref[...] += gram[:, :S]
    cross_ref[...] += gram[:, S:]

    @pl.when(step == STEPS - 1)
    def _():
        cross = cross_ref[...]
        gram = (gram_ref[...] + (cross + cross.T)) * (1.0 / NCELLS)
        upper = upper_ref[0] == 1
        keep_ref[...] = jnp.where(upper, gram[S // 2 :], gram[: S // 2])
        give_ref[...] = jnp.where(upper, gram[: S // 2], gram[S // 2 :])


def make_second(base, halos, gg, shares, upper, odd):
    three = pl.BlockSpec((3, NEAR, S), lambda i: (0, 0, 0))
    return pl.pallas_call(
        second_kernel,
        grid=(STEPS,),
        in_specs=[plane_spec()]
        + [whole(MESSAGE.shape[0])] * 2
        + [part_spec(0), part_spec(1), three, three, whole(NEAR), SCALARS, SCALARS],
        out_specs=[plane_spec(), whole(S // 2), whole(S // 2)],
        out_shape=[FULL, sds((S // 2, S)), sds((S // 2, S))],
        scratch_shapes=[pltpu.VMEM((S, S), F32)] * 3 + [pltpu.VMEM((B, ROWS, S), F32)],
        compiler_params=params(16),
        cost_estimate=cost(1 << 27, 8 << 20),
        name="second",
    )(base, *halos, gg, gg, *shares, upper, odd)


def exact(a, b):
    return jnp.dot(a, b, precision=lax.Precision.HIGHEST, preferred_element_type=F32)


def inverse_factor(gram_ref, a_ref, x_ref, state_ref):
    row = lax.broadcasted_iota(jnp.int32, (S, S), 0)
    column = lax.broadcasted_iota(jnp.int32, (S, S), 1)
    unit = jnp.where(row == column, 1.0, 0.0)
    gram = gram_ref[...]
    diagonal = jnp.where(row == column, gram, 0.0)
    down = lax.rsqrt(jnp.sum(diagonal, axis=1, keepdims=True))
    across = lax.rsqrt(jnp.sum(diagonal, axis=0, keepdims=True))
    a_ref[...] = gram * down * across
    x_ref[...] = unit

    def residual():
        x = x_ref[...]
        return unit - exact(exact(x, a_ref[...]), x.T)

    def size(e):
        return jnp.sum(e * e)

    def improve(e):
        lower = jnp.where(row > column, e, jnp.where(row == column, 0.5 * e, 0.0))
        x_ref[...] += exact(lower, x_ref[...])

    state_ref[0] = 0
    start = unit - a_ref[...]
    start_size = size(start)

    @pl.when(start_size < 0.16)
    def _():
        improve(start)
        state_ref[0] = jnp.where(start_size < 1e-6, 2, 1)

    for _ in range(5):

        @pl.when(state_ref[0] == 1)
        def _():
            e = residual()
            e_size = size(e)
            improve(e)
            state_ref[0] = jnp.where(e_size < 1e-6, 2, 1)

    @pl.when(state_ref[0] != 2)
    def _():
        x_ref[...] = unit
        lanes = lax.broadcasted_iota(jnp.int32, (1, S), 1)

        def step(j, _):
            line = a_ref[pl.ds(j, 1), :]
            scale = lax.rsqrt(jnp.sum(jnp.where(lanes == j, line, 0.0), axis=1, keepdims=True))
            a = a_ref[...]
            factor = jnp.sum(jnp.where(column == j, a, 0.0), axis=1, keepdims=True) * scale
            factor = jnp.where(row[:, :1] > j, factor, 0.0)
            x_line = x_ref[pl.ds(j, 1), :] * scale
            a_ref[...] = a - factor * (line * scale)
            x_ref[...] = jnp.where(row == j, x_line, x_ref[...] - factor * x_line)
            return 0

        lax.fori_loop(0, S, step, 0)

    x_ref[...] = x_ref[...] * across


def turn_kernel(second_ref, own_ref, other_ref, upper_ref, out_ref, gram_ref, a_ref, x_ref, i_high_ref, i_low_ref, state_ref):
    @pl.when(pl.program_id(0) == 0)
    def _():
        upper = upper_ref[0] == 1
        gram_ref[: S // 2, :] = jnp.where(upper, other_ref[...], own_ref[...])
        gram_ref[S // 2 :, :] = jnp.where(upper, own_ref[...], other_ref[...])
        inverse_factor(gram_ref, a_ref, x_ref, state_ref)
        i_high, i_low = split(x_ref[...].T)
        i_high_ref[...] = i_high
        i_low_ref[...] = i_low

    i_high, i_low = i_high_ref[...], i_low_ref[...]
    i_twice = jnp.concatenate([i_high, i_high])
    for p in range(B):
        high, low = split(second_ref[p])
        out_ref[p] = mm(jnp.concatenate([high, low], axis=1), i_twice) + mm(high, i_low)


def turn(second, own, other, upper):
    return pl.pallas_call(
        turn_kernel,
        grid=(STEPS,),
        in_specs=[plane_spec(), whole(S // 2), whole(S // 2), SCALARS],
        out_specs=plane_spec(),
        out_shape=FULL,
        scratch_shapes=[pltpu.VMEM((S, S), F32)] * 3 + [pltpu.VMEM((S, S), BF16)] * 2 + [pltpu.SMEM((1,), jnp.int32)],
        compiler_params=params(16),
        cost_estimate=cost(1 << 28, 4 << 20),
        name="turn",
    )(second, own, other, upper)


def per_device(states, potential, atom_sites, projectors, energies):
    gx, gy = lax.axis_index("gx"), lax.axis_index("gy")
    depth = lax.axis_size("gzs")
    count = 4 * depth
    barrier = lax.optimization_barrier

    def send(value, flip):
        return lax.ppermute(value, AXES, [(d, d ^ flip) for d in range(count)])

    over_x, over_y = 2 * depth, depth

    def to_pairs(one, two):
        near = [(d, d ^ 1) for d in range(count)]
        far = [(d, d // depth * depth + (d + (1 if d % 2 else -1)) % depth) for d in range(count)]
        return lax.ppermute(one, AXES, near), lax.ppermute(two, AXES, far)

    inner_ones = [d for d in range(count) if d % 4 in (1, 2)]
    outer_ones = [d for d in range(count) if d % 4 in (0, 3)]
    inner = ((lax.axis_index("gzs") + 1) // 2 % 2).astype(jnp.int32).reshape(1)
    s = states.reshape(C, ROWS, S)
    pot = potential.reshape(32, 128)

    atoms = jnp.concatenate(
        [projectors.reshape(4, TAPS), atom_sites.astype(F32), energies[:, None], jnp.zeros((4, 768 - TAPS - 4), F32)],
        axis=1,
    ).reshape(24, 128)
    mate = send(s, over_x)
    corner = jnp.stack([gx * C, gy * C]).astype(jnp.int32)
    upper = gx.astype(jnp.int32).reshape(1)
    odd = (lax.axis_index("gzs") % 2).astype(jnp.int32).reshape(1)
    to_pack, corner, upper, inner, odd = barrier((s, corner, upper, inner, odd))
    beside_one, beside_two = to_pairs(atoms, atoms)
    one_edge, halo_one, halo_two = pack(to_pack, odd)
    one_edge = send(one_edge, over_y)
    halo_one, halo_two, beside_one, beside_two = barrier((halo_one, halo_two, beside_one, beside_two))
    parcel = column(atoms, beside_one, beside_two, pot, odd)
    parcel_xy = send(parcel, over_x ^ over_y)
    parcel_x = send(parcel, over_x)
    halos = to_pairs(halo_one, halo_two)
    message, relay, mid = pack_rest(s, inner)
    vb = spread(parcel)
    beside = side_x(s, mate)
    parcel_xy, one_edge, message, relay, beside = barrier((parcel_xy, one_edge, message, relay, beside))
    relayed = lax.ppermute(relay, AXES, [(d, d ^ over_y ^ 1) for d in outer_ones])
    message = send(message, over_y)
    parcel_y = send(parcel_xy, over_x)
    gg, part, energy = prep([parcel, parcel_x, parcel_y, parcel_xy], corner, vb, s)

    part, relayed = barrier((part, relayed))
    relayed = lax.ppermute(relayed, AXES, [(d, d ^ 1) for d in inner_ones])
    part = part + send(part, over_x)
    part_mate = send(part, over_y)
    side_part = side_z(s, beside, halos, odd)
    edges = [one_edge, message.reshape(C - FIRST, EDGE, S), relayed]
    vb = vb.reshape(C, ROWS, S)
    q, mix, halo_one, halo_two = make_first(s, side_part, vb, edges, inner, odd, part, part_mate)
    halos = to_pairs(halo_one, halo_two)
    mate = send(mix, over_x)
    mid, part_mate = barrier((mid, part_mate))
    mid = lax.ppermute(mid, AXES, [(d, d ^ over_y) for d in inner_ones])
    vb_mate = spread(parcel_y).reshape(C, ROWS, S)
    part_two = side_again(mix, mate)
    base = make_base(s, mid, vb, vb_mate, q, side_part, part_two, edges, inner)
    gg = gg.reshape(2, C, ROWS, S)
    second, own, give = make_second(base, halos, gg, [part, part_mate, energy], upper, odd)

    own = own + send(give, over_x)
    for flip in (32, 36, 1, 3, 8, 24):
        own = own + lax.ppermute(own, AXES, [(d, d ^ flip) for d in range(count)])
    return turn(second, own, send(own, over_x), upper).reshape(C, C, C, S)


def solution(mesh):
    return jax.shard_map(
        per_device,
        mesh=mesh,
        in_specs=(
            P("gx", "gy", "gzs", None),
            P("gx", "gy", "gzs"),
            P(("gx", "gy", "gzs"), None),
            P(("gx", "gy", "gzs"), None, None, None),
            P(("gx", "gy", "gzs")),
        ),
        out_specs=P("gx", "gy", "gzs", None),
        check_vma=False,
    )
```

```python
import math

import jax
import jax.numpy as jnp
from jax import lax
from jax.experimental import pallas as pl
from jax.experimental.pallas import tpu as pltpu
from jax.sharding import PartitionSpec as P

AXES = ("gx", "gy", "gzs")
H = 6
C = 16
ROWS = C * C
CELLS = C * C * C
NCELLS = 32 * 32 * 512
S = 128
W = 9
R = 4
NEAR = 48
TAPS = W * W * W
F32 = jnp.float32
BF16 = jnp.bfloat16

grid_step = 0.6
filter_centre = 36.0
filter_half = 26.0


def weights():
    taps = []
    for k in range(1, 7):
        top = 2.0 * (-1) ** (k + 1) * math.factorial(6) ** 2
        under = k * k * math.factorial(6 - k) * math.factorial(6 + k)
        taps.append(top / under)
    scale = -0.5 / (grid_step * grid_step)
    off = [scale * t / filter_half for t in taps]
    diagonal = 3.0 * scale * (-2.0 * sum(taps))
    return off, diagonal


OFF, DIAGONAL = weights()


def params(mib):
    return pltpu.CompilerParams(vmem_limit_bytes=mib * 1024 * 1024)


def cost(flops, nbytes):
    return pl.CostEstimate(flops=flops, bytes_accessed=nbytes, transcendentals=0)


def sds(shape, dtype=F32):
    return jax.ShapeDtypeStruct(shape, dtype)


def split(value):
    high = value.astype(BF16)
    low = (value - high.astype(F32)).astype(BF16)
    return high, low


def mm(a, b):
    return jnp.dot(a, b, preferred_element_type=F32)


def tap_sum(at, index):
    total = None
    for k in range(1, 7):
        term = OFF[k - 1] * (at(index + k) + at(index - k))
        total = term if total is None else total + term
    return total


B = 4
STEPS = C // B
N = 2
MIDDLE = 10
EDGE = 192
MID = 64
MID_START = MIDDLE * EDGE


def stride_rows(z):
    return pl.ds(z, C, stride=C)


def plane_spec(rows=ROWS, planes=B):
    return pl.BlockSpec((planes, rows, S), lambda i: (i, 0, 0))


def halo_spec(planes=B):
    return pl.BlockSpec((H, planes, C, S), lambda i: (0, i, 0, 0))


def part_spec(part):
    return pl.BlockSpec((1, B, ROWS, S), lambda i: (part, i, 0, 0))


def whole(rows=S):
    return pl.BlockSpec((rows, S), lambda i: (0, 0))


def edge_spec(start):
    return pl.BlockSpec((N, EDGE, S), lambda i: (jnp.maximum(i - start // N, 0), 0, 0))


def for_piece(edges, inner_ref, body):
    direct = (inner_ref[0] == 1) | (pl.program_id(0) < MIDDLE // N)

    @pl.when(direct)
    def _():
        body(edges[0])

    @pl.when(jnp.logical_not(direct))
    def _():
        body(edges[1])


SCALARS = pl.BlockSpec(memory_space=pltpu.SMEM)
FULL = sds((C, ROWS, S))
FULL_ROWS = sds((CELLS, S))
HALO_ROWS = H * ROWS
MESSAGE = sds((HALO_ROWS + 2 * NEAR, S))
ATOM_ROWS = 24
HALO = sds((HALO_ROWS + 2 * ATOM_ROWS, S))
DIRECT = sds((C * EDGE, S))
RELAY = sds((C - MIDDLE, EDGE, S))


def halo_rows(x, z):
    return pl.ds(pl.multiple_of(z * ROWS + x * C, C), C)


def halves(y, half):
    return slice(y * C + half * 8, y * C + half * 8 + 8)


def pack_edges(s_ref, out_ref):
    out_ref[:, 0:96, :] = s_ref[:, 0:96, :]
    out_ref[:, 96:192, :] = s_ref[:, 160:256, :]


def by_side(odd_ref, body, one, two):
    odd = odd_ref[0] == 1

    @pl.when(odd)
    def _():
        body(one, two)

    @pl.when(jnp.logical_not(odd))
    def _():
        body(two, one)


def pack_kernel(s_ref, inner_ref, odd_ref, own_ref, other_ref, message_ref, relay_ref, mid_ref, one_ref, two_ref):
    step = pl.program_id(0)
    inner = inner_ref[0] == 1
    mid_ref[...] = s_ref[:, 96:160, :]

    @pl.when(step == 0)
    def _():
        for ref in (one_ref, two_ref):
            ref[HALO_ROWS : HALO_ROWS + ATOM_ROWS, :] = own_ref[:ATOM_ROWS, :]
            ref[HALO_ROWS + ATOM_ROWS :, :] = other_ref[:ATOM_ROWS, :]

    @pl.when(step >= MIDDLE // N)
    def _():
        pack_edges(s_ref, relay_ref)

    @pl.when(inner | (step < MIDDLE // N))
    def _():
        for p in range(N):
            row = pl.multiple_of((step * N + p) * EDGE, MID)
            message_ref[pl.ds(row, 96), :] = s_ref[p, 0:96, :]
            message_ref[pl.ds(row + 96, 96), :] = s_ref[p, 160:256, :]

    @pl.when(jnp.logical_not(inner))
    def _():
        for p in range(N):
            row = pl.multiple_of(MID_START + (step * N + p) * MID, MID)
            message_ref[pl.ds(row, MID), :] = s_ref[p, 96:160, :]

    def halos(head_ref, tail_ref):
        for p in range(N):
            for z in range(H):
                rows = halo_rows(step * N + p, z)
                head_ref[rows, :] = s_ref[p, stride_rows(z), :]
                tail_ref[rows, :] = s_ref[p, stride_rows(C - H + z), :]

    by_side(odd_ref, halos, one_ref, two_ref)


def pack(s, inner, odd, parcel, parcel_mate):
    return pl.pallas_call(
        pack_kernel,
        grid=(C // N,),
        in_specs=[plane_spec(ROWS, N), SCALARS, SCALARS, whole(56), whole(56)],
        out_specs=[whole(C * EDGE), edge_spec(MIDDLE), plane_spec(MID, N)] + [whole(HALO.shape[0])] * 2,
        out_shape=[DIRECT, RELAY, sds((C, MID, S)), HALO, HALO],
        compiler_params=params(12),
        cost_estimate=cost(1 << 31, 8 << 20),
        name="pack",
    )(s, inner, odd, parcel, parcel_mate)


def stack_kernel(atoms_ref, pot_ref, out_ref):
    out_ref[0:24, :] = atoms_ref[...]
    out_ref[24:56, :] = pot_ref[...]


def stack(atoms, pot):
    return pl.pallas_call(stack_kernel, out_shape=sds((56, S)), compiler_params=params(4), name="stack")(atoms, pot)


def column_kernel(own_ref, other_ref, one_ref, two_ref, odd_ref, out_ref):
    def beside(below_ref, above_ref):
        out_ref[0:48, :] = below_ref[HALO_ROWS:, :]
        out_ref[96:144, :] = above_ref[HALO_ROWS:, :]

    by_side(odd_ref, beside, one_ref, two_ref)
    out_ref[48:72, :] = own_ref[:ATOM_ROWS, :]
    out_ref[72:96, :] = other_ref[:ATOM_ROWS, :]


def column(own, other, halos, odd):
    return pl.pallas_call(
        column_kernel,
        in_specs=[pl.BlockSpec(memory_space=pltpu.VMEM)] * 4 + [SCALARS],
        out_shape=sds((144, S)),
        compiler_params=params(8),
        name="column",
    )(own, other, *halos, odd)


def along_x(s_ref, mate_ref, out_ref, add):
    def column(block, _):
        rows = pl.ds(pl.multiple_of(block * 8, 8), 8)
        ring = [mate_ref[C - H + i, rows, :] for i in range(H)]
        ring += [s_ref[x, rows, :] for x in range(C)]
        ring += [mate_ref[i, rows, :] for i in range(H)]
        for x in range(C):
            value = tap_sum(lambda i: ring[H + i], x)
            if add:
                value = value + out_ref[x, rows, :]
            out_ref[x, rows, :] = value
        return 0

    lax.fori_loop(0, ROWS // 8, column, 0)


def z_taps(ext_ref, y):
    return tap_sum(lambda k: ext_ref[y * 32 + 8 + k : y * 32 + 24 + k, :], 0)


def side_x_kernel(s_ref, mate_ref, out_ref):
    along_x(s_ref, mate_ref, out_ref, False)


def side_x(s, mate):
    return pl.pallas_call(
        side_x_kernel,
        out_shape=FULL,
        compiler_params=params(12),
        cost_estimate=cost(1 << 24, 6 << 20),
        name="side_x",
    )(s, mate)


def side_z_kernel(s_ref, part_ref, one_ref, two_ref, odd_ref, out_ref, ext_ref):
    def planes(low_ref, high_ref):
        def plane(x, _):
            for y in range(C):
                ext_ref[y * 32 + 8 : y * 32 + 24, :] = s_ref[x, y * C : (y + 1) * C, :]
            for z in range(H):
                ext_ref[pl.ds(2 + z, C, stride=32), :] = low_ref[halo_rows(x, z), :]
                ext_ref[pl.ds(24 + z, C, stride=32), :] = high_ref[halo_rows(x, z), :]
            for y in range(C):
                rows = slice(y * C, (y + 1) * C)
                out_ref[x, rows, :] = part_ref[x, rows, :] + z_taps(ext_ref, y)
            return 0

        lax.fori_loop(0, C, plane, 0)

    by_side(odd_ref, planes, one_ref, two_ref)


def side_z(s, part, halos, odd):
    return pl.pallas_call(
        side_z_kernel,
        in_specs=[pl.BlockSpec(memory_space=pltpu.VMEM)] * 4 + [SCALARS],
        out_shape=FULL,
        scratch_shapes=[pltpu.VMEM((C * 32, S), F32)],
        compiler_params=params(14),
        cost_estimate=cost(1 << 24, 8 << 20),
        name="side_z",
    )(s, part, *halos, odd)


def side_again_kernel(s_ref, mate_ref, out_ref, ext_ref):
    for y in range(C):
        ext_ref[y * 32 : y * 32 + 8, :] = jnp.zeros((8, S), F32)
        ext_ref[y * 32 + 24 : y * 32 + 32, :] = jnp.zeros((8, S), F32)

    def plane(x, _):
        for y in range(C):
            ext_ref[y * 32 + 8 : y * 32 + 24, :] = s_ref[x, y * C : (y + 1) * C, :]
        for y in range(C):
            out_ref[x, y * C : (y + 1) * C, :] = z_taps(ext_ref, y)
        return 0

    lax.fori_loop(0, C, plane, 0)
    along_x(s_ref, mate_ref, out_ref, True)


def side_again(s, mate):
    return pl.pallas_call(
        side_again_kernel,
        out_shape=FULL,
        scratch_shapes=[pltpu.VMEM((C * 32, S), F32)],
        compiler_params=params(12),
        cost_estimate=cost(1 << 25, 6 << 20),
        name="side_again",
    )(s, mate)


def tap_weight(distance):
    value = jnp.zeros(distance.shape, F32)
    for k in range(1, 7):
        value = jnp.where(distance == k, OFF[k - 1], value)
    return value


def ring_tables(coordinate):
    masks, factors = [], []
    for t in range(W):
        away = (coordinate - t) & 31
        masks.append(away == 0)
        factors.append(tap_weight(jnp.minimum(away, 32 - away)))
    return masks, factors


def spread_kernel(parcel_ref, vb_ref):
    def spread_row(row, _):
        line = (parcel_ref[pl.ds(24 + row, 1), :] + (DIAGONAL - filter_centre)) * (1.0 / filter_half)
        start = pl.multiple_of(row * 128, 128)
        vb_ref[pl.ds(start, 128), :] = jnp.broadcast_to(line, (128, 128)).T
        return 0

    lax.fori_loop(0, CELLS // 128, spread_row, 0, unroll=8)


def spread(parcel):
    return pl.pallas_call(
        spread_kernel,
        out_shape=FULL_ROWS,
        compiler_params=params(8),
        cost_estimate=cost(1 << 20, 2 << 20),
        name="spread",
    )(parcel)


def prep_kernel(*refs):
    own_ref, other_ref, corner_ref, vb_ref, s_ref, gg_ref, coef_ref, energy_ref, near_ref, table_ref = refs[:10]
    a1_ref, a1z_ref, a2_ref, a2s_ref = refs[10:]
    upper_x, upper_y = corner_ref[0] > 0, corner_ref[1] > 0
    for slab in range(3):
        own = [own_ref[slab * 48 + j * 24 : slab * 48 + j * 24 + 24, :] for j in range(2)]
        other = [other_ref[slab * 48 + j * 24 : slab * 48 + j * 24 + 24, :] for j in range(2)]
        lower = [jnp.where(upper_x, o, m) for m, o in zip(own, other)]
        higher = [jnp.where(upper_x, m, o) for m, o in zip(own, other)]
        ordered = []
        for pair in (lower, higher):
            ordered += [jnp.where(upper_y, pair[1], pair[0]), jnp.where(upper_y, pair[0], pair[1])]
        for j in range(4):
            near_ref[slab * 96 + j * 24 : slab * 96 + j * 24 + 24, :] = ordered[j]
    blank = jnp.zeros((16, 128), F32)
    for block in range(6):
        rows = near_ref[pl.ds(block, NEAR, stride=6), :]
        table_ref[block * 128 : block * 128 + 128, :] = jnp.concatenate([rows, blank, rows, blank]).T
    at = TAPS + 3 - 640
    energy_ref[...] = jnp.broadcast_to(rows[:, at : at + 1] * (1.0 / filter_half), (NEAR, S))

    shape = (8, 128)
    sub = lax.broadcasted_iota(jnp.int32, shape, 0)
    lane = lax.broadcasted_iota(jnp.int32, shape, 1)
    first_lanes = lane < 64
    sites = [jnp.broadcast_to(table_ref[TAPS + d : TAPS + d + 1, :], shape).astype(jnp.int32) for d in range(3)]
    px = sites[0] - corner_ref[0]
    py = sites[1] - corner_ref[1]
    pz = (sites[2] & 15) + (((lane & 63) >> 4) - 1) * C
    zero = jnp.zeros(shape, F32)

    dz = sub + (lane >> 6) * 8 - pz + R
    z_masks = [dz == t for t in range(W)]
    z_factors = [tap_weight(jnp.abs(dz - t)) for t in range(W)]

    def place_z(ij, _):
        acc = zero
        along = zero
        for t in range(W):
            row = jnp.broadcast_to(table_ref[pl.ds(ij * W + t, 1), :], shape)
            acc = jnp.where(z_masks[t], row, acc)
            along = along + z_factors[t] * row
        a1_ref[ij] = acc
        a1z_ref[ij] = along
        return 0

    lax.fori_loop(0, W * W, place_z, 0, unroll=3)

    def place_y(y, _):
        masks, factors = ring_tables(y - py + R)
        for i in range(W):
            acc = zero
            along = zero
            moved = zero
            for t in range(W):
                value = a1_ref[i * W + t]
                acc = jnp.where(masks[t], value, acc)
                along = along + factors[t] * value
                moved = jnp.where(masks[t], a1z_ref[i * W + t], moved)
            a2_ref[i, y] = acc
            a2s_ref[i, y] = along + moved
        return 0

    lax.fori_loop(0, C, place_y, 0)

    def place_x(x, _):
        masks, factors = ring_tables(x - px + R)

        def per_y(y, _):
            row = pl.multiple_of(x * ROWS + y * C, C)
            acc = zero
            along = zero
            moved = zero
            for t in range(W):
                value = a2_ref[t, y]
                acc = jnp.where(masks[t], value, acc)
                along = along + factors[t] * value
                moved = jnp.where(masks[t], a2s_ref[t, y], moved)
            v = vb_ref[pl.ds(row, C), :]
            moved = along + moved + jnp.where(first_lanes, v[:8], v[8:]) * acc
            lower = jnp.where(first_lanes, acc, pltpu.roll(moved, 64, 1))
            upper = jnp.where(first_lanes, pltpu.roll(acc, 64, 1), moved)
            high, low = split(jnp.concatenate([lower, upper], axis=0))
            gg_ref[0, pl.ds(row, C), :] = high
            gg_ref[1, pl.ds(row, C), :] = low
            return 0

        lax.fori_loop(0, C, per_y, 0, unroll=16)
        return 0

    lax.fori_loop(0, C, place_x, 0)

    coef_ref[...] = jnp.zeros((3, NEAR, S), F32)

    def contract(x, _):
        rows = pl.ds(pl.multiple_of(x * 2 * ROWS, ROWS), 2 * ROWS)
        g_high, g_low = gg_ref[0, rows, :], gg_ref[1, rows, :]
        t_high, t_low = g_high.T, g_low.T
        high, low = split(s_ref[rows, :])
        got = mm(t_high, high) + (mm(t_high, low) + mm(t_low, high))
        t_high, t_low = t_high[:NEAR], t_low[:NEAR]
        pair = mm(t_high, g_high) + (mm(t_high, g_low) + mm(t_low, g_high))
        for slab in range(3):
            rows = slice(slab * C, slab * C + C)
            coef_ref[slab, 0:16] += got[rows]
            coef_ref[slab, 16:32] += got[64 + slab * C : 80 + slab * C]
            coef_ref[slab, 32:48] += pair[rows]
        return 0

    lax.fori_loop(0, C // 2, contract, 0, unroll=2)


def prep(parcels, corner, vb, s):
    vmem = pl.BlockSpec(memory_space=pltpu.VMEM)
    return pl.pallas_call(
        prep_kernel,
        in_specs=[vmem] * 2 + [pl.BlockSpec(memory_space=pltpu.SMEM), vmem, vmem],
        out_shape=[sds((2, CELLS, S), BF16), sds((3, NEAR, S)), sds((NEAR, S))],
        scratch_shapes=[
            pltpu.VMEM((288, 128), F32),
            pltpu.VMEM((768, 128), F32),
            pltpu.VMEM((W * W, 8, 128), F32),
            pltpu.VMEM((W * W, 8, 128), F32),
            pltpu.VMEM((W, C, 8, 128), F32),
            pltpu.VMEM((W, C, 8, 128), F32),
        ],
        compiler_params=params(16),
        cost_estimate=cost(1 << 27, 10 << 20),
        name="prep",
    )(*parcels, corner, vb, s.reshape(CELLS, S))


def move_pair(shares, away):
    lane = lax.broadcasted_iota(jnp.int32, (16, 128), 1)
    keep = (lane < 32) if away < 0 else (lane >= 16) & (lane < 48)
    pair = jnp.where(keep, pltpu.roll(shares[32:48], (away * 16) % 128, 1), 0.0)
    return jnp.concatenate([shares[0:32], pair])


def first_kernel(s_ref, side_ref, vb_ref, *refs):
    inner_ref, odd_ref, part_ref, mate_ref, q_ref, mix_ref, one_ref, two_ref = refs[2:]
    step = pl.program_id(0)

    @pl.when(step == 0)
    def _():
        def shares(head_ref, tail_ref):
            for j in range(2):
                rows = slice(HALO_ROWS + j * NEAR, HALO_ROWS + (j + 1) * NEAR)
                head_ref[rows, :] = part_ref[j] + mate_ref[j]
                tail_ref[rows, :] = part_ref[j + 1] + mate_ref[j + 1]

        by_side(odd_ref, shares, one_ref, two_ref)

    def planes(edge_ref):
        for p in range(N):
            for half in range(2):
                ring = {y: s_ref[p, halves(y, half), :] for y in range(C)}
                for y in range(H):
                    ring[C + y] = edge_ref[p, halves(y, half), :]
                    ring[y - H] = edge_ref[p, halves(H + y, half), :]
                for y in range(C):
                    rows = halves(y, half)
                    dy = tap_sum(lambda i: ring[i], y)
                    q = dy + vb_ref[p, rows, :] * ring[y]
                    q_ref[p, rows, :] = q
                    mix_ref[p, rows, :] = side_ref[p, rows, :] + q + dy

    for_piece(refs[:2], inner_ref, planes)

    def halos(head_ref, tail_ref):
        for p in range(N):
            for z in range(H):
                rows = halo_rows(step * N + p, z)
                head_ref[rows, :] = mix_ref[p, stride_rows(z), :]
                tail_ref[rows, :] = mix_ref[p, stride_rows(C - H + z), :]

    by_side(odd_ref, halos, one_ref, two_ref)


def make_first(s, side_part, vb, edges, inner, odd, part, part_mate):
    shares = pl.BlockSpec((3, NEAR, S), lambda i: (0, 0, 0))
    return pl.pallas_call(
        first_kernel,
        grid=(C // N,),
        in_specs=[plane_spec(ROWS, N)] * 3 + [edge_spec(0), edge_spec(MIDDLE)] + [SCALARS] * 2 + [shares] * 2,
        out_specs=[plane_spec(ROWS, N), plane_spec(ROWS, N), whole(MESSAGE.shape[0]), whole(MESSAGE.shape[0])],
        out_shape=[FULL, FULL, MESSAGE, MESSAGE],
        compiler_params=params(16),
        cost_estimate=cost(1 << 24, 14 << 20),
        name="first",
    )(s, side_part, vb, *edges, inner, odd, part, part_mate)


def base_kernel(s_ref, mid_ref, vb_ref, vb_mate_ref, q_ref, side_ref, part_ref, *refs):
    inner_ref, message_ref, out_ref, middle_ref = refs[2:]
    step = pl.program_id(0)
    inner = inner_ref[0] == 1

    @pl.when(inner)
    def _():
        middle_ref[...] = mid_ref[...]

    @pl.when(jnp.logical_not(inner))
    def _():
        for p in range(N):
            middle_ref[p] = message_ref[pl.ds(pl.multiple_of(MID_START + (step * N + p) * MID, MID), MID), :]

    def planes(edge_ref):
        for p in range(N):
            for half in range(2):

                def other(y, p=p, half=half):
                    if y < H:
                        return edge_ref[p, halves(y, half), :]
                    if y < C - H:
                        return middle_ref[p, halves(y - H, half), :]
                    return edge_ref[p, halves(y - 4, half), :]

                ring = [s_ref[p, halves(y, half), :] for y in range(C)] + [other(y) for y in range(C)]
                q = {y: q_ref[p, halves(y, half), :] for y in range(C)}
                for y in list(range(H)) + list(range(C - H, C)):
                    v = vb_mate_ref[p, halves(y, half), :]
                    q[C + y] = tap_sum(lambda i: ring[i % 32], C + y) + v * ring[C + y]
                for y in range(C):
                    rows = halves(y, half)
                    total = tap_sum(lambda i: q[i % 32], y)
                    total = total + vb_ref[p, rows, :] * (side_ref[p, rows, :] + q[y])
                    out_ref[p, rows, :] = 2.0 * (total + part_ref[p, rows, :]) - ring[y]

    for_piece(refs[:2], inner_ref, planes)


def make_base(s, mid, vb, vb_mate, q, side_part, part, edges, inner):
    return pl.pallas_call(
        base_kernel,
        grid=(C // N,),
        in_specs=[plane_spec(ROWS, N), plane_spec(MID, N)]
        + [plane_spec(ROWS, N)] * 5
        + [edge_spec(0), edge_spec(MIDDLE), SCALARS, whole(C * EDGE)],
        out_specs=plane_spec(ROWS, N),
        out_shape=FULL,
        scratch_shapes=[pltpu.VMEM((N, MID, S), F32)],
        compiler_params=params(16),
        cost_estimate=cost(1 << 25, 16 << 20),
        name="base",
    )(s, mid, vb, vb_mate, q, side_part, part, *edges, inner, edges[0].reshape(-1, S))


def second_kernel(base_ref, one_ref, two_ref, gg_high_ref, gg_low_ref, *rest):
    part_ref, mate_ref, energy_ref, upper_ref, odd_ref, second_ref, keep_ref, give_ref, gram_ref, cross_ref, w_ref, halo_ref = rest
    step = pl.program_id(0)

    @pl.when(step == 0)
    def _():
        gram_ref[...] = jnp.zeros((S, S), F32)
        cross_ref[...] = jnp.zeros((S, S), F32)
        w_ref[...] = jnp.zeros((S, S), F32)
        halo_ref[...] = jnp.zeros((B, ROWS, S), F32)
        mine = [part_ref[j] + mate_ref[j] for j in range(3)]
        odd = odd_ref[0] == 1
        got = [[ref[HALO_ROWS + j * NEAR : HALO_ROWS + (j + 1) * NEAR, :] for j in range(2)] for ref in (one_ref, two_ref)]
        below = [move_pair(jnp.where(odd, a, b), -1) for a, b in zip(*got)]
        above = [move_pair(jnp.where(odd, b, a), 1) for a, b in zip(*got)]
        slabs = [mine[0] + below[0], mine[1] + below[1] + above[0], mine[2] + above[1]]
        near = jnp.concatenate([slab[0:16] for slab in slabs]) * energy_ref[...]
        lane = lax.broadcasted_iota(jnp.int32, (NEAR, S), 1)
        pair = jnp.where(lane < NEAR, jnp.concatenate([slab[32:48] for slab in slabs]), 0.0)
        two = jnp.concatenate([slab[16:32] for slab in slabs])
        two = two + exact(pair, jnp.concatenate([near, jnp.zeros((S - NEAR, S), F32)]))
        w_ref[0:NEAR, :] = 2.0 * energy_ref[...] * two
        w_ref[64 : 64 + NEAR, :] = 2.0 * near

    def halo_part(low_ref, high_ref):
        for p in range(B):
            low = [low_ref[halo_rows(step * B + p, j), :] for j in range(H)]
            high = [high_ref[halo_rows(step * B + p, j), :] for j in range(H)]
            for z in range(H):
                add = sum((2.0 * OFF[k - 1]) * low[z - k + H] for k in range(z + 1, H + 1))
                halo_ref[p, stride_rows(z), :] = add
                add = sum((2.0 * OFF[H + j - z - 1]) * high[j] for j in range(z + 1))
                halo_ref[p, stride_rows(C - H + z), :] = add

    by_side(odd_ref, halo_part, one_ref, two_ref)

    w_high, w_low = split(w_ref[...])
    w_twice = jnp.concatenate([w_high, w_high])
    gram = jnp.zeros((S, 2 * S), F32)
    for p in range(B):
        g_high, g_low = gg_high_ref[0, p], gg_low_ref[0, p]
        near = mm(jnp.concatenate([g_high, g_low], axis=1), w_twice) + mm(g_high, w_low)
        value = base_ref[p] + halo_ref[p] + near
        second_ref[p] = value
        s_high, s_low = split(value)
        gram += mm(s_high.T, jnp.concatenate([s_high, s_low], axis=1))
    gram_ref[...] += gram[:, :S]
    cross_ref[...] += gram[:, S:]

    @pl.when(step == STEPS - 1)
    def _():
        cross = cross_ref[...]
        gram = (gram_ref[...] + (cross + cross.T)) * (1.0 / NCELLS)
        upper = upper_ref[0] == 1
        keep_ref[...] = jnp.where(upper, gram[S // 2 :], gram[: S // 2])
        give_ref[...] = jnp.where(upper, gram[: S // 2], gram[S // 2 :])


def make_second(base, halos, gg, shares, upper, odd):
    three = pl.BlockSpec((3, NEAR, S), lambda i: (0, 0, 0))
    return pl.pallas_call(
        second_kernel,
        grid=(STEPS,),
        in_specs=[plane_spec()]
        + [whole(MESSAGE.shape[0])] * 2
        + [part_spec(0), part_spec(1), three, three, whole(NEAR), SCALARS, SCALARS],
        out_specs=[plane_spec(), whole(S // 2), whole(S // 2)],
        out_shape=[FULL, sds((S // 2, S)), sds((S // 2, S))],
        scratch_shapes=[pltpu.VMEM((S, S), F32)] * 3 + [pltpu.VMEM((B, ROWS, S), F32)],
        compiler_params=params(16),
        cost_estimate=cost(1 << 27, 8 << 20),
        name="second",
    )(base, *halos, gg, gg, *shares, upper, odd)


def exact(a, b):
    return jnp.dot(a, b, precision=lax.Precision.HIGHEST, preferred_element_type=F32)


def inverse_factor(gram_ref, a_ref, x_ref, state_ref):
    row = lax.broadcasted_iota(jnp.int32, (S, S), 0)
    column = lax.broadcasted_iota(jnp.int32, (S, S), 1)
    unit = jnp.where(row == column, 1.0, 0.0)
    gram = gram_ref[...]
    diagonal = jnp.where(row == column, gram, 0.0)
    down = lax.rsqrt(jnp.sum(diagonal, axis=1, keepdims=True))
    across = lax.rsqrt(jnp.sum(diagonal, axis=0, keepdims=True))
    a_ref[...] = gram * down * across
    x_ref[...] = unit

    def residual():
        x = x_ref[...]
        return unit - exact(exact(x, a_ref[...]), x.T)

    def size(e):
        return jnp.sum(e * e)

    def improve(e):
        lower = jnp.where(row > column, e, jnp.where(row == column, 0.5 * e, 0.0))
        x_ref[...] += exact(lower, x_ref[...])

    state_ref[0] = 0
    start = unit - a_ref[...]
    start_size = size(start)

    @pl.when(start_size < 0.16)
    def _():
        improve(start)
        state_ref[0] = jnp.where(start_size < 1e-6, 2, 1)

    for _ in range(5):

        @pl.when(state_ref[0] == 1)
        def _():
            e = residual()
            e_size = size(e)
            improve(e)
            state_ref[0] = jnp.where(e_size < 1e-6, 2, 1)

    @pl.when(state_ref[0] != 2)
    def _():
        x_ref[...] = unit
        lanes = lax.broadcasted_iota(jnp.int32, (1, S), 1)

        def step(j, _):
            line = a_ref[pl.ds(j, 1), :]
            scale = lax.rsqrt(jnp.sum(jnp.where(lanes == j, line, 0.0), axis=1, keepdims=True))
            a = a_ref[...]
            factor = jnp.sum(jnp.where(column == j, a, 0.0), axis=1, keepdims=True) * scale
            factor = jnp.where(row[:, :1] > j, factor, 0.0)
            x_line = x_ref[pl.ds(j, 1), :] * scale
            a_ref[...] = a - factor * (line * scale)
            x_ref[...] = jnp.where(row == j, x_line, x_ref[...] - factor * x_line)
            return 0

        lax.fori_loop(0, S, step, 0)

    x_ref[...] = x_ref[...] * across


def turn_kernel(second_ref, own_ref, other_ref, upper_ref, out_ref, gram_ref, a_ref, x_ref, i_high_ref, i_low_ref, state_ref):
    @pl.when(pl.program_id(0) == 0)
    def _():
        upper = upper_ref[0] == 1
        gram_ref[: S // 2, :] = jnp.where(upper, other_ref[...], own_ref[...])
        gram_ref[S // 2 :, :] = jnp.where(upper, own_ref[...], other_ref[...])
        inverse_factor(gram_ref, a_ref, x_ref, state_ref)
        i_high, i_low = split(x_ref[...].T)
        i_high_ref[...] = i_high
        i_low_ref[...] = i_low

    i_high, i_low = i_high_ref[...], i_low_ref[...]
    i_twice = jnp.concatenate([i_high, i_high])
    for p in range(B):
        high, low = split(second_ref[p])
        out_ref[p] = mm(jnp.concatenate([high, low], axis=1), i_twice) + mm(high, i_low)


def turn(second, own, other, upper):
    return pl.pallas_call(
        turn_kernel,
        grid=(STEPS,),
        in_specs=[plane_spec(), whole(S // 2), whole(S // 2), SCALARS],
        out_specs=plane_spec(),
        out_shape=FULL,
        scratch_shapes=[pltpu.VMEM((S, S), F32)] * 3 + [pltpu.VMEM((S, S), BF16)] * 2 + [pltpu.SMEM((1,), jnp.int32)],
        compiler_params=params(16),
        cost_estimate=cost(1 << 28, 4 << 20),
        name="turn",
    )(second, own, other, upper)


def per_device(states, potential, atom_sites, projectors, energies):
    gx, gy = lax.axis_index("gx"), lax.axis_index("gy")
    depth = lax.axis_size("gzs")
    count = 4 * depth
    barrier = lax.optimization_barrier

    def send(value, flip):
        return lax.ppermute(value, AXES, [(d, d ^ flip) for d in range(count)])

    over_x, over_y = 2 * depth, depth

    def to_pairs(one, two):
        near = [(d, d ^ 1) for d in range(count)]
        far = [(d, d // depth * depth + (d + (1 if d % 2 else -1)) % depth) for d in range(count)]
        return lax.ppermute(one, AXES, near), lax.ppermute(two, AXES, far)

    inner_ones = [d for d in range(count) if d % 4 in (1, 2)]
    outer_ones = [d for d in range(count) if d % 4 in (0, 3)]
    inner = ((lax.axis_index("gzs") + 1) // 2 % 2).astype(jnp.int32).reshape(1)
    s = states.reshape(C, ROWS, S)
    mate = send(s, over_x)
    corner = jnp.stack([gx * C, gy * C]).astype(jnp.int32)
    upper = gx.astype(jnp.int32).reshape(1)
    odd = (lax.axis_index("gzs") % 2).astype(jnp.int32).reshape(1)
    pot = potential.reshape(32, 128)
    atoms = jnp.concatenate(
        [projectors.reshape(4, TAPS), atom_sites.astype(F32), energies[:, None], jnp.zeros((4, 768 - TAPS - 4), F32)],
        axis=1,
    ).reshape(24, 128)
    pot, corner, upper, inner, odd, atoms = barrier((pot, corner, upper, inner, odd, atoms))
    parcel = stack(atoms, pot)
    parcel_mate = send(parcel, over_y)
    message, relay, mid, halo_one, halo_two = pack(s, inner, odd, parcel, parcel_mate)
    message = send(message, over_y)
    relayed = lax.ppermute(relay, AXES, [(d, d ^ over_y ^ 1) for d in outer_ones])
    halos = to_pairs(halo_one, halo_two)
    vb = spread(parcel)
    mate, relayed = barrier((mate, relayed))
    beside = side_x(s, mate)
    halos, beside, vb = barrier((halos, beside, vb))
    relayed = lax.ppermute(relayed, AXES, [(d, d ^ 1) for d in inner_ones])
    side_part = side_z(s, beside, halos, odd)
    atoms = column(parcel, parcel_mate, halos, odd)
    atoms, side_part = barrier((atoms, side_part))
    atoms_mate = send(atoms, over_x)
    gg, part, energy = prep([atoms, atoms_mate], corner, vb, s)

    part = part + send(part, over_x)
    part_mate = send(part, over_y)
    edges = [message.reshape(C, EDGE, S), relayed]
    vb = vb.reshape(C, ROWS, S)
    q, mix, halo_one, halo_two = make_first(s, side_part, vb, edges, inner, odd, part, part_mate)
    halos = to_pairs(halo_one, halo_two)
    mate = send(mix, over_x)
    mid, part_mate = barrier((mid, part_mate))
    mid = lax.ppermute(mid, AXES, [(d, d ^ over_y) for d in inner_ones])
    vb_mate = spread(parcel_mate).reshape(C, ROWS, S)
    part_two = side_again(mix, mate)
    base = make_base(s, mid, vb, vb_mate, q, side_part, part_two, edges, inner)
    gg = gg.reshape(2, C, ROWS, S)
    second, own, give = make_second(base, halos, gg, [part, part_mate, energy], upper, odd)

    own = own + send(give, over_x)
    for flip in (32, 36, 1, 3, 8, 24):
        own = own + lax.ppermute(own, AXES, [(d, d ^ flip) for d in range(count)])
    return turn(second, own, send(own, over_x), upper).reshape(C, C, C, S)


def solution(mesh):
    return jax.shard_map(
        per_device,
        mesh=mesh,
        in_specs=(
            P("gx", "gy", "gzs", None),
            P("gx", "gy", "gzs"),
            P(("gx", "gy", "gzs"), None),
            P(("gx", "gy", "gzs"), None, None, None),
            P(("gx", "gy", "gzs")),
        ),
        out_specs=P("gx", "gy", "gzs", None),
        check_vma=False,
    )
```

```python
import math

import jax
import jax.numpy as jnp
from jax import lax
from jax.experimental import pallas as pl
from jax.experimental.pallas import tpu as pltpu
from jax.sharding import PartitionSpec as P

AXES = ("gx", "gy", "gzs")
H = 6
C = 16
ROWS = C * C
CELLS = C * C * C
NCELLS = 32 * 32 * 512
S = 128
W = 9
R = 4
NEAR = 48
TAPS = W * W * W
F32 = jnp.float32
BF16 = jnp.bfloat16

grid_step = 0.6
filter_centre = 36.0
filter_half = 26.0


def weights():
    taps = []
    for k in range(1, 7):
        top = 2.0 * (-1) ** (k + 1) * math.factorial(6) ** 2
        under = k * k * math.factorial(6 - k) * math.factorial(6 + k)
        taps.append(top / under)
    scale = -0.5 / (grid_step * grid_step)
    off = [scale * t / filter_half for t in taps]
    diagonal = 3.0 * scale * (-2.0 * sum(taps))
    return off, diagonal


OFF, DIAGONAL = weights()


def params(mib):
    return pltpu.CompilerParams(vmem_limit_bytes=mib * 1024 * 1024)


def cost(flops, nbytes):
    return pl.CostEstimate(flops=flops, bytes_accessed=nbytes, transcendentals=0)


def sds(shape, dtype=F32):
    return jax.ShapeDtypeStruct(shape, dtype)


def split(value):
    high = value.astype(BF16)
    low = (value - high.astype(F32)).astype(BF16)
    return high, low


def mm(a, b):
    return jnp.dot(a, b, preferred_element_type=F32)


def tap_sum(at, index):
    total = None
    for k in range(1, 7):
        term = OFF[k - 1] * (at(index + k) + at(index - k))
        total = term if total is None else total + term
    return total


B = 8
STEPS = C // B
N = 2
MIDDLE = 10
EDGE = 192
MID = 64
MID_START = MIDDLE * EDGE


def stride_rows(z):
    return pl.ds(z, C, stride=C)


def plane_spec(rows=ROWS, planes=B):
    return pl.BlockSpec((planes, rows, S), lambda i: (i, 0, 0))


def halo_spec(planes=B):
    return pl.BlockSpec((H, planes, C, S), lambda i: (0, i, 0, 0))


def part_spec(part):
    return pl.BlockSpec((1, B, ROWS, S), lambda i: (part, i, 0, 0))


def whole(rows=S):
    return pl.BlockSpec((rows, S), lambda i: (0, 0))


def edge_spec(start):
    return pl.BlockSpec((N, EDGE, S), lambda i: (jnp.maximum(i - start // N, 0), 0, 0))


def for_piece(edges, inner_ref, body):
    direct = (inner_ref[0] == 1) | (pl.program_id(0) < MIDDLE // N)

    @pl.when(direct)
    def _():
        body(edges[0])

    @pl.when(jnp.logical_not(direct))
    def _():
        body(edges[1])


SCALARS = pl.BlockSpec(memory_space=pltpu.SMEM)
FULL = sds((C, ROWS, S))
FULL_ROWS = sds((CELLS, S))
HALO_ROWS = H * ROWS
MESSAGE = sds((HALO_ROWS + 2 * NEAR, S))
ATOM_ROWS = 24
HALO = sds((HALO_ROWS + 2 * ATOM_ROWS, S))
DIRECT = sds((C * EDGE, S))
RELAY = sds((C - MIDDLE, EDGE, S))


def halo_rows(x, z):
    return pl.ds(pl.multiple_of(z * ROWS + x * C, C), C)


def halves(y, half):
    return slice(y * C + half * 8, y * C + half * 8 + 8)


def pack_edges(s_ref, out_ref):
    out_ref[:, 0:96, :] = s_ref[:, 0:96, :]
    out_ref[:, 96:192, :] = s_ref[:, 160:256, :]


def by_side(odd_ref, body, one, two):
    odd = odd_ref[0] == 1

    @pl.when(odd)
    def _():
        body(one, two)

    @pl.when(jnp.logical_not(odd))
    def _():
        body(two, one)


def pack_kernel(s_ref, inner_ref, message_ref, relay_ref, mid_ref):
    step = pl.program_id(0)
    inner = inner_ref[0] == 1
    mid_ref[...] = s_ref[:, 96:160, :]

    @pl.when(step >= MIDDLE // N)
    def _():
        pack_edges(s_ref, relay_ref)

    @pl.when(inner | (step < MIDDLE // N))
    def _():
        for p in range(N):
            row = pl.multiple_of((step * N + p) * EDGE, MID)
            message_ref[pl.ds(row, 96), :] = s_ref[p, 0:96, :]
            message_ref[pl.ds(row + 96, 96), :] = s_ref[p, 160:256, :]

    @pl.when(jnp.logical_not(inner))
    def _():
        for p in range(N):
            row = pl.multiple_of(MID_START + (step * N + p) * MID, MID)
            message_ref[pl.ds(row, MID), :] = s_ref[p, 96:160, :]


def pack(s, inner):
    return pl.pallas_call(
        pack_kernel,
        grid=(C // N,),
        in_specs=[plane_spec(ROWS, N), SCALARS],
        out_specs=[whole(C * EDGE), edge_spec(MIDDLE), plane_spec(MID, N)],
        out_shape=[DIRECT, RELAY, sds((C, MID, S))],
        compiler_params=params(12),
        cost_estimate=cost(1 << 31, 6 << 20),
        name="pack",
    )(s, inner)


def pack_halos_kernel(s_ref, odd_ref, own_ref, other_ref, one_ref, two_ref):
    step = pl.program_id(0)

    @pl.when(step == 0)
    def _():
        for ref in (one_ref, two_ref):
            ref[HALO_ROWS : HALO_ROWS + ATOM_ROWS, :] = own_ref[:ATOM_ROWS, :]
            ref[HALO_ROWS + ATOM_ROWS :, :] = other_ref[:ATOM_ROWS, :]

    def halos(head_ref, tail_ref):
        for p in range(B):
            for z in range(H):
                rows = halo_rows(step * B + p, z)
                head_ref[rows, :] = s_ref[p, stride_rows(z), :]
                tail_ref[rows, :] = s_ref[p, stride_rows(C - H + z), :]

    by_side(odd_ref, halos, one_ref, two_ref)


def pack_halos(s, odd, parcel, parcel_mate):
    return pl.pallas_call(
        pack_halos_kernel,
        grid=(STEPS,),
        in_specs=[plane_spec(), SCALARS, whole(56), whole(56)],
        out_specs=[whole(HALO.shape[0])] * 2,
        out_shape=[HALO, HALO],
        compiler_params=params(12),
        cost_estimate=cost(1 << 20, 4 << 20),
        name="pack_halos",
    )(s, odd, parcel, parcel_mate)


def stack_kernel(atoms_ref, pot_ref, out_ref):
    out_ref[0:24, :] = atoms_ref[...]
    out_ref[24:56, :] = pot_ref[...]


def stack(atoms, pot):
    return pl.pallas_call(stack_kernel, out_shape=sds((56, S)), compiler_params=params(4), name="stack")(atoms, pot)


def column_kernel(own_ref, other_ref, one_ref, two_ref, odd_ref, out_ref):
    def beside(below_ref, above_ref):
        out_ref[0:48, :] = below_ref[HALO_ROWS:, :]
        out_ref[96:144, :] = above_ref[HALO_ROWS:, :]

    by_side(odd_ref, beside, one_ref, two_ref)
    out_ref[48:72, :] = own_ref[:ATOM_ROWS, :]
    out_ref[72:96, :] = other_ref[:ATOM_ROWS, :]


def column(own, other, halos, odd):
    return pl.pallas_call(
        column_kernel,
        in_specs=[pl.BlockSpec(memory_space=pltpu.VMEM)] * 4 + [SCALARS],
        out_shape=sds((144, S)),
        compiler_params=params(8),
        name="column",
    )(own, other, *halos, odd)


def along_x(s_ref, mate_ref, out_ref, add):
    def column(block, _):
        rows = pl.ds(pl.multiple_of(block * 8, 8), 8)
        ring = [mate_ref[C - H + i, rows, :] for i in range(H)]
        ring += [s_ref[x, rows, :] for x in range(C)]
        ring += [mate_ref[i, rows, :] for i in range(H)]
        for x in range(C):
            value = tap_sum(lambda i: ring[H + i], x)
            if add:
                value = value + out_ref[x, rows, :]
            out_ref[x, rows, :] = value
        return 0

    lax.fori_loop(0, ROWS // 8, column, 0)


def z_taps(ext_ref, y):
    return tap_sum(lambda k: ext_ref[y * 32 + 8 + k : y * 32 + 24 + k, :], 0)


def side_x_kernel(s_ref, mate_ref, out_ref):
    along_x(s_ref, mate_ref, out_ref, False)


def side_x(s, mate):
    return pl.pallas_call(
        side_x_kernel,
        out_shape=FULL,
        compiler_params=params(12),
        cost_estimate=cost(1 << 24, 6 << 20),
        name="side_x",
    )(s, mate)


def side_z_kernel(s_ref, part_ref, one_ref, two_ref, odd_ref, out_ref, ext_ref):
    def planes(low_ref, high_ref):
        def plane(x, _):
            for y in range(C):
                ext_ref[y * 32 + 8 : y * 32 + 24, :] = s_ref[x, y * C : (y + 1) * C, :]
            for z in range(H):
                ext_ref[pl.ds(2 + z, C, stride=32), :] = low_ref[halo_rows(x, z), :]
                ext_ref[pl.ds(24 + z, C, stride=32), :] = high_ref[halo_rows(x, z), :]
            for y in range(C):
                rows = slice(y * C, (y + 1) * C)
                out_ref[x, rows, :] = part_ref[x, rows, :] + z_taps(ext_ref, y)
            return 0

        lax.fori_loop(0, C, plane, 0)

    by_side(odd_ref, planes, one_ref, two_ref)


def side_z(s, part, halos, odd):
    return pl.pallas_call(
        side_z_kernel,
        in_specs=[pl.BlockSpec(memory_space=pltpu.VMEM)] * 4 + [SCALARS],
        out_shape=FULL,
        scratch_shapes=[pltpu.VMEM((C * 32, S), F32)],
        compiler_params=params(14),
        cost_estimate=cost(1 << 24, 8 << 20),
        name="side_z",
    )(s, part, *halos, odd)


def side_again_kernel(s_ref, mate_ref, out_ref, ext_ref):
    for y in range(C):
        ext_ref[y * 32 : y * 32 + 8, :] = jnp.zeros((8, S), F32)
        ext_ref[y * 32 + 24 : y * 32 + 32, :] = jnp.zeros((8, S), F32)

    def plane(x, _):
        for y in range(C):
            ext_ref[y * 32 + 8 : y * 32 + 24, :] = s_ref[x, y * C : (y + 1) * C, :]
        for y in range(C):
            out_ref[x, y * C : (y + 1) * C, :] = z_taps(ext_ref, y)
        return 0

    lax.fori_loop(0, C, plane, 0)
    along_x(s_ref, mate_ref, out_ref, True)


def side_again(s, mate):
    return pl.pallas_call(
        side_again_kernel,
        out_shape=FULL,
        scratch_shapes=[pltpu.VMEM((C * 32, S), F32)],
        compiler_params=params(12),
        cost_estimate=cost(1 << 25, 6 << 20),
        name="side_again",
    )(s, mate)


def tap_weight(distance):
    value = jnp.zeros(distance.shape, F32)
    for k in range(1, 7):
        value = jnp.where(distance == k, OFF[k - 1], value)
    return value


def ring_tables(coordinate):
    masks, factors = [], []
    for t in range(W):
        away = (coordinate - t) & 31
        masks.append(away == 0)
        factors.append(tap_weight(jnp.minimum(away, 32 - away)))
    return masks, factors


def spread_kernel(parcel_ref, vb_ref):
    def spread_row(row, _):
        line = (parcel_ref[pl.ds(24 + row, 1), :] + (DIAGONAL - filter_centre)) * (1.0 / filter_half)
        start = pl.multiple_of(row * 128, 128)
        vb_ref[pl.ds(start, 128), :] = jnp.broadcast_to(line, (128, 128)).T
        return 0

    lax.fori_loop(0, CELLS // 128, spread_row, 0, unroll=8)


def spread(parcel):
    return pl.pallas_call(
        spread_kernel,
        out_shape=FULL_ROWS,
        compiler_params=params(8),
        cost_estimate=cost(1 << 20, 2 << 20),
        name="spread",
    )(parcel)


def prep_kernel(*refs):
    own_ref, other_ref, corner_ref, vb_ref, s_ref, gg_ref, coef_ref, energy_ref, near_ref, table_ref = refs[:10]
    a1_ref, a1z_ref, a2_ref, a2s_ref = refs[10:]
    upper_x, upper_y = corner_ref[0] > 0, corner_ref[1] > 0
    for slab in range(3):
        own = [own_ref[slab * 48 + j * 24 : slab * 48 + j * 24 + 24, :] for j in range(2)]
        other = [other_ref[slab * 48 + j * 24 : slab * 48 + j * 24 + 24, :] for j in range(2)]
        lower = [jnp.where(upper_x, o, m) for m, o in zip(own, other)]
        higher = [jnp.where(upper_x, m, o) for m, o in zip(own, other)]
        ordered = []
        for pair in (lower, higher):
            ordered += [jnp.where(upper_y, pair[1], pair[0]), jnp.where(upper_y, pair[0], pair[1])]
        for j in range(4):
            near_ref[slab * 96 + j * 24 : slab * 96 + j * 24 + 24, :] = ordered[j]
    blank = jnp.zeros((16, 128), F32)
    for block in range(6):
        rows = near_ref[pl.ds(block, NEAR, stride=6), :]
        table_ref[block * 128 : block * 128 + 128, :] = jnp.concatenate([rows, blank, rows, blank]).T
    at = TAPS + 3 - 640
    energy_ref[...] = jnp.broadcast_to(rows[:, at : at + 1] * (1.0 / filter_half), (NEAR, S))

    shape = (8, 128)
    sub = lax.broadcasted_iota(jnp.int32, shape, 0)
    lane = lax.broadcasted_iota(jnp.int32, shape, 1)
    first_lanes = lane < 64
    sites = [jnp.broadcast_to(table_ref[TAPS + d : TAPS + d + 1, :], shape).astype(jnp.int32) for d in range(3)]
    px = sites[0] - corner_ref[0]
    py = sites[1] - corner_ref[1]
    pz = (sites[2] & 15) + (((lane & 63) >> 4) - 1) * C
    zero = jnp.zeros(shape, F32)

    dz = sub + (lane >> 6) * 8 - pz + R
    z_masks = [dz == t for t in range(W)]
    z_factors = [tap_weight(jnp.abs(dz - t)) for t in range(W)]

    def place_z(ij, _):
        acc = zero
        along = zero
        for t in range(W):
            row = jnp.broadcast_to(table_ref[pl.ds(ij * W + t, 1), :], shape)
            acc = jnp.where(z_masks[t], row, acc)
            along = along + z_factors[t] * row
        a1_ref[ij] = acc
        a1z_ref[ij] = along
        return 0

    lax.fori_loop(0, W * W, place_z, 0, unroll=3)

    def place_y(y, _):
        masks, factors = ring_tables(y - py + R)
        for i in range(W):
            acc = zero
            along = zero
            moved = zero
            for t in range(W):
                value = a1_ref[i * W + t]
                acc = jnp.where(masks[t], value, acc)
                along = along + factors[t] * value
                moved = jnp.where(masks[t], a1z_ref[i * W + t], moved)
            a2_ref[i, y] = acc
            a2s_ref[i, y] = along + moved
        return 0

    lax.fori_loop(0, C, place_y, 0)

    def place_x(x, _):
        masks, factors = ring_tables(x - px + R)

        def per_y(y, _):
            row = pl.multiple_of(x * ROWS + y * C, C)
            acc = zero
            along = zero
            moved = zero
            for t in range(W):
                value = a2_ref[t, y]
                acc = jnp.where(masks[t], value, acc)
                along = along + factors[t] * value
                moved = jnp.where(masks[t], a2s_ref[t, y], moved)
            v = vb_ref[pl.ds(row, C), :]
            moved = along + moved + jnp.where(first_lanes, v[:8], v[8:]) * acc
            lower = jnp.where(first_lanes, acc, pltpu.roll(moved, 64, 1))
            upper = jnp.where(first_lanes, pltpu.roll(acc, 64, 1), moved)
            high, low = split(jnp.concatenate([lower, upper], axis=0))
            gg_ref[0, pl.ds(row, C), :] = high
            gg_ref[1, pl.ds(row, C), :] = low
            return 0

        lax.fori_loop(0, C, per_y, 0, unroll=16)
        return 0

    lax.fori_loop(0, C, place_x, 0)

    coef_ref[...] = jnp.zeros((3, NEAR, S), F32)

    def contract(x, _):
        rows = pl.ds(pl.multiple_of(x * 2 * ROWS, ROWS), 2 * ROWS)
        g_high, g_low = gg_ref[0, rows, :], gg_ref[1, rows, :]
        t_high, t_low = g_high.T, g_low.T
        high, low = split(s_ref[rows, :])
        got = mm(t_high, high) + (mm(t_high, low) + mm(t_low, high))
        t_high, t_low = t_high[:NEAR], t_low[:NEAR]
        pair = mm(t_high, g_high) + (mm(t_high, g_low) + mm(t_low, g_high))
        for slab in range(3):
            rows = slice(slab * C, slab * C + C)
            coef_ref[slab, 0:16] += got[rows]
            coef_ref[slab, 16:32] += got[64 + slab * C : 80 + slab * C]
            coef_ref[slab, 32:48] += pair[rows]
        return 0

    lax.fori_loop(0, C // 2, contract, 0, unroll=2)


def prep(parcels, corner, vb, s):
    vmem = pl.BlockSpec(memory_space=pltpu.VMEM)
    return pl.pallas_call(
        prep_kernel,
        in_specs=[vmem] * 2 + [pl.BlockSpec(memory_space=pltpu.SMEM), vmem, vmem],
        out_shape=[sds((2, CELLS, S), BF16), sds((3, NEAR, S)), sds((NEAR, S))],
        scratch_shapes=[
            pltpu.VMEM((288, 128), F32),
            pltpu.VMEM((768, 128), F32),
            pltpu.VMEM((W * W, 8, 128), F32),
            pltpu.VMEM((W * W, 8, 128), F32),
            pltpu.VMEM((W, C, 8, 128), F32),
            pltpu.VMEM((W, C, 8, 128), F32),
        ],
        compiler_params=params(16),
        cost_estimate=cost(1 << 27, 10 << 20),
        name="prep",
    )(*parcels, corner, vb, s.reshape(CELLS, S))


def move_pair(shares, away):
    lane = lax.broadcasted_iota(jnp.int32, (16, 128), 1)
    keep = (lane < 32) if away < 0 else (lane >= 16) & (lane < 48)
    pair = jnp.where(keep, pltpu.roll(shares[32:48], (away * 16) % 128, 1), 0.0)
    return jnp.concatenate([shares[0:32], pair])


def first_kernel(s_ref, side_ref, vb_ref, *refs):
    inner_ref, odd_ref, part_ref, mate_ref, q_ref, mix_ref, one_ref, two_ref = refs[2:]
    step = pl.program_id(0)

    @pl.when(step == 0)
    def _():
        def shares(head_ref, tail_ref):
            for j in range(2):
                rows = slice(HALO_ROWS + j * NEAR, HALO_ROWS + (j + 1) * NEAR)
                head_ref[rows, :] = part_ref[j] + mate_ref[j]
                tail_ref[rows, :] = part_ref[j + 1] + mate_ref[j + 1]

        by_side(odd_ref, shares, one_ref, two_ref)

    def planes(edge_ref):
        for p in range(N):
            for half in range(2):
                ring = {y: s_ref[p, halves(y, half), :] for y in range(C)}
                for y in range(H):
                    ring[C + y] = edge_ref[p, halves(y, half), :]
                    ring[y - H] = edge_ref[p, halves(H + y, half), :]
                for y in range(C):
                    rows = halves(y, half)
                    dy = tap_sum(lambda i: ring[i], y)
                    q = dy + vb_ref[p, rows, :] * ring[y]
                    q_ref[p, rows, :] = q
                    mix_ref[p, rows, :] = side_ref[p, rows, :] + q + dy

    for_piece(refs[:2], inner_ref, planes)

    def halos(head_ref, tail_ref):
        for p in range(N):
            for z in range(H):
                rows = halo_rows(step * N + p, z)
                head_ref[rows, :] = mix_ref[p, stride_rows(z), :]
                tail_ref[rows, :] = mix_ref[p, stride_rows(C - H + z), :]

    by_side(odd_ref, halos, one_ref, two_ref)


def make_first(s, side_part, vb, edges, inner, odd, part, part_mate):
    shares = pl.BlockSpec((3, NEAR, S), lambda i: (0, 0, 0))
    return pl.pallas_call(
        first_kernel,
        grid=(C // N,),
        in_specs=[plane_spec(ROWS, N)] * 3 + [edge_spec(0), edge_spec(MIDDLE)] + [SCALARS] * 2 + [shares] * 2,
        out_specs=[plane_spec(ROWS, N), plane_spec(ROWS, N), whole(MESSAGE.shape[0]), whole(MESSAGE.shape[0])],
        out_shape=[FULL, FULL, MESSAGE, MESSAGE],
        compiler_params=params(16),
        cost_estimate=cost(1 << 24, 14 << 20),
        name="first",
    )(s, side_part, vb, *edges, inner, odd, part, part_mate)


def base_kernel(s_ref, mid_ref, vb_ref, vb_mate_ref, q_ref, side_ref, part_ref, *refs):
    inner_ref, message_ref, out_ref, middle_ref = refs[2:]
    step = pl.program_id(0)
    inner = inner_ref[0] == 1

    @pl.when(inner)
    def _():
        middle_ref[...] = mid_ref[...]

    @pl.when(jnp.logical_not(inner))
    def _():
        for p in range(N):
            middle_ref[p] = message_ref[pl.ds(pl.multiple_of(MID_START + (step * N + p) * MID, MID), MID), :]

    def planes(edge_ref):
        for p in range(N):
            for half in range(2):

                def other(y, p=p, half=half):
                    if y < H:
                        return edge_ref[p, halves(y, half), :]
                    if y < C - H:
                        return middle_ref[p, halves(y - H, half), :]
                    return edge_ref[p, halves(y - 4, half), :]

                ring = [s_ref[p, halves(y, half), :] for y in range(C)] + [other(y) for y in range(C)]
                q = {y: q_ref[p, halves(y, half), :] for y in range(C)}
                for y in list(range(H)) + list(range(C - H, C)):
                    v = vb_mate_ref[p, halves(y, half), :]
                    q[C + y] = tap_sum(lambda i: ring[i % 32], C + y) + v * ring[C + y]
                for y in range(C):
                    rows = halves(y, half)
                    total = tap_sum(lambda i: q[i % 32], y)
                    total = total + vb_ref[p, rows, :] * (side_ref[p, rows, :] + q[y])
                    out_ref[p, rows, :] = 2.0 * (total + part_ref[p, rows, :]) - ring[y]

    for_piece(refs[:2], inner_ref, planes)


def make_base(s, mid, vb, vb_mate, q, side_part, part, edges, inner):
    return pl.pallas_call(
        base_kernel,
        grid=(C // N,),
        in_specs=[plane_spec(ROWS, N), plane_spec(MID, N)]
        + [plane_spec(ROWS, N)] * 5
        + [edge_spec(0), edge_spec(MIDDLE), SCALARS, whole(C * EDGE)],
        out_specs=plane_spec(ROWS, N),
        out_shape=FULL,
        scratch_shapes=[pltpu.VMEM((N, MID, S), F32)],
        compiler_params=params(16),
        cost_estimate=cost(1 << 25, 16 << 20),
        name="base",
    )(s, mid, vb, vb_mate, q, side_part, part, *edges, inner, edges[0].reshape(-1, S))


def second_kernel(base_ref, one_ref, two_ref, gg_high_ref, gg_low_ref, *rest):
    part_ref, mate_ref, energy_ref, upper_ref, odd_ref, second_ref, keep_ref, give_ref, gram_ref, cross_ref, w_ref, halo_ref = rest
    step = pl.program_id(0)

    @pl.when(step == 0)
    def _():
        gram_ref[...] = jnp.zeros((S, S), F32)
        cross_ref[...] = jnp.zeros((S, S), F32)
        w_ref[...] = jnp.zeros((S, S), F32)
        halo_ref[...] = jnp.zeros((B, ROWS, S), F32)
        mine = [part_ref[j] + mate_ref[j] for j in range(3)]
        odd = odd_ref[0] == 1
        got = [[ref[HALO_ROWS + j * NEAR : HALO_ROWS + (j + 1) * NEAR, :] for j in range(2)] for ref in (one_ref, two_ref)]
        below = [move_pair(jnp.where(odd, a, b), -1) for a, b in zip(*got)]
        above = [move_pair(jnp.where(odd, b, a), 1) for a, b in zip(*got)]
        slabs = [mine[0] + below[0], mine[1] + below[1] + above[0], mine[2] + above[1]]
        near = jnp.concatenate([slab[0:16] for slab in slabs]) * energy_ref[...]
        lane = lax.broadcasted_iota(jnp.int32, (NEAR, S), 1)
        pair = jnp.where(lane < NEAR, jnp.concatenate([slab[32:48] for slab in slabs]), 0.0)
        two = jnp.concatenate([slab[16:32] for slab in slabs])
        two = two + exact(pair, jnp.concatenate([near, jnp.zeros((S - NEAR, S), F32)]))
        w_ref[0:NEAR, :] = 2.0 * energy_ref[...] * two
        w_ref[64 : 64 + NEAR, :] = 2.0 * near

    def halo_part(low_ref, high_ref):
        for p in range(B):
            low = [low_ref[halo_rows(step * B + p, j), :] for j in range(H)]
            high = [high_ref[halo_rows(step * B + p, j), :] for j in range(H)]
            for z in range(H):
                add = sum((2.0 * OFF[k - 1]) * low[z - k + H] for k in range(z + 1, H + 1))
                halo_ref[p, stride_rows(z), :] = add
                add = sum((2.0 * OFF[H + j - z - 1]) * high[j] for j in range(z + 1))
                halo_ref[p, stride_rows(C - H + z), :] = add

    by_side(odd_ref, halo_part, one_ref, two_ref)

    w_high, w_low = split(w_ref[...])
    w_twice = jnp.concatenate([w_high, w_high])
    gram = jnp.zeros((S, 2 * S), F32)
    for p in range(B):
        g_high, g_low = gg_high_ref[0, p], gg_low_ref[0, p]
        near = mm(jnp.concatenate([g_high, g_low], axis=1), w_twice) + mm(g_high, w_low)
        value = base_ref[p] + halo_ref[p] + near
        second_ref[p] = value
        s_high, s_low = split(value)
        gram += mm(s_high.T, jnp.concatenate([s_high, s_low], axis=1))
    gram_ref[...] += gram[:, :S]
    cross_ref[...] += gram[:, S:]

    @pl.when(step == STEPS - 1)
    def _():
        cross = cross_ref[...]
        gram = (gram_ref[...] + (cross + cross.T)) * (1.0 / NCELLS)
        upper = upper_ref[0] == 1
        keep_ref[...] = jnp.where(upper, gram[S // 2 :], gram[: S // 2])
        give_ref[...] = jnp.where(upper, gram[: S // 2], gram[S // 2 :])


def make_second(base, halos, gg, shares, upper, odd):
    three = pl.BlockSpec((3, NEAR, S), lambda i: (0, 0, 0))
    return pl.pallas_call(
        second_kernel,
        grid=(STEPS,),
        in_specs=[plane_spec()]
        + [whole(MESSAGE.shape[0])] * 2
        + [part_spec(0), part_spec(1), three, three, whole(NEAR), SCALARS, SCALARS],
        out_specs=[plane_spec(), whole(S // 2), whole(S // 2)],
        out_shape=[FULL, sds((S // 2, S)), sds((S // 2, S))],
        scratch_shapes=[pltpu.VMEM((S, S), F32)] * 3 + [pltpu.VMEM((B, ROWS, S), F32)],
        compiler_params=params(16),
        cost_estimate=cost(1 << 27, 8 << 20),
        name="second",
    )(base, *halos, gg, gg, *shares, upper, odd)


def exact(a, b):
    return jnp.dot(a, b, precision=lax.Precision.HIGHEST, preferred_element_type=F32)


def close(a, b):
    a_high, a_low = split(a)
    b_high, b_low = split(b)
    return mm(jnp.concatenate([a_high, a_low], axis=1), jnp.concatenate([b_high, b_high])) + mm(a_high, b_low)


def inverse_factor(gram_ref, a_ref, x_ref, state_ref):
    row = lax.broadcasted_iota(jnp.int32, (S, S), 0)
    column = lax.broadcasted_iota(jnp.int32, (S, S), 1)
    unit = jnp.where(row == column, 1.0, 0.0)
    gram = gram_ref[...]
    diagonal = jnp.where(row == column, gram, 0.0)
    down = lax.rsqrt(jnp.sum(diagonal, axis=1, keepdims=True))
    across = lax.rsqrt(jnp.sum(diagonal, axis=0, keepdims=True))
    a_ref[...] = gram * down * across
    x_ref[...] = unit

    def residual():
        x = x_ref[...]
        return unit - close(close(x, a_ref[...]), x.T)

    def size(e):
        return jnp.sum(e * e)

    def improve(e):
        lower = jnp.where(row > column, e, jnp.where(row == column, 0.5 * e, 0.0))
        x_ref[...] += close(lower, x_ref[...])

    state_ref[0] = 0
    start = unit - a_ref[...]
    start_size = size(start)

    @pl.when(start_size < 0.16)
    def _():
        improve(start)
        state_ref[0] = jnp.where(start_size < 1e-6, 2, 1)

    for _ in range(5):

        @pl.when(state_ref[0] == 1)
        def _():
            e = residual()
            e_size = size(e)
            improve(e)
            state_ref[0] = jnp.where(e_size < 1e-6, 2, 1)

    @pl.when(state_ref[0] != 2)
    def _():
        x_ref[...] = unit
        lanes = lax.broadcasted_iota(jnp.int32, (1, S), 1)

        def step(j, _):
            line = a_ref[pl.ds(j, 1), :]
            scale = lax.rsqrt(jnp.sum(jnp.where(lanes == j, line, 0.0), axis=1, keepdims=True))
            a = a_ref[...]
            factor = jnp.sum(jnp.where(column == j, a, 0.0), axis=1, keepdims=True) * scale
            factor = jnp.where(row[:, :1] > j, factor, 0.0)
            x_line = x_ref[pl.ds(j, 1), :] * scale
            a_ref[...] = a - factor * (line * scale)
            x_ref[...] = jnp.where(row == j, x_line, x_ref[...] - factor * x_line)
            return 0

        lax.fori_loop(0, S, step, 0)

    x_ref[...] = x_ref[...] * across


def turn_kernel(second_ref, own_ref, other_ref, upper_ref, out_ref, gram_ref, a_ref, x_ref, i_high_ref, i_low_ref, state_ref):
    @pl.when(pl.program_id(0) == 0)
    def _():
        upper = upper_ref[0] == 1
        gram_ref[: S // 2, :] = jnp.where(upper, other_ref[...], own_ref[...])
        gram_ref[S // 2 :, :] = jnp.where(upper, own_ref[...], other_ref[...])
        inverse_factor(gram_ref, a_ref, x_ref, state_ref)
        i_high, i_low = split(x_ref[...].T)
        i_high_ref[...] = i_high
        i_low_ref[...] = i_low

    i_high, i_low = i_high_ref[...], i_low_ref[...]
    i_twice = jnp.concatenate([i_high, i_high])
    for p in range(B):
        high, low = split(second_ref[p])
        out_ref[p] = mm(jnp.concatenate([high, low], axis=1), i_twice) + mm(high, i_low)


def turn(second, own, other, upper):
    return pl.pallas_call(
        turn_kernel,
        grid=(STEPS,),
        in_specs=[plane_spec(), whole(S // 2), whole(S // 2), SCALARS],
        out_specs=plane_spec(),
        out_shape=FULL,
        scratch_shapes=[pltpu.VMEM((S, S), F32)] * 3 + [pltpu.VMEM((S, S), BF16)] * 2 + [pltpu.SMEM((1,), jnp.int32)],
        compiler_params=params(16),
        cost_estimate=cost(1 << 28, 4 << 20),
        name="turn",
    )(second, own, other, upper)


def per_device(states, potential, atom_sites, projectors, energies):
    gx, gy = lax.axis_index("gx"), lax.axis_index("gy")
    depth = lax.axis_size("gzs")
    count = 4 * depth
    barrier = lax.optimization_barrier

    def send(value, flip):
        return lax.ppermute(value, AXES, [(d, d ^ flip) for d in range(count)])

    over_x, over_y = 2 * depth, depth

    def to_pairs(one, two):
        near = [(d, d ^ 1) for d in range(count)]
        far = [(d, d // depth * depth + (d + (1 if d % 2 else -1)) % depth) for d in range(count)]
        return lax.ppermute(one, AXES, near), lax.ppermute(two, AXES, far)

    inner_ones = [d for d in range(count) if d % 4 in (1, 2)]
    outer_ones = [d for d in range(count) if d % 4 in (0, 3)]
    inner = ((lax.axis_index("gzs") + 1) // 2 % 2).astype(jnp.int32).reshape(1)
    s = states.reshape(C, ROWS, S)
    mate = send(s, over_x)
    corner = jnp.stack([gx * C, gy * C]).astype(jnp.int32)
    upper = gx.astype(jnp.int32).reshape(1)
    odd = (lax.axis_index("gzs") % 2).astype(jnp.int32).reshape(1)
    pot = potential.reshape(32, 128)
    atoms = jnp.concatenate(
        [projectors.reshape(4, TAPS), atom_sites.astype(F32), energies[:, None], jnp.zeros((4, 768 - TAPS - 4), F32)],
        axis=1,
    ).reshape(24, 128)
    pot, corner, upper, inner, odd, atoms = barrier((pot, corner, upper, inner, odd, atoms))
    parcel = stack(atoms, pot)
    to_pack, parcel = barrier((s, parcel))
    parcel_mate = send(parcel, over_y)
    message, relay, mid = pack(to_pack, inner)
    parcel_mate, message, relay = barrier((parcel_mate, message, relay))
    halo_one, halo_two = pack_halos(s, odd, parcel, parcel_mate)
    message = send(message, over_y)
    relayed = lax.ppermute(relay, AXES, [(d, d ^ over_y ^ 1) for d in outer_ones])
    halos = to_pairs(halo_one, halo_two)
    vb = spread(parcel)
    mate, relayed = barrier((mate, relayed))
    beside = side_x(s, mate)
    halos, beside, vb = barrier((halos, beside, vb))
    relayed = lax.ppermute(relayed, AXES, [(d, d ^ 1) for d in inner_ones])
    side_part = side_z(s, beside, halos, odd)
    atoms = column(parcel, parcel_mate, halos, odd)
    atoms, side_part = barrier((atoms, side_part))
    atoms_mate = send(atoms, over_x)
    gg, part, energy = prep([atoms, atoms_mate], corner, vb, s)

    part = part + send(part, over_x)
    part_mate = send(part, over_y)
    edges = [message.reshape(C, EDGE, S), relayed]
    vb = vb.reshape(C, ROWS, S)
    q, mix, halo_one, halo_two = make_first(s, side_part, vb, edges, inner, odd, part, part_mate)
    halos = to_pairs(halo_one, halo_two)
    mate = send(mix, over_x)
    mid, part_mate = barrier((mid, part_mate))
    mid = lax.ppermute(mid, AXES, [(d, d ^ over_y) for d in inner_ones])
    vb_mate = spread(parcel_mate).reshape(C, ROWS, S)
    part_two = side_again(mix, mate)
    base = make_base(s, mid, vb, vb_mate, q, side_part, part_two, edges, inner)
    gg = gg.reshape(2, C, ROWS, S)
    second, own, give = make_second(base, halos, gg, [part, part_mate, energy], upper, odd)

    own = own + send(give, over_x)
    for flip in (32, 36, 1, 3, 8, 24):
        own = own + lax.ppermute(own, AXES, [(d, d ^ flip) for d in range(count)])
    return turn(second, own, send(own, over_x), upper).reshape(C, C, C, S)


def solution(mesh):
    return jax.shard_map(
        per_device,
        mesh=mesh,
        in_specs=(
            P("gx", "gy", "gzs", None),
            P("gx", "gy", "gzs"),
            P(("gx", "gy", "gzs"), None),
            P(("gx", "gy", "gzs"), None, None, None),
            P(("gx", "gy", "gzs")),
        ),
        out_specs=P("gx", "gy", "gzs", None),
        check_vma=False,
    )
```

```python
import math

import jax
import jax.numpy as jnp
from jax import lax
from jax.experimental import pallas as pl
from jax.experimental.pallas import tpu as pltpu
from jax.sharding import PartitionSpec as P

AXES = ("gx", "gy", "gzs")
H = 6
C = 16
ROWS = C * C
CELLS = C * C * C
NCELLS = 32 * 32 * 512
S = 128
W = 9
R = 4
NEAR = 48
TAPS = W * W * W
F32 = jnp.float32
BF16 = jnp.bfloat16

grid_step = 0.6
filter_centre = 36.0
filter_half = 26.0


def weights():
    taps = []
    for k in range(1, 7):
        top = 2.0 * (-1) ** (k + 1) * math.factorial(6) ** 2
        under = k * k * math.factorial(6 - k) * math.factorial(6 + k)
        taps.append(top / under)
    scale = -0.5 / (grid_step * grid_step)
    off = [scale * t / filter_half for t in taps]
    diagonal = 3.0 * scale * (-2.0 * sum(taps))
    return off, diagonal


OFF, DIAGONAL = weights()


def params(mib):
    return pltpu.CompilerParams(vmem_limit_bytes=mib * 1024 * 1024)


def cost(flops, nbytes):
    return pl.CostEstimate(flops=flops, bytes_accessed=nbytes, transcendentals=0)


def sds(shape, dtype=F32):
    return jax.ShapeDtypeStruct(shape, dtype)


def split(value):
    high = value.astype(BF16)
    low = (value - high.astype(F32)).astype(BF16)
    return high, low


def mm(a, b):
    return jnp.dot(a, b, preferred_element_type=F32)


def tap_sum(at, index):
    total = None
    for k in range(1, 7):
        term = OFF[k - 1] * (at(index + k) + at(index - k))
        total = term if total is None else total + term
    return total


B = 8
STEPS = C // B
N = 2
MIDDLE = 10
EDGE = 192
MID = 64
MID_START = MIDDLE * EDGE


def stride_rows(z):
    return pl.ds(z, C, stride=C)


def plane_spec(rows=ROWS, planes=B):
    return pl.BlockSpec((planes, rows, S), lambda i: (i, 0, 0))


def halo_spec(planes=B):
    return pl.BlockSpec((H, planes, C, S), lambda i: (0, i, 0, 0))


def part_spec(part):
    return pl.BlockSpec((1, B, ROWS, S), lambda i: (part, i, 0, 0))


def whole(rows=S):
    return pl.BlockSpec((rows, S), lambda i: (0, 0))


def edge_spec(start):
    return pl.BlockSpec((N, EDGE, S), lambda i: (jnp.maximum(i - start // N, 0), 0, 0))


def for_piece(edges, inner_ref, body):
    direct = (inner_ref[0] == 1) | (pl.program_id(0) < MIDDLE // N)

    @pl.when(direct)
    def _():
        body(edges[0])

    @pl.when(jnp.logical_not(direct))
    def _():
        body(edges[1])


SCALARS = pl.BlockSpec(memory_space=pltpu.SMEM)
FULL = sds((C, ROWS, S))
FULL_ROWS = sds((CELLS, S))
HALO_ROWS = H * ROWS
MESSAGE = sds((HALO_ROWS + 2 * NEAR, S))
ATOM_ROWS = 24
HALO = sds((HALO_ROWS + 2 * ATOM_ROWS, S))
DIRECT = sds((C * EDGE, S))
RELAY = sds((C - MIDDLE, EDGE, S))


def halo_rows(x, z):
    return pl.ds(pl.multiple_of(z * ROWS + x * C, C), C)


def halves(y, half):
    return slice(y * C + half * 8, y * C + half * 8 + 8)


def pack_edges(s_ref, out_ref):
    out_ref[:, 0:96, :] = s_ref[:, 0:96, :]
    out_ref[:, 96:192, :] = s_ref[:, 160:256, :]


def by_side(odd_ref, body, one, two):
    odd = odd_ref[0] == 1

    @pl.when(odd)
    def _():
        body(one, two)

    @pl.when(jnp.logical_not(odd))
    def _():
        body(two, one)


def pack_kernel(s_ref, inner_ref, message_ref, relay_ref, mid_ref):
    step = pl.program_id(0)
    inner = inner_ref[0] == 1
    mid_ref[...] = s_ref[:, 96:160, :]

    @pl.when(step >= MIDDLE // N)
    def _():
        pack_edges(s_ref, relay_ref)

    @pl.when(inner | (step < MIDDLE // N))
    def _():
        for p in range(N):
            row = pl.multiple_of((step * N + p) * EDGE, MID)
            message_ref[pl.ds(row, 96), :] = s_ref[p, 0:96, :]
            message_ref[pl.ds(row + 96, 96), :] = s_ref[p, 160:256, :]

    @pl.when(jnp.logical_not(inner))
    def _():
        for p in range(N):
            row = pl.multiple_of(MID_START + (step * N + p) * MID, MID)
            message_ref[pl.ds(row, MID), :] = s_ref[p, 96:160, :]


def pack(s, inner):
    return pl.pallas_call(
        pack_kernel,
        grid=(C // N,),
        in_specs=[plane_spec(ROWS, N), SCALARS],
        out_specs=[whole(C * EDGE), edge_spec(MIDDLE), plane_spec(MID, N)],
        out_shape=[DIRECT, RELAY, sds((C, MID, S))],
        compiler_params=params(12),
        cost_estimate=cost(1 << 31, 6 << 20),
        name="pack",
    )(s, inner)


def atom_rows(out_ref, start, atoms_ref):
    for block in range(6):
        out_ref[start + block * 4 : start + block * 4 + 4, :] = atoms_ref[:, block * 128 : block * 128 + 128]


def pack_halos_kernel(s_ref, odd_ref, own_ref, other_ref, one_ref, two_ref):
    step = pl.program_id(0)

    @pl.when(step == 0)
    def _():
        for ref in (one_ref, two_ref):
            atom_rows(ref, HALO_ROWS, own_ref)
            atom_rows(ref, HALO_ROWS + ATOM_ROWS, other_ref)

    def halos(head_ref, tail_ref):
        for p in range(B):
            for z in range(H):
                rows = halo_rows(step * B + p, z)
                head_ref[rows, :] = s_ref[p, stride_rows(z), :]
                tail_ref[rows, :] = s_ref[p, stride_rows(C - H + z), :]

    by_side(odd_ref, halos, one_ref, two_ref)


def pack_halos(s, odd, own, other):
    return pl.pallas_call(
        pack_halos_kernel,
        grid=(STEPS,),
        in_specs=[plane_spec(), SCALARS] + [pl.BlockSpec((4, 768), lambda i: (0, 0))] * 2,
        out_specs=[whole(HALO.shape[0])] * 2,
        out_shape=[HALO, HALO],
        compiler_params=params(12),
        cost_estimate=cost(1 << 20, 4 << 20),
        name="pack_halos",
    )(s, odd, own, other)


def column_kernel(own_ref, other_ref, one_ref, two_ref, odd_ref, out_ref):
    def beside(below_ref, above_ref):
        out_ref[0:48, :] = below_ref[HALO_ROWS:, :]
        out_ref[96:144, :] = above_ref[HALO_ROWS:, :]

    by_side(odd_ref, beside, one_ref, two_ref)
    atom_rows(out_ref, 48, own_ref)
    atom_rows(out_ref, 72, other_ref)


def column(own, other, halos, odd):
    return pl.pallas_call(
        column_kernel,
        in_specs=[pl.BlockSpec(memory_space=pltpu.VMEM)] * 4 + [SCALARS],
        out_shape=sds((144, S)),
        compiler_params=params(8),
        name="column",
    )(own, other, *halos, odd)


def along_x(s_ref, mate_ref, out_ref, add):
    def column(block, _):
        rows = pl.ds(pl.multiple_of(block * 8, 8), 8)
        ring = [mate_ref[C - H + i, rows, :] for i in range(H)]
        ring += [s_ref[x, rows, :] for x in range(C)]
        ring += [mate_ref[i, rows, :] for i in range(H)]
        for x in range(C):
            value = tap_sum(lambda i: ring[H + i], x)
            if add:
                value = value + out_ref[x, rows, :]
            out_ref[x, rows, :] = value
        return 0

    lax.fori_loop(0, ROWS // 8, column, 0)


def z_taps(ext_ref, y):
    return tap_sum(lambda k: ext_ref[y * 32 + 8 + k : y * 32 + 24 + k, :], 0)


def side_x_kernel(s_ref, mate_ref, out_ref):
    along_x(s_ref, mate_ref, out_ref, False)


def side_x(s, mate):
    return pl.pallas_call(
        side_x_kernel,
        out_shape=FULL,
        compiler_params=params(12),
        cost_estimate=cost(1 << 24, 6 << 20),
        name="side_x",
    )(s, mate)


def side_z_kernel(s_ref, part_ref, one_ref, two_ref, odd_ref, out_ref, ext_ref):
    def planes(low_ref, high_ref):
        def plane(x, _):
            for y in range(C):
                ext_ref[y * 32 + 8 : y * 32 + 24, :] = s_ref[x, y * C : (y + 1) * C, :]
            for z in range(H):
                ext_ref[pl.ds(2 + z, C, stride=32), :] = low_ref[halo_rows(x, z), :]
                ext_ref[pl.ds(24 + z, C, stride=32), :] = high_ref[halo_rows(x, z), :]
            for y in range(C):
                rows = slice(y * C, (y + 1) * C)
                out_ref[x, rows, :] = part_ref[x, rows, :] + z_taps(ext_ref, y)
            return 0

        lax.fori_loop(0, C, plane, 0)

    by_side(odd_ref, planes, one_ref, two_ref)


def side_z(s, part, halos, odd):
    return pl.pallas_call(
        side_z_kernel,
        in_specs=[pl.BlockSpec(memory_space=pltpu.VMEM)] * 4 + [SCALARS],
        out_shape=FULL,
        scratch_shapes=[pltpu.VMEM((C * 32, S), F32)],
        compiler_params=params(14),
        cost_estimate=cost(1 << 24, 8 << 20),
        name="side_z",
    )(s, part, *halos, odd)


def side_again_kernel(s_ref, mate_ref, out_ref, ext_ref):
    for y in range(C):
        ext_ref[y * 32 : y * 32 + 8, :] = jnp.zeros((8, S), F32)
        ext_ref[y * 32 + 24 : y * 32 + 32, :] = jnp.zeros((8, S), F32)

    def plane(x, _):
        for y in range(C):
            ext_ref[y * 32 + 8 : y * 32 + 24, :] = s_ref[x, y * C : (y + 1) * C, :]
        for y in range(C):
            out_ref[x, y * C : (y + 1) * C, :] = z_taps(ext_ref, y)
        return 0

    lax.fori_loop(0, C, plane, 0)
    along_x(s_ref, mate_ref, out_ref, True)


def side_again(s, mate):
    return pl.pallas_call(
        side_again_kernel,
        out_shape=FULL,
        scratch_shapes=[pltpu.VMEM((C * 32, S), F32)],
        compiler_params=params(12),
        cost_estimate=cost(1 << 25, 6 << 20),
        name="side_again",
    )(s, mate)


def tap_weight(distance):
    value = jnp.zeros(distance.shape, F32)
    for k in range(1, 7):
        value = jnp.where(distance == k, OFF[k - 1], value)
    return value


def ring_tables(coordinate):
    masks, factors = [], []
    for t in range(W):
        away = (coordinate - t) & 31
        masks.append(away == 0)
        factors.append(tap_weight(jnp.minimum(away, 32 - away)))
    return masks, factors


def spread_kernel(pot_ref, vb_ref):
    def spread_row(row, _):
        line = (pot_ref[pl.ds(row, 1), :] + (DIAGONAL - filter_centre)) * (1.0 / filter_half)
        start = pl.multiple_of(row * 128, 128)
        vb_ref[pl.ds(start, 128), :] = jnp.broadcast_to(line, (128, 128)).T
        return 0

    lax.fori_loop(0, CELLS // 128, spread_row, 0, unroll=8)


def spread(pot):
    return pl.pallas_call(
        spread_kernel,
        out_shape=FULL_ROWS,
        compiler_params=params(8),
        cost_estimate=cost(1 << 20, 2 << 20),
        name="spread",
    )(pot)


def prep_kernel(*refs):
    own_ref, other_ref, corner_ref, vb_ref, s_ref, gg_ref, coef_ref, energy_ref, near_ref, table_ref = refs[:10]
    a1_ref, a1z_ref, a2_ref, a2s_ref = refs[10:]
    upper_x, upper_y = corner_ref[0] > 0, corner_ref[1] > 0
    for slab in range(3):
        own = [own_ref[slab * 48 + j * 24 : slab * 48 + j * 24 + 24, :] for j in range(2)]
        other = [other_ref[slab * 48 + j * 24 : slab * 48 + j * 24 + 24, :] for j in range(2)]
        lower = [jnp.where(upper_x, o, m) for m, o in zip(own, other)]
        higher = [jnp.where(upper_x, m, o) for m, o in zip(own, other)]
        ordered = []
        for pair in (lower, higher):
            ordered += [jnp.where(upper_y, pair[1], pair[0]), jnp.where(upper_y, pair[0], pair[1])]
        for j in range(4):
            for block in range(6):
                row = block * NEAR + slab * 16 + j * 4
                near_ref[row : row + 4, :] = ordered[j][block * 4 : block * 4 + 4]
    blank = jnp.zeros((16, 128), F32)
    for block in range(6):
        rows = near_ref[block * NEAR : (block + 1) * NEAR, :]
        table_ref[block * 128 : block * 128 + 128, :] = jnp.concatenate([rows, blank, rows, blank]).T
    at = TAPS + 3 - 640
    energy_ref[...] = jnp.broadcast_to(rows[:, at : at + 1] * (1.0 / filter_half), (NEAR, S))

    shape = (8, 128)
    sub = lax.broadcasted_iota(jnp.int32, shape, 0)
    lane = lax.broadcasted_iota(jnp.int32, shape, 1)
    first_lanes = lane < 64
    sites = [jnp.broadcast_to(table_ref[TAPS + d : TAPS + d + 1, :], shape).astype(jnp.int32) for d in range(3)]
    px = sites[0] - corner_ref[0]
    py = sites[1] - corner_ref[1]
    pz = (sites[2] & 15) + (((lane & 63) >> 4) - 1) * C
    zero = jnp.zeros(shape, F32)

    dz = sub + (lane >> 6) * 8 - pz + R
    z_masks = [dz == t for t in range(W)]
    z_factors = [tap_weight(jnp.abs(dz - t)) for t in range(W)]

    def place_z(ij, _):
        acc = zero
        along = zero
        for t in range(W):
            row = jnp.broadcast_to(table_ref[pl.ds(ij * W + t, 1), :], shape)
            acc = jnp.where(z_masks[t], row, acc)
            along = along + z_factors[t] * row
        a1_ref[ij] = acc
        a1z_ref[ij] = along
        return 0

    lax.fori_loop(0, W * W, place_z, 0, unroll=3)

    def place_y(y, _):
        masks, factors = ring_tables(y - py + R)
        for i in range(W):
            acc = zero
            along = zero
            moved = zero
            for t in range(W):
                value = a1_ref[i * W + t]
                acc = jnp.where(masks[t], value, acc)
                along = along + factors[t] * value
                moved = jnp.where(masks[t], a1z_ref[i * W + t], moved)
            a2_ref[i, y] = acc
            a2s_ref[i, y] = along + moved
        return 0

    lax.fori_loop(0, C, place_y, 0)

    def place_x(x, _):
        masks, factors = ring_tables(x - px + R)

        def per_y(y, _):
            row = pl.multiple_of(x * ROWS + y * C, C)
            acc = zero
            along = zero
            moved = zero
            for t in range(W):
                value = a2_ref[t, y]
                acc = jnp.where(masks[t], value, acc)
                along = along + factors[t] * value
                moved = jnp.where(masks[t], a2s_ref[t, y], moved)
            v = vb_ref[pl.ds(row, C), :]
            moved = along + moved + jnp.where(first_lanes, v[:8], v[8:]) * acc
            lower = jnp.where(first_lanes, acc, pltpu.roll(moved, 64, 1))
            upper = jnp.where(first_lanes, pltpu.roll(acc, 64, 1), moved)
            high, low = split(jnp.concatenate([lower, upper], axis=0))
            gg_ref[0, pl.ds(row, C), :] = high
            gg_ref[1, pl.ds(row, C), :] = low
            return 0

        lax.fori_loop(0, C, per_y, 0, unroll=16)
        return 0

    lax.fori_loop(0, C, place_x, 0)

    coef_ref[...] = jnp.zeros((3, NEAR, S), F32)

    def contract(x, _):
        rows = pl.ds(pl.multiple_of(x * 2 * ROWS, ROWS), 2 * ROWS)
        g_high, g_low = gg_ref[0, rows, :], gg_ref[1, rows, :]
        t_high, t_low = g_high.T, g_low.T
        high, low = split(s_ref[rows, :])
        got = mm(t_high, high) + (mm(t_high, low) + mm(t_low, high))
        t_high, t_low = t_high[:NEAR], t_low[:NEAR]
        pair = mm(t_high, g_high) + (mm(t_high, g_low) + mm(t_low, g_high))
        for slab in range(3):
            rows = slice(slab * C, slab * C + C)
            coef_ref[slab, 0:16] += got[rows]
            coef_ref[slab, 16:32] += got[64 + slab * C : 80 + slab * C]
            coef_ref[slab, 32:48] += pair[rows]
        return 0

    lax.fori_loop(0, C // 2, contract, 0, unroll=2)


def prep(parcels, corner, vb, s):
    vmem = pl.BlockSpec(memory_space=pltpu.VMEM)
    return pl.pallas_call(
        prep_kernel,
        in_specs=[vmem] * 2 + [pl.BlockSpec(memory_space=pltpu.SMEM), vmem, vmem],
        out_shape=[sds((2, CELLS, S), BF16), sds((3, NEAR, S)), sds((NEAR, S))],
        scratch_shapes=[
            pltpu.VMEM((288, 128), F32),
            pltpu.VMEM((768, 128), F32),
            pltpu.VMEM((W * W, 8, 128), F32),
            pltpu.VMEM((W * W, 8, 128), F32),
            pltpu.VMEM((W, C, 8, 128), F32),
            pltpu.VMEM((W, C, 8, 128), F32),
        ],
        compiler_params=params(16),
        cost_estimate=cost(1 << 27, 10 << 20),
        name="prep",
    )(*parcels, corner, vb, s.reshape(CELLS, S))


def move_pair(shares, away):
    lane = lax.broadcasted_iota(jnp.int32, (16, 128), 1)
    keep = (lane < 32) if away < 0 else (lane >= 16) & (lane < 48)
    pair = jnp.where(keep, pltpu.roll(shares[32:48], (away * 16) % 128, 1), 0.0)
    return jnp.concatenate([shares[0:32], pair])


def first_kernel(s_ref, side_ref, vb_ref, *refs):
    inner_ref, odd_ref, part_ref, mate_ref, q_ref, mix_ref, one_ref, two_ref = refs[2:]
    step = pl.program_id(0)

    @pl.when(step == 0)
    def _():
        def shares(head_ref, tail_ref):
            for j in range(2):
                rows = slice(HALO_ROWS + j * NEAR, HALO_ROWS + (j + 1) * NEAR)
                head_ref[rows, :] = part_ref[j] + mate_ref[j]
                tail_ref[rows, :] = part_ref[j + 1] + mate_ref[j + 1]

        by_side(odd_ref, shares, one_ref, two_ref)

    def planes(edge_ref):
        for p in range(N):
            for half in range(2):
                ring = {y: s_ref[p, halves(y, half), :] for y in range(C)}
                for y in range(H):
                    ring[C + y] = edge_ref[p, halves(y, half), :]
                    ring[y - H] = edge_ref[p, halves(H + y, half), :]
                for y in range(C):
                    rows = halves(y, half)
                    dy = tap_sum(lambda i: ring[i], y)
                    q = dy + vb_ref[p, rows, :] * ring[y]
                    q_ref[p, rows, :] = q
                    mix_ref[p, rows, :] = side_ref[p, rows, :] + q + dy

    for_piece(refs[:2], inner_ref, planes)

    def halos(head_ref, tail_ref):
        for p in range(N):
            for z in range(H):
                rows = halo_rows(step * N + p, z)
                head_ref[rows, :] = mix_ref[p, stride_rows(z), :]
                tail_ref[rows, :] = mix_ref[p, stride_rows(C - H + z), :]

    by_side(odd_ref, halos, one_ref, two_ref)


def make_first(s, side_part, vb, edges, inner, odd, part, part_mate):
    shares = pl.BlockSpec((3, NEAR, S), lambda i: (0, 0, 0))
    return pl.pallas_call(
        first_kernel,
        grid=(C // N,),
        in_specs=[plane_spec(ROWS, N)] * 3 + [edge_spec(0), edge_spec(MIDDLE)] + [SCALARS] * 2 + [shares] * 2,
        out_specs=[plane_spec(ROWS, N), plane_spec(ROWS, N), whole(MESSAGE.shape[0]), whole(MESSAGE.shape[0])],
        out_shape=[FULL, FULL, MESSAGE, MESSAGE],
        compiler_params=params(16),
        cost_estimate=cost(1 << 24, 14 << 20),
        name="first",
    )(s, side_part, vb, *edges, inner, odd, part, part_mate)


def base_kernel(s_ref, mid_ref, vb_ref, vb_mate_ref, q_ref, side_ref, part_ref, *refs):
    inner_ref, message_ref, out_ref, middle_ref = refs[2:]
    step = pl.program_id(0)
    inner = inner_ref[0] == 1

    @pl.when(inner)
    def _():
        middle_ref[...] = mid_ref[...]

    @pl.when(jnp.logical_not(inner))
    def _():
        for p in range(N):
            middle_ref[p] = message_ref[pl.ds(pl.multiple_of(MID_START + (step * N + p) * MID, MID), MID), :]

    def planes(edge_ref):
        for p in range(N):
            for half in range(2):

                def other(y, p=p, half=half):
                    if y < H:
                        return edge_ref[p, halves(y, half), :]
                    if y < C - H:
                        return middle_ref[p, halves(y - H, half), :]
                    return edge_ref[p, halves(y - 4, half), :]

                ring = [s_ref[p, halves(y, half), :] for y in range(C)] + [other(y) for y in range(C)]
                q = {y: q_ref[p, halves(y, half), :] for y in range(C)}
                for y in list(range(H)) + list(range(C - H, C)):
                    v = vb_mate_ref[p, halves(y, half), :]
                    q[C + y] = tap_sum(lambda i: ring[i % 32], C + y) + v * ring[C + y]
                for y in range(C):
                    rows = halves(y, half)
                    total = tap_sum(lambda i: q[i % 32], y)
                    total = total + vb_ref[p, rows, :] * (side_ref[p, rows, :] + q[y])
                    out_ref[p, rows, :] = 2.0 * (total + part_ref[p, rows, :]) - ring[y]

    for_piece(refs[:2], inner_ref, planes)


def make_base(s, mid, vb, vb_mate, q, side_part, part, edges, inner):
    return pl.pallas_call(
        base_kernel,
        grid=(C // N,),
        in_specs=[plane_spec(ROWS, N), plane_spec(MID, N)]
        + [plane_spec(ROWS, N)] * 5
        + [edge_spec(0), edge_spec(MIDDLE), SCALARS, whole(C * EDGE)],
        out_specs=plane_spec(ROWS, N),
        out_shape=FULL,
        scratch_shapes=[pltpu.VMEM((N, MID, S), F32)],
        compiler_params=params(16),
        cost_estimate=cost(1 << 25, 16 << 20),
        name="base",
    )(s, mid, vb, vb_mate, q, side_part, part, *edges, inner, edges[0].reshape(-1, S))


def second_kernel(base_ref, one_ref, two_ref, gg_high_ref, gg_low_ref, *rest):
    part_ref, mate_ref, energy_ref, upper_ref, odd_ref, second_ref, keep_ref, give_ref, gram_ref, cross_ref, w_ref, halo_ref = rest
    step = pl.program_id(0)

    @pl.when(step == 0)
    def _():
        gram_ref[...] = jnp.zeros((S, S), F32)
        cross_ref[...] = jnp.zeros((S, S), F32)
        w_ref[...] = jnp.zeros((S, S), F32)
        halo_ref[...] = jnp.zeros((B, ROWS, S), F32)
        mine = [part_ref[j] + mate_ref[j] for j in range(3)]
        odd = odd_ref[0] == 1
        got = [[ref[HALO_ROWS + j * NEAR : HALO_ROWS + (j + 1) * NEAR, :] for j in range(2)] for ref in (one_ref, two_ref)]
        below = [move_pair(jnp.where(odd, a, b), -1) for a, b in zip(*got)]
        above = [move_pair(jnp.where(odd, b, a), 1) for a, b in zip(*got)]
        slabs = [mine[0] + below[0], mine[1] + below[1] + above[0], mine[2] + above[1]]
        near = jnp.concatenate([slab[0:16] for slab in slabs]) * energy_ref[...]
        lane = lax.broadcasted_iota(jnp.int32, (NEAR, S), 1)
        pair = jnp.where(lane < NEAR, jnp.concatenate([slab[32:48] for slab in slabs]), 0.0)
        two = jnp.concatenate([slab[16:32] for slab in slabs])
        two = two + exact(pair, jnp.concatenate([near, jnp.zeros((S - NEAR, S), F32)]))
        w_ref[0:NEAR, :] = 2.0 * energy_ref[...] * two
        w_ref[64 : 64 + NEAR, :] = 2.0 * near

    def halo_part(low_ref, high_ref):
        for p in range(B):
            low = [low_ref[halo_rows(step * B + p, j), :] for j in range(H)]
            high = [high_ref[halo_rows(step * B + p, j), :] for j in range(H)]
            for z in range(H):
                add = sum((2.0 * OFF[k - 1]) * low[z - k + H] for k in range(z + 1, H + 1))
                halo_ref[p, stride_rows(z), :] = add
                add = sum((2.0 * OFF[H + j - z - 1]) * high[j] for j in range(z + 1))
                halo_ref[p, stride_rows(C - H + z), :] = add

    by_side(odd_ref, halo_part, one_ref, two_ref)

    w_high, w_low = split(w_ref[...])
    w_twice = jnp.concatenate([w_high, w_high])
    gram = jnp.zeros((S, 2 * S), F32)
    for p in range(B):
        g_high, g_low = gg_high_ref[0, p], gg_low_ref[0, p]
        near = mm(jnp.concatenate([g_high, g_low], axis=1), w_twice) + mm(g_high, w_low)
        value = base_ref[p] + halo_ref[p] + near
        second_ref[p] = value
        s_high, s_low = split(value)
        gram += mm(s_high.T, jnp.concatenate([s_high, s_low], axis=1))
    gram_ref[...] += gram[:, :S]
    cross_ref[...] += gram[:, S:]

    @pl.when(step == STEPS - 1)
    def _():
        cross = cross_ref[...]
        gram = (gram_ref[...] + (cross + cross.T)) * (1.0 / NCELLS)
        upper = upper_ref[0] == 1
        keep_ref[...] = jnp.where(upper, gram[S // 2 :], gram[: S // 2])
        give_ref[...] = jnp.where(upper, gram[: S // 2], gram[S // 2 :])


def make_second(base, halos, gg, shares, upper, odd):
    three = pl.BlockSpec((3, NEAR, S), lambda i: (0, 0, 0))
    return pl.pallas_call(
        second_kernel,
        grid=(STEPS,),
        in_specs=[plane_spec()]
        + [whole(MESSAGE.shape[0])] * 2
        + [part_spec(0), part_spec(1), three, three, whole(NEAR), SCALARS, SCALARS],
        out_specs=[plane_spec(), whole(S // 2), whole(S // 2)],
        out_shape=[FULL, sds((S // 2, S)), sds((S // 2, S))],
        scratch_shapes=[pltpu.VMEM((S, S), F32)] * 3 + [pltpu.VMEM((B, ROWS, S), F32)],
        compiler_params=params(16),
        cost_estimate=cost(1 << 27, 8 << 20),
        name="second",
    )(base, *halos, gg, gg, *shares, upper, odd)


def exact(a, b):
    return jnp.dot(a, b, precision=lax.Precision.HIGHEST, preferred_element_type=F32)


def close(a, b):
    a_high, a_low = split(a)
    b_high, b_low = split(b)
    return mm(jnp.concatenate([a_high, a_low], axis=1), jnp.concatenate([b_high, b_high])) + mm(a_high, b_low)


def inverse_factor(gram_ref, a_ref, x_ref, state_ref):
    row = lax.broadcasted_iota(jnp.int32, (S, S), 0)
    column = lax.broadcasted_iota(jnp.int32, (S, S), 1)
    unit = jnp.where(row == column, 1.0, 0.0)
    gram = gram_ref[...]
    diagonal = jnp.where(row == column, gram, 0.0)
    down = lax.rsqrt(jnp.sum(diagonal, axis=1, keepdims=True))
    across = lax.rsqrt(jnp.sum(diagonal, axis=0, keepdims=True))
    a_ref[...] = gram * down * across
    x_ref[...] = unit

    def residual():
        x = x_ref[...]
        return unit - close(close(x, a_ref[...]), x.T)

    def size(e):
        return jnp.sum(e * e)

    def improve(e):
        lower = jnp.where(row > column, e, jnp.where(row == column, 0.5 * e, 0.0))
        x_ref[...] += close(lower, x_ref[...])

    state_ref[0] = 0
    start = unit - a_ref[...]
    start_size = size(start)

    @pl.when(start_size < 0.16)
    def _():
        improve(start)
        state_ref[0] = jnp.where(start_size < 1e-6, 2, 1)

    for _ in range(5):

        @pl.when(state_ref[0] == 1)
        def _():
            e = residual()
            e_size = size(e)
            improve(e)
            state_ref[0] = jnp.where(e_size < 1e-6, 2, 1)

    @pl.when(state_ref[0] != 2)
    def _():
        x_ref[...] = unit
        lanes = lax.broadcasted_iota(jnp.int32, (1, S), 1)

        def step(j, _):
            line = a_ref[pl.ds(j, 1), :]
            scale = lax.rsqrt(jnp.sum(jnp.where(lanes == j, line, 0.0), axis=1, keepdims=True))
            a = a_ref[...]
            factor = jnp.sum(jnp.where(column == j, a, 0.0), axis=1, keepdims=True) * scale
            factor = jnp.where(row[:, :1] > j, factor, 0.0)
            x_line = x_ref[pl.ds(j, 1), :] * scale
            a_ref[...] = a - factor * (line * scale)
            x_ref[...] = jnp.where(row == j, x_line, x_ref[...] - factor * x_line)
            return 0

        lax.fori_loop(0, S, step, 0)

    x_ref[...] = x_ref[...] * across


def turn_kernel(second_ref, own_ref, other_ref, upper_ref, out_ref, gram_ref, a_ref, x_ref, i_high_ref, i_low_ref, state_ref):
    @pl.when(pl.program_id(0) == 0)
    def _():
        upper = upper_ref[0] == 1
        gram_ref[: S // 2, :] = jnp.where(upper, other_ref[...], own_ref[...])
        gram_ref[S // 2 :, :] = jnp.where(upper, own_ref[...], other_ref[...])
        inverse_factor(gram_ref, a_ref, x_ref, state_ref)
        i_high, i_low = split(x_ref[...].T)
        i_high_ref[...] = i_high
        i_low_ref[...] = i_low

    i_high, i_low = i_high_ref[...], i_low_ref[...]
    i_twice = jnp.concatenate([i_high, i_high])
    for p in range(B):
        high, low = split(second_ref[p])
        out_ref[p] = mm(jnp.concatenate([high, low], axis=1), i_twice) + mm(high, i_low)


def turn(second, own, other, upper):
    return pl.pallas_call(
        turn_kernel,
        grid=(STEPS,),
        in_specs=[plane_spec(), whole(S // 2), whole(S // 2), SCALARS],
        out_specs=plane_spec(),
        out_shape=FULL,
        scratch_shapes=[pltpu.VMEM((S, S), F32)] * 3 + [pltpu.VMEM((S, S), BF16)] * 2 + [pltpu.SMEM((1,), jnp.int32)],
        compiler_params=params(16),
        cost_estimate=cost(1 << 28, 4 << 20),
        name="turn",
    )(second, own, other, upper)


def per_device(states, potential, atom_sites, projectors, energies):
    gx, gy = lax.axis_index("gx"), lax.axis_index("gy")
    depth = lax.axis_size("gzs")
    count = 4 * depth
    barrier = lax.optimization_barrier

    def send(value, flip):
        return lax.ppermute(value, AXES, [(d, d ^ flip) for d in range(count)])

    over_x, over_y = 2 * depth, depth

    def to_pairs(one, two):
        near = [(d, d ^ 1) for d in range(count)]
        far = [(d, d // depth * depth + (d + (1 if d % 2 else -1)) % depth) for d in range(count)]
        return lax.ppermute(one, AXES, near), lax.ppermute(two, AXES, far)

    inner_ones = [d for d in range(count) if d % 4 in (1, 2)]
    outer_ones = [d for d in range(count) if d % 4 in (0, 3)]
    inner = ((lax.axis_index("gzs") + 1) // 2 % 2).astype(jnp.int32).reshape(1)
    s = states.reshape(C, ROWS, S)
    mate = send(s, over_x)
    corner = jnp.stack([gx * C, gy * C]).astype(jnp.int32)
    upper = gx.astype(jnp.int32).reshape(1)
    odd = (lax.axis_index("gzs") % 2).astype(jnp.int32).reshape(1)
    atoms = jnp.concatenate(
        [projectors.reshape(4, TAPS), atom_sites.astype(F32), energies[:, None], jnp.zeros((4, 768 - TAPS - 4), F32)],
        axis=1,
    )
    corner, upper, inner, odd, atoms = barrier((corner, upper, inner, odd, atoms))
    to_pack, parcel = barrier((s, atoms))
    parcel_mate = send(parcel, over_y)
    message, relay, mid = pack(to_pack, inner)
    parcel_mate, message, relay = barrier((parcel_mate, message, relay))
    halo_one, halo_two = pack_halos(s, odd, parcel, parcel_mate)
    message = send(message, over_y)
    relayed = lax.ppermute(relay, AXES, [(d, d ^ over_y ^ 1) for d in outer_ones])
    halos = to_pairs(halo_one, halo_two)
    potential, relay = barrier((potential, relay))
    pot = potential.reshape(32, 128)
    vb = spread(pot)
    mate, relayed = barrier((mate, relayed))
    beside = side_x(s, mate)
    halos, beside, vb = barrier((halos, beside, vb))
    relayed = lax.ppermute(relayed, AXES, [(d, d ^ 1) for d in inner_ones])
    side_part = side_z(s, beside, halos, odd)
    atoms = column(parcel, parcel_mate, halos, odd)
    atoms, side_part = barrier((atoms, side_part))
    atoms_mate = send(atoms, over_x)
    gg, part, energy = prep([atoms, atoms_mate], corner, vb, s)

    part = part + send(part, over_x)
    part_mate = send(part, over_y)
    edges = [message.reshape(C, EDGE, S), relayed]
    vb = vb.reshape(C, ROWS, S)
    q, mix, halo_one, halo_two = make_first(s, side_part, vb, edges, inner, odd, part, part_mate)
    halos = to_pairs(halo_one, halo_two)
    mate = send(mix, over_x)
    pot, part_mate = barrier((pot, part_mate))
    pot_mate = send(pot, over_y)
    mid, pot_mate = barrier((mid, pot_mate))
    mid = lax.ppermute(mid, AXES, [(d, d ^ over_y) for d in inner_ones])
    vb_mate = spread(pot_mate).reshape(C, ROWS, S)
    part_two = side_again(mix, mate)
    base = make_base(s, mid, vb, vb_mate, q, side_part, part_two, edges, inner)
    gg = gg.reshape(2, C, ROWS, S)
    second, own, give = make_second(base, halos, gg, [part, part_mate, energy], upper, odd)

    own = own + send(give, over_x)
    for flip in (32, 36, 1, 3, 8, 24):
        own = own + lax.ppermute(own, AXES, [(d, d ^ flip) for d in range(count)])
    return turn(second, own, send(own, over_x), upper).reshape(C, C, C, S)


def solution(mesh):
    return jax.shard_map(
        per_device,
        mesh=mesh,
        in_specs=(
            P("gx", "gy", "gzs", None),
            P("gx", "gy", "gzs"),
            P(("gx", "gy", "gzs"), None),
            P(("gx", "gy", "gzs"), None, None, None),
            P(("gx", "gy", "gzs")),
        ),
        out_specs=P("gx", "gy", "gzs", None),
        check_vma=False,
    )
```

```python
import math

import jax
import jax.numpy as jnp
from jax import lax
from jax.experimental import pallas as pl
from jax.experimental.pallas import tpu as pltpu
from jax.sharding import PartitionSpec as P

AXES = ("gx", "gy", "gzs")
H = 6
C = 16
ROWS = C * C
CELLS = C * C * C
NCELLS = 32 * 32 * 512
S = 128
W = 9
R = 4
NEAR = 48
TAPS = W * W * W
F32 = jnp.float32
BF16 = jnp.bfloat16

grid_step = 0.6
filter_centre = 36.0
filter_half = 26.0


def weights():
    taps = []
    for k in range(1, 7):
        top = 2.0 * (-1) ** (k + 1) * math.factorial(6) ** 2
        under = k * k * math.factorial(6 - k) * math.factorial(6 + k)
        taps.append(top / under)
    scale = -0.5 / (grid_step * grid_step)
    off = [scale * t / filter_half for t in taps]
    diagonal = 3.0 * scale * (-2.0 * sum(taps))
    return off, diagonal


OFF, DIAGONAL = weights()


def params(mib):
    return pltpu.CompilerParams(vmem_limit_bytes=mib * 1024 * 1024)


def cost(flops, nbytes):
    return pl.CostEstimate(flops=flops, bytes_accessed=nbytes, transcendentals=0)


def sds(shape, dtype=F32):
    return jax.ShapeDtypeStruct(shape, dtype)


def split(value):
    high = value.astype(BF16)
    low = (value - high.astype(F32)).astype(BF16)
    return high, low


def mm(a, b):
    return jnp.dot(a, b, preferred_element_type=F32)


def tap_sum(at, index):
    total = None
    for k in range(1, 7):
        term = OFF[k - 1] * (at(index + k) + at(index - k))
        total = term if total is None else total + term
    return total


B = 8
STEPS = C // B
N = 2
MIDDLE = 10
EDGE = 192
MID = 64
MID_START = MIDDLE * EDGE


def stride_rows(z):
    return pl.ds(z, C, stride=C)


def plane_spec(rows=ROWS, planes=B):
    return pl.BlockSpec((planes, rows, S), lambda i: (i, 0, 0))


def halo_spec(planes=B):
    return pl.BlockSpec((H, planes, C, S), lambda i: (0, i, 0, 0))


def part_spec(part):
    return pl.BlockSpec((1, B, ROWS, S), lambda i: (part, i, 0, 0))


def whole(rows=S):
    return pl.BlockSpec((rows, S), lambda i: (0, 0))


def edge_spec(start):
    return pl.BlockSpec((N, EDGE, S), lambda i: (jnp.maximum(i - start // N, 0), 0, 0))


def for_piece(edges, inner_ref, body):
    direct = (inner_ref[0] == 1) | (pl.program_id(0) < MIDDLE // N)

    @pl.when(direct)
    def _():
        body(edges[0])

    @pl.when(jnp.logical_not(direct))
    def _():
        body(edges[1])


SCALARS = pl.BlockSpec(memory_space=pltpu.SMEM)
FULL = sds((C, ROWS, S))
FULL_ROWS = sds((CELLS, S))
HALO_ROWS = H * ROWS
MESSAGE = sds((HALO_ROWS + 2 * NEAR, S))
ATOM_ROWS = 24
HALO = sds((HALO_ROWS + 2 * ATOM_ROWS, S))
DIRECT = sds((C * EDGE, S))
RELAY = sds((C - MIDDLE, EDGE, S))


def halo_rows(x, z):
    return pl.ds(pl.multiple_of(z * ROWS + x * C, C), C)


def halves(y, half):
    return slice(y * C + half * 8, y * C + half * 8 + 8)


def pack_edges(s_ref, out_ref):
    out_ref[:, 0:96, :] = s_ref[:, 0:96, :]
    out_ref[:, 96:192, :] = s_ref[:, 160:256, :]


def by_side(odd_ref, body, one, two):
    odd = odd_ref[0] == 1

    @pl.when(odd)
    def _():
        body(one, two)

    @pl.when(jnp.logical_not(odd))
    def _():
        body(two, one)


def pack_kernel(s_ref, inner_ref, message_ref, relay_ref, mid_ref):
    step = pl.program_id(0)
    inner = inner_ref[0] == 1
    mid_ref[...] = s_ref[:, 96:160, :]

    @pl.when(step >= MIDDLE // N)
    def _():
        pack_edges(s_ref, relay_ref)

    @pl.when(inner | (step < MIDDLE // N))
    def _():
        for p in range(N):
            row = pl.multiple_of((step * N + p) * EDGE, MID)
            message_ref[pl.ds(row, 96), :] = s_ref[p, 0:96, :]
            message_ref[pl.ds(row + 96, 96), :] = s_ref[p, 160:256, :]

    @pl.when(jnp.logical_not(inner))
    def _():
        for p in range(N):
            row = pl.multiple_of(MID_START + (step * N + p) * MID, MID)
            message_ref[pl.ds(row, MID), :] = s_ref[p, 96:160, :]


def pack(s, inner):
    return pl.pallas_call(
        pack_kernel,
        grid=(C // N,),
        in_specs=[plane_spec(ROWS, N), SCALARS],
        out_specs=[whole(C * EDGE), edge_spec(MIDDLE), plane_spec(MID, N)],
        out_shape=[DIRECT, RELAY, sds((C, MID, S))],
        compiler_params=params(12),
        cost_estimate=cost(1 << 31, 6 << 20),
        name="pack",
    )(s, inner)


def pack_halos_kernel(s_ref, odd_ref, own_ref, other_ref, one_ref, two_ref):
    step = pl.program_id(0)

    @pl.when(step == 0)
    def _():
        for ref in (one_ref, two_ref):
            ref[HALO_ROWS : HALO_ROWS + ATOM_ROWS, :] = own_ref[:ATOM_ROWS, :]
            ref[HALO_ROWS + ATOM_ROWS :, :] = other_ref[:ATOM_ROWS, :]

    def halos(head_ref, tail_ref):
        for p in range(B):
            for z in range(H):
                rows = halo_rows(step * B + p, z)
                head_ref[rows, :] = s_ref[p, stride_rows(z), :]
                tail_ref[rows, :] = s_ref[p, stride_rows(C - H + z), :]

    by_side(odd_ref, halos, one_ref, two_ref)


def pack_halos(s, odd, parcel, parcel_mate):
    return pl.pallas_call(
        pack_halos_kernel,
        grid=(STEPS,),
        in_specs=[plane_spec(), SCALARS, whole(56), whole(56)],
        out_specs=[whole(HALO.shape[0])] * 2,
        out_shape=[HALO, HALO],
        compiler_params=params(12),
        cost_estimate=cost(1 << 20, 4 << 20),
        name="pack_halos",
    )(s, odd, parcel, parcel_mate)


def stack_kernel(atoms_ref, pot_ref, out_ref):
    out_ref[0:24, :] = atoms_ref[...]
    out_ref[24:56, :] = pot_ref[...]


def stack(atoms, pot):
    return pl.pallas_call(stack_kernel, out_shape=sds((56, S)), compiler_params=params(4), name="stack")(atoms, pot)


def column_kernel(own_ref, other_ref, two_ref, one_ref, odd_ref, out_ref):
    def beside(below_ref, above_ref):
        out_ref[0:48, :] = below_ref[HALO_ROWS:, :]
        out_ref[96:144, :] = above_ref[HALO_ROWS:, :]

    by_side(odd_ref, beside, one_ref, two_ref)
    out_ref[48:72, :] = own_ref[:ATOM_ROWS, :]
    out_ref[72:96, :] = other_ref[:ATOM_ROWS, :]


def column(own, other, halos, odd):
    return pl.pallas_call(
        column_kernel,
        in_specs=[pl.BlockSpec(memory_space=pltpu.VMEM)] * 4 + [SCALARS],
        out_shape=sds((144, S)),
        compiler_params=params(8),
        name="column",
    )(own, other, *halos, odd)


def along_x(s_ref, mate_ref, out_ref, add):
    def column(block, _):
        rows = pl.ds(pl.multiple_of(block * 8, 8), 8)
        ring = [mate_ref[C - H + i, rows, :] for i in range(H)]
        ring += [s_ref[x, rows, :] for x in range(C)]
        ring += [mate_ref[i, rows, :] for i in range(H)]
        for x in range(C):
            value = tap_sum(lambda i: ring[H + i], x)
            if add:
                value = value + out_ref[x, rows, :]
            out_ref[x, rows, :] = value
        return 0

    lax.fori_loop(0, ROWS // 8, column, 0)


def z_taps(ext_ref, y):
    return tap_sum(lambda k: ext_ref[y * 32 + 8 + k : y * 32 + 24 + k, :], 0)


def side_x_kernel(s_ref, mate_ref, out_ref):
    along_x(s_ref, mate_ref, out_ref, False)


def side_x(s, mate):
    return pl.pallas_call(
        side_x_kernel,
        out_shape=FULL,
        compiler_params=params(12),
        cost_estimate=cost(1 << 24, 6 << 20),
        name="side_x",
    )(s, mate)


def side_z_kernel(s_ref, part_ref, two_ref, one_ref, odd_ref, out_ref, ext_ref):
    def planes(low_ref, high_ref):
        def plane(x, _):
            for y in range(C):
                ext_ref[y * 32 + 8 : y * 32 + 24, :] = s_ref[x, y * C : (y + 1) * C, :]
            for z in range(H):
                ext_ref[pl.ds(2 + z, C, stride=32), :] = low_ref[halo_rows(x, z), :]
                ext_ref[pl.ds(24 + z, C, stride=32), :] = high_ref[halo_rows(x, z), :]
            for y in range(C):
                rows = slice(y * C, (y + 1) * C)
                out_ref[x, rows, :] = part_ref[x, rows, :] + z_taps(ext_ref, y)
            return 0

        lax.fori_loop(0, C, plane, 0)

    by_side(odd_ref, planes, one_ref, two_ref)


def side_z(s, part, halos, odd):
    return pl.pallas_call(
        side_z_kernel,
        in_specs=[pl.BlockSpec(memory_space=pltpu.VMEM)] * 4 + [SCALARS],
        out_shape=FULL,
        scratch_shapes=[pltpu.VMEM((C * 32, S), F32)],
        compiler_params=params(14),
        cost_estimate=cost(1 << 24, 8 << 20),
        name="side_z",
    )(s, part, *halos, odd)


def side_again_kernel(s_ref, mate_ref, out_ref, ext_ref):
    for y in range(C):
        ext_ref[y * 32 : y * 32 + 8, :] = jnp.zeros((8, S), F32)
        ext_ref[y * 32 + 24 : y * 32 + 32, :] = jnp.zeros((8, S), F32)

    def plane(x, _):
        for y in range(C):
            ext_ref[y * 32 + 8 : y * 32 + 24, :] = s_ref[x, y * C : (y + 1) * C, :]
        for y in range(C):
            out_ref[x, y * C : (y + 1) * C, :] = z_taps(ext_ref, y)
        return 0

    lax.fori_loop(0, C, plane, 0)
    along_x(s_ref, mate_ref, out_ref, True)


def side_again(s, mate):
    return pl.pallas_call(
        side_again_kernel,
        out_shape=FULL,
        scratch_shapes=[pltpu.VMEM((C * 32, S), F32)],
        compiler_params=params(12),
        cost_estimate=cost(1 << 25, 6 << 20),
        name="side_again",
    )(s, mate)


def tap_weight(distance):
    value = jnp.zeros(distance.shape, F32)
    for k in range(1, 7):
        value = jnp.where(distance == k, OFF[k - 1], value)
    return value


def ring_tables(coordinate):
    masks, factors = [], []
    for t in range(W):
        away = (coordinate - t) & 31
        masks.append(away == 0)
        factors.append(tap_weight(jnp.minimum(away, 32 - away)))
    return masks, factors


def spread_kernel(parcel_ref, vb_ref):
    def spread_row(row, _):
        line = (parcel_ref[pl.ds(24 + row, 1), :] + (DIAGONAL - filter_centre)) * (1.0 / filter_half)
        start = pl.multiple_of(row * 128, 128)
        vb_ref[pl.ds(start, 128), :] = jnp.broadcast_to(line, (128, 128)).T
        return 0

    lax.fori_loop(0, CELLS // 128, spread_row, 0, unroll=8)


def spread(parcel):
    return pl.pallas_call(
        spread_kernel,
        out_shape=FULL_ROWS,
        compiler_params=params(8),
        cost_estimate=cost(1 << 20, 2 << 20),
        name="spread",
    )(parcel)


def prep_kernel(*refs):
    own_ref, other_ref, corner_ref, vb_ref, s_ref, gg_ref, coef_ref, energy_ref, near_ref, table_ref = refs[:10]
    a1_ref, a1z_ref, a2_ref, a2s_ref = refs[10:]
    upper_x, upper_y = corner_ref[0] > 0, corner_ref[1] > 0
    for slab in range(3):
        own = [own_ref[slab * 48 + j * 24 : slab * 48 + j * 24 + 24, :] for j in range(2)]
        other = [other_ref[slab * 48 + j * 24 : slab * 48 + j * 24 + 24, :] for j in range(2)]
        lower = [jnp.where(upper_x, o, m) for m, o in zip(own, other)]
        higher = [jnp.where(upper_x, m, o) for m, o in zip(own, other)]
        ordered = []
        for pair in (lower, higher):
            ordered += [jnp.where(upper_y, pair[1], pair[0]), jnp.where(upper_y, pair[0], pair[1])]
        for j in range(4):
            near_ref[slab * 96 + j * 24 : slab * 96 + j * 24 + 24, :] = ordered[j]
    blank = jnp.zeros((16, 128), F32)
    for block in range(6):
        rows = near_ref[pl.ds(block, NEAR, stride=6), :]
        table_ref[block * 128 : block * 128 + 128, :] = jnp.concatenate([rows, blank, rows, blank]).T
    at = TAPS + 3 - 640
    energy_ref[...] = jnp.broadcast_to(rows[:, at : at + 1] * (1.0 / filter_half), (NEAR, S))

    shape = (8, 128)
    sub = lax.broadcasted_iota(jnp.int32, shape, 0)
    lane = lax.broadcasted_iota(jnp.int32, shape, 1)
    first_lanes = lane < 64
    sites = [jnp.broadcast_to(table_ref[TAPS + d : TAPS + d + 1, :], shape).astype(jnp.int32) for d in range(3)]
    px = sites[0] - corner_ref[0]
    py = sites[1] - corner_ref[1]
    pz = (sites[2] & 15) + (((lane & 63) >> 4) - 1) * C
    zero = jnp.zeros(shape, F32)

    dz = sub + (lane >> 6) * 8 - pz + R
    z_masks = [dz == t for t in range(W)]
    z_factors = [tap_weight(jnp.abs(dz - t)) for t in range(W)]

    def place_z(ij, _):
        acc = zero
        along = zero
        for t in range(W):
            row = jnp.broadcast_to(table_ref[pl.ds(ij * W + t, 1), :], shape)
            acc = jnp.where(z_masks[t], row, acc)
            along = along + z_factors[t] * row
        a1_ref[ij] = acc
        a1z_ref[ij] = along
        return 0

    lax.fori_loop(0, W * W, place_z, 0, unroll=3)

    def place_y(y, _):
        masks, factors = ring_tables(y - py + R)
        for i in range(W):
            acc = zero
            along = zero
            moved = zero
            for t in range(W):
                value = a1_ref[i * W + t]
                acc = jnp.where(masks[t], value, acc)
                along = along + factors[t] * value
                moved = jnp.where(masks[t], a1z_ref[i * W + t], moved)
            a2_ref[i, y] = acc
            a2s_ref[i, y] = along + moved
        return 0

    lax.fori_loop(0, C, place_y, 0)

    def place_x(x, _):
        masks, factors = ring_tables(x - px + R)

        def per_y(y, _):
            row = pl.multiple_of(x * ROWS + y * C, C)
            acc = zero
            along = zero
            moved = zero
            for t in range(W):
                value = a2_ref[t, y]
                acc = jnp.where(masks[t], value, acc)
                along = along + factors[t] * value
                moved = jnp.where(masks[t], a2s_ref[t, y], moved)
            v = vb_ref[pl.ds(row, C), :]
            moved = along + moved + jnp.where(first_lanes, v[:8], v[8:]) * acc
            lower = jnp.where(first_lanes, acc, pltpu.roll(moved, 64, 1))
            upper = jnp.where(first_lanes, pltpu.roll(acc, 64, 1), moved)
            high, low = split(jnp.concatenate([lower, upper], axis=0))
            gg_ref[0, pl.ds(row, C), :] = high
            gg_ref[1, pl.ds(row, C), :] = low
            return 0

        lax.fori_loop(0, C, per_y, 0, unroll=16)
        return 0

    lax.fori_loop(0, C, place_x, 0)

    coef_ref[...] = jnp.zeros((3, NEAR, S), F32)

    def contract(x, _):
        rows = pl.ds(pl.multiple_of(x * 2 * ROWS, ROWS), 2 * ROWS)
        g_high, g_low = gg_ref[0, rows, :], gg_ref[1, rows, :]
        t_high, t_low = g_high.T, g_low.T
        high, low = split(s_ref[rows, :])
        got = mm(t_high, high) + (mm(t_high, low) + mm(t_low, high))
        t_high, t_low = t_high[:NEAR], t_low[:NEAR]
        pair = mm(t_high, g_high) + (mm(t_high, g_low) + mm(t_low, g_high))
        for slab in range(3):
            rows = slice(slab * C, slab * C + C)
            coef_ref[slab, 0:16] += got[rows]
            coef_ref[slab, 16:32] += got[64 + slab * C : 80 + slab * C]
            coef_ref[slab, 32:48] += pair[rows]
        return 0

    lax.fori_loop(0, C // 2, contract, 0, unroll=2)


def prep(parcels, corner, vb, s):
    vmem = pl.BlockSpec(memory_space=pltpu.VMEM)
    return pl.pallas_call(
        prep_kernel,
        in_specs=[vmem] * 2 + [pl.BlockSpec(memory_space=pltpu.SMEM), vmem, vmem],
        out_shape=[sds((2, CELLS, S), BF16), sds((3, NEAR, S)), sds((NEAR, S))],
        scratch_shapes=[
            pltpu.VMEM((288, 128), F32),
            pltpu.VMEM((768, 128), F32),
            pltpu.VMEM((W * W, 8, 128), F32),
            pltpu.VMEM((W * W, 8, 128), F32),
            pltpu.VMEM((W, C, 8, 128), F32),
            pltpu.VMEM((W, C, 8, 128), F32),
        ],
        compiler_params=params(16),
        cost_estimate=cost(1 << 27, 10 << 20),
        name="prep",
    )(*parcels, corner, vb, s.reshape(CELLS, S))


def move_pair(shares, away):
    lane = lax.broadcasted_iota(jnp.int32, (16, 128), 1)
    keep = (lane < 32) if away < 0 else (lane >= 16) & (lane < 48)
    pair = jnp.where(keep, pltpu.roll(shares[32:48], (away * 16) % 128, 1), 0.0)
    return jnp.concatenate([shares[0:32], pair])


def first_kernel(s_ref, side_ref, vb_ref, *refs):
    inner_ref, odd_ref, part_ref, mate_ref, q_ref, mix_ref, one_ref, two_ref = refs[2:]
    step = pl.program_id(0)

    @pl.when(step == 0)
    def _():
        def shares(head_ref, tail_ref):
            for j in range(2):
                rows = slice(HALO_ROWS + j * NEAR, HALO_ROWS + (j + 1) * NEAR)
                head_ref[rows, :] = part_ref[j] + mate_ref[j]
                tail_ref[rows, :] = part_ref[j + 1] + mate_ref[j + 1]

        by_side(odd_ref, shares, one_ref, two_ref)

    def planes(edge_ref):
        for p in range(N):
            for half in range(2):
                ring = {y: s_ref[p, halves(y, half), :] for y in range(C)}
                for y in range(H):
                    ring[C + y] = edge_ref[p, halves(y, half), :]
                    ring[y - H] = edge_ref[p, halves(H + y, half), :]
                for y in range(C):
                    rows = halves(y, half)
                    dy = tap_sum(lambda i: ring[i], y)
                    q = dy + vb_ref[p, rows, :] * ring[y]
                    q_ref[p, rows, :] = q
                    mix_ref[p, rows, :] = side_ref[p, rows, :] + q + dy

    for_piece(refs[:2], inner_ref, planes)

    def halos(head_ref, tail_ref):
        for p in range(N):
            for z in range(H):
                rows = halo_rows(step * N + p, z)
                head_ref[rows, :] = mix_ref[p, stride_rows(z), :]
                tail_ref[rows, :] = mix_ref[p, stride_rows(C - H + z), :]

    by_side(odd_ref, halos, one_ref, two_ref)


def make_first(s, side_part, vb, edges, inner, odd, part, part_mate):
    shares = pl.BlockSpec((3, NEAR, S), lambda i: (0, 0, 0))
    return pl.pallas_call(
        first_kernel,
        grid=(C // N,),
        in_specs=[plane_spec(ROWS, N)] * 3 + [edge_spec(0), edge_spec(MIDDLE)] + [SCALARS] * 2 + [shares] * 2,
        out_specs=[plane_spec(ROWS, N), plane_spec(ROWS, N), whole(MESSAGE.shape[0]), whole(MESSAGE.shape[0])],
        out_shape=[FULL, FULL, MESSAGE, MESSAGE],
        compiler_params=params(16),
        cost_estimate=cost(1 << 24, 14 << 20),
        name="first",
    )(s, side_part, vb, *edges, inner, odd, part, part_mate)


def base_kernel(s_ref, mid_ref, vb_ref, vb_mate_ref, q_ref, side_ref, part_ref, *refs):
    inner_ref, message_ref, out_ref, middle_ref = refs[2:]
    step = pl.program_id(0)
    inner = inner_ref[0] == 1

    @pl.when(inner)
    def _():
        middle_ref[...] = mid_ref[...]

    @pl.when(jnp.logical_not(inner))
    def _():
        for p in range(N):
            middle_ref[p] = message_ref[pl.ds(pl.multiple_of(MID_START + (step * N + p) * MID, MID), MID), :]

    def planes(edge_ref):
        for p in range(N):
            for half in range(2):

                def other(y, p=p, half=half):
                    if y < H:
                        return edge_ref[p, halves(y, half), :]
                    if y < C - H:
                        return middle_ref[p, halves(y - H, half), :]
                    return edge_ref[p, halves(y - 4, half), :]

                ring = [s_ref[p, halves(y, half), :] for y in range(C)] + [other(y) for y in range(C)]
                q = {y: q_ref[p, halves(y, half), :] for y in range(C)}
                for y in list(range(H)) + list(range(C - H, C)):
                    v = vb_mate_ref[p, halves(y, half), :]
                    q[C + y] = tap_sum(lambda i: ring[i % 32], C + y) + v * ring[C + y]
                for y in range(C):
                    rows = halves(y, half)
                    total = tap_sum(lambda i: q[i % 32], y)
                    total = total + vb_ref[p, rows, :] * (side_ref[p, rows, :] + q[y])
                    out_ref[p, rows, :] = 2.0 * (total + part_ref[p, rows, :]) - ring[y]

    for_piece(refs[:2], inner_ref, planes)


def make_base(s, mid, vb, vb_mate, q, side_part, part, edges, inner):
    return pl.pallas_call(
        base_kernel,
        grid=(C // N,),
        in_specs=[plane_spec(ROWS, N), plane_spec(MID, N)]
        + [plane_spec(ROWS, N)] * 5
        + [edge_spec(0), edge_spec(MIDDLE), SCALARS, whole(C * EDGE)],
        out_specs=plane_spec(ROWS, N),
        out_shape=FULL,
        scratch_shapes=[pltpu.VMEM((N, MID, S), F32)],
        compiler_params=params(16),
        cost_estimate=cost(1 << 25, 16 << 20),
        name="base",
    )(s, mid, vb, vb_mate, q, side_part, part, *edges, inner, edges[0].reshape(-1, S))


def second_kernel(base_ref, two_ref, one_ref, gg_high_ref, gg_low_ref, *rest):
    part_ref, mate_ref, energy_ref, upper_ref, odd_ref, second_ref, keep_ref, give_ref, gram_ref, cross_ref, w_ref, halo_ref = rest
    step = pl.program_id(0)

    @pl.when(step == 0)
    def _():
        gram_ref[...] = jnp.zeros((S, S), F32)
        cross_ref[...] = jnp.zeros((S, S), F32)
        w_ref[...] = jnp.zeros((S, S), F32)
        halo_ref[...] = jnp.zeros((B, ROWS, S), F32)
        mine = [part_ref[j] + mate_ref[j] for j in range(3)]
        odd = odd_ref[0] == 1
        got = [[ref[HALO_ROWS + j * NEAR : HALO_ROWS + (j + 1) * NEAR, :] for j in range(2)] for ref in (one_ref, two_ref)]
        below = [move_pair(jnp.where(odd, a, b), -1) for a, b in zip(*got)]
        above = [move_pair(jnp.where(odd, b, a), 1) for a, b in zip(*got)]
        slabs = [mine[0] + below[0], mine[1] + below[1] + above[0], mine[2] + above[1]]
        near = jnp.concatenate([slab[0:16] for slab in slabs]) * energy_ref[...]
        lane = lax.broadcasted_iota(jnp.int32, (NEAR, S), 1)
        pair = jnp.where(lane < NEAR, jnp.concatenate([slab[32:48] for slab in slabs]), 0.0)
        two = jnp.concatenate([slab[16:32] for slab in slabs])
        two = two + exact(pair, jnp.concatenate([near, jnp.zeros((S - NEAR, S), F32)]))
        w_ref[0:NEAR, :] = 2.0 * energy_ref[...] * two
        w_ref[64 : 64 + NEAR, :] = 2.0 * near

    def halo_part(low_ref, high_ref):
        for p in range(B):
            low = [low_ref[halo_rows(step * B + p, j), :] for j in range(H)]
            high = [high_ref[halo_rows(step * B + p, j), :] for j in range(H)]
            for z in range(H):
                add = sum((2.0 * OFF[k - 1]) * low[z - k + H] for k in range(z + 1, H + 1))
                halo_ref[p, stride_rows(z), :] = add
                add = sum((2.0 * OFF[H + j - z - 1]) * high[j] for j in range(z + 1))
                halo_ref[p, stride_rows(C - H + z), :] = add

    by_side(odd_ref, halo_part, one_ref, two_ref)

    w_high, w_low = split(w_ref[...])
    w_twice = jnp.concatenate([w_high, w_high])
    gram = jnp.zeros((S, 2 * S), F32)
    for p in range(B):
        g_high, g_low = gg_high_ref[0, p], gg_low_ref[0, p]
        near = mm(jnp.concatenate([g_high, g_low], axis=1), w_twice) + mm(g_high, w_low)
        value = base_ref[p] + halo_ref[p] + near
        second_ref[p] = value
        s_high, s_low = split(value)
        gram += mm(s_high.T, jnp.concatenate([s_high, s_low], axis=1))
    gram_ref[...] += gram[:, :S]
    cross_ref[...] += gram[:, S:]

    @pl.when(step == STEPS - 1)
    def _():
        cross = cross_ref[...]
        gram = (gram_ref[...] + (cross + cross.T)) * (1.0 / NCELLS)
        upper = upper_ref[0] == 1
        keep_ref[...] = jnp.where(upper, gram[S // 2 :], gram[: S // 2])
        give_ref[...] = jnp.where(upper, gram[: S // 2], gram[S // 2 :])


def make_second(base, halos, gg, shares, upper, odd):
    three = pl.BlockSpec((3, NEAR, S), lambda i: (0, 0, 0))
    return pl.pallas_call(
        second_kernel,
        grid=(STEPS,),
        in_specs=[plane_spec()]
        + [whole(MESSAGE.shape[0])] * 2
        + [part_spec(0), part_spec(1), three, three, whole(NEAR), SCALARS, SCALARS],
        out_specs=[plane_spec(), whole(S // 2), whole(S // 2)],
        out_shape=[FULL, sds((S // 2, S)), sds((S // 2, S))],
        scratch_shapes=[pltpu.VMEM((S, S), F32)] * 3 + [pltpu.VMEM((B, ROWS, S), F32)],
        compiler_params=params(16),
        cost_estimate=cost(1 << 27, 8 << 20),
        name="second",
    )(base, *halos, gg, gg, *shares, upper, odd)


def exact(a, b):
    return jnp.dot(a, b, precision=lax.Precision.HIGHEST, preferred_element_type=F32)


def close(a, b):
    a_high, a_low = split(a)
    b_high, b_low = split(b)
    return mm(jnp.concatenate([a_high, a_low], axis=1), jnp.concatenate([b_high, b_high])) + mm(a_high, b_low)


def inverse_factor(gram_ref, a_ref, x_ref, state_ref):
    row = lax.broadcasted_iota(jnp.int32, (S, S), 0)
    column = lax.broadcasted_iota(jnp.int32, (S, S), 1)
    unit = jnp.where(row == column, 1.0, 0.0)
    gram = gram_ref[...]
    diagonal = jnp.where(row == column, gram, 0.0)
    down = lax.rsqrt(jnp.sum(diagonal, axis=1, keepdims=True))
    across = lax.rsqrt(jnp.sum(diagonal, axis=0, keepdims=True))
    a_ref[...] = gram * down * across
    x_ref[...] = unit

    def residual():
        x = x_ref[...]
        return unit - close(close(x, a_ref[...]), x.T)

    def size(e):
        return jnp.sum(e * e)

    def improve(e):
        lower = jnp.where(row > column, e, jnp.where(row == column, 0.5 * e, 0.0))
        x_ref[...] += close(lower, x_ref[...])

    state_ref[0] = 0
    start = unit - a_ref[...]
    start_size = size(start)

    @pl.when(start_size < 0.16)
    def _():
        improve(start)
        state_ref[0] = jnp.where(start_size < 1e-6, 2, 1)

    for _ in range(5):

        @pl.when(state_ref[0] == 1)
        def _():
            e = residual()
            e_size = size(e)
            improve(e)
            state_ref[0] = jnp.where(e_size < 1e-6, 2, 1)

    @pl.when(state_ref[0] != 2)
    def _():
        x_ref[...] = unit
        lanes = lax.broadcasted_iota(jnp.int32, (1, S), 1)

        def step(j, _):
            line = a_ref[pl.ds(j, 1), :]
            scale = lax.rsqrt(jnp.sum(jnp.where(lanes == j, line, 0.0), axis=1, keepdims=True))
            a = a_ref[...]
            factor = jnp.sum(jnp.where(column == j, a, 0.0), axis=1, keepdims=True) * scale
            factor = jnp.where(row[:, :1] > j, factor, 0.0)
            x_line = x_ref[pl.ds(j, 1), :] * scale
            a_ref[...] = a - factor * (line * scale)
            x_ref[...] = jnp.where(row == j, x_line, x_ref[...] - factor * x_line)
            return 0

        lax.fori_loop(0, S, step, 0)

    x_ref[...] = x_ref[...] * across


def turn_kernel(second_ref, own_ref, other_ref, upper_ref, out_ref, gram_ref, a_ref, x_ref, i_high_ref, i_low_ref, state_ref):
    @pl.when(pl.program_id(0) == 0)
    def _():
        upper = upper_ref[0] == 1
        gram_ref[: S // 2, :] = jnp.where(upper, other_ref[...], own_ref[...])
        gram_ref[S // 2 :, :] = jnp.where(upper, own_ref[...], other_ref[...])
        inverse_factor(gram_ref, a_ref, x_ref, state_ref)
        i_high, i_low = split(x_ref[...].T)
        i_high_ref[...] = i_high
        i_low_ref[...] = i_low

    i_high, i_low = i_high_ref[...], i_low_ref[...]
    i_twice = jnp.concatenate([i_high, i_high])
    for p in range(B):
        high, low = split(second_ref[p])
        out_ref[p] = mm(jnp.concatenate([high, low], axis=1), i_twice) + mm(high, i_low)


def turn(second, own, other, upper):
    return pl.pallas_call(
        turn_kernel,
        grid=(STEPS,),
        in_specs=[plane_spec(), whole(S // 2), whole(S // 2), SCALARS],
        out_specs=plane_spec(),
        out_shape=FULL,
        scratch_shapes=[pltpu.VMEM((S, S), F32)] * 3 + [pltpu.VMEM((S, S), BF16)] * 2 + [pltpu.SMEM((1,), jnp.int32)],
        compiler_params=params(16),
        cost_estimate=cost(1 << 28, 4 << 20),
        name="turn",
    )(second, own, other, upper)


def per_device(states, potential, atom_sites, projectors, energies):
    gx, gy = lax.axis_index("gx"), lax.axis_index("gy")
    depth = lax.axis_size("gzs")
    count = 4 * depth
    barrier = lax.optimization_barrier

    def send(value, flip):
        return lax.ppermute(value, AXES, [(d, d ^ flip) for d in range(count)])

    over_x, over_y = 2 * depth, depth

    def to_pairs(one, two):
        near = [(d, d ^ 1) for d in range(count)]
        far = [(d, d // depth * depth + (d + (1 if d % 2 else -1)) % depth) for d in range(count)]
        return lax.ppermute(two, AXES, far), lax.ppermute(one, AXES, near)

    inner_ones = [d for d in range(count) if d % 4 in (1, 2)]
    outer_ones = [d for d in range(count) if d % 4 in (0, 3)]
    inner = ((lax.axis_index("gzs") + 1) // 2 % 2).astype(jnp.int32).reshape(1)
    s = states.reshape(C, ROWS, S)
    mate = send(s, over_x)
    corner = jnp.stack([gx * C, gy * C]).astype(jnp.int32)
    upper = gx.astype(jnp.int32).reshape(1)
    odd = (lax.axis_index("gzs") % 2).astype(jnp.int32).reshape(1)
    pot = potential.reshape(32, 128)
    atoms = jnp.concatenate(
        [projectors.reshape(4, TAPS), atom_sites.astype(F32), energies[:, None], jnp.zeros((4, 768 - TAPS - 4), F32)],
        axis=1,
    ).reshape(24, 128)
    pot, corner, upper, inner, odd, atoms = barrier((pot, corner, upper, inner, odd, atoms))
    parcel = stack(atoms, pot)
    to_pack, parcel = barrier((s, parcel))
    parcel_mate = send(parcel, over_y)
    message, relay, mid = pack(to_pack, inner)
    parcel_mate, message, relay = barrier((parcel_mate, message, relay))
    halo_one, halo_two = pack_halos(s, odd, parcel, parcel_mate)
    message = send(message, over_y)
    relayed = lax.ppermute(relay, AXES, [(d, d ^ over_y ^ 1) for d in outer_ones])
    halos = to_pairs(halo_one, halo_two)
    vb = spread(parcel)
    mate, relayed = barrier((mate, relayed))
    beside = side_x(s, mate)
    halos, beside, vb = barrier((halos, beside, vb))
    relayed = lax.ppermute(relayed, AXES, [(d, d ^ 1) for d in inner_ones])
    side_part = side_z(s, beside, halos, odd)
    atoms = column(parcel, parcel_mate, halos, odd)
    atoms, side_part = barrier((atoms, side_part))
    atoms_mate = send(atoms, over_x)
    gg, part, energy = prep([atoms, atoms_mate], corner, vb, s)

    part = part + send(part, over_x)
    part_mate = send(part, over_y)
    edges = [message.reshape(C, EDGE, S), relayed]
    vb = vb.reshape(C, ROWS, S)
    q, mix, halo_one, halo_two = make_first(s, side_part, vb, edges, inner, odd, part, part_mate)
    halos = to_pairs(halo_one, halo_two)
    mate = send(mix, over_x)
    mid, part_mate = barrier((mid, part_mate))
    mid = lax.ppermute(mid, AXES, [(d, d ^ over_y) for d in inner_ones])
    vb_mate = spread(parcel_mate).reshape(C, ROWS, S)
    part_two = side_again(mix, mate)
    base = make_base(s, mid, vb, vb_mate, q, side_part, part_two, edges, inner)
    gg = gg.reshape(2, C, ROWS, S)
    second, own, give = make_second(base, halos, gg, [part, part_mate, energy], upper, odd)

    own = own + send(give, over_x)
    for flip in (32, 36, 1, 3, 8, 24):
        own = own + lax.ppermute(own, AXES, [(d, d ^ flip) for d in range(count)])
    return turn(second, own, send(own, over_x), upper).reshape(C, C, C, S)


def solution(mesh):
    return jax.shard_map(
        per_device,
        mesh=mesh,
        in_specs=(
            P("gx", "gy", "gzs", None),
            P("gx", "gy", "gzs"),
            P(("gx", "gy", "gzs"), None),
            P(("gx", "gy", "gzs"), None, None, None),
            P(("gx", "gy", "gzs")),
        ),
        out_specs=P("gx", "gy", "gzs", None),
        check_vma=False,
    )
```

```python
import math

import jax
import jax.numpy as jnp
from jax import lax
from jax.experimental import pallas as pl
from jax.experimental.pallas import tpu as pltpu
from jax.sharding import PartitionSpec as P

AXES = ("gx", "gy", "gzs")
H = 6
C = 16
ROWS = C * C
CELLS = C * C * C
NCELLS = 32 * 32 * 512
S = 128
W = 9
R = 4
NEAR = 48
TAPS = W * W * W
F32 = jnp.float32
BF16 = jnp.bfloat16

grid_step = 0.6
filter_centre = 36.0
filter_half = 26.0


def weights():
    taps = []
    for k in range(1, 7):
        top = 2.0 * (-1) ** (k + 1) * math.factorial(6) ** 2
        under = k * k * math.factorial(6 - k) * math.factorial(6 + k)
        taps.append(top / under)
    scale = -0.5 / (grid_step * grid_step)
    off = [scale * t / filter_half for t in taps]
    diagonal = 3.0 * scale * (-2.0 * sum(taps))
    return off, diagonal


OFF, DIAGONAL = weights()


def params(mib):
    return pltpu.CompilerParams(vmem_limit_bytes=mib * 1024 * 1024)


def cost(flops, nbytes):
    return pl.CostEstimate(flops=flops, bytes_accessed=nbytes, transcendentals=0)


def sds(shape, dtype=F32):
    return jax.ShapeDtypeStruct(shape, dtype)


def split(value):
    high = value.astype(BF16)
    low = (value - high.astype(F32)).astype(BF16)
    return high, low


def mm(a, b):
    return jnp.dot(a, b, preferred_element_type=F32)


def tap_sum(at, index):
    total = None
    for k in range(1, 7):
        term = OFF[k - 1] * (at(index + k) + at(index - k))
        total = term if total is None else total + term
    return total


B = 8
STEPS = C // B
N = 2
MIDDLE = 10
EDGE = 192
MID = 64
MID_START = MIDDLE * EDGE


def stride_rows(z):
    return pl.ds(z, C, stride=C)


def plane_spec(rows=ROWS, planes=B):
    return pl.BlockSpec((planes, rows, S), lambda i: (i, 0, 0))


def halo_spec(planes=B):
    return pl.BlockSpec((H, planes, C, S), lambda i: (0, i, 0, 0))


def part_spec(part):
    return pl.BlockSpec((1, B, ROWS, S), lambda i: (part, i, 0, 0))


def whole(rows=S):
    return pl.BlockSpec((rows, S), lambda i: (0, 0))


def edge_spec(start):
    return pl.BlockSpec((N, EDGE, S), lambda i: (jnp.maximum(i - start // N, 0), 0, 0))


def for_piece(edges, inner_ref, body):
    direct = (inner_ref[0] == 1) | (pl.program_id(0) < MIDDLE // N)

    @pl.when(direct)
    def _():
        body(edges[0])

    @pl.when(jnp.logical_not(direct))
    def _():
        body(edges[1])


SCALARS = pl.BlockSpec(memory_space=pltpu.SMEM)
FULL = sds((C, ROWS, S))
FULL_ROWS = sds((CELLS, S))
HALO_ROWS = H * ROWS
MESSAGE = sds((HALO_ROWS + 2 * NEAR, S))
ATOM_ROWS = 24
HALO = sds((HALO_ROWS + 2 * ATOM_ROWS, S))
DIRECT = sds((C * EDGE, S))
RELAY = sds((C - MIDDLE, EDGE, S))


def halo_rows(x, z):
    return pl.ds(pl.multiple_of(z * ROWS + x * C, C), C)


def halves(y, half):
    return slice(y * C + half * 8, y * C + half * 8 + 8)


def pack_edges(s_ref, out_ref):
    out_ref[:, 0:96, :] = s_ref[:, 0:96, :]
    out_ref[:, 96:192, :] = s_ref[:, 160:256, :]


def by_side(odd_ref, body, one, two):
    odd = odd_ref[0] == 1

    @pl.when(odd)
    def _():
        body(one, two)

    @pl.when(jnp.logical_not(odd))
    def _():
        body(two, one)


def pack_kernel(s_ref, inner_ref, message_ref, relay_ref, mid_ref):
    step = pl.program_id(0)
    inner = inner_ref[0] == 1
    mid_ref[...] = s_ref[:, 96:160, :]

    @pl.when(step >= MIDDLE // N)
    def _():
        pack_edges(s_ref, relay_ref)

    @pl.when(inner | (step < MIDDLE // N))
    def _():
        for p in range(N):
            row = pl.multiple_of((step * N + p) * EDGE, MID)
            message_ref[pl.ds(row, 96), :] = s_ref[p, 0:96, :]
            message_ref[pl.ds(row + 96, 96), :] = s_ref[p, 160:256, :]

    @pl.when(jnp.logical_not(inner))
    def _():
        for p in range(N):
            row = pl.multiple_of(MID_START + (step * N + p) * MID, MID)
            message_ref[pl.ds(row, MID), :] = s_ref[p, 96:160, :]


def pack(s, inner):
    return pl.pallas_call(
        pack_kernel,
        grid=(C // N,),
        in_specs=[plane_spec(ROWS, N), SCALARS],
        out_specs=[whole(C * EDGE), edge_spec(MIDDLE), plane_spec(MID, N)],
        out_shape=[DIRECT, RELAY, sds((C, MID, S))],
        compiler_params=params(12),
        cost_estimate=cost(1 << 31, 6 << 20),
        name="pack",
    )(s, inner)


def pack_halos_kernel(s_ref, odd_ref, own_ref, other_ref, one_ref, two_ref):
    step = pl.program_id(0)

    @pl.when(step == 0)
    def _():
        for ref in (one_ref, two_ref):
            ref[HALO_ROWS : HALO_ROWS + ATOM_ROWS, :] = own_ref[:ATOM_ROWS, :]
            ref[HALO_ROWS + ATOM_ROWS :, :] = other_ref[:ATOM_ROWS, :]

    def halos(head_ref, tail_ref):
        for p in range(B):
            for z in range(H):
                rows = halo_rows(step * B + p, z)
                head_ref[rows, :] = s_ref[p, stride_rows(z), :]
                tail_ref[rows, :] = s_ref[p, stride_rows(C - H + z), :]

    by_side(odd_ref, halos, one_ref, two_ref)


def pack_halos(s, odd, parcel, parcel_mate):
    return pl.pallas_call(
        pack_halos_kernel,
        grid=(STEPS,),
        in_specs=[plane_spec(), SCALARS, whole(56), whole(56)],
        out_specs=[whole(HALO.shape[0])] * 2,
        out_shape=[HALO, HALO],
        compiler_params=params(12),
        cost_estimate=cost(1 << 20, 4 << 20),
        name="pack_halos",
    )(s, odd, parcel, parcel_mate)


def stack_kernel(shape_ref, pot_ref, sites_ref, energies_ref, out_ref, row_ref):
    row_ref[...] = jnp.zeros((4, 768), F32)
    row_ref[:, :TAPS] = shape_ref[...]
    lane = lax.broadcasted_iota(jnp.int32, (1, S), 1) + 5 * S
    for atom in range(4):
        for block in range(6):
            row = row_ref[atom : atom + 1, block * S : block * S + S]
            if block == 5:
                for d in range(3):
                    row = jnp.where(lane == TAPS + d, sites_ref[atom, d].astype(F32), row)
                row = jnp.where(lane == TAPS + 3, energies_ref[atom], row)
            out_ref[atom * 6 + block : atom * 6 + block + 1, :] = row
    out_ref[24:56, :] = pot_ref[...]


def stack(shapes, pot, sites, energies):
    vmem = pl.BlockSpec(memory_space=pltpu.VMEM)
    return pl.pallas_call(
        stack_kernel,
        in_specs=[vmem, vmem, SCALARS, SCALARS],
        out_shape=sds((56, S)),
        scratch_shapes=[pltpu.VMEM((4, 768), F32)],
        compiler_params=params(4),
        name="stack",
    )(shapes, pot, sites, energies)


def column_kernel(own_ref, other_ref, one_ref, two_ref, odd_ref, out_ref):
    def beside(below_ref, above_ref):
        out_ref[0:48, :] = below_ref[HALO_ROWS:, :]
        out_ref[96:144, :] = above_ref[HALO_ROWS:, :]

    by_side(odd_ref, beside, one_ref, two_ref)
    out_ref[48:72, :] = own_ref[:ATOM_ROWS, :]
    out_ref[72:96, :] = other_ref[:ATOM_ROWS, :]


def column(own, other, halos, odd):
    return pl.pallas_call(
        column_kernel,
        in_specs=[pl.BlockSpec(memory_space=pltpu.VMEM)] * 4 + [SCALARS],
        out_shape=sds((144, S)),
        compiler_params=params(8),
        name="column",
    )(own, other, *halos, odd)


def along_x(s_ref, mate_ref, out_ref, add):
    def column(block, _):
        rows = pl.ds(pl.multiple_of(block * 8, 8), 8)
        ring = [mate_ref[C - H + i, rows, :] for i in range(H)]
        ring += [s_ref[x, rows, :] for x in range(C)]
        ring += [mate_ref[i, rows, :] for i in range(H)]
        for x in range(C):
            value = tap_sum(lambda i: ring[H + i], x)
            if add:
                value = value + out_ref[x, rows, :]
            out_ref[x, rows, :] = value
        return 0

    lax.fori_loop(0, ROWS // 8, column, 0)


def z_taps(ext_ref, y):
    return tap_sum(lambda k: ext_ref[y * 32 + 8 + k : y * 32 + 24 + k, :], 0)


def side_x_kernel(s_ref, mate_ref, out_ref):
    along_x(s_ref, mate_ref, out_ref, False)


def side_x(s, mate):
    return pl.pallas_call(
        side_x_kernel,
        out_shape=FULL,
        compiler_params=params(12),
        cost_estimate=cost(1 << 24, 6 << 20),
        name="side_x",
    )(s, mate)


def side_z_kernel(s_ref, part_ref, one_ref, two_ref, odd_ref, out_ref, ext_ref):
    def planes(low_ref, high_ref):
        def plane(x, _):
            for y in range(C):
                ext_ref[y * 32 + 8 : y * 32 + 24, :] = s_ref[x, y * C : (y + 1) * C, :]
            for z in range(H):
                ext_ref[pl.ds(2 + z, C, stride=32), :] = low_ref[halo_rows(x, z), :]
                ext_ref[pl.ds(24 + z, C, stride=32), :] = high_ref[halo_rows(x, z), :]
            for y in range(C):
                rows = slice(y * C, (y + 1) * C)
                out_ref[x, rows, :] = part_ref[x, rows, :] + z_taps(ext_ref, y)
            return 0

        lax.fori_loop(0, C, plane, 0)

    by_side(odd_ref, planes, one_ref, two_ref)


def side_z(s, part, halos, odd):
    return pl.pallas_call(
        side_z_kernel,
        in_specs=[pl.BlockSpec(memory_space=pltpu.VMEM)] * 4 + [SCALARS],
        out_shape=FULL,
        scratch_shapes=[pltpu.VMEM((C * 32, S), F32)],
        compiler_params=params(14),
        cost_estimate=cost(1 << 24, 8 << 20),
        name="side_z",
    )(s, part, *halos, odd)


def side_again_kernel(s_ref, mate_ref, out_ref, ext_ref):
    for y in range(C):
        ext_ref[y * 32 : y * 32 + 8, :] = jnp.zeros((8, S), F32)
        ext_ref[y * 32 + 24 : y * 32 + 32, :] = jnp.zeros((8, S), F32)

    def plane(x, _):
        for y in range(C):
            ext_ref[y * 32 + 8 : y * 32 + 24, :] = s_ref[x, y * C : (y + 1) * C, :]
        for y in range(C):
            out_ref[x, y * C : (y + 1) * C, :] = z_taps(ext_ref, y)
        return 0

    lax.fori_loop(0, C, plane, 0)
    along_x(s_ref, mate_ref, out_ref, True)


def side_again(s, mate):
    return pl.pallas_call(
        side_again_kernel,
        out_shape=FULL,
        scratch_shapes=[pltpu.VMEM((C * 32, S), F32)],
        compiler_params=params(12),
        cost_estimate=cost(1 << 25, 6 << 20),
        name="side_again",
    )(s, mate)


def tap_weight(distance):
    value = jnp.zeros(distance.shape, F32)
    for k in range(1, 7):
        value = jnp.where(distance == k, OFF[k - 1], value)
    return value


def ring_tables(coordinate):
    masks, factors = [], []
    for t in range(W):
        away = (coordinate - t) & 31
        masks.append(away == 0)
        factors.append(tap_weight(jnp.minimum(away, 32 - away)))
    return masks, factors


def spread_kernel(parcel_ref, vb_ref):
    def spread_row(row, _):
        line = (parcel_ref[pl.ds(24 + row, 1), :] + (DIAGONAL - filter_centre)) * (1.0 / filter_half)
        start = pl.multiple_of(row * 128, 128)
        vb_ref[pl.ds(start, 128), :] = jnp.broadcast_to(line, (128, 128)).T
        return 0

    lax.fori_loop(0, CELLS // 128, spread_row, 0, unroll=8)


def spread(parcel):
    return pl.pallas_call(
        spread_kernel,
        out_shape=FULL_ROWS,
        compiler_params=params(8),
        cost_estimate=cost(1 << 20, 2 << 20),
        name="spread",
    )(parcel)


def prep_kernel(*refs):
    own_ref, other_ref, corner_ref, vb_ref, s_ref, gg_ref, coef_ref, energy_ref, near_ref, table_ref = refs[:10]
    a1_ref, a1z_ref, a2_ref, a2s_ref = refs[10:]
    upper_x, upper_y = corner_ref[0] > 0, corner_ref[1] > 0
    for slab in range(3):
        own = [own_ref[slab * 48 + j * 24 : slab * 48 + j * 24 + 24, :] for j in range(2)]
        other = [other_ref[slab * 48 + j * 24 : slab * 48 + j * 24 + 24, :] for j in range(2)]
        lower = [jnp.where(upper_x, o, m) for m, o in zip(own, other)]
        higher = [jnp.where(upper_x, m, o) for m, o in zip(own, other)]
        ordered = []
        for pair in (lower, higher):
            ordered += [jnp.where(upper_y, pair[1], pair[0]), jnp.where(upper_y, pair[0], pair[1])]
        for j in range(4):
            near_ref[slab * 96 + j * 24 : slab * 96 + j * 24 + 24, :] = ordered[j]
    blank = jnp.zeros((16, 128), F32)
    for block in range(6):
        rows = near_ref[pl.ds(block, NEAR, stride=6), :]
        table_ref[block * 128 : block * 128 + 128, :] = jnp.concatenate([rows, blank, rows, blank]).T
    at = TAPS + 3 - 640
    energy_ref[...] = jnp.broadcast_to(rows[:, at : at + 1] * (1.0 / filter_half), (NEAR, S))

    shape = (8, 128)
    sub = lax.broadcasted_iota(jnp.int32, shape, 0)
    lane = lax.broadcasted_iota(jnp.int32, shape, 1)
    first_lanes = lane < 64
    sites = [jnp.broadcast_to(table_ref[TAPS + d : TAPS + d + 1, :], shape).astype(jnp.int32) for d in range(3)]
    px = sites[0] - corner_ref[0]
    py = sites[1] - corner_ref[1]
    pz = (sites[2] & 15) + (((lane & 63) >> 4) - 1) * C
    zero = jnp.zeros(shape, F32)

    dz = sub + (lane >> 6) * 8 - pz + R
    z_masks = [dz == t for t in range(W)]
    z_factors = [tap_weight(jnp.abs(dz - t)) for t in range(W)]

    def place_z(ij, _):
        acc = zero
        along = zero
        for t in range(W):
            row = jnp.broadcast_to(table_ref[pl.ds(ij * W + t, 1), :], shape)
            acc = jnp.where(z_masks[t], row, acc)
            along = along + z_factors[t] * row
        a1_ref[ij] = acc
        a1z_ref[ij] = along
        return 0

    lax.fori_loop(0, W * W, place_z, 0, unroll=3)

    def place_y(y, _):
        masks, factors = ring_tables(y - py + R)
        for i in range(W):
            acc = zero
            along = zero
            moved = zero
            for t in range(W):
                value = a1_ref[i * W + t]
                acc = jnp.where(masks[t], value, acc)
                along = along + factors[t] * value
                moved = jnp.where(masks[t], a1z_ref[i * W + t], moved)
            a2_ref[i, y] = acc
            a2s_ref[i, y] = along + moved
        return 0

    lax.fori_loop(0, C, place_y, 0)

    def place_x(x, _):
        masks, factors = ring_tables(x - px + R)

        def per_y(y, _):
            row = pl.multiple_of(x * ROWS + y * C, C)
            acc = zero
            along = zero
            moved = zero
            for t in range(W):
                value = a2_ref[t, y]
                acc = jnp.where(masks[t], value, acc)
                along = along + factors[t] * value
                moved = jnp.where(masks[t], a2s_ref[t, y], moved)
            v = vb_ref[pl.ds(row, C), :]
            moved = along + moved + jnp.where(first_lanes, v[:8], v[8:]) * acc
            lower = jnp.where(first_lanes, acc, pltpu.roll(moved, 64, 1))
            upper = jnp.where(first_lanes, pltpu.roll(acc, 64, 1), moved)
            high, low = split(jnp.concatenate([lower, upper], axis=0))
            gg_ref[0, pl.ds(row, C), :] = high
            gg_ref[1, pl.ds(row, C), :] = low
            return 0

        lax.fori_loop(0, C, per_y, 0, unroll=16)
        return 0

    lax.fori_loop(0, C, place_x, 0)

    coef_ref[...] = jnp.zeros((3, NEAR, S), F32)

    def contract(x, _):
        rows = pl.ds(pl.multiple_of(x * 2 * ROWS, ROWS), 2 * ROWS)
        g_high, g_low = gg_ref[0, rows, :], gg_ref[1, rows, :]
        t_high, t_low = g_high.T, g_low.T
        high, low = split(s_ref[rows, :])
        got = mm(t_high, high) + (mm(t_high, low) + mm(t_low, high))
        t_high, t_low = t_high[:NEAR], t_low[:NEAR]
        pair = mm(t_high, g_high) + (mm(t_high, g_low) + mm(t_low, g_high))
        for slab in range(3):
            rows = slice(slab * C, slab * C + C)
            coef_ref[slab, 0:16] += got[rows]
            coef_ref[slab, 16:32] += got[64 + slab * C : 80 + slab * C]
            coef_ref[slab, 32:48] += pair[rows]
        return 0

    lax.fori_loop(0, C // 2, contract, 0, unroll=2)


def prep(parcels, corner, vb, s):
    vmem = pl.BlockSpec(memory_space=pltpu.VMEM)
    return pl.pallas_call(
        prep_kernel,
        in_specs=[vmem] * 2 + [pl.BlockSpec(memory_space=pltpu.SMEM), vmem, vmem],
        out_shape=[sds((2, CELLS, S), BF16), sds((3, NEAR, S)), sds((NEAR, S))],
        scratch_shapes=[
            pltpu.VMEM((288, 128), F32),
            pltpu.VMEM((768, 128), F32),
            pltpu.VMEM((W * W, 8, 128), F32),
            pltpu.VMEM((W * W, 8, 128), F32),
            pltpu.VMEM((W, C, 8, 128), F32),
            pltpu.VMEM((W, C, 8, 128), F32),
        ],
        compiler_params=params(16),
        cost_estimate=cost(1 << 27, 10 << 20),
        name="prep",
    )(*parcels, corner, vb, s.reshape(CELLS, S))


def move_pair(shares, away):
    lane = lax.broadcasted_iota(jnp.int32, (16, 128), 1)
    keep = (lane < 32) if away < 0 else (lane >= 16) & (lane < 48)
    pair = jnp.where(keep, pltpu.roll(shares[32:48], (away * 16) % 128, 1), 0.0)
    return jnp.concatenate([shares[0:32], pair])


def first_kernel(s_ref, side_ref, vb_ref, *refs):
    inner_ref, odd_ref, part_ref, mate_ref, q_ref, mix_ref, one_ref, two_ref = refs[2:]
    step = pl.program_id(0)

    @pl.when(step == 0)
    def _():
        def shares(head_ref, tail_ref):
            for j in range(2):
                rows = slice(HALO_ROWS + j * NEAR, HALO_ROWS + (j + 1) * NEAR)
                head_ref[rows, :] = part_ref[j] + mate_ref[j]
                tail_ref[rows, :] = part_ref[j + 1] + mate_ref[j + 1]

        by_side(odd_ref, shares, one_ref, two_ref)

    def planes(edge_ref):
        for p in range(N):
            for half in range(2):
                ring = {y: s_ref[p, halves(y, half), :] for y in range(C)}
                for y in range(H):
                    ring[C + y] = edge_ref[p, halves(y, half), :]
                    ring[y - H] = edge_ref[p, halves(H + y, half), :]
                for y in range(C):
                    rows = halves(y, half)
                    dy = tap_sum(lambda i: ring[i], y)
                    q = dy + vb_ref[p, rows, :] * ring[y]
                    q_ref[p, rows, :] = q
                    mix_ref[p, rows, :] = side_ref[p, rows, :] + q + dy

    for_piece(refs[:2], inner_ref, planes)

    def halos(head_ref, tail_ref):
        for p in range(N):
            for z in range(H):
                rows = halo_rows(step * N + p, z)
                head_ref[rows, :] = mix_ref[p, stride_rows(z), :]
                tail_ref[rows, :] = mix_ref[p, stride_rows(C - H + z), :]

    by_side(odd_ref, halos, one_ref, two_ref)


def make_first(s, side_part, vb, edges, inner, odd, part, part_mate):
    shares = pl.BlockSpec((3, NEAR, S), lambda i: (0, 0, 0))
    return pl.pallas_call(
        first_kernel,
        grid=(C // N,),
        in_specs=[plane_spec(ROWS, N)] * 3 + [edge_spec(0), edge_spec(MIDDLE)] + [SCALARS] * 2 + [shares] * 2,
        out_specs=[plane_spec(ROWS, N), plane_spec(ROWS, N), whole(MESSAGE.shape[0]), whole(MESSAGE.shape[0])],
        out_shape=[FULL, FULL, MESSAGE, MESSAGE],
        compiler_params=params(16),
        cost_estimate=cost(1 << 24, 14 << 20),
        name="first",
    )(s, side_part, vb, *edges, inner, odd, part, part_mate)


def base_kernel(s_ref, mid_ref, vb_ref, vb_mate_ref, q_ref, side_ref, part_ref, *refs):
    inner_ref, message_ref, out_ref, middle_ref = refs[2:]
    step = pl.program_id(0)
    inner = inner_ref[0] == 1

    @pl.when(inner)
    def _():
        middle_ref[...] = mid_ref[...]

    @pl.when(jnp.logical_not(inner))
    def _():
        for p in range(N):
            middle_ref[p] = message_ref[pl.ds(pl.multiple_of(MID_START + (step * N + p) * MID, MID), MID), :]

    def planes(edge_ref):
        for p in range(N):
            for half in range(2):

                def other(y, p=p, half=half):
                    if y < H:
                        return edge_ref[p, halves(y, half), :]
                    if y < C - H:
                        return middle_ref[p, halves(y - H, half), :]
                    return edge_ref[p, halves(y - 4, half), :]

                ring = [s_ref[p, halves(y, half), :] for y in range(C)] + [other(y) for y in range(C)]
                q = {y: q_ref[p, halves(y, half), :] for y in range(C)}
                for y in list(range(H)) + list(range(C - H, C)):
                    v = vb_mate_ref[p, halves(y, half), :]
                    q[C + y] = tap_sum(lambda i: ring[i % 32], C + y) + v * ring[C + y]
                for y in range(C):
                    rows = halves(y, half)
                    total = tap_sum(lambda i: q[i % 32], y)
                    total = total + vb_ref[p, rows, :] * (side_ref[p, rows, :] + q[y])
                    out_ref[p, rows, :] = 2.0 * (total + part_ref[p, rows, :]) - ring[y]

    for_piece(refs[:2], inner_ref, planes)


def make_base(s, mid, vb, vb_mate, q, side_part, part, edges, inner):
    return pl.pallas_call(
        base_kernel,
        grid=(C // N,),
        in_specs=[plane_spec(ROWS, N), plane_spec(MID, N)]
        + [plane_spec(ROWS, N)] * 5
        + [edge_spec(0), edge_spec(MIDDLE), SCALARS, whole(C * EDGE)],
        out_specs=plane_spec(ROWS, N),
        out_shape=FULL,
        scratch_shapes=[pltpu.VMEM((N, MID, S), F32)],
        compiler_params=params(16),
        cost_estimate=cost(1 << 25, 16 << 20),
        name="base",
    )(s, mid, vb, vb_mate, q, side_part, part, *edges, inner, edges[0].reshape(-1, S))


def second_kernel(base_ref, one_ref, two_ref, gg_high_ref, gg_low_ref, *rest):
    part_ref, mate_ref, energy_ref, upper_ref, odd_ref, second_ref, keep_ref, give_ref, gram_ref, cross_ref, w_ref, halo_ref = rest
    step = pl.program_id(0)

    @pl.when(step == 0)
    def _():
        gram_ref[...] = jnp.zeros((S, S), F32)
        cross_ref[...] = jnp.zeros((S, S), F32)
        w_ref[...] = jnp.zeros((S, S), F32)
        halo_ref[...] = jnp.zeros((B, ROWS, S), F32)
        mine = [part_ref[j] + mate_ref[j] for j in range(3)]
        odd = odd_ref[0] == 1
        got = [[ref[HALO_ROWS + j * NEAR : HALO_ROWS + (j + 1) * NEAR, :] for j in range(2)] for ref in (one_ref, two_ref)]
        below = [move_pair(jnp.where(odd, a, b), -1) for a, b in zip(*got)]
        above = [move_pair(jnp.where(odd, b, a), 1) for a, b in zip(*got)]
        slabs = [mine[0] + below[0], mine[1] + below[1] + above[0], mine[2] + above[1]]
        near = jnp.concatenate([slab[0:16] for slab in slabs]) * energy_ref[...]
        lane = lax.broadcasted_iota(jnp.int32, (NEAR, S), 1)
        pair = jnp.where(lane < NEAR, jnp.concatenate([slab[32:48] for slab in slabs]), 0.0)
        two = jnp.concatenate([slab[16:32] for slab in slabs])
        two = two + exact(pair, jnp.concatenate([near, jnp.zeros((S - NEAR, S), F32)]))
        w_ref[0:NEAR, :] = 2.0 * energy_ref[...] * two
        w_ref[64 : 64 + NEAR, :] = 2.0 * near

    def halo_part(low_ref, high_ref):
        for p in range(B):
            low = [low_ref[halo_rows(step * B + p, j), :] for j in range(H)]
            high = [high_ref[halo_rows(step * B + p, j), :] for j in range(H)]
            for z in range(H):
                add = sum((2.0 * OFF[k - 1]) * low[z - k + H] for k in range(z + 1, H + 1))
                halo_ref[p, stride_rows(z), :] = add
                add = sum((2.0 * OFF[H + j - z - 1]) * high[j] for j in range(z + 1))
                halo_ref[p, stride_rows(C - H + z), :] = add

    by_side(odd_ref, halo_part, one_ref, two_ref)

    w_high, w_low = split(w_ref[...])
    w_twice = jnp.concatenate([w_high, w_high])
    gram = jnp.zeros((S, 2 * S), F32)
    for p in range(B):
        g_high, g_low = gg_high_ref[0, p], gg_low_ref[0, p]
        near = mm(jnp.concatenate([g_high, g_low], axis=1), w_twice) + mm(g_high, w_low)
        value = base_ref[p] + halo_ref[p] + near
        second_ref[p] = value
        s_high, s_low = split(value)
        gram += mm(s_high.T, jnp.concatenate([s_high, s_low], axis=1))
    gram_ref[...] += gram[:, :S]
    cross_ref[...] += gram[:, S:]

    @pl.when(step == STEPS - 1)
    def _():
        cross = cross_ref[...]
        gram = (gram_ref[...] + (cross + cross.T)) * (1.0 / NCELLS)
        upper = upper_ref[0] == 1
        keep_ref[...] = jnp.where(upper, gram[S // 2 :], gram[: S // 2])
        give_ref[...] = jnp.where(upper, gram[: S // 2], gram[S // 2 :])


def make_second(base, halos, gg, shares, upper, odd):
    three = pl.BlockSpec((3, NEAR, S), lambda i: (0, 0, 0))
    return pl.pallas_call(
        second_kernel,
        grid=(STEPS,),
        in_specs=[plane_spec()]
        + [whole(MESSAGE.shape[0])] * 2
        + [part_spec(0), part_spec(1), three, three, whole(NEAR), SCALARS, SCALARS],
        out_specs=[plane_spec(), whole(S // 2), whole(S // 2)],
        out_shape=[FULL, sds((S // 2, S)), sds((S // 2, S))],
        scratch_shapes=[pltpu.VMEM((S, S), F32)] * 3 + [pltpu.VMEM((B, ROWS, S), F32)],
        compiler_params=params(16),
        cost_estimate=cost(1 << 27, 8 << 20),
        name="second",
    )(base, *halos, gg, gg, *shares, upper, odd)


def exact(a, b):
    return jnp.dot(a, b, precision=lax.Precision.HIGHEST, preferred_element_type=F32)


def close(a, b):
    a_high, a_low = split(a)
    b_high, b_low = split(b)
    return mm(jnp.concatenate([a_high, a_low], axis=1), jnp.concatenate([b_high, b_high])) + mm(a_high, b_low)


def inverse_factor(gram_ref, a_ref, x_ref, state_ref):
    row = lax.broadcasted_iota(jnp.int32, (S, S), 0)
    column = lax.broadcasted_iota(jnp.int32, (S, S), 1)
    unit = jnp.where(row == column, 1.0, 0.0)
    gram = gram_ref[...]
    diagonal = jnp.where(row == column, gram, 0.0)
    down = lax.rsqrt(jnp.sum(diagonal, axis=1, keepdims=True))
    across = lax.rsqrt(jnp.sum(diagonal, axis=0, keepdims=True))
    a_ref[...] = gram * down * across
    x_ref[...] = unit

    def residual():
        x = x_ref[...]
        return unit - close(close(x, a_ref[...]), x.T)

    def size(e):
        return jnp.sum(e * e)

    def improve(e):
        lower = jnp.where(row > column, e, jnp.where(row == column, 0.5 * e, 0.0))
        x_ref[...] += close(lower, x_ref[...])

    state_ref[0] = 0
    start = unit - a_ref[...]
    start_size = size(start)

    @pl.when(start_size < 0.16)
    def _():
        improve(start)
        state_ref[0] = jnp.where(start_size < 1e-6, 2, 1)

    for _ in range(5):

        @pl.when(state_ref[0] == 1)
        def _():
            e = residual()
            e_size = size(e)
            improve(e)
            state_ref[0] = jnp.where(e_size < 1e-6, 2, 1)

    @pl.when(state_ref[0] != 2)
    def _():
        x_ref[...] = unit
        lanes = lax.broadcasted_iota(jnp.int32, (1, S), 1)

        def step(j, _):
            line = a_ref[pl.ds(j, 1), :]
            scale = lax.rsqrt(jnp.sum(jnp.where(lanes == j, line, 0.0), axis=1, keepdims=True))
            a = a_ref[...]
            factor = jnp.sum(jnp.where(column == j, a, 0.0), axis=1, keepdims=True) * scale
            factor = jnp.where(row[:, :1] > j, factor, 0.0)
            x_line = x_ref[pl.ds(j, 1), :] * scale
            a_ref[...] = a - factor * (line * scale)
            x_ref[...] = jnp.where(row == j, x_line, x_ref[...] - factor * x_line)
            return 0

        lax.fori_loop(0, S, step, 0)

    x_ref[...] = x_ref[...] * across


def turn_kernel(second_ref, own_ref, other_ref, upper_ref, out_ref, gram_ref, a_ref, x_ref, i_high_ref, i_low_ref, state_ref):
    @pl.when(pl.program_id(0) == 0)
    def _():
        upper = upper_ref[0] == 1
        gram_ref[: S // 2, :] = jnp.where(upper, other_ref[...], own_ref[...])
        gram_ref[S // 2 :, :] = jnp.where(upper, own_ref[...], other_ref[...])
        inverse_factor(gram_ref, a_ref, x_ref, state_ref)
        i_high, i_low = split(x_ref[...].T)
        i_high_ref[...] = i_high
        i_low_ref[...] = i_low

    i_high, i_low = i_high_ref[...], i_low_ref[...]
    i_twice = jnp.concatenate([i_high, i_high])
    for p in range(B):
        high, low = split(second_ref[p])
        out_ref[p] = mm(jnp.concatenate([high, low], axis=1), i_twice) + mm(high, i_low)


def turn(second, own, other, upper):
    return pl.pallas_call(
        turn_kernel,
        grid=(STEPS,),
        in_specs=[plane_spec(), whole(S // 2), whole(S // 2), SCALARS],
        out_specs=plane_spec(),
        out_shape=FULL,
        scratch_shapes=[pltpu.VMEM((S, S), F32)] * 3 + [pltpu.VMEM((S, S), BF16)] * 2 + [pltpu.SMEM((1,), jnp.int32)],
        compiler_params=params(16),
        cost_estimate=cost(1 << 28, 4 << 20),
        name="turn",
    )(second, own, other, upper)


def per_device(states, potential, atom_sites, projectors, energies):
    gx, gy = lax.axis_index("gx"), lax.axis_index("gy")
    depth = lax.axis_size("gzs")
    count = 4 * depth
    barrier = lax.optimization_barrier

    def send(value, flip):
        return lax.ppermute(value, AXES, [(d, d ^ flip) for d in range(count)])

    over_x, over_y = 2 * depth, depth

    def to_pairs(one, two):
        near = [(d, d ^ 1) for d in range(count)]
        far = [(d, d // depth * depth + (d + (1 if d % 2 else -1)) % depth) for d in range(count)]
        return lax.ppermute(one, AXES, near), lax.ppermute(two, AXES, far)

    inner_ones = [d for d in range(count) if d % 4 in (1, 2)]
    outer_ones = [d for d in range(count) if d % 4 in (0, 3)]
    inner = ((lax.axis_index("gzs") + 1) // 2 % 2).astype(jnp.int32).reshape(1)
    s = states.reshape(C, ROWS, S)
    mate = send(s, over_x)
    corner = jnp.stack([gx * C, gy * C]).astype(jnp.int32)
    upper = gx.astype(jnp.int32).reshape(1)
    odd = (lax.axis_index("gzs") % 2).astype(jnp.int32).reshape(1)
    pot = potential.reshape(32, 128)
    shapes = projectors.reshape(4, TAPS)
    pot, corner, upper, inner, odd, shapes = barrier((pot, corner, upper, inner, odd, shapes))
    parcel = stack(shapes, pot, atom_sites, energies)
    to_pack, parcel = barrier((s, parcel))
    parcel_mate = send(parcel, over_y)
    message, relay, mid = pack(to_pack, inner)
    parcel_mate, message, relay = barrier((parcel_mate, message, relay))
    halo_one, halo_two = pack_halos(s, odd, parcel, parcel_mate)
    message = send(message, over_y)
    relayed = lax.ppermute(relay, AXES, [(d, d ^ over_y ^ 1) for d in outer_ones])
    halos = to_pairs(halo_one, halo_two)
    vb = spread(parcel)
    mate, relayed = barrier((mate, relayed))
    beside = side_x(s, mate)
    halos, beside, vb = barrier((halos, beside, vb))
    relayed = lax.ppermute(relayed, AXES, [(d, d ^ 1) for d in inner_ones])
    side_part = side_z(s, beside, halos, odd)
    atoms = column(parcel, parcel_mate, halos, odd)
    atoms, side_part = barrier((atoms, side_part))
    atoms_mate = send(atoms, over_x)
    gg, part, energy = prep([atoms, atoms_mate], corner, vb, s)

    part = part + send(part, over_x)
    part_mate = send(part, over_y)
    edges = [message.reshape(C, EDGE, S), relayed]
    vb = vb.reshape(C, ROWS, S)
    q, mix, halo_one, halo_two = make_first(s, side_part, vb, edges, inner, odd, part, part_mate)
    halos = to_pairs(halo_one, halo_two)
    mate = send(mix, over_x)
    mid, part_mate = barrier((mid, part_mate))
    mid = lax.ppermute(mid, AXES, [(d, d ^ over_y) for d in inner_ones])
    vb_mate = spread(parcel_mate).reshape(C, ROWS, S)
    part_two = side_again(mix, mate)
    base = make_base(s, mid, vb, vb_mate, q, side_part, part_two, edges, inner)
    gg = gg.reshape(2, C, ROWS, S)
    second, own, give = make_second(base, halos, gg, [part, part_mate, energy], upper, odd)

    own = own + send(give, over_x)
    for flip in (32, 36, 1, 3, 8, 24):
        own = own + lax.ppermute(own, AXES, [(d, d ^ flip) for d in range(count)])
    return turn(second, own, send(own, over_x), upper).reshape(C, C, C, S)


def solution(mesh):
    return jax.shard_map(
        per_device,
        mesh=mesh,
        in_specs=(
            P("gx", "gy", "gzs", None),
            P("gx", "gy", "gzs"),
            P(("gx", "gy", "gzs"), None),
            P(("gx", "gy", "gzs"), None, None, None),
            P(("gx", "gy", "gzs")),
        ),
        out_specs=P("gx", "gy", "gzs", None),
        check_vma=False,
    )
```

```python
import math

import jax
import jax.numpy as jnp
from jax import lax
from jax.experimental import pallas as pl
from jax.experimental.pallas import tpu as pltpu
from jax.sharding import PartitionSpec as P

AXES = ("gx", "gy", "gzs")
H = 6
C = 16
ROWS = C * C
CELLS = C * C * C
NCELLS = 32 * 32 * 512
S = 128
W = 9
R = 4
NEAR = 48
TAPS = W * W * W
F32 = jnp.float32
BF16 = jnp.bfloat16

grid_step = 0.6
filter_centre = 36.0
filter_half = 26.0


def weights():
    taps = []
    for k in range(1, 7):
        top = 2.0 * (-1) ** (k + 1) * math.factorial(6) ** 2
        under = k * k * math.factorial(6 - k) * math.factorial(6 + k)
        taps.append(top / under)
    scale = -0.5 / (grid_step * grid_step)
    off = [scale * t / filter_half for t in taps]
    diagonal = 3.0 * scale * (-2.0 * sum(taps))
    return off, diagonal


OFF, DIAGONAL = weights()


def params(mib):
    return pltpu.CompilerParams(vmem_limit_bytes=mib * 1024 * 1024)


def cost(flops, nbytes):
    return pl.CostEstimate(flops=flops, bytes_accessed=nbytes, transcendentals=0)


def sds(shape, dtype=F32):
    return jax.ShapeDtypeStruct(shape, dtype)


def split(value):
    high = value.astype(BF16)
    low = (value - high.astype(F32)).astype(BF16)
    return high, low


def mm(a, b):
    return jnp.dot(a, b, preferred_element_type=F32)


def tap_sum(at, index):
    total = None
    for k in range(1, 7):
        term = OFF[k - 1] * (at(index + k) + at(index - k))
        total = term if total is None else total + term
    return total


B = 8
STEPS = C // B
N = 2
MIDDLE = 10
EDGE = 192
MID = 64
MID_START = MIDDLE * EDGE


def stride_rows(z):
    return pl.ds(z, C, stride=C)


def plane_spec(rows=ROWS, planes=B):
    return pl.BlockSpec((planes, rows, S), lambda i: (i, 0, 0))


def halo_spec(planes=B):
    return pl.BlockSpec((H, planes, C, S), lambda i: (0, i, 0, 0))


def part_spec(part):
    return pl.BlockSpec((1, B, ROWS, S), lambda i: (part, i, 0, 0))


def whole(rows=S):
    return pl.BlockSpec((rows, S), lambda i: (0, 0))


def edge_spec(start):
    return pl.BlockSpec((N, EDGE, S), lambda i: (jnp.maximum(i - start // N, 0), 0, 0))


def for_piece(edges, inner_ref, body):
    direct = (inner_ref[0] == 1) | (pl.program_id(0) < MIDDLE // N)

    @pl.when(direct)
    def _():
        body(edges[0])

    @pl.when(jnp.logical_not(direct))
    def _():
        body(edges[1])


SCALARS = pl.BlockSpec(memory_space=pltpu.SMEM)
FULL = sds((C, ROWS, S))
FULL_ROWS = sds((CELLS, S))
HALO_ROWS = H * ROWS
MESSAGE = sds((HALO_ROWS + 2 * NEAR, S))
ATOM_ROWS = 24
HALO = sds((HALO_ROWS + 2 * ATOM_ROWS, S))
DIRECT = sds((C * EDGE, S))
RELAY = sds((C - MIDDLE, EDGE, S))


def halo_rows(x, z):
    return pl.ds(pl.multiple_of(z * ROWS + x * C, C), C)


def halves(y, half):
    return slice(y * C + half * 8, y * C + half * 8 + 8)


def pack_edges(s_ref, out_ref):
    out_ref[:, 0:96, :] = s_ref[:, 0:96, :]
    out_ref[:, 96:192, :] = s_ref[:, 160:256, :]


def by_side(odd_ref, body, one, two):
    odd = odd_ref[0] == 1

    @pl.when(odd)
    def _():
        body(one, two)

    @pl.when(jnp.logical_not(odd))
    def _():
        body(two, one)


def pack_kernel(s_ref, inner_ref, message_ref, relay_ref, mid_ref):
    step = pl.program_id(0)
    inner = inner_ref[0] == 1
    mid_ref[...] = s_ref[:, 96:160, :]

    @pl.when(step >= MIDDLE // N)
    def _():
        pack_edges(s_ref, relay_ref)

    @pl.when(inner | (step < MIDDLE // N))
    def _():
        for p in range(N):
            row = pl.multiple_of((step * N + p) * EDGE, MID)
            message_ref[pl.ds(row, 96), :] = s_ref[p, 0:96, :]
            message_ref[pl.ds(row + 96, 96), :] = s_ref[p, 160:256, :]

    @pl.when(jnp.logical_not(inner))
    def _():
        for p in range(N):
            row = pl.multiple_of(MID_START + (step * N + p) * MID, MID)
            message_ref[pl.ds(row, MID), :] = s_ref[p, 96:160, :]


def pack(s, inner):
    return pl.pallas_call(
        pack_kernel,
        grid=(C // N,),
        in_specs=[plane_spec(ROWS, N), SCALARS],
        out_specs=[whole(C * EDGE), edge_spec(MIDDLE), plane_spec(MID, N)],
        out_shape=[DIRECT, RELAY, sds((C, MID, S))],
        compiler_params=params(12),
        cost_estimate=cost(1 << 31, 6 << 20),
        name="pack",
    )(s, inner)


def pack_halos_kernel(s_ref, odd_ref, own_ref, other_ref, one_ref, two_ref):
    step = pl.program_id(0)

    @pl.when(step == 0)
    def _():
        for ref in (one_ref, two_ref):
            ref[HALO_ROWS : HALO_ROWS + ATOM_ROWS, :] = own_ref[:ATOM_ROWS, :]
            ref[HALO_ROWS + ATOM_ROWS :, :] = other_ref[:ATOM_ROWS, :]

    def halos(head_ref, tail_ref):
        for p in range(B):
            for z in range(H):
                rows = halo_rows(step * B + p, z)
                head_ref[rows, :] = s_ref[p, stride_rows(z), :]
                tail_ref[rows, :] = s_ref[p, stride_rows(C - H + z), :]

    by_side(odd_ref, halos, one_ref, two_ref)


def pack_halos(s, odd, parcel, parcel_mate):
    return pl.pallas_call(
        pack_halos_kernel,
        grid=(STEPS,),
        in_specs=[plane_spec(), SCALARS, whole(56), whole(56)],
        out_specs=[whole(HALO.shape[0])] * 2,
        out_shape=[HALO, HALO],
        compiler_params=params(12),
        cost_estimate=cost(1 << 20, 4 << 20),
        name="pack_halos",
    )(s, odd, parcel, parcel_mate)


def stack_kernel(atoms_ref, pot_ref, out_ref):
    out_ref[0:24, :] = atoms_ref[...]
    out_ref[24:56, :] = pot_ref[...]


def stack(atoms, pot):
    return pl.pallas_call(stack_kernel, out_shape=sds((56, S)), compiler_params=params(4), name="stack")(atoms, pot)


def column_kernel(own_ref, other_ref, one_ref, two_ref, odd_ref, out_ref):
    def beside(below_ref, above_ref):
        out_ref[0:48, :] = below_ref[HALO_ROWS:, :]
        out_ref[96:144, :] = above_ref[HALO_ROWS:, :]

    by_side(odd_ref, beside, one_ref, two_ref)
    out_ref[48:72, :] = own_ref[:ATOM_ROWS, :]
    out_ref[72:96, :] = other_ref[:ATOM_ROWS, :]


def column(own, other, halos, odd):
    return pl.pallas_call(
        column_kernel,
        in_specs=[pl.BlockSpec(memory_space=pltpu.VMEM)] * 4 + [SCALARS],
        out_shape=sds((144, S)),
        compiler_params=params(8),
        name="column",
    )(own, other, *halos, odd)


def along_x(s_ref, mate_ref, out_ref, add):
    def column(block, _):
        rows = pl.ds(pl.multiple_of(block * 8, 8), 8)
        ring = [mate_ref[C - H + i, rows, :] for i in range(H)]
        ring += [s_ref[x, rows, :] for x in range(C)]
        ring += [mate_ref[i, rows, :] for i in range(H)]
        for x in range(C):
            value = tap_sum(lambda i: ring[H + i], x)
            if add:
                value = value + out_ref[x, rows, :]
            out_ref[x, rows, :] = value
        return 0

    lax.fori_loop(0, ROWS // 8, column, 0)


def z_taps(ext_ref, y):
    return tap_sum(lambda k: ext_ref[y * 32 + 8 + k : y * 32 + 24 + k, :], 0)


def side_x_kernel(s_ref, mate_ref, out_ref):
    along_x(s_ref, mate_ref, out_ref, False)


def side_x(s, mate):
    return pl.pallas_call(
        side_x_kernel,
        out_shape=FULL,
        compiler_params=params(12),
        cost_estimate=cost(1 << 24, 6 << 20),
        name="side_x",
    )(s, mate)


def side_z_kernel(s_ref, part_ref, one_ref, two_ref, odd_ref, out_ref, ext_ref):
    def planes(low_ref, high_ref):
        def plane(x, _):
            for y in range(C):
                ext_ref[y * 32 + 8 : y * 32 + 24, :] = s_ref[x, y * C : (y + 1) * C, :]
            for z in range(H):
                ext_ref[pl.ds(2 + z, C, stride=32), :] = low_ref[halo_rows(x, z), :]
                ext_ref[pl.ds(24 + z, C, stride=32), :] = high_ref[halo_rows(x, z), :]
            for y in range(C):
                rows = slice(y * C, (y + 1) * C)
                out_ref[x, rows, :] = part_ref[x, rows, :] + z_taps(ext_ref, y)
            return 0

        lax.fori_loop(0, C, plane, 0)

    by_side(odd_ref, planes, one_ref, two_ref)


def side_z(s, part, halos, odd):
    return pl.pallas_call(
        side_z_kernel,
        in_specs=[pl.BlockSpec(memory_space=pltpu.VMEM)] * 4 + [SCALARS],
        out_shape=FULL,
        scratch_shapes=[pltpu.VMEM((C * 32, S), F32)],
        compiler_params=params(14),
        cost_estimate=cost(1 << 24, 8 << 20),
        name="side_z",
    )(s, part, *halos, odd)


def side_again_kernel(s_ref, mate_ref, out_ref, ext_ref):
    for y in range(C):
        ext_ref[y * 32 : y * 32 + 8, :] = jnp.zeros((8, S), F32)
        ext_ref[y * 32 + 24 : y * 32 + 32, :] = jnp.zeros((8, S), F32)

    def plane(x, _):
        for y in range(C):
            ext_ref[y * 32 + 8 : y * 32 + 24, :] = s_ref[x, y * C : (y + 1) * C, :]
        for y in range(C):
            out_ref[x, y * C : (y + 1) * C, :] = z_taps(ext_ref, y)
        return 0

    lax.fori_loop(0, C, plane, 0)
    along_x(s_ref, mate_ref, out_ref, True)


def side_again(s, mate):
    return pl.pallas_call(
        side_again_kernel,
        out_shape=FULL,
        scratch_shapes=[pltpu.VMEM((C * 32, S), F32)],
        compiler_params=params(12),
        cost_estimate=cost(1 << 25, 6 << 20),
        name="side_again",
    )(s, mate)


def tap_weight(distance):
    value = jnp.zeros(distance.shape, F32)
    for k in range(1, 7):
        value = jnp.where(distance == k, OFF[k - 1], value)
    return value


def ring_tables(coordinate):
    masks, factors = [], []
    for t in range(W):
        away = (coordinate - t) & 31
        masks.append(away == 0)
        factors.append(tap_weight(jnp.minimum(away, 32 - away)))
    return masks, factors


def spread_kernel(parcel_ref, vb_ref):
    def spread_row(row, _):
        line = (parcel_ref[pl.ds(24 + row, 1), :] + (DIAGONAL - filter_centre)) * (1.0 / filter_half)
        start = pl.multiple_of(row * 128, 128)
        vb_ref[pl.ds(start, 128), :] = jnp.broadcast_to(line, (128, 128)).T
        return 0

    lax.fori_loop(0, CELLS // 128, spread_row, 0, unroll=8)


def spread(parcel):
    return pl.pallas_call(
        spread_kernel,
        out_shape=FULL_ROWS,
        compiler_params=params(8),
        cost_estimate=cost(1 << 20, 2 << 20),
        name="spread",
    )(parcel)


def prep_kernel(*refs):
    own_ref, other_ref, corner_ref, vb_ref, s_ref, gg_ref, coef_ref, energy_ref, near_ref, table_ref = refs[:10]
    a1_ref, a1z_ref, a2_ref, a2s_ref = refs[10:]
    upper_x, upper_y = corner_ref[0] > 0, corner_ref[1] > 0
    for slab in range(3):
        own = [own_ref[slab * 48 + j * 24 : slab * 48 + j * 24 + 24, :] for j in range(2)]
        other = [other_ref[slab * 48 + j * 24 : slab * 48 + j * 24 + 24, :] for j in range(2)]
        lower = [jnp.where(upper_x, o, m) for m, o in zip(own, other)]
        higher = [jnp.where(upper_x, m, o) for m, o in zip(own, other)]
        ordered = []
        for pair in (lower, higher):
            ordered += [jnp.where(upper_y, pair[1], pair[0]), jnp.where(upper_y, pair[0], pair[1])]
        for j in range(4):
            near_ref[slab * 96 + j * 24 : slab * 96 + j * 24 + 24, :] = ordered[j]
    blank = jnp.zeros((16, 128), F32)
    for block in range(6):
        rows = near_ref[pl.ds(block, NEAR, stride=6), :]
        table_ref[block * 128 : block * 128 + 128, :] = jnp.concatenate([rows, blank, rows, blank]).T
    at = TAPS + 3 - 640
    energy_ref[...] = jnp.broadcast_to(rows[:, at : at + 1] * (1.0 / filter_half), (NEAR, S))

    shape = (8, 128)
    sub = lax.broadcasted_iota(jnp.int32, shape, 0)
    lane = lax.broadcasted_iota(jnp.int32, shape, 1)
    first_lanes = lane < 64
    sites = [jnp.broadcast_to(table_ref[TAPS + d : TAPS + d + 1, :], shape).astype(jnp.int32) for d in range(3)]
    px = sites[0] - corner_ref[0]
    py = sites[1] - corner_ref[1]
    pz = (sites[2] & 15) + (((lane & 63) >> 4) - 1) * C
    zero = jnp.zeros(shape, F32)

    dz = sub + (lane >> 6) * 8 - pz + R
    z_masks = [dz == t for t in range(W)]
    z_factors = [tap_weight(jnp.abs(dz - t)) for t in range(W)]

    def place_z(ij, _):
        acc = zero
        along = zero
        for t in range(W):
            row = jnp.broadcast_to(table_ref[pl.ds(ij * W + t, 1), :], shape)
            acc = jnp.where(z_masks[t], row, acc)
            along = along + z_factors[t] * row
        a1_ref[ij] = acc
        a1z_ref[ij] = along
        return 0

    lax.fori_loop(0, W * W, place_z, 0, unroll=3)

    def place_y(y, _):
        masks, factors = ring_tables(y - py + R)
        for i in range(W):
            acc = zero
            along = zero
            moved = zero
            for t in range(W):
                value = a1_ref[i * W + t]
                acc = jnp.where(masks[t], value, acc)
                along = along + factors[t] * value
                moved = jnp.where(masks[t], a1z_ref[i * W + t], moved)
            a2_ref[i, y] = acc
            a2s_ref[i, y] = along + moved
        return 0

    lax.fori_loop(0, C, place_y, 0)

    def place_x(x, _):
        masks, factors = ring_tables(x - px + R)

        def per_y(y, _):
            row = pl.multiple_of(x * ROWS + y * C, C)
            acc = zero
            along = zero
            moved = zero
            for t in range(W):
                value = a2_ref[t, y]
                acc = jnp.where(masks[t], value, acc)
                along = along + factors[t] * value
                moved = jnp.where(masks[t], a2s_ref[t, y], moved)
            v = vb_ref[pl.ds(row, C), :]
            moved = along + moved + jnp.where(first_lanes, v[:8], v[8:]) * acc
            lower = jnp.where(first_lanes, acc, pltpu.roll(moved, 64, 1))
            upper = jnp.where(first_lanes, pltpu.roll(acc, 64, 1), moved)
            high, low = split(jnp.concatenate([lower, upper], axis=0))
            gg_ref[0, pl.ds(row, C), :] = high
            gg_ref[1, pl.ds(row, C), :] = low
            return 0

        lax.fori_loop(0, C, per_y, 0, unroll=16)
        return 0

    lax.fori_loop(0, C, place_x, 0)

    coef_ref[...] = jnp.zeros((3, NEAR, S), F32)

    def contract(x, _):
        rows = pl.ds(pl.multiple_of(x * 2 * ROWS, ROWS), 2 * ROWS)
        g_high, g_low = gg_ref[0, rows, :], gg_ref[1, rows, :]
        t_high, t_low = g_high.T, g_low.T
        high, low = split(s_ref[rows, :])
        got = mm(t_high, high) + (mm(t_high, low) + mm(t_low, high))
        t_high, t_low = t_high[:NEAR], t_low[:NEAR]
        pair = mm(t_high, g_high) + (mm(t_high, g_low) + mm(t_low, g_high))
        for slab in range(3):
            rows = slice(slab * C, slab * C + C)
            coef_ref[slab, 0:16] += got[rows]
            coef_ref[slab, 16:32] += got[64 + slab * C : 80 + slab * C]
            coef_ref[slab, 32:48] += pair[rows]
        return 0

    lax.fori_loop(0, C // 2, contract, 0, unroll=2)


def prep(parcels, corner, vb, s):
    vmem = pl.BlockSpec(memory_space=pltpu.VMEM)
    return pl.pallas_call(
        prep_kernel,
        in_specs=[vmem] * 2 + [pl.BlockSpec(memory_space=pltpu.SMEM), vmem, vmem],
        out_shape=[sds((2, CELLS, S), BF16), sds((3, NEAR, S)), sds((NEAR, S))],
        scratch_shapes=[
            pltpu.VMEM((288, 128), F32),
            pltpu.VMEM((768, 128), F32),
            pltpu.VMEM((W * W, 8, 128), F32),
            pltpu.VMEM((W * W, 8, 128), F32),
            pltpu.VMEM((W, C, 8, 128), F32),
            pltpu.VMEM((W, C, 8, 128), F32),
        ],
        compiler_params=params(16),
        cost_estimate=cost(1 << 27, 10 << 20),
        name="prep",
    )(*parcels, corner, vb, s.reshape(CELLS, S))


def move_pair(shares, away):
    lane = lax.broadcasted_iota(jnp.int32, (16, 128), 1)
    keep = (lane < 32) if away < 0 else (lane >= 16) & (lane < 48)
    pair = jnp.where(keep, pltpu.roll(shares[32:48], (away * 16) % 128, 1), 0.0)
    return jnp.concatenate([shares[0:32], pair])


def first_kernel(s_ref, side_ref, vb_ref, *refs):
    inner_ref, odd_ref, part_ref, mate_ref, q_ref, mix_ref, one_ref, two_ref = refs[2:]
    step = pl.program_id(0)

    @pl.when(step == 0)
    def _():
        def shares(head_ref, tail_ref):
            for j in range(2):
                rows = slice(HALO_ROWS + j * NEAR, HALO_ROWS + (j + 1) * NEAR)
                head_ref[rows, :] = part_ref[j] + mate_ref[j]
                tail_ref[rows, :] = part_ref[j + 1] + mate_ref[j + 1]

        by_side(odd_ref, shares, one_ref, two_ref)

    def planes(edge_ref):
        for p in range(N):
            for half in range(2):
                ring = {y: s_ref[p, halves(y, half), :] for y in range(C)}
                for y in range(H):
                    ring[C + y] = edge_ref[p, halves(y, half), :]
                    ring[y - H] = edge_ref[p, halves(H + y, half), :]
                for y in range(C):
                    rows = halves(y, half)
                    dy = tap_sum(lambda i: ring[i], y)
                    q = dy + vb_ref[p, rows, :] * ring[y]
                    q_ref[p, rows, :] = q
                    mix_ref[p, rows, :] = side_ref[p, rows, :] + q + dy

    for_piece(refs[:2], inner_ref, planes)

    def halos(head_ref, tail_ref):
        for p in range(N):
            for z in range(H):
                rows = halo_rows(step * N + p, z)
                head_ref[rows, :] = mix_ref[p, stride_rows(z), :]
                tail_ref[rows, :] = mix_ref[p, stride_rows(C - H + z), :]

    by_side(odd_ref, halos, one_ref, two_ref)


def make_first(s, side_part, vb, edges, inner, odd, part, part_mate):
    shares = pl.BlockSpec((3, NEAR, S), lambda i: (0, 0, 0))
    return pl.pallas_call(
        first_kernel,
        grid=(C // N,),
        in_specs=[plane_spec(ROWS, N)] * 3 + [edge_spec(0), edge_spec(MIDDLE)] + [SCALARS] * 2 + [shares] * 2,
        out_specs=[plane_spec(ROWS, N), plane_spec(ROWS, N), whole(MESSAGE.shape[0]), whole(MESSAGE.shape[0])],
        out_shape=[FULL, FULL, MESSAGE, MESSAGE],
        compiler_params=params(16),
        cost_estimate=cost(1 << 24, 14 << 20),
        name="first",
    )(s, side_part, vb, *edges, inner, odd, part, part_mate)


def base_kernel(s_ref, mid_ref, vb_ref, vb_mate_ref, q_ref, side_ref, part_ref, *refs):
    inner_ref, message_ref, out_ref, middle_ref = refs[2:]
    step = pl.program_id(0)
    inner = inner_ref[0] == 1

    @pl.when(inner)
    def _():
        middle_ref[...] = mid_ref[...]

    @pl.when(jnp.logical_not(inner))
    def _():
        for p in range(N):
            middle_ref[p] = message_ref[pl.ds(pl.multiple_of(MID_START + (step * N + p) * MID, MID), MID), :]

    def planes(edge_ref):
        for p in range(N):
            for half in range(2):

                def other(y, p=p, half=half):
                    if y < H:
                        return edge_ref[p, halves(y, half), :]
                    if y < C - H:
                        return middle_ref[p, halves(y - H, half), :]
                    return edge_ref[p, halves(y - 4, half), :]

                ring = [s_ref[p, halves(y, half), :] for y in range(C)] + [other(y) for y in range(C)]
                q = {y: q_ref[p, halves(y, half), :] for y in range(C)}
                for y in list(range(H)) + list(range(C - H, C)):
                    v = vb_mate_ref[p, halves(y, half), :]
                    q[C + y] = tap_sum(lambda i: ring[i % 32], C + y) + v * ring[C + y]
                for y in range(C):
                    rows = halves(y, half)
                    total = tap_sum(lambda i: q[i % 32], y)
                    total = total + vb_ref[p, rows, :] * (side_ref[p, rows, :] + q[y])
                    out_ref[p, rows, :] = 2.0 * (total + part_ref[p, rows, :]) - ring[y]

    for_piece(refs[:2], inner_ref, planes)


def make_base(s, mid, vb, vb_mate, q, side_part, part, edges, inner):
    return pl.pallas_call(
        base_kernel,
        grid=(C // N,),
        in_specs=[plane_spec(ROWS, N), plane_spec(MID, N)]
        + [plane_spec(ROWS, N)] * 5
        + [edge_spec(0), edge_spec(MIDDLE), SCALARS, whole(C * EDGE)],
        out_specs=plane_spec(ROWS, N),
        out_shape=FULL,
        scratch_shapes=[pltpu.VMEM((N, MID, S), F32)],
        compiler_params=params(16),
        cost_estimate=cost(1 << 25, 16 << 20),
        name="base",
    )(s, mid, vb, vb_mate, q, side_part, part, *edges, inner, edges[0].reshape(-1, S))


def second_kernel(base_ref, one_ref, two_ref, gg_high_ref, gg_low_ref, *rest):
    part_ref, mate_ref, energy_ref, upper_ref, odd_ref, second_ref, keep_ref, give_ref, gram_ref, cross_ref, w_ref, halo_ref = rest
    step = pl.program_id(0)

    @pl.when(step == 0)
    def _():
        gram_ref[...] = jnp.zeros((S, S), F32)
        cross_ref[...] = jnp.zeros((S, S), F32)
        w_ref[...] = jnp.zeros((S, S), F32)
        halo_ref[...] = jnp.zeros((B, ROWS, S), F32)
        mine = [part_ref[j] + mate_ref[j] for j in range(3)]
        odd = odd_ref[0] == 1
        got = [[ref[HALO_ROWS + j * NEAR : HALO_ROWS + (j + 1) * NEAR, :] for j in range(2)] for ref in (one_ref, two_ref)]
        below = [move_pair(jnp.where(odd, a, b), -1) for a, b in zip(*got)]
        above = [move_pair(jnp.where(odd, b, a), 1) for a, b in zip(*got)]
        slabs = [mine[0] + below[0], mine[1] + below[1] + above[0], mine[2] + above[1]]
        near = jnp.concatenate([slab[0:16] for slab in slabs]) * energy_ref[...]
        lane = lax.broadcasted_iota(jnp.int32, (NEAR, S), 1)
        pair = jnp.where(lane < NEAR, jnp.concatenate([slab[32:48] for slab in slabs]), 0.0)
        two = jnp.concatenate([slab[16:32] for slab in slabs])
        two = two + exact(pair, jnp.concatenate([near, jnp.zeros((S - NEAR, S), F32)]))
        w_ref[0:NEAR, :] = 2.0 * energy_ref[...] * two
        w_ref[64 : 64 + NEAR, :] = 2.0 * near

    def halo_part(low_ref, high_ref):
        for p in range(B):
            low = [low_ref[halo_rows(step * B + p, j), :] for j in range(H)]
            high = [high_ref[halo_rows(step * B + p, j), :] for j in range(H)]
            for z in range(H):
                add = sum((2.0 * OFF[k - 1]) * low[z - k + H] for k in range(z + 1, H + 1))
                halo_ref[p, stride_rows(z), :] = add
                add = sum((2.0 * OFF[H + j - z - 1]) * high[j] for j in range(z + 1))
                halo_ref[p, stride_rows(C - H + z), :] = add

    by_side(odd_ref, halo_part, one_ref, two_ref)

    w_high, w_low = split(w_ref[...])
    w_twice = jnp.concatenate([w_high, w_high])
    gram = jnp.zeros((S, 2 * S), F32)
    for p in range(B):
        g_high, g_low = gg_high_ref[0, p], gg_low_ref[0, p]
        near = mm(jnp.concatenate([g_high, g_low], axis=1), w_twice) + mm(g_high, w_low)
        value = base_ref[p] + halo_ref[p] + near
        second_ref[p] = value
        s_high, s_low = split(value)
        gram += mm(s_high.T, jnp.concatenate([s_high, s_low], axis=1))
    gram_ref[...] += gram[:, :S]
    cross_ref[...] += gram[:, S:]

    @pl.when(step == STEPS - 1)
    def _():
        cross = cross_ref[...]
        gram = (gram_ref[...] + (cross + cross.T)) * (1.0 / NCELLS)
        upper = upper_ref[0] == 1
        keep_ref[...] = jnp.where(upper, gram[S // 2 :], gram[: S // 2])
        give_ref[...] = jnp.where(upper, gram[: S // 2], gram[S // 2 :])


def make_second(base, halos, gg, shares, upper, odd):
    three = pl.BlockSpec((3, NEAR, S), lambda i: (0, 0, 0))
    return pl.pallas_call(
        second_kernel,
        grid=(STEPS,),
        in_specs=[plane_spec()]
        + [whole(MESSAGE.shape[0])] * 2
        + [part_spec(0), part_spec(1), three, three, whole(NEAR), SCALARS, SCALARS],
        out_specs=[plane_spec(), whole(S // 2), whole(S // 2)],
        out_shape=[FULL, sds((S // 2, S)), sds((S // 2, S))],
        scratch_shapes=[pltpu.VMEM((S, S), F32)] * 3 + [pltpu.VMEM((B, ROWS, S), F32)],
        compiler_params=params(16),
        cost_estimate=cost(1 << 27, 8 << 20),
        name="second",
    )(base, *halos, gg, gg, *shares, upper, odd)


def exact(a, b):
    return jnp.dot(a, b, precision=lax.Precision.HIGHEST, preferred_element_type=F32)


def close(a, b):
    a_high, a_low = split(a)
    b_high, b_low = split(b)
    return mm(jnp.concatenate([a_high, a_low], axis=1), jnp.concatenate([b_high, b_high])) + mm(a_high, b_low)


def inverse_factor(gram_ref, a_ref, x_ref, state_ref):
    row = lax.broadcasted_iota(jnp.int32, (S, S), 0)
    column = lax.broadcasted_iota(jnp.int32, (S, S), 1)
    unit = jnp.where(row == column, 1.0, 0.0)
    gram = gram_ref[...]
    diagonal = jnp.where(row == column, gram, 0.0)
    down = lax.rsqrt(jnp.sum(diagonal, axis=1, keepdims=True))
    across = lax.rsqrt(jnp.sum(diagonal, axis=0, keepdims=True))
    a_ref[...] = gram * down * across
    x_ref[...] = unit

    def residual():
        x = x_ref[...]
        return unit - close(close(x, a_ref[...]), x.T)

    def size(e):
        return jnp.sum(e * e)

    def improve(e):
        lower = jnp.where(row > column, e, jnp.where(row == column, 0.5 * e, 0.0))
        x_ref[...] += close(lower, x_ref[...])

    state_ref[0] = 0
    start = unit - a_ref[...]
    start_size = size(start)

    @pl.when(start_size < 0.16)
    def _():
        improve(start)
        state_ref[0] = jnp.where(start_size < 1e-6, 2, 1)

    for _ in range(5):

        @pl.when(state_ref[0] == 1)
        def _():
            e = residual()
            e_size = size(e)
            improve(e)
            state_ref[0] = jnp.where(e_size < 1e-6, 2, 1)

    @pl.when(state_ref[0] != 2)
    def _():
        x_ref[...] = unit
        lanes = lax.broadcasted_iota(jnp.int32, (1, S), 1)

        def step(j, _):
            line = a_ref[pl.ds(j, 1), :]
            scale = lax.rsqrt(jnp.sum(jnp.where(lanes == j, line, 0.0), axis=1, keepdims=True))
            a = a_ref[...]
            factor = jnp.sum(jnp.where(column == j, a, 0.0), axis=1, keepdims=True) * scale
            factor = jnp.where(row[:, :1] > j, factor, 0.0)
            x_line = x_ref[pl.ds(j, 1), :] * scale
            a_ref[...] = a - factor * (line * scale)
            x_ref[...] = jnp.where(row == j, x_line, x_ref[...] - factor * x_line)
            return 0

        lax.fori_loop(0, S, step, 0)

    x_ref[...] = x_ref[...] * across


def turn_kernel(second_ref, own_ref, other_ref, upper_ref, out_ref, gram_ref, a_ref, x_ref, i_high_ref, i_low_ref, state_ref):
    @pl.when(pl.program_id(0) == 0)
    def _():
        upper = upper_ref[0] == 1
        gram_ref[: S // 2, :] = jnp.where(upper, other_ref[...], own_ref[...])
        gram_ref[S // 2 :, :] = jnp.where(upper, own_ref[...], other_ref[...])
        inverse_factor(gram_ref, a_ref, x_ref, state_ref)
        i_high, i_low = split(x_ref[...].T)
        i_high_ref[...] = i_high
        i_low_ref[...] = i_low

    i_high, i_low = i_high_ref[...], i_low_ref[...]
    i_twice = jnp.concatenate([i_high, i_high])
    for p in range(B):
        high, low = split(second_ref[p])
        out_ref[p] = mm(jnp.concatenate([high, low], axis=1), i_twice) + mm(high, i_low)


def turn(second, own, other, upper):
    return pl.pallas_call(
        turn_kernel,
        grid=(STEPS,),
        in_specs=[plane_spec(), whole(S // 2), whole(S // 2), SCALARS],
        out_specs=plane_spec(),
        out_shape=FULL,
        scratch_shapes=[pltpu.VMEM((S, S), F32)] * 3 + [pltpu.VMEM((S, S), BF16)] * 2 + [pltpu.SMEM((1,), jnp.int32)],
        compiler_params=params(16),
        cost_estimate=cost(1 << 28, 4 << 20),
        name="turn",
    )(second, own, other, upper)


def per_device(states, potential, atom_sites, projectors, energies):
    gx, gy = lax.axis_index("gx"), lax.axis_index("gy")
    depth = lax.axis_size("gzs")
    count = 4 * depth
    barrier = lax.optimization_barrier

    def send(value, flip):
        return lax.ppermute(value, AXES, [(d, d ^ flip) for d in range(count)])

    over_x, over_y = 2 * depth, depth

    def to_pairs(one, two):
        near = [(d, d ^ 1) for d in range(count)]
        far = [(d, d // depth * depth + (d + (1 if d % 2 else -1)) % depth) for d in range(count)]
        return lax.ppermute(one, AXES, near), lax.ppermute(two, AXES, far)

    inner_ones = [d for d in range(count) if d % 4 in (1, 2)]
    outer_ones = [d for d in range(count) if d % 4 in (0, 3)]
    inner = ((lax.axis_index("gzs") + 1) // 2 % 2).astype(jnp.int32).reshape(1)
    s = states.reshape(C, ROWS, S)
    mate = send(s, over_x)
    corner = jnp.stack([gx * C, gy * C]).astype(jnp.int32)
    upper = gx.astype(jnp.int32).reshape(1)
    odd = (lax.axis_index("gzs") % 2).astype(jnp.int32).reshape(1)
    pot = potential.reshape(32, 128)
    atoms = jnp.concatenate(
        [projectors.reshape(4, TAPS), atom_sites.astype(F32), energies[:, None], jnp.zeros((4, 768 - TAPS - 4), F32)],
        axis=1,
    ).reshape(24, 128)
    pot, corner, upper, inner, odd, atoms = barrier((pot, corner, upper, inner, odd, atoms))
    parcel = stack(atoms, pot)
    to_pack, parcel = barrier((s, parcel))
    parcel_mate = send(parcel, over_y)
    message, relay, mid = pack(to_pack, inner)
    parcel_mate, message, relay = barrier((parcel_mate, message, relay))
    halo_one, halo_two = pack_halos(s, odd, parcel, parcel_mate)
    message = send(message, over_y)
    relayed = lax.ppermute(relay, AXES, [(d, d ^ over_y ^ 1) for d in outer_ones])
    halos = to_pairs(halo_one, halo_two)
    vb = spread(parcel)
    mate, relayed = barrier((mate, relayed))
    beside = side_x(s, mate)
    halos, beside, vb = barrier((halos, beside, vb))
    relayed = lax.ppermute(relayed, AXES, [(d, d ^ 1) for d in inner_ones])
    side_part = side_z(s, beside, halos, odd)
    atoms = column(parcel, parcel_mate, halos, odd)
    atoms, side_part = barrier((atoms, side_part))
    atoms_mate = send(atoms, over_x)
    gg, part, energy = prep([atoms, atoms_mate], corner, vb, s)

    part = part + send(part, over_x)
    part_mate = send(part, over_y)
    edges = [message.reshape(C, EDGE, S), relayed]
    vb = vb.reshape(C, ROWS, S)
    q, mix, halo_one, halo_two = make_first(s, side_part, vb, edges, inner, odd, part, part_mate)
    halos = to_pairs(halo_one, halo_two)
    mate = send(mix, over_x)
    mid, part_mate = barrier((mid, part_mate))
    mid = lax.ppermute(mid, AXES, [(d, d ^ over_y) for d in inner_ones])
    vb_mate = spread(parcel_mate).reshape(C, ROWS, S)
    part_two = side_again(mix, mate)
    base = make_base(s, mid, vb, vb_mate, q, side_part, part_two, edges, inner)
    gg = gg.reshape(2, C, ROWS, S)
    second, own, give = make_second(base, halos, gg, [part, part_mate, energy], upper, odd)

    own = own + send(give, over_x)
    for flip in (1, 3, 8, 24, 32, 36):
        own = own + lax.ppermute(own, AXES, [(d, d ^ flip) for d in range(count)])
    return turn(second, own, send(own, over_x), upper).reshape(C, C, C, S)


def solution(mesh):
    return jax.shard_map(
        per_device,
        mesh=mesh,
        in_specs=(
            P("gx", "gy", "gzs", None),
            P("gx", "gy", "gzs"),
            P(("gx", "gy", "gzs"), None),
            P(("gx", "gy", "gzs"), None, None, None),
            P(("gx", "gy", "gzs")),
        ),
        out_specs=P("gx", "gy", "gzs", None),
        check_vma=False,
    )
```
